32 devices in a mesh: dp: 16 (over z, x, core), mp: 2 (over y).
Axes of the slice: x: 2, y: 2, z: 4, core: 2. Of those that a mesh axis runs over, the one named last changes fastest.
Arguments:
- tokens: bfloat16 [16, 1024, 768], P('dp'), may hold values from -6 to 6
- teacher_tokens: bfloat16 [16, 1024, 768], P('dp'), may hold values from -6 to 6
- cotangent: bfloat16 [16, 1024, 768], P('dp')
- lengths: int32 [16], P('dp'), may hold values from 256 to 1024, as said below
- masked: int32 [16, 128], P('dp'), may hold values from 0 to 1023, as said below
- attn_weight: float32 [3, 768, 768], P(None, 'dp', 'mp')
- out_weight: float32 [768, 768], P('mp', 'dp')
- up_weight: float32 [768, 3072], P('dp', 'mp')
- down_weight: float32 [3072, 768], P('mp', 'dp')
- attn_first: float32 [3, 768, 768], P(None, 'dp', 'mp')
- out_first: float32 [768, 768], P('mp', 'dp')
- up_first: float32 [768, 3072], P('dp', 'mp')
- down_first: float32 [3072, 768], P('mp', 'dp')
- attn_second: float32 [3, 768, 768], P(None, 'dp', 'mp'), may hold values from 1.024 to 4.096
- out_second: float32 [768, 768], P('mp', 'dp'), may hold values from 0.65536 to 2.62144
- up_second: float32 [768, 3072], P('dp', 'mp'), may hold values from 1.024 to 4.096
- down_second: float32 [3072, 768], P('mp', 'dp'), may hold values from 4.9152 to 19.6608
- vectors: float32 [9216], replicated, as said below
- vector_first: float32 [9216], replicated, may hold values from -64 to 64
- vector_second: float32 [9216], replicated, may hold values from 8.192 to 32.768
- teacher_attn: bfloat16 [3, 768, 768], P(None, 'dp', 'mp'), may hold values from -0.3125 to 0.3125
- teacher_out: bfloat16 [768, 768], P('mp', 'dp'), may hold values from -0.75 to 0.75
- teacher_up: bfloat16 [768, 3072], P('dp', 'mp'), may hold values from -0.21875 to 0.21875
- teacher_down: bfloat16 [3072, 768], P('mp', 'dp'), may hold values from -0.109375 to 0.109375
- teacher_vectors: bfloat16 [9216], replicated, as said below
Outputs:
- student_out: bfloat16 [16, 1024, 768], P('dp')
- input_grad: float32 [16, 1024, 768], P('dp')
- attn_updated: float32 [3, 768, 768], P(None, 'dp', 'mp')
- out_updated: float32 [768, 768], P('mp', 'dp')
- up_updated: float32 [768, 3072], P('dp', 'mp')
- down_updated: float32 [3072, 768], P('mp', 'dp')
- attn_moment: float32 [3, 768, 768], P(None, 'dp', 'mp')
- out_moment: float32 [768, 768], P('mp', 'dp')
- up_moment: float32 [768, 3072], P('dp', 'mp')
- down_moment: float32 [3072, 768], P('mp', 'dp')
- attn_square: float32 [3, 768, 768], P(None, 'dp', 'mp')
- out_square: float32 [768, 768], P('mp', 'dp')
- up_square: float32 [768, 3072], P('dp', 'mp')
- down_square: float32 [3072, 768], P('mp', 'dp')
- vector_moment: float32 [9216], replicated
- vector_square: float32 [9216], replicated
- vector_updated: float32 [9216], replicated
- matrix_norms: float32 [2, 6], replicated
- trust_ratios: float32 [6], replicated
The draws below stay inside these ranges and needn't reach their ends.
Inputs may be any that keep to these rules, and one draw needn't show every extreme that they name: `lengths`: keys at or past a sequence's length are padding and take no attention; some sequence is full in every draw. `masked`: each position lies below its sequence's length; positions may repeat. `vectors`: gains near one, biases of either sign. `teacher_vectors`: gains near one, biases of either sign.
All inputs are finite; a program needn't handle non-finite values.
Results may differ from the reference program's by a relative error of at most 0.014.
The reference program's roundings to bfloat16 on the way count: a program that leaves them out, or rounds other values in their place, can miss the bound.
Values may be sent and summed in bfloat16 or wider, within the bound.
A program may use at most 128 MiB of HBM per device.

```python
import math
import jax
import jax.numpy as jnp
from jax import lax

D = 768
HEADS = 12
HDIM = 64
FF = 3072
LEN = 1024
NMASK = 128
STEP = 5
SEQS = 16
TOKENS = 16384
VEC = 9216


def ramp_level(shape_all, dim_axis, top_scale):
    line_count = shape_all[dim_axis]
    position = jnp.arange(line_count, dtype=jnp.float32) / max(line_count - 1, 1)
    level_row = (1.0 + (top_scale - 1.0) * position) / jnp.sqrt((top_scale * top_scale + top_scale + 1.0) / 3.0)
    return level_row.reshape(tuple((line_count if place_now == dim_axis else 1 for place_now in range(len(shape_all)))))


def apply_rise(base_draw, dim_axis, top_scale, scale_now):
    return base_draw * scale_now * ramp_level(base_draw.shape, dim_axis, top_scale)


def length_draw(key):
    key = jax.random.fold_in(key, 41)
    key_len, key_pick = jax.random.split(key)
    counts_all = jax.random.randint(key_len, (SEQS,), LEN // 4, LEN + 1)
    chosen = jax.random.randint(key_pick, (), 0, SEQS)
    counts_all = jnp.where(jnp.arange(SEQS) == chosen, LEN, counts_all)
    return (counts_all.astype(jnp.int32), chosen)


def vector_pack(key):
    key_noise, key_gain, key_hidden = jax.random.split(key, 3)
    noise_rows = jax.random.normal(key_noise, (8, D), jnp.float32) * 0.2
    gain_rows = 1.0 + jax.random.uniform(key_gain, (8, D), jnp.float32, -0.4, 0.4)
    choose_gain = jnp.array([0.0, 0.0, 0.0, 1.0, 0.0, 0.0, 1.0, 0.0], jnp.float32).reshape(8, 1)
    packed_rows = choose_gain * gain_rows + (1.0 - choose_gain) * noise_rows
    hidden_bias = jax.random.normal(key_hidden, (FF,), jnp.float32) * 0.2
    return jnp.concatenate([packed_rows.reshape(8 * D), hidden_bias])


def draw_lengths(key, part):
    counts_all, chosen = length_draw(key)
    key = jax.random.fold_in(key, 3)
    return counts_all


def draw_masked(key, part):
    counts_all, chosen = length_draw(key)
    key = jax.random.fold_in(key, 5)
    raw_bits = jax.random.randint(key, (SEQS, NMASK), 0, 1073741824)
    positions = raw_bits % counts_all[:, None]
    corner = (jnp.arange(SEQS)[:, None] == chosen) & (jnp.arange(NMASK)[None, :] == 0)
    return jnp.where(corner, LEN - 1, positions).astype(jnp.int32)


def draw_cotangent(key, part):
    key = jax.random.fold_in(key, 7)
    shape_all = (SEQS, LEN, D)
    base_draw = jax.random.normal(key, shape_all, jnp.float32)
    top_scale = 3.0
    return apply_rise(base_draw, 0, top_scale, 1.0).astype(jnp.bfloat16)


def draw_attn_weight(key, part):
    key = jax.random.fold_in(key, 11)
    shape_all = (3, D, D)
    base_draw = jax.random.normal(key, shape_all, jnp.float32)
    top_scale = 3.0
    fan_scale = jnp.sqrt(jnp.array([2.0 / D, 2.0 / D, 1.0 / D], jnp.float32)).reshape(3, 1, 1)
    return apply_rise(base_draw * fan_scale, 1, top_scale, 1.0)


def draw_out_weight(key, part):
    key = jax.random.fold_in(key, 13)
    shape_all = (D, D)
    base_draw = jax.random.normal(key, shape_all, jnp.float32)
    top_scale = 3.0
    return apply_rise(base_draw, 1, top_scale, HDIM ** (-0.5))


def draw_up_weight(key, part):
    key = jax.random.fold_in(key, 17)
    shape_all = (D, FF)
    base_draw = jax.random.normal(key, shape_all, jnp.float32)
    top_scale = 3.0
    return apply_rise(base_draw, 0, top_scale, D ** (-0.5))


def draw_down_weight(key, part):
    key = jax.random.fold_in(key, 19)
    shape_all = (FF, D)
    base_draw = jax.random.normal(key, shape_all, jnp.float32)
    top_scale = 3.0
    return apply_rise(base_draw, 1, top_scale, FF ** (-0.5))


def draw_attn_first(key, part):
    key = jax.random.fold_in(key, 23)
    shape_all = (3, D, D)
    base_draw = jax.random.normal(key, shape_all, jnp.float32)
    top_scale = 3.0
    return apply_rise(base_draw, 1, top_scale, 0.028 * (SEQS * LEN) ** 0.5)


def draw_out_first(key, part):
    key = jax.random.fold_in(key, 29)
    shape_all = (D, D)
    base_draw = jax.random.normal(key, shape_all, jnp.float32)
    top_scale = 3.0
    return apply_rise(base_draw, 1, top_scale, 0.022 * (SEQS * LEN) ** 0.5)


def draw_up_first(key, part):
    key = jax.random.fold_in(key, 31)
    shape_all = (D, FF)
    base_draw = jax.random.normal(key, shape_all, jnp.float32)
    top_scale = 3.0
    return apply_rise(base_draw, 0, top_scale, 0.028 * (SEQS * LEN) ** 0.5)


def draw_down_first(key, part):
    key = jax.random.fold_in(key, 37)
    shape_all = (FF, D)
    base_draw = jax.random.normal(key, shape_all, jnp.float32)
    top_scale = 3.0
    return apply_rise(base_draw, 1, top_scale, 0.061 * (SEQS * LEN) ** 0.5)


def draw_vectors(key, part):
    key = jax.random.fold_in(key, 43)
    return vector_pack(key)


def draw_teacher_vectors(key, part):
    key = jax.random.fold_in(key, 47)
    return vector_pack(key).astype(jnp.bfloat16)


def shard_levels(own_key, dims, shards, low, largest):
    def one(axis_at, shards_of):
        steps = jax.random.uniform(jax.random.fold_in(jax.random.fold_in(own_key, 6), axis_at), (shards_of,), jnp.float32, low / len(shards), largest / len(shards))
        return jnp.repeat(jnp.exp(steps), dims[axis_at] // shards_of).reshape((-1,) + (1,) * (len(dims) - axis_at - 1))

    loudness = one(*shards[0])
    for cut in shards[1:]:
        loudness = loudness * one(*cut)
    return loudness


def gaussian(key, shape, scale, bound, shards=(), kind=jnp.bfloat16):
    entries = scale * jax.random.normal(key, shape, jnp.float32)
    if shards:
        entries = entries * shard_levels(key, shape, shards, -0.22, 0.18)
    return jnp.clip(entries, -bound, bound).astype(kind)


def setup_inputs(seed: int = 0) -> dict:
    key_list = jax.random.split(jax.random.key(seed), 26)
    return {
        "tokens": gaussian(key_list[0], (SEQS, LEN, D), 1.0, 6.0, ((0, 16),)),
        "teacher_tokens": gaussian(key_list[1], (SEQS, LEN, D), 1.0, 6.0, ((0, 16),)),
        "cotangent": draw_cotangent(jax.random.fold_in(key_list[25], 71), 0),
        "lengths": draw_lengths(jax.random.fold_in(key_list[25], 71), 0),
        "masked": draw_masked(jax.random.fold_in(key_list[25], 71), 0),
        "attn_weight": draw_attn_weight(jax.random.fold_in(key_list[25], 71), 0),
        "out_weight": draw_out_weight(jax.random.fold_in(key_list[25], 71), 0),
        "up_weight": draw_up_weight(jax.random.fold_in(key_list[25], 71), 0),
        "down_weight": draw_down_weight(jax.random.fold_in(key_list[25], 71), 0),
        "attn_first": draw_attn_first(jax.random.fold_in(key_list[25], 71), 0),
        "out_first": draw_out_first(jax.random.fold_in(key_list[25], 71), 0),
        "up_first": draw_up_first(jax.random.fold_in(key_list[25], 71), 0),
        "down_first": draw_down_first(jax.random.fold_in(key_list[25], 71), 0),
        "attn_second": jnp.clip(jnp.exp(math.log(4.096) - 1.3862944 * jax.random.uniform(key_list[13], (3, D, D), jnp.float32) ** shard_levels(key_list[13], (3, D, D), ((1, 16), (2, 2)), -0.2, 0.2)), 1.024, 4.096),
        "out_second": jnp.clip(jnp.exp(math.log(2.62144) - 1.3862944 * jax.random.uniform(key_list[14], (D, D), jnp.float32) ** shard_levels(key_list[14], (D, D), ((0, 2), (1, 16)), -0.2, 0.2)), 0.65536, 2.62144),
        "up_second": jnp.clip(jnp.exp(math.log(4.096) - 1.3862944 * jax.random.uniform(key_list[15], (D, FF), jnp.float32) ** shard_levels(key_list[15], (D, FF), ((0, 16), (1, 2)), -0.2, 0.2)), 1.024, 4.096),
        "down_second": jnp.clip(jnp.exp(math.log(19.6608) - 1.3862944 * jax.random.uniform(key_list[16], (FF, D), jnp.float32) ** shard_levels(key_list[16], (FF, D), ((0, 2), (1, 16)), -0.2, 0.2)), 4.9152, 19.6608),
        "vectors": draw_vectors(jax.random.fold_in(key_list[25], 71), 0),
        "vector_first": gaussian(key_list[18], (VEC,), (0.078 * TOKENS ** 0.5), 64.0, (), jnp.float32),
        "vector_second": jnp.clip(jnp.exp(jax.random.uniform(key_list[19], (VEC,), jnp.float32, math.log(8.192), math.log(32.768))), 8.192, 32.768),
        "teacher_attn": gaussian(key_list[20], (3, D, D), (D // 2) ** -0.5, 0.3125, ((1, 16), (2, 2))),
        "teacher_out": gaussian(key_list[21], (D, D), HDIM ** -0.5, 0.75, ((0, 2), (1, 16))),
        "teacher_up": gaussian(key_list[22], (D, FF), D ** -0.5, 0.21875, ((0, 16), (1, 2))),
        "teacher_down": gaussian(key_list[23], (FF, D), FF ** -0.5, 0.109375, ((0, 2), (1, 16))),
        "teacher_vectors": draw_teacher_vectors(jax.random.fold_in(key_list[25], 71), 0),
    }


@jax.custom_vjp
def low(v):
    return lax.optimization_barrier(v.astype(jnp.bfloat16)).astype(jnp.float32)

@jax.custom_vjp
def low_back(v):
    return v

def low_keep(v):
    return (low(v), None)

def low_pass(kept, grad):
    return (grad,)

def back_keep(v):
    return (v, None)

def back_low(kept, grad):
    return (low(grad),)
low.defvjp(low_keep, low_pass)
low_back.defvjp(back_keep, back_low)
beta_one = 0.9
beta_two = 0.999
adam_eps = 1e-06
decay_rate = 0.01
matrix_rate = 0.3
vector_rate = 0.2
cosine_weight = 32.0
cosine_eps = 1e-06
layer_eps = 1e-12
masked_score = -1e+30
highest = lax.Precision.HIGHEST

def layer_norm(row_values, gain_vec, shift_vec):
    center = row_values - lax.optimization_barrier(jnp.mean(row_values, -1, keepdims=True))
    spread = lax.optimization_barrier(jnp.mean(center * center, -1, keepdims=True))
    return center * lax.rsqrt(spread + layer_eps) * gain_vec + shift_vec

def encoder_layer(row_values, weights, packed, length_now):
    attn_w, out_w, up_w, down_w = weights
    pieces = [packed[position * D:(position + 1) * D] for position in range(8)]
    hidden_bias = packed[8 * D:8 * D + FF]
    query = low(low_back(jnp.dot(row_values, attn_w[0], precision=highest) + pieces[0]))
    key_rows = low(low_back(jnp.dot(row_values, attn_w[1], precision=highest)))
    value_rows = low(low_back(jnp.dot(row_values, attn_w[2], precision=highest) + pieces[1]))
    query_heads = query.reshape(LEN, HEADS, HDIM)
    key_heads = key_rows.reshape(LEN, HEADS, HDIM)
    value_heads = value_rows.reshape(LEN, HEADS, HDIM)
    raw_scores = jnp.einsum('qhe,khe->hqk', query_heads, key_heads, precision=highest) * HDIM ** (-0.5)
    visible = jnp.arange(LEN) < length_now
    scores = jnp.where(visible[None, None, :], low_back(raw_scores), masked_score)
    probs = low(jax.nn.softmax(scores, axis=-1))
    mixed = jnp.einsum('hqk,khe->qhe', probs, value_heads, precision=highest).reshape(LEN, D)
    mixed = low(low_back(mixed))
    branch = low_back(jnp.dot(mixed, out_w, precision=highest) + pieces[2])
    normed = layer_norm(row_values + branch, pieces[3], pieces[4])
    gate_in = low_back(jnp.dot(low(normed), up_w, precision=highest) + hidden_bias)
    activated = low(jax.nn.gelu(gate_in, approximate=False))
    feed = low_back(jnp.dot(activated, down_w, precision=highest) + pieces[5])
    return layer_norm(normed + feed, pieces[6], pieces[7])

def adam_moments(grad_now, first_old, second_old):
    first_new = beta_one * first_old + (1.0 - beta_one) * grad_now
    second_new = beta_two * second_old + (1.0 - beta_two) * grad_now * grad_now
    step_now = first_new / (1.0 - beta_one ** STEP) / (jnp.sqrt(second_new / (1.0 - beta_two ** STEP)) + adam_eps)
    return (first_new, second_new, step_now)

def matrix_squares(attn_w, out_w, up_w, down_w):
    return jnp.concatenate([lax.optimization_barrier(jnp.sum(attn_w * attn_w, axis=(1, 2))), jnp.stack([jnp.sum(out_w * out_w), jnp.sum(up_w * up_w), jnp.sum(down_w * down_w)])])

def reference(tokens, teacher_tokens, cotangent, lengths, masked, attn_weight, out_weight, up_weight, down_weight, attn_first, out_first, up_first, down_first, attn_second, out_second, up_second, down_second, vectors, vector_first, vector_second, teacher_attn, teacher_out, teacher_up, teacher_down, teacher_vectors):
    teacher_weights = (teacher_attn.astype(jnp.float32), teacher_out.astype(jnp.float32), teacher_up.astype(jnp.float32), teacher_down.astype(jnp.float32))
    teacher_packed = teacher_vectors.astype(jnp.float32)
    teacher_y = lax.map(lambda sequence: encoder_layer(sequence[0], teacher_weights, teacher_packed, sequence[1]), (teacher_tokens.astype(jnp.float32), lengths))

    def objective(all_rows, attn_w, out_w, up_w, down_w, packed):
        weights = (low(attn_w), low(out_w), low(up_w), low(down_w))

        def one_sequence(carry, entry):
            row_values, target, back_rows, length_now, positions = entry
            outcome = encoder_layer(row_values, weights, packed, length_now)
            linear = jnp.sum(back_rows * outcome)
            picked = outcome[positions]
            aimed = target[positions]
            inner = lax.optimization_barrier(jnp.sum(picked * aimed, -1))
            scale_own = jnp.sqrt(lax.optimization_barrier(jnp.sum(picked * picked, -1)) + cosine_eps)
            scale_aim = jnp.sqrt(lax.optimization_barrier(jnp.sum(aimed * aimed, -1)) + cosine_eps)
            part_loss = linear + cosine_weight * jnp.sum(1.0 - inner / (scale_own * scale_aim))
            return (carry + part_loss, outcome)
        loss_total, outcomes = lax.scan(jax.checkpoint(one_sequence), jnp.zeros((), jnp.float32), (all_rows, teacher_y, cotangent.astype(jnp.float32), lengths, masked))
        return (loss_total, outcomes)
    loss_total, pull_all, outcomes = jax.vjp(objective, tokens.astype(jnp.float32), attn_weight, out_weight, up_weight, down_weight, vectors, has_aux=True)
    grad_rows, grad_attn, grad_out, grad_up, grad_down, grad_vectors = pull_all(jnp.ones((), jnp.float32))
    attn_moment, attn_square, step_attn = adam_moments(grad_attn, attn_first, attn_second)
    out_moment, out_square, step_out = adam_moments(grad_out, out_first, out_second)
    up_moment, up_square, step_up = adam_moments(grad_up, up_first, up_second)
    down_moment, down_square, step_down = adam_moments(grad_down, down_first, down_second)
    step_attn = step_attn + decay_rate * attn_weight
    step_out = step_out + decay_rate * out_weight
    step_up = step_up + decay_rate * up_weight
    step_down = step_down + decay_rate * down_weight
    weight_norms = jnp.sqrt(matrix_squares(attn_weight, out_weight, up_weight, down_weight))
    update_norms = jnp.sqrt(matrix_squares(step_attn, step_out, step_up, step_down))
    trust_ratio = weight_norms / update_norms
    attn_updated = attn_weight - matrix_rate * trust_ratio[0:3][:, None, None] * step_attn
    out_updated = out_weight - matrix_rate * trust_ratio[3] * step_out
    up_updated = up_weight - matrix_rate * trust_ratio[4] * step_up
    down_updated = down_weight - matrix_rate * trust_ratio[5] * step_down
    vector_moment, vector_square, step_vector = adam_moments(grad_vectors, vector_first, vector_second)
    vector_updated = vectors - vector_rate * step_vector
    return (outcomes.astype(jnp.bfloat16), grad_rows, attn_updated, out_updated, up_updated, down_updated, attn_moment, out_moment, up_moment, down_moment, attn_square, out_square, up_square, down_square, vector_moment, vector_square, vector_updated, jnp.stack([weight_norms, update_norms]), trust_ratio)
```

```python
from functools import partial

import jax
import jax.numpy as jnp
from jax import lax
from jax.sharding import PartitionSpec as P

HDIM = 64
STEP = 5


beta_one = 0.9
beta_two = 0.999
adam_eps = 1e-06
decay_rate = 0.01
matrix_rate = 0.3
vector_rate = 0.2
cosine_weight = 32.0
cosine_eps = 1e-06
layer_eps = 1e-12
masked_score = -1e30


def layer_norm(row_values, gain_vec, shift_vec):
    center = row_values - jnp.mean(row_values, -1, keepdims=True)
    spread = jnp.mean(center * center, -1, keepdims=True)
    return center * lax.rsqrt(spread + layer_eps) * gain_vec + shift_vec


def vector_parts(packed, model_width):
    pieces = [
        packed[position * model_width : (position + 1) * model_width] for position in range(8)
    ]
    return pieces + [packed[8 * model_width :]]


def row_share(term_fn, share_rows):
    return lax.psum_scatter(
        term_fn(jnp.int32(0), share_rows * lax.axis_size("mp")),
        "mp",
        scatter_dimension=0,
        tiled=True,
    )


def row_join_low(share_values):
    return lax.all_gather(share_values, "mp", axis=0, tiled=True)


def row_join(share_values):
    return lax.all_gather(share_values, "mp", axis=0, tiled=True)


def product_rows(left_rows, right_matrix):

    def term_fn(start, count):
        return jnp.dot(left_rows, right_matrix, preferred_element_type=jnp.float32)

    return term_fn


def split_heads(flat_rows, seq_count, length):
    return flat_rows.reshape(seq_count, length, flat_rows.shape[1] // HDIM, HDIM).transpose(
        2, 0, 1, 3
    )


def merge_heads(split_rows):
    head_count, seq_count, length, head_size = split_rows.shape
    return split_rows.transpose(1, 2, 0, 3).reshape(seq_count * length, head_count * head_size)


def head_scores(query, key_rows, visible):
    scale_factor = query.shape[-1] ** (-0.5)
    scores = (
        jnp.einsum("sqe,ske->sqk", query, key_rows, preferred_element_type=jnp.float32)
        * scale_factor
    )
    return jnp.where(visible[:, None, :], scores, masked_score)


def head_forward(query, key_rows, value_rows, visible):
    scores = head_scores(query, key_rows, visible)
    row_peak = jnp.max(scores, -1, keepdims=True)
    exponent = jnp.exp(scores - row_peak)
    row_total = jnp.sum(exponent, -1, keepdims=True)
    weights_low = (exponent / row_total).astype(jnp.bfloat16)
    mixed = jnp.einsum("sqk,ske->sqe", weights_low, value_rows, preferred_element_type=jnp.float32)
    return (mixed.astype(jnp.bfloat16), (row_peak + jnp.log(row_total))[..., 0])


def head_backward(query, key_rows, value_rows, grad_mixed, log_total, visible):
    scale_factor = query.shape[-1] ** (-0.5)
    scores = head_scores(query, key_rows, visible)
    probs = jnp.exp(scores - log_total[..., None])
    grad_probs = jnp.einsum(
        "sqe,ske->sqk", grad_mixed, value_rows, preferred_element_type=jnp.float32
    )
    inner = jnp.sum(probs * grad_probs, -1, keepdims=True)
    grad_scores = (probs * (grad_probs - inner)).astype(jnp.bfloat16)
    grad_query = (
        jnp.einsum("sqk,ske->sqe", grad_scores, key_rows, preferred_element_type=jnp.float32)
        * scale_factor
    ).astype(jnp.bfloat16)
    grad_keys = (
        jnp.einsum("sqk,sqe->ske", grad_scores, query, preferred_element_type=jnp.float32)
        * scale_factor
    ).astype(jnp.bfloat16)
    grad_values = jnp.einsum(
        "sqk,sqe->ske", probs.astype(jnp.bfloat16), grad_mixed, preferred_element_type=jnp.float32
    ).astype(jnp.bfloat16)
    return (grad_query, grad_keys, grad_values)


def forward_model(tokens, visible, weights, packed, shard_at, share_rows):
    attn_w, out_w, up_w, down_w = weights
    seq_count, length, model_width = tokens.shape
    local_width = attn_w.shape[2]
    hidden_local = up_w.shape[1]
    pieces = vector_parts(packed, model_width)
    bias_query = lax.dynamic_slice_in_dim(pieces[0], shard_at * local_width, local_width)
    bias_value = lax.dynamic_slice_in_dim(pieces[1], shard_at * local_width, local_width)
    bias_up = lax.dynamic_slice_in_dim(pieces[8], shard_at * hidden_local, hidden_local)
    row_values = tokens.reshape(seq_count * length, model_width)
    projected = jnp.einsum("rd,pde->pre", row_values, attn_w, preferred_element_type=jnp.float32)
    query_heads = split_heads((projected[0] + bias_query).astype(jnp.bfloat16), seq_count, length)
    key_heads = split_heads(projected[1].astype(jnp.bfloat16), seq_count, length)
    value_heads = split_heads((projected[2] + bias_value).astype(jnp.bfloat16), seq_count, length)
    mixed, log_total = lax.map(
        lambda grouped: head_forward(grouped[0], grouped[1], grouped[2], visible),
        (query_heads, key_heads, value_heads),
    )
    attended = merge_heads(mixed)
    share_start = shard_at * share_rows
    own_rows = lax.dynamic_slice_in_dim(row_values, share_start, share_rows, 0).astype(jnp.float32)
    first_sum = own_rows + row_share(product_rows(attended, out_w), share_rows) + pieces[2]
    normed = layer_norm(first_sum, pieces[3], pieces[4])
    normed_low = row_join_low(normed.astype(jnp.bfloat16))
    gate_in = jnp.dot(normed_low, up_w, preferred_element_type=jnp.float32) + bias_up
    activated = jax.nn.gelu(gate_in, approximate=False).astype(jnp.bfloat16)
    second_sum = normed + row_share(product_rows(activated, down_w), share_rows) + pieces[5]
    outcome = row_join(layer_norm(second_sum, pieces[6], pieces[7]))
    saved = (
        row_values,
        query_heads,
        key_heads,
        value_heads,
        log_total,
        attended,
        first_sum,
        normed_low,
        gate_in,
        activated,
        second_sum,
    )
    return (outcome, saved)


def adam_moments(grad_now, first_old, second_old):
    first_new = beta_one * first_old + (1.0 - beta_one) * grad_now
    second_new = beta_two * second_old + (1.0 - beta_two) * grad_now * grad_now
    step_now = (
        first_new
        / (1.0 - beta_one**STEP)
        / (jnp.sqrt(second_new / (1.0 - beta_two**STEP)) + adam_eps)
    )
    return (first_new, second_new, step_now)


def matrix_squares(attn_w, out_w, up_w, down_w):
    return jnp.concatenate(
        [
            jnp.sum(attn_w * attn_w, axis=(1, 2)),
            jnp.stack([jnp.sum(out_w * out_w), jnp.sum(up_w * up_w), jnp.sum(down_w * down_w)]),
        ]
    )


def split_units(
    tokens,
    teacher_tokens,
    cotangent,
    lengths,
    masked,
    attn_weight,
    out_weight,
    up_weight,
    down_weight,
    attn_first,
    out_first,
    up_first,
    down_first,
    attn_second,
    out_second,
    up_second,
    down_second,
    vectors,
    vector_first,
    vector_second,
    teacher_attn,
    teacher_out,
    teacher_up,
    teacher_down,
    teacher_vectors,
):
    shard_at = lax.axis_index("mp")
    leading = (shard_at == 0).astype(jnp.float32)
    seq_count, length, model_width = tokens.shape
    share_rows = seq_count * length // lax.axis_size("mp")
    share_start = shard_at * share_rows
    visible = jnp.arange(length)[None, :] < lengths[:, None]
    student = (
        lax.all_gather(attn_weight.astype(jnp.bfloat16), "dp", axis=1, tiled=True),
        lax.all_gather(out_weight.astype(jnp.bfloat16), "dp", axis=1, tiled=True),
        lax.all_gather(up_weight.astype(jnp.bfloat16), "dp", axis=0, tiled=True),
        lax.all_gather(down_weight.astype(jnp.bfloat16), "dp", axis=1, tiled=True),
    )
    teacher = (
        lax.all_gather(teacher_attn, "dp", axis=1, tiled=True),
        lax.all_gather(teacher_out, "dp", axis=1, tiled=True),
        lax.all_gather(teacher_up, "dp", axis=0, tiled=True),
        lax.all_gather(teacher_down, "dp", axis=1, tiled=True),
    )
    attn_w, out_w, up_w, down_w = student
    local_width = attn_w.shape[2]
    hidden_local = up_w.shape[1]
    teacher_rows, unused_saved = forward_model(
        teacher_tokens, visible, teacher, teacher_vectors.astype(jnp.float32), shard_at, share_rows
    )
    student_rows, saved = forward_model(tokens, visible, student, vectors, shard_at, share_rows)
    (
        row_values,
        query_heads,
        key_heads,
        value_heads,
        log_total,
        attended,
        first_sum,
        normed_low,
        gate_in,
        activated,
        second_sum,
    ) = saved
    student_out = student_rows.astype(jnp.bfloat16).reshape(seq_count, length, model_width)
    teacher_shaped = teacher_rows.reshape(seq_count, length, model_width)
    picks = masked[:, :, None]

    def loss_rows(outcome):
        shaped = outcome.reshape(seq_count, length, model_width)
        linear = jnp.sum(cotangent.astype(jnp.float32) * shaped)
        picked = jnp.take_along_axis(shaped, picks, axis=1)
        aimed = jnp.take_along_axis(teacher_shaped, picks, axis=1)
        inner = jnp.sum(picked * aimed, -1)
        scale_own = jnp.sqrt(jnp.sum(picked * picked, -1) + cosine_eps)
        scale_aim = jnp.sqrt(jnp.sum(aimed * aimed, -1) + cosine_eps)
        return linear + cosine_weight * jnp.sum(1.0 - inner / (scale_own * scale_aim))

    unused_loss, pull_loss = jax.vjp(loss_rows, student_rows)
    (grad_result,) = pull_loss(jnp.ones((), jnp.float32))
    pieces = vector_parts(vectors, model_width)
    grad_top = lax.dynamic_slice_in_dim(grad_result, share_start, share_rows, 0)
    gain_scale = 1.0
    unused_top, pull_top = jax.vjp(layer_norm, second_sum, pieces[6], pieces[7])
    grad_second, grad_gain_two, grad_shift_two = pull_top(grad_top)
    feed_low = grad_second.astype(jnp.bfloat16)
    feed_low = row_join_low(feed_low)
    grad_bias_down = jnp.sum(feed_low.astype(jnp.float32), 0)
    grad_down = jnp.einsum("rf,rd->fd", activated, feed_low, preferred_element_type=jnp.float32)
    grad_act = jnp.einsum("rd,fd->rf", feed_low, down_w, preferred_element_type=jnp.float32)
    unused_gelu, pull_gelu = jax.vjp(partial(jax.nn.gelu, approximate=False), gate_in)
    (grad_gate,) = pull_gelu(grad_act)
    gate_low = grad_gate.astype(jnp.bfloat16)
    grad_bias_up = jnp.sum(gate_low.astype(jnp.float32), 0)
    grad_up = jnp.einsum("rd,rf->df", normed_low, gate_low, preferred_element_type=jnp.float32)
    grad_normed = grad_second + row_share(product_rows(gate_low, up_w.T), share_rows)
    unused_mid, pull_mid = jax.vjp(layer_norm, first_sum, pieces[3], pieces[4])
    grad_first, grad_gain_one, grad_shift_one = pull_mid(grad_normed)
    branch_low = grad_first.astype(jnp.bfloat16)
    branch_low = row_join_low(branch_low)
    grad_bias_out = jnp.sum(branch_low.astype(jnp.float32), 0)
    grad_out = jnp.einsum("rh,rd->hd", attended, branch_low, preferred_element_type=jnp.float32)
    grad_attended = jnp.einsum(
        "rd,hd->rh", branch_low, out_w, preferred_element_type=jnp.float32
    ).astype(jnp.bfloat16)
    grad_heads = split_heads(grad_attended, seq_count, length)
    grad_query, grad_keys, grad_values = lax.map(
        lambda grouped: head_backward(
            grouped[0], grouped[1], grouped[2], grouped[3], grouped[4], visible
        ),
        (query_heads, key_heads, value_heads, grad_heads, log_total),
    )
    grad_projected = jnp.stack(
        [merge_heads(grad_query), merge_heads(grad_keys), merge_heads(grad_values)]
    )
    grad_attn = jnp.einsum(
        "rd,pre->pde", row_values, grad_projected, preferred_element_type=jnp.float32
    )
    summed_attn, summed_out, summed_up, summed_down = (
        lax.psum_scatter(grad_attn, "dp", scatter_dimension=1, tiled=True),
        lax.psum_scatter(grad_out, "dp", scatter_dimension=1, tiled=True),
        lax.psum_scatter(grad_up, "dp", scatter_dimension=0, tiled=True),
        lax.psum_scatter(grad_down, "dp", scatter_dimension=1, tiled=True),
    )

    def input_term(start, count):
        return jnp.einsum("pre,pde->rd", grad_projected, attn_w, preferred_element_type=jnp.float32)

    input_grad = row_join(grad_first + row_share(input_term, share_rows)).reshape(
        seq_count, length, model_width
    )
    grad_bias_query = jnp.sum(grad_projected[0].astype(jnp.float32), 0)
    grad_bias_value = jnp.sum(grad_projected[2].astype(jnp.float32), 0)
    zeros_model = jnp.zeros((model_width,), jnp.float32)
    zeros_hidden = jnp.zeros((pieces[8].shape[0],), jnp.float32)
    vector_grad = jnp.concatenate(
        [
            lax.dynamic_update_slice_in_dim(
                zeros_model, grad_bias_query, shard_at * local_width, 0
            ),
            lax.dynamic_update_slice_in_dim(
                zeros_model, grad_bias_value, shard_at * local_width, 0
            ),
            leading * grad_bias_out,
            gain_scale * grad_gain_one,
            gain_scale * grad_shift_one,
            leading * grad_bias_down,
            gain_scale * grad_gain_two,
            gain_scale * grad_shift_two,
            lax.dynamic_update_slice_in_dim(zeros_hidden, grad_bias_up, shard_at * hidden_local, 0),
        ]
    )
    attn_moment, attn_square, step_attn = adam_moments(summed_attn, attn_first, attn_second)
    out_moment, out_square, step_out = adam_moments(summed_out, out_first, out_second)
    up_moment, up_square, step_up = adam_moments(summed_up, up_first, up_second)
    down_moment, down_square, step_down = adam_moments(summed_down, down_first, down_second)
    step_attn = step_attn + decay_rate * attn_weight
    step_out = step_out + decay_rate * out_weight
    step_up = step_up + decay_rate * up_weight
    step_down = step_down + decay_rate * down_weight
    update_squares = matrix_squares(step_attn, step_out, step_up, step_down)
    weight_total, update_total, vector_total = lax.psum(
        (
            matrix_squares(attn_weight, out_weight, up_weight, down_weight),
            update_squares,
            vector_grad,
        ),
        ("dp", "mp"),
    )
    weight_norms = jnp.sqrt(weight_total)
    update_norms = jnp.sqrt(update_total)
    trust_ratio = weight_norms / update_norms
    attn_updated = attn_weight - matrix_rate * trust_ratio[0:3][:, None, None] * step_attn
    out_updated = out_weight - matrix_rate * trust_ratio[3] * step_out
    up_updated = up_weight - matrix_rate * trust_ratio[4] * step_up
    down_updated = down_weight - matrix_rate * trust_ratio[5] * step_down
    vector_moment, vector_square, step_vector = adam_moments(
        vector_total, vector_first, vector_second
    )
    vector_updated = vectors - vector_rate * step_vector
    return (
        student_out,
        input_grad,
        attn_updated,
        out_updated,
        up_updated,
        down_updated,
        attn_moment,
        out_moment,
        up_moment,
        down_moment,
        attn_square,
        out_square,
        up_square,
        down_square,
        vector_moment,
        vector_square,
        vector_updated,
        jnp.stack([weight_norms, update_norms]),
        trust_ratio,
    )


def shard_pack(attn_w, out_w, up_w, down_w):
    return jnp.concatenate(
        [attn_w[0], attn_w[1], attn_w[2], out_w.T, up_w, down_w.T], axis=1
    )


def vector_pieces(packed, model_width):
    return vector_parts(packed, model_width)


def cosine_pull(rows, places, aimed, row_start):
    row_count = rows.shape[0]
    local_at = places - row_start
    here = (local_at >= 0) & (local_at < row_count)
    picked = rows[jnp.clip(local_at, 0, row_count - 1)]
    inner = jnp.sum(picked * aimed, -1, keepdims=True)
    square_own = jnp.sum(picked * picked, -1, keepdims=True) + cosine_eps
    square_aim = jnp.sum(aimed * aimed, -1, keepdims=True) + cosine_eps
    inverse = lax.rsqrt(square_own) * lax.rsqrt(square_aim)
    pull = -cosine_weight * (aimed * inverse - picked * (inner * inverse / square_own))
    pull = jnp.where(here[:, None], pull, 0.0)
    return jnp.zeros_like(rows).at[jnp.clip(local_at, 0, row_count - 1)].add(pull)


def heads_of(flat):
    return flat.reshape(flat.shape[0], flat.shape[1] // HDIM, HDIM).transpose(1, 0, 2)


def flat_of(split):
    return split.transpose(1, 0, 2).reshape(split.shape[1], -1)


def dot32(left, right):
    return jnp.dot(left, right, preferred_element_type=jnp.float32)


def dot_nt(left, right):
    return lax.dot_general(
        left, right, (((1,), (1,)), ((), ())), preferred_element_type=jnp.float32
    )


def dot_tn(left, right):
    return lax.dot_general(
        left, right, (((0,), (0,)), ((), ())), preferred_element_type=jnp.float32
    )


def split_rows(
    tokens,
    teacher_tokens,
    cotangent,
    lengths,
    masked,
    attn_weight,
    out_weight,
    up_weight,
    down_weight,
    attn_first,
    out_first,
    up_first,
    down_first,
    attn_second,
    out_second,
    up_second,
    down_second,
    vectors,
    vector_first,
    vector_second,
    teacher_attn,
    teacher_out,
    teacher_up,
    teacher_down,
    teacher_vectors,
):
    low = jnp.bfloat16
    everyone = ("dp", "mp")
    shard_at = lax.axis_index("mp")
    halves = lax.axis_size("mp")
    seq_count, length, width = tokens.shape
    rows = length // halves
    row_start = shard_at * rows
    part = attn_weight.shape[2]
    units = up_weight.shape[1]
    cuts = [0, part, 2 * part, 3 * part, 4 * part, 4 * part + units, 4 * part + 2 * units]
    visible = (jnp.arange(length) < lengths[0])[None, None, :]
    places = masked[0]

    student = lax.all_gather(
        shard_pack(attn_weight, out_weight, up_weight, down_weight).astype(low),
        ("mp", "dp"),
        axis=0,
        tiled=True,
    ).reshape(halves, width, cuts[6])
    teacher = lax.all_gather(
        shard_pack(teacher_attn, teacher_out, teacher_up, teacher_down),
        "dp",
        axis=0,
        tiled=True,
    )

    def whole(index):
        return jnp.concatenate(
            [student[half, :, cuts[index] : cuts[index + 1]] for half in range(halves)], axis=1
        )

    teacher_parts = vector_parts(teacher_vectors.astype(jnp.float32), width)
    bias_q = lax.dynamic_slice_in_dim(teacher_parts[0], shard_at * part, part)
    bias_v = lax.dynamic_slice_in_dim(teacher_parts[1], shard_at * part, part)
    bias_up = lax.dynamic_slice_in_dim(teacher_parts[8], shard_at * units, units)
    teacher_rows = teacher_tokens[0]
    listed = teacher_rows[places]
    t_query = (dot32(listed, teacher[:, : cuts[1]]) + bias_q).astype(low)
    t_keys = dot32(teacher_rows, teacher[:, cuts[1] : cuts[2]]).astype(low)
    t_values = (dot32(teacher_rows, teacher[:, cuts[2] : cuts[3]]) + bias_v).astype(low)
    t_mixed, unused_log = head_forward(
        heads_of(t_query), heads_of(t_keys), heads_of(t_values), visible[0]
    )
    t_branch = lax.psum(dot_nt(flat_of(t_mixed), teacher[:, cuts[3] : cuts[4]]), "mp")
    t_first = listed.astype(jnp.float32) + t_branch + teacher_parts[2]
    t_normed = layer_norm(t_first, teacher_parts[3], teacher_parts[4])
    t_gate = dot32(t_normed.astype(low), teacher[:, cuts[4] : cuts[5]]) + bias_up
    t_act = jax.nn.gelu(t_gate, approximate=False).astype(low)
    t_feed = lax.psum(dot_nt(t_act, teacher[:, cuts[5] : cuts[6]]), "mp")
    aimed = layer_norm(t_normed + t_feed + teacher_parts[5], teacher_parts[6], teacher_parts[7])

    pieces = vector_parts(vectors, width)
    all_rows = tokens[0]
    own_rows = lax.dynamic_slice_in_dim(all_rows, row_start, rows, 0)
    w_q, w_k, w_v, w_out, w_up, w_down = [whole(index) for index in range(6)]
    query = heads_of((dot32(own_rows, w_q) + pieces[0]).astype(low))
    keys = heads_of(dot32(all_rows, w_k).astype(low))
    values = heads_of((dot32(all_rows, w_v) + pieces[1]).astype(low))
    mixed, log_total = lax.map(
        lambda g: jax.tree.map(
            lambda v: v[0], head_forward(g[0][None], g[1][None], g[2][None], visible[0])
        ),
        (query, keys, values),
    )
    attended = flat_of(mixed)
    first_sum = own_rows.astype(jnp.float32) + dot_nt(attended, w_out) + pieces[2]
    normed = layer_norm(first_sum, pieces[3], pieces[4])
    normed_low = normed.astype(low)
    gate_in = dot32(normed_low, w_up) + pieces[8]
    activated = jax.nn.gelu(gate_in, approximate=False).astype(low)
    second_sum = normed + dot_nt(activated, w_down) + pieces[5]
    outcome = layer_norm(second_sum, pieces[6], pieces[7])
    student_out = lax.all_gather(outcome.astype(low), "mp", axis=0, tiled=True)[None]

    own_cotangent = lax.dynamic_slice_in_dim(cotangent[0], row_start, rows, 0)
    grad_top = own_cotangent.astype(jnp.float32) + cosine_pull(outcome, places, aimed, row_start)
    unused_top, pull_top = jax.vjp(layer_norm, second_sum, pieces[6], pieces[7])
    grad_second, grad_gain_two, grad_shift_two = pull_top(grad_top)
    feed_low = grad_second.astype(low)
    grad_down = dot_tn(feed_low, activated)
    grad_act = dot32(feed_low, w_down)
    unused_gelu, pull_gelu = jax.vjp(partial(jax.nn.gelu, approximate=False), gate_in)
    (grad_gate,) = pull_gelu(grad_act)
    gate_low = grad_gate.astype(low)
    grad_up = dot_tn(normed_low, gate_low)
    grad_normed = grad_second + dot_nt(gate_low, w_up)
    unused_mid, pull_mid = jax.vjp(layer_norm, first_sum, pieces[3], pieces[4])
    grad_first, grad_gain_one, grad_shift_one = pull_mid(grad_normed)
    branch_low = grad_first.astype(low)
    grad_out = dot_tn(branch_low, attended)
    grad_heads = heads_of(dot32(branch_low, w_out).astype(low))

    def one_head(g):
        query_h, keys_h, values_h, mixed_h, log_h = g
        scale_factor = HDIM**-0.5
        scores = jnp.where(visible[0], dot_nt(query_h, keys_h) * scale_factor, masked_score)
        probs = jnp.exp(scores - log_h[:, None])
        grad_probs = dot_nt(mixed_h, values_h)
        inner = jnp.sum(probs * grad_probs, -1, keepdims=True)
        grad_scores = (probs * (grad_probs - inner)).astype(low)
        return (
            (dot32(grad_scores, keys_h) * scale_factor).astype(low),
            (dot_tn(grad_scores, query_h) * scale_factor).astype(low),
            dot_tn(probs.astype(low), mixed_h).astype(low),
        )

    grad_query, grad_keys, grad_values = lax.map(
        one_head, (query, keys, values, grad_heads, log_total)
    )
    grad_query = flat_of(grad_query)

    def row_sum(term):
        other = lax.dynamic_slice_in_dim(term, (1 - shard_at) * rows, rows, 0)
        mine = lax.dynamic_slice_in_dim(term, row_start, rows, 0)
        came = lax.ppermute(other, "mp", [(0, 1), (1, 0)])
        return (mine.astype(jnp.float32) + came.astype(jnp.float32)).astype(low)

    grad_keys = row_sum(flat_of(grad_keys))
    grad_values = row_sum(flat_of(grad_values))
    grad_q = dot_tn(own_rows, grad_query)
    grad_k = dot_tn(own_rows, grad_keys)
    grad_v = dot_tn(own_rows, grad_values)
    input_own = (
        grad_first + dot_nt(grad_query, w_q) + dot_nt(grad_keys, w_k) + dot_nt(grad_values, w_v)
    )
    input_grad = lax.all_gather(input_own, "mp", axis=0, tiled=True)[None]

    def half_of(matrix, half):
        span = matrix.shape[1] // halves
        return matrix[:, half * span : (half + 1) * span]

    grads = [grad_q, grad_k, grad_v, grad_out, grad_up, grad_down]
    packed_grad = jnp.concatenate(
        [
            jnp.concatenate([half_of(g, half) for g in grads], axis=1).astype(low)
            for half in range(halves)
        ],
        axis=0,
    )
    summed = lax.psum_scatter(
        packed_grad, ("mp", "dp"), scatter_dimension=0, tiled=True
    ).astype(jnp.float32)
    summed_attn = jnp.stack([summed[:, cuts[i] : cuts[i + 1]] for i in range(3)])
    summed_out = summed[:, cuts[3] : cuts[4]].T
    summed_up = summed[:, cuts[4] : cuts[5]]
    summed_down = summed[:, cuts[5] : cuts[6]].T

    vector_grad = jnp.concatenate(
        [
            jnp.sum(grad_query.astype(jnp.float32), 0),
            jnp.sum(grad_values.astype(jnp.float32), 0),
            jnp.sum(branch_low.astype(jnp.float32), 0),
            grad_gain_one,
            grad_shift_one,
            jnp.sum(feed_low.astype(jnp.float32), 0),
            grad_gain_two,
            grad_shift_two,
            jnp.sum(gate_low.astype(jnp.float32), 0),
        ]
    )
    return (student_out, input_grad) + lamb_update(
        (summed_attn, summed_out, summed_up, summed_down),
        (attn_weight, out_weight, up_weight, down_weight),
        (attn_first, out_first, up_first, down_first),
        (attn_second, out_second, up_second, down_second),
        vector_grad,
        vectors,
        vector_first,
        vector_second,
    )


def lamb_update(grads, weights, firsts, seconds, vector_grad, vectors, vector_first, vector_second):
    moments, squares, steps = [], [], []
    for grad_now, weight, first_old, second_old in zip(grads, weights, firsts, seconds):
        first_new, second_new, step_now = adam_moments(grad_now, first_old, second_old)
        moments.append(first_new)
        squares.append(second_new)
        steps.append(step_now + decay_rate * weight)
    weight_total, update_total, vector_total = lax.psum(
        (matrix_squares(*weights), matrix_squares(*steps), vector_grad), ("dp", "mp")
    )
    weight_norms = jnp.sqrt(weight_total)
    update_norms = jnp.sqrt(update_total)
    trust_ratio = weight_norms / update_norms
    ratios = [trust_ratio[0:3][:, None, None], trust_ratio[3], trust_ratio[4], trust_ratio[5]]
    updated = [
        weight - matrix_rate * ratio * step for weight, ratio, step in zip(weights, ratios, steps)
    ]
    vector_moment, vector_square, step_vector = adam_moments(
        vector_total, vector_first, vector_second
    )
    vector_updated = vectors - vector_rate * step_vector
    return (
        *updated,
        *moments,
        *squares,
        vector_moment,
        vector_square,
        vector_updated,
        jnp.stack([weight_norms, update_norms]),
        trust_ratio,
    )


def solution(mesh):
    return jax.shard_map(
        split_rows,
        mesh=mesh,
        in_specs=(
            P("dp", None, None),
            P("dp", None, None),
            P("dp", None, None),
            P("dp"),
            P("dp", None),
            P(None, "dp", "mp"),
            P("mp", "dp"),
            P("dp", "mp"),
            P("mp", "dp"),
            P(None, "dp", "mp"),
            P("mp", "dp"),
            P("dp", "mp"),
            P("mp", "dp"),
            P(None, "dp", "mp"),
            P("mp", "dp"),
            P("dp", "mp"),
            P("mp", "dp"),
            P(),
            P(),
            P(),
            P(None, "dp", "mp"),
            P("mp", "dp"),
            P("dp", "mp"),
            P("mp", "dp"),
            P(),
        ),
        out_specs=(
            P("dp", None, None),
            P("dp", None, None),
            P(None, "dp", "mp"),
            P("mp", "dp"),
            P("dp", "mp"),
            P("mp", "dp"),
            P(None, "dp", "mp"),
            P("mp", "dp"),
            P("dp", "mp"),
            P("mp", "dp"),
            P(None, "dp", "mp"),
            P("mp", "dp"),
            P("dp", "mp"),
            P("mp", "dp"),
            P(),
            P(),
            P(),
            P(),
            P(),
        ),
        check_vma=False,
    )
```

```python
from functools import partial

import jax
import jax.numpy as jnp
from jax import lax
from jax.experimental import pallas as pl
from jax.experimental.pallas import tpu as pltpu
from jax.sharding import PartitionSpec as P

HDIM = 64
STEP = 5


beta_one = 0.9
beta_two = 0.999
adam_eps = 1e-06
decay_rate = 0.01
matrix_rate = 0.3
vector_rate = 0.2
cosine_weight = 32.0
cosine_eps = 1e-06
layer_eps = 1e-12
masked_score = -1e30


def layer_norm(row_values, gain_vec, shift_vec):
    center = row_values - jnp.mean(row_values, -1, keepdims=True)
    spread = jnp.mean(center * center, -1, keepdims=True)
    return center * lax.rsqrt(spread + layer_eps) * gain_vec + shift_vec


def vector_parts(packed, model_width):
    pieces = [
        packed[position * model_width : (position + 1) * model_width] for position in range(8)
    ]
    return pieces + [packed[8 * model_width :]]


def head_scores(query, key_rows, visible):
    scale_factor = query.shape[-1] ** (-0.5)
    scores = (
        jnp.einsum("sqe,ske->sqk", query, key_rows, preferred_element_type=jnp.float32)
        * scale_factor
    )
    return jnp.where(visible[:, None, :], scores, masked_score)


def head_forward(query, key_rows, value_rows, visible):
    scores = head_scores(query, key_rows, visible)
    row_peak = jnp.max(scores, -1, keepdims=True)
    exponent = jnp.exp(scores - row_peak)
    row_total = jnp.sum(exponent, -1, keepdims=True)
    weights_low = (exponent / row_total).astype(jnp.bfloat16)
    mixed = jnp.einsum("sqk,ske->sqe", weights_low, value_rows, preferred_element_type=jnp.float32)
    return (mixed.astype(jnp.bfloat16), (row_peak + jnp.log(row_total))[..., 0])


def adam_moments(grad_now, first_old, second_old):
    first_new = beta_one * first_old + (1.0 - beta_one) * grad_now
    second_new = beta_two * second_old + (1.0 - beta_two) * grad_now * grad_now
    step_now = (
        first_new
        / (1.0 - beta_one**STEP)
        / (jnp.sqrt(second_new / (1.0 - beta_two**STEP)) + adam_eps)
    )
    return (first_new, second_new, step_now)


def matrix_squares(attn_w, out_w, up_w, down_w):
    return jnp.concatenate(
        [
            jnp.sum(attn_w * attn_w, axis=(1, 2)),
            jnp.stack([jnp.sum(out_w * out_w), jnp.sum(up_w * up_w), jnp.sum(down_w * down_w)]),
        ]
    )


def shard_pack(attn_w, out_w, up_w, down_w):
    return jnp.concatenate(
        [attn_w[0], attn_w[1], attn_w[2], out_w.T, up_w, down_w.T], axis=1
    )


def cosine_pull(rows, places, aimed, row_start):
    row_count = rows.shape[0]
    local_at = places - row_start
    here = (local_at >= 0) & (local_at < row_count)
    picked = rows[jnp.clip(local_at, 0, row_count - 1)]
    inner = jnp.sum(picked * aimed, -1, keepdims=True)
    square_own = jnp.sum(picked * picked, -1, keepdims=True) + cosine_eps
    square_aim = jnp.sum(aimed * aimed, -1, keepdims=True) + cosine_eps
    inverse = lax.rsqrt(square_own) * lax.rsqrt(square_aim)
    pull = -cosine_weight * (aimed * inverse - picked * (inner * inverse / square_own))
    pull = jnp.where(here[:, None], pull, 0.0)
    return jnp.zeros_like(rows).at[jnp.clip(local_at, 0, row_count - 1)].add(pull)


def heads_of(flat):
    return flat.reshape(flat.shape[0], flat.shape[1] // HDIM, HDIM).transpose(1, 0, 2)


def flat_of(split):
    return split.transpose(1, 0, 2).reshape(split.shape[1], -1)


def dot32(left, right):
    return jnp.dot(left, right, preferred_element_type=jnp.float32)


def dot_nt(left, right):
    return lax.dot_general(
        left, right, (((1,), (1,)), ((), ())), preferred_element_type=jnp.float32
    )


def dot_tn(left, right):
    return lax.dot_general(
        left, right, (((0,), (0,)), ((), ())), preferred_element_type=jnp.float32
    )


def split_rows(
    tokens,
    teacher_tokens,
    cotangent,
    lengths,
    masked,
    attn_weight,
    out_weight,
    up_weight,
    down_weight,
    attn_first,
    out_first,
    up_first,
    down_first,
    attn_second,
    out_second,
    up_second,
    down_second,
    vectors,
    vector_first,
    vector_second,
    teacher_attn,
    teacher_out,
    teacher_up,
    teacher_down,
    teacher_vectors,
):
    low = jnp.bfloat16
    everyone = ("dp", "mp")
    shard_at = lax.axis_index("mp")
    halves = lax.axis_size("mp")
    seq_count, length, width = tokens.shape
    rows = length // halves
    row_start = shard_at * rows
    part = attn_weight.shape[2]
    units = up_weight.shape[1]
    cuts = [0, part, 2 * part, 3 * part, 4 * part, 4 * part + units, 4 * part + 2 * units]
    visible = (jnp.arange(length) < lengths[0])[None, None, :]
    places = masked[0]

    student = lax.all_gather(
        shard_pack(attn_weight, out_weight, up_weight, down_weight).astype(low),
        ("mp", "dp"),
        axis=0,
        tiled=True,
    ).reshape(halves, width, cuts[6])
    teacher = lax.all_gather(
        shard_pack(teacher_attn, teacher_out, teacher_up, teacher_down),
        "dp",
        axis=0,
        tiled=True,
    )

    def whole(index):
        return jnp.concatenate(
            [student[half, :, cuts[index] : cuts[index + 1]] for half in range(halves)], axis=1
        )

    teacher_parts = vector_parts(teacher_vectors.astype(jnp.float32), width)
    bias_q = lax.dynamic_slice_in_dim(teacher_parts[0], shard_at * part, part)
    bias_v = lax.dynamic_slice_in_dim(teacher_parts[1], shard_at * part, part)
    bias_up = lax.dynamic_slice_in_dim(teacher_parts[8], shard_at * units, units)
    teacher_rows = teacher_tokens[0]
    listed = teacher_rows[places]
    t_query = (dot32(listed, teacher[:, : cuts[1]]) + bias_q).astype(low)
    t_keys = dot32(teacher_rows, teacher[:, cuts[1] : cuts[2]]).astype(low)
    t_values = (dot32(teacher_rows, teacher[:, cuts[2] : cuts[3]]) + bias_v).astype(low)
    t_mixed, unused_log = head_forward(
        heads_of(t_query), heads_of(t_keys), heads_of(t_values), visible[0]
    )
    t_branch = lax.psum(dot_nt(flat_of(t_mixed), teacher[:, cuts[3] : cuts[4]]), "mp")
    t_first = listed.astype(jnp.float32) + t_branch + teacher_parts[2]
    t_normed = layer_norm(t_first, teacher_parts[3], teacher_parts[4])
    t_gate = dot32(t_normed.astype(low), teacher[:, cuts[4] : cuts[5]]) + bias_up
    t_act = jax.nn.gelu(t_gate, approximate=False).astype(low)
    t_feed = lax.psum(dot_nt(t_act, teacher[:, cuts[5] : cuts[6]]), "mp")
    aimed = layer_norm(t_normed + t_feed + teacher_parts[5], teacher_parts[6], teacher_parts[7])

    pieces = vector_parts(vectors, width)
    all_rows = tokens[0]
    own_rows = lax.dynamic_slice_in_dim(all_rows, row_start, rows, 0)
    w_q, w_k, w_v, w_out, w_up, w_down = [whole(index) for index in range(6)]
    query = heads_of((dot32(own_rows, w_q) + pieces[0]).astype(low))
    keys = heads_of(dot32(all_rows, w_k).astype(low))
    values = heads_of((dot32(all_rows, w_v) + pieces[1]).astype(low))
    mixed, log_total = lax.map(
        lambda g: jax.tree.map(
            lambda v: v[0], head_forward(g[0][None], g[1][None], g[2][None], visible[0])
        ),
        (query, keys, values),
    )
    attended = flat_of(mixed)
    first_sum = own_rows.astype(jnp.float32) + dot_nt(attended, w_out) + pieces[2]
    normed = layer_norm(first_sum, pieces[3], pieces[4])
    normed_low = normed.astype(low)
    gate_in = dot32(normed_low, w_up) + pieces[8]
    activated = jax.nn.gelu(gate_in, approximate=False).astype(low)
    second_sum = normed + dot_nt(activated, w_down) + pieces[5]
    outcome = layer_norm(second_sum, pieces[6], pieces[7])
    student_out = lax.all_gather(outcome.astype(low), "mp", axis=0, tiled=True)[None]

    own_cotangent = lax.dynamic_slice_in_dim(cotangent[0], row_start, rows, 0)
    grad_top = own_cotangent.astype(jnp.float32) + cosine_pull(outcome, places, aimed, row_start)
    unused_top, pull_top = jax.vjp(layer_norm, second_sum, pieces[6], pieces[7])
    grad_second, grad_gain_two, grad_shift_two = pull_top(grad_top)
    feed_low = grad_second.astype(low)
    grad_down = dot_tn(feed_low, activated)
    grad_act = dot32(feed_low, w_down)
    unused_gelu, pull_gelu = jax.vjp(partial(jax.nn.gelu, approximate=False), gate_in)
    (grad_gate,) = pull_gelu(grad_act)
    gate_low = grad_gate.astype(low)
    grad_up = dot_tn(normed_low, gate_low)
    grad_normed = grad_second + dot_nt(gate_low, w_up)
    unused_mid, pull_mid = jax.vjp(layer_norm, first_sum, pieces[3], pieces[4])
    grad_first, grad_gain_one, grad_shift_one = pull_mid(grad_normed)
    branch_low = grad_first.astype(low)
    grad_out = dot_tn(branch_low, attended)
    grad_heads = heads_of(dot32(branch_low, w_out).astype(low))

    def one_head(g):
        query_h, keys_h, values_h, mixed_h, log_h = g
        scale_factor = HDIM**-0.5
        scores = jnp.where(visible[0], dot_nt(query_h, keys_h) * scale_factor, masked_score)
        probs = jnp.exp(scores - log_h[:, None])
        grad_probs = dot_nt(mixed_h, values_h)
        inner = jnp.sum(probs * grad_probs, -1, keepdims=True)
        grad_scores = (probs * (grad_probs - inner)).astype(low)
        return (
            (dot32(grad_scores, keys_h) * scale_factor).astype(low),
            (dot_tn(grad_scores, query_h) * scale_factor).astype(low),
            dot_tn(probs.astype(low), mixed_h).astype(low),
        )

    grad_query, grad_keys, grad_values = lax.map(
        one_head, (query, keys, values, grad_heads, log_total)
    )
    grad_query = flat_of(grad_query)

    def row_sum(term):
        other = lax.dynamic_slice_in_dim(term, (1 - shard_at) * rows, rows, 0)
        mine = lax.dynamic_slice_in_dim(term, row_start, rows, 0)
        came = lax.ppermute(other, "mp", [(0, 1), (1, 0)])
        return (mine.astype(jnp.float32) + came.astype(jnp.float32)).astype(low)

    grad_keys = row_sum(flat_of(grad_keys))
    grad_values = row_sum(flat_of(grad_values))
    grad_q = dot_tn(own_rows, grad_query)
    grad_k = dot_tn(own_rows, grad_keys)
    grad_v = dot_tn(own_rows, grad_values)
    input_own = (
        grad_first + dot_nt(grad_query, w_q) + dot_nt(grad_keys, w_k) + dot_nt(grad_values, w_v)
    )
    input_grad = lax.all_gather(input_own, "mp", axis=0, tiled=True)[None]

    def half_of(matrix, half):
        span = matrix.shape[1] // halves
        return matrix[:, half * span : (half + 1) * span]

    grads = [grad_q, grad_k, grad_v, grad_out, grad_up, grad_down]
    packed_grad = jnp.concatenate(
        [
            jnp.concatenate([half_of(g, half) for g in grads], axis=1).astype(low)
            for half in range(halves)
        ],
        axis=0,
    )
    summed = lax.psum_scatter(
        packed_grad, ("mp", "dp"), scatter_dimension=0, tiled=True
    ).astype(jnp.float32)
    summed_attn = jnp.stack([summed[:, cuts[i] : cuts[i + 1]] for i in range(3)])
    summed_out = summed[:, cuts[3] : cuts[4]].T
    summed_up = summed[:, cuts[4] : cuts[5]]
    summed_down = summed[:, cuts[5] : cuts[6]].T

    vector_grad = jnp.concatenate(
        [
            jnp.sum(grad_query.astype(jnp.float32), 0),
            jnp.sum(grad_values.astype(jnp.float32), 0),
            jnp.sum(branch_low.astype(jnp.float32), 0),
            grad_gain_one,
            grad_shift_one,
            jnp.sum(feed_low.astype(jnp.float32), 0),
            grad_gain_two,
            grad_shift_two,
            jnp.sum(gate_low.astype(jnp.float32), 0),
        ]
    )
    return (student_out, input_grad) + lamb_update(
        (summed_attn, summed_out, summed_up, summed_down),
        (attn_weight, out_weight, up_weight, down_weight),
        (attn_first, out_first, up_first, down_first),
        (attn_second, out_second, up_second, down_second),
        vector_grad,
        vectors,
        vector_first,
        vector_second,
    )


def lamb_update(grads, weights, firsts, seconds, vector_grad, vectors, vector_first, vector_second):
    moments, squares, steps = [], [], []
    for grad_now, weight, first_old, second_old in zip(grads, weights, firsts, seconds):
        first_new, second_new, step_now = adam_moments(grad_now, first_old, second_old)
        moments.append(first_new)
        squares.append(second_new)
        steps.append(step_now + decay_rate * weight)
    weight_total, update_total, vector_total = lax.psum(
        (matrix_squares(*weights), matrix_squares(*steps), vector_grad), ("dp", "mp")
    )
    weight_norms = jnp.sqrt(weight_total)
    update_norms = jnp.sqrt(update_total)
    trust_ratio = weight_norms / update_norms
    ratios = [trust_ratio[0:3][:, None, None], trust_ratio[3], trust_ratio[4], trust_ratio[5]]
    updated = [
        weight - matrix_rate * ratio * step for weight, ratio, step in zip(weights, ratios, steps)
    ]
    vector_moment, vector_square, step_vector = adam_moments(
        vector_total, vector_first, vector_second
    )
    vector_updated = vectors - vector_rate * step_vector
    return (
        *updated,
        *moments,
        *squares,
        vector_moment,
        vector_square,
        vector_updated,
        jnp.stack([weight_norms, update_norms]),
        trust_ratio,
    )


LOG_PAIR = 128
MESH = pl.DeviceIdType.MESH
low = jnp.bfloat16
f32 = jnp.float32
VMEM_SPEC = pl.BlockSpec(memory_space=pltpu.VMEM)
ANY_SPEC = pl.BlockSpec(memory_space=pl.ANY)
LIMIT = 60 * 2**20


def dnn(left, right):
    return jnp.dot(left, right, preferred_element_type=f32)


def dnt(left, right):
    return lax.dot_general(left, right, (((1,), (1,)), ((), ())), preferred_element_type=f32)


def lane_index(shape):
    return lax.broadcasted_iota(jnp.int32, shape, 1)


def split_three(value):
    top = value.astype(low).astype(f32)
    rest = value - top
    middle = rest.astype(low).astype(f32)
    return (top, middle, rest - middle)


def flip(value):
    return value.astype(f32).T.astype(low)


def place():
    at = lax.axis_index("dp")
    return (at, lax.axis_index("mp"), at // 4, (at // 2) % 2, at % 2)


def near():
    at, y, z, x, core = place()
    return dict(
        twin=(at + 1 - 2 * core, y),
        x=(at + 2 - 4 * x, y),
        y=(at, 1 - y),
        z=[(((z + step) % 4) * 4 + 2 * x + core, y) for step in (1, 2, 3)],
    )


def greet(peers):
    sem = pltpu.get_barrier_semaphore()
    for peer in peers:
        pl.semaphore_signal(sem, inc=1, device_id=peer, device_id_type=MESH)
    pl.semaphore_wait(sem, len(peers))


def remote(src, dst, sends, recvs, at, peer):
    return pltpu.make_async_remote_copy(
        src_ref=src,
        dst_ref=dst,
        send_sem=sends.at[at],
        recv_sem=recvs.at[at],
        device_id=peer,
        device_id_type=MESH,
    )


def row_norm(rows):
    center = rows - jnp.mean(rows, -1, keepdims=True)
    scale = lax.rsqrt(jnp.mean(center * center, -1, keepdims=True) + layer_eps)
    return (center * scale, scale)


def norm_pull(grad, unit, scale, gain):
    lifted = grad * gain
    return scale * (
        lifted
        - jnp.mean(lifted, -1, keepdims=True)
        - unit * jnp.mean(lifted * unit, -1, keepdims=True)
    )


def normal_share(value):
    return 0.5 * (1.0 + lax.erf(value * 0.7071067811865476))


def pair_forward(query, keys, values, bias):
    count, span = query.shape[0], keys.shape[0]
    lane_q, lane_k = lane_index((count, LOG_PAIR)), lane_index((span, LOG_PAIR))
    outs, logs = [], []
    for head in range(2):
        spare = HDIM * (1 - head)
        keys_now = jnp.where(
            lane_k // HDIM == head,
            keys.astype(f32),
            jnp.where(lane_k == spare, bias, 0.0),
        ).astype(low)
        query_now = jnp.where(
            lane_q // HDIM == head,
            query.astype(f32),
            jnp.where(lane_q == spare, 1.0, 0.0),
        ).astype(low)
        scores = dnt(query_now, keys_now)
        peak = jnp.max(scores, -1, keepdims=True)
        exponent = jnp.exp(scores - peak)
        total = jnp.sum(exponent, -1, keepdims=True)
        outs.append(dnn((exponent * (1.0 / total)).astype(low), values))
        logs.append(peak + jnp.log(total))
    return (
        jnp.where(lane_q < HDIM, outs[0], outs[1]),
        jnp.where(lane_q < HDIM, logs[0], logs[1]),
    )


def project_rows(x_ref, w_ref, vec_ref, y, q_ref, k_ref, v_ref):
    length, width = x_ref.shape
    part = width // 2
    block = 256

    def keys_values(step, carry):
        at = pl.ds(pl.multiple_of(step * block, block), block)
        rows = x_ref[at, :]
        for half in range(2):
            cols = slice(half * part, (half + 1) * part)
            k_ref[at, cols] = dnn(rows, w_ref[half, :, part : 2 * part]).astype(low)
            v_ref[at, cols] = (
                dnn(rows, w_ref[half, :, 2 * part : 3 * part]) + vec_ref[1:2, cols]
            ).astype(low)
        return carry

    lax.fori_loop(0, length // block, keys_values, 0)

    def queries(step, carry):
        at = pl.ds(pl.multiple_of(step * block, block), block)
        rows = x_ref[pl.ds(pl.multiple_of(y * (length // 2) + step * block, block), block), :]
        for half in range(2):
            cols = slice(half * part, (half + 1) * part)
            q_ref[at, cols] = (
                (dnn(rows, w_ref[half, :, 0:part]) + vec_ref[0:1, cols]).astype(low).astype(f32)
                * HDIM**-0.5
            ).astype(low)
        return carry

    lax.fori_loop(0, length // 2 // block, queries, 0)


def attend_rows(q_ref, k_ref, v_ref, bias_ref, a_ref, af_ref, log_ref):
    block = 256
    rows = q_ref.shape[0]

    def one_pair(pair, carry):
        cols = pl.ds(pl.multiple_of(pair * LOG_PAIR, LOG_PAIR), LOG_PAIR)
        keys, values, bias = k_ref[:, cols], v_ref[:, cols], bias_ref[...]
        for start in range(0, rows, block):
            at = slice(start, start + block)
            mixed, logs = pair_forward(q_ref[at, cols], keys, values, bias)
            a_ref[at, cols] = mixed.astype(low)
            af_ref[at, cols] = mixed
            log_ref[pair, at, :] = logs
        return carry

    lax.fori_loop(0, q_ref.shape[1] // LOG_PAIR, one_pair, 0)


def feed_rows(x_ref, a_ref, w_ref, vec_ref, y, r1_ref, z_ref, u_ref, r2_ref, out_ref):
    rows, width = a_ref.shape
    part = width // 2
    block = 256

    def some_rows(step, carry):
        at = pl.ds(pl.multiple_of(step * block, block), block)
        x_at = pl.ds(pl.multiple_of(y * rows + step * block, block), block)
        first = x_ref[x_at, :].astype(f32) + vec_ref[2:3, :]
        for half in range(2):
            first += dnt(
                a_ref[at, half * part : (half + 1) * part], w_ref[half, :, 3 * part : 4 * part]
            )
        r1_ref[at, :] = first
        unit, unused = row_norm(first)
        normed = unit * vec_ref[3:4, :] + vec_ref[4:5, :]
        normed_low = normed.astype(low)
        r2_ref[at, :] = normed + vec_ref[5:6, :]
        for piece in range(4):
            half, base = piece // 2, 4 * part + (piece % 2) * width
            cols = slice(piece * width, (piece + 1) * width)
            gate = dnn(normed_low, w_ref[half, :, base : base + width]) + vec_ref[
                8 + piece : 9 + piece, :
            ]
            z_ref[at, cols] = gate
            active = (gate * normal_share(gate)).astype(low)
            u_ref[at, cols] = active
            r2_ref[at, :] += dnt(active, w_ref[half, :, base + 2 * width : base + 3 * width])
        unit, unused = row_norm(r2_ref[at, :])
        out_ref[at, :] = unit * vec_ref[6:7, :] + vec_ref[7:8, :]
        return carry

    lax.fori_loop(0, rows // block, some_rows, 0)


def forward_kernel(
    x_ref, w_ref, vec_ref, bias_ref,
    q_ref, k_ref, v_ref, a_ref, af_ref, log_ref, r1_ref, z_ref, u_ref, r2_ref, out_ref,
):
    y = lax.axis_index("mp")
    project_rows(x_ref, w_ref, vec_ref, y, q_ref, k_ref, v_ref)
    attend_rows(q_ref, k_ref, v_ref, bias_ref, a_ref, af_ref, log_ref)
    feed_rows(x_ref, a_ref, w_ref, vec_ref, y, r1_ref, z_ref, u_ref, r2_ref, out_ref)


def shape_of(*dims, kind=f32):
    return jax.ShapeDtypeStruct(dims, kind)


def forward_call(x, w, vec, bias):
    length, width = x.shape
    rows = length // 2
    hidden = 4 * width
    return pl.pallas_call(
        forward_kernel,
        name="student_forward",
        out_shape=[
            shape_of(rows, width, kind=low),
            shape_of(length, width, kind=low),
            shape_of(length, width, kind=low),
            shape_of(rows, width, kind=low),
            shape_of(rows, width),
            shape_of(width // LOG_PAIR, rows, LOG_PAIR),
            shape_of(rows, width),
            shape_of(rows, hidden),
            shape_of(rows, hidden, kind=low),
            shape_of(rows, width),
            shape_of(rows, width),
        ],
        in_specs=[VMEM_SPEC] * 4,
        out_specs=[VMEM_SPEC] * 11,
        compiler_params=pltpu.CompilerParams(vmem_limit_bytes=LIMIT),
    )(x, w, vec, bias)


def teacher_kernel(
    x_ref, w_ref, vec_ref, bias_ref, places_ref, aimed_ref, k_ref, v_ref, part_ref, come_ref,
    sends, recvs,
):
    y = lax.axis_index("mp")
    peer = near()["y"]
    greet([peer])
    length, width = x_ref.shape
    part = width // 2
    count = places_ref.shape[0]
    mine = pl.ds(pl.multiple_of(y * part, LOG_PAIR), part)
    block = 256

    def keys_values(step, carry):
        at = pl.ds(pl.multiple_of(step * block, block), block)
        rows = x_ref[at, :]
        k_ref[at, :] = dnn(rows, w_ref[:, part : 2 * part]).astype(low)
        v_ref[at, :] = (dnn(rows, w_ref[:, 2 * part : 3 * part]) + vec_ref[1:2, mine]).astype(low)
        return carry

    lax.fori_loop(0, length // block, keys_values, 0)
    pick = jnp.where(places_ref[:, 0:1] == lane_index((count, length)), 1.0, 0.0).astype(low)
    listed = dnn(pick, x_ref[...])
    query = (dnn(listed.astype(low), w_ref[:, 0:part]) + vec_ref[0:1, mine]).astype(low)
    query = (query.astype(f32) * HDIM**-0.5).astype(low)
    branch = jnp.zeros((count, width), f32)
    for pair in range(part // LOG_PAIR):
        cols = slice(pair * LOG_PAIR, (pair + 1) * LOG_PAIR)
        mixed, unused = pair_forward(query[:, cols], k_ref[:, cols], v_ref[:, cols], bias_ref[...])
        branch += dnt(mixed.astype(low), w_ref[:, 3 * part + pair * LOG_PAIR : 3 * part + (pair + 1) * LOG_PAIR])

    def joined(value, at):
        part_ref[at] = value
        copy = remote(part_ref.at[at], come_ref.at[at], sends, recvs, at, peer)
        copy.start()
        copy.wait()
        return value + come_ref[at]

    first = listed + joined(branch, 0) + vec_ref[2:3, :]
    unit, unused = row_norm(first)
    normed = unit * vec_ref[3:4, :] + vec_ref[4:5, :]
    normed_low = normed.astype(low)
    feed = jnp.zeros((count, width), f32)
    for piece in range(2):
        base = 4 * part + piece * width
        gate = dnn(normed_low, w_ref[:, base : base + width])
        gate += vec_ref[pl.ds(8 + 2 * y + piece, 1), :]
        active = (gate * normal_share(gate)).astype(low)
        feed += dnt(active, w_ref[:, base + 2 * width : base + 3 * width])
    second = normed + joined(feed, 1) + vec_ref[5:6, :]
    unit, unused = row_norm(second)
    aimed_ref[...] = unit * vec_ref[6:7, :] + vec_ref[7:8, :]


def teacher_call(x, w, vec, bias, places, number):
    length, width = x.shape
    count = places.shape[0]
    return pl.pallas_call(
        teacher_kernel,
        name="teacher_forward",
        out_shape=shape_of(count, width),
        in_specs=[VMEM_SPEC] * 5,
        out_specs=VMEM_SPEC,
        scratch_shapes=[
            pltpu.VMEM((length, width // 2), low),
            pltpu.VMEM((length, width // 2), low),
            pltpu.VMEM((2, count, width), f32),
            pltpu.VMEM((2, count, width), f32),
            pltpu.SemaphoreType.DMA((2,)),
            pltpu.SemaphoreType.DMA((2,)),
        ],
        compiler_params=pltpu.CompilerParams(
            vmem_limit_bytes=LIMIT, collective_id=number, has_side_effects=True
        ),
    )(x, w, vec, bias, places)


def feed_back_kernel(
    out_ref, cot_ref, aimed_ref, places_ref, r1_ref, r2_ref, z_ref, u_ref, a_ref, w_ref, vec_ref,
    grad_ref, ga_ref, g1_ref, sums_ref, flipped_ref, normed_flip_ref, gr2_ref,
):
    y = lax.axis_index("mp")
    rows, width = out_ref.shape
    part = width // 2
    block = 256
    sums_ref[...] = jnp.zeros(sums_ref.shape, f32)

    def top(step, carry):
        at = pl.ds(pl.multiple_of(step * block, block), block)
        row_at = lax.broadcasted_iota(jnp.int32, (block, places_ref.shape[1]), 0)
        pick = jnp.where(row_at + (y * rows + step * block) == places_ref[0:1, :], 1.0, 0.0)
        times = jnp.sum(pick, -1, keepdims=True)
        aimed = jnp.dot(
            pick, aimed_ref[...], precision=lax.Precision.HIGHEST, preferred_element_type=f32
        ) / jnp.maximum(times, 1.0)
        own = out_ref[at, :]
        inner = jnp.sum(own * aimed, -1, keepdims=True)
        square_own = jnp.sum(own * own, -1, keepdims=True) + cosine_eps
        square_aim = jnp.sum(aimed * aimed, -1, keepdims=True) + cosine_eps
        scale = cosine_weight * times * lax.rsqrt(square_own) * lax.rsqrt(square_aim)
        grad = cot_ref[at, :].astype(f32) - scale * (aimed - own * (inner / square_own))
        unit, spread = row_norm(r2_ref[at, :])
        sums_ref[6:7, :] += jnp.sum(grad * unit, 0, keepdims=True)
        sums_ref[7:8, :] += jnp.sum(grad, 0, keepdims=True)
        back = norm_pull(grad, unit, spread, vec_ref[6:7, :])
        gr2_ref[at, :] = back
        back_low = back.astype(low)
        sums_ref[5:6, :] += jnp.sum(back_low.astype(f32), 0, keepdims=True)
        ga_ref[at, :] = back_low
        flipped_ref[:, at] = flip(back_low)
        unit, unused = row_norm(r1_ref[at, :])
        normed_flip_ref[:, at] = flip(unit * vec_ref[3:4, :] + vec_ref[4:5, :])
        return carry

    lax.fori_loop(0, rows // block, top, 0)
    feed_low = ga_ref[...]
    for piece in range(4):
        half, base = piece // 2, 4 * part + (piece % 2) * width
        up_cols = slice(base, base + width)
        down_cols = slice(base + 2 * width, base + 3 * width)
        cols = slice(piece * width, (piece + 1) * width)
        grad_ref[half, :, down_cols] = dnn(flipped_ref[...], u_ref[:, cols]).astype(low)
        gate = z_ref[:, cols]
        slope = normal_share(gate) + gate * (
            jnp.exp(-0.5 * gate * gate) * 0.3989422804014327
        )
        gate_low = (dnn(feed_low, w_ref[half, :, down_cols]) * slope).astype(low)
        sums_ref[8 + piece : 9 + piece, :] = jnp.sum(gate_low.astype(f32), 0, keepdims=True)
        grad_ref[half, :, up_cols] = dnn(normed_flip_ref[...], gate_low).astype(low)
        gr2_ref[...] += dnt(gate_low, w_ref[half, :, up_cols])

    def middle(step, carry):
        at = pl.ds(pl.multiple_of(step * block, block), block)
        grad = gr2_ref[at, :]
        unit, spread = row_norm(r1_ref[at, :])
        sums_ref[3:4, :] += jnp.sum(grad * unit, 0, keepdims=True)
        sums_ref[4:5, :] += jnp.sum(grad, 0, keepdims=True)
        back = norm_pull(grad, unit, spread, vec_ref[3:4, :])
        g1_ref[at, :] = back
        back_low = back.astype(low)
        sums_ref[2:3, :] += jnp.sum(back_low.astype(f32), 0, keepdims=True)
        flipped_ref[:, at] = flip(back_low)
        for half in range(2):
            cols = slice(half * part, (half + 1) * part)
            ga_ref[at, cols] = dnn(back_low, w_ref[half, :, 3 * part : 4 * part]).astype(low)
        return carry

    lax.fori_loop(0, rows // block, middle, 0)
    for half in range(2):
        grad_ref[half, :, 3 * part : 4 * part] = dnn(
            flipped_ref[...], a_ref[:, half * part : (half + 1) * part]
        ).astype(low)


def feed_back_call(out, cot, aimed, places, r1, r2, z, u, a, w, vec):
    rows, width = out.shape
    return pl.pallas_call(
        feed_back_kernel,
        name="feed_backward",
        out_shape=[
            shape_of(*w.shape, kind=low),
            shape_of(rows, width, kind=low),
            shape_of(rows, width),
            shape_of(*vec.shape),
        ],
        in_specs=[VMEM_SPEC] * 11,
        out_specs=[VMEM_SPEC] * 4,
        scratch_shapes=[
            pltpu.VMEM((width, rows), low),
            pltpu.VMEM((width, rows), low),
            pltpu.VMEM((rows, width), f32),
        ],
        compiler_params=pltpu.CompilerParams(vmem_limit_bytes=LIMIT),
    )(out, cot, aimed, places, r1, r2, z, u, a, w, vec)


def pair_back(query, grad_mixed, mixed, logs, keys, values, bias):
    count, span = query.shape[0], keys.shape[0]
    lane_q, lane_k = lane_index((count, LOG_PAIR)), lane_index((span, LOG_PAIR))
    query_wide, grad_wide = query.astype(f32), grad_mixed.astype(f32)
    keys_wide, values_wide = keys.astype(f32), values.astype(f32)
    product = grad_wide * mixed
    grad_keys, grad_values, grad_query = [], [], []
    for head in range(2):
        spare = HDIM * (1 - head)
        own_q, own_k = lane_q // HDIM == head, lane_k // HDIM == head
        inner = jnp.sum(jnp.where(own_q, product, 0.0), -1, keepdims=True)
        query_now = jnp.where(own_q, query_wide, jnp.where(lane_q == spare, 1.0, 0.0))
        grad_now = jnp.where(own_q, grad_wide, 0.0)
        for place_at, (log_term, inner_term) in enumerate(
            zip(split_three(logs[:, HDIM * head : HDIM * head + 1]), split_three(inner))
        ):
            here = lane_q == spare + 1 + place_at
            query_now = jnp.where(here, log_term, query_now)
            grad_now = jnp.where(here, inner_term, grad_now)
        minus = jnp.where((lane_k > spare) & (lane_k < spare + 4), -1.0, 0.0)
        keys_now = jnp.where(own_k, keys_wide, jnp.where(lane_k == spare, bias, minus)).astype(low)
        values_now = jnp.where(own_k, values_wide, minus).astype(low)
        probs = jnp.exp(dnt(keys_now, query_now.astype(low)))
        grad_scores = (probs * dnt(values_now, grad_now.astype(low))).astype(low)
        grad_keys.append(dnn(grad_scores, query))
        grad_values.append(dnn(probs.astype(low), grad_mixed))
        flipped = keys_wide.T[HDIM * head : HDIM * (head + 1)].astype(low)
        grad_query.append(dnn(flipped, grad_scores))
    return (
        jnp.concatenate(grad_query, 0).T * HDIM**-0.5,
        jnp.where(lane_k < HDIM, grad_keys[0], grad_keys[1]),
        jnp.where(lane_k < HDIM, grad_values[0], grad_values[1]),
    )


def attend_back_kernel(
    x_ref, q_ref, k_ref, v_ref, bias_ref, log_ref, af_ref, ga_ref, g1_ref, out_ref, w_ref,
    grad_ref, input_ref, student_ref, sums_ref,
    gq_ref, gk_ref, gv_ref, come_ref, x_flip_ref, send_ref, come_in_ref, sends, recvs,
):
    y = lax.axis_index("mp")
    peer = near()["y"]
    greet([peer])
    rows, width = q_ref.shape
    part = width // 2
    own = pl.ds(pl.multiple_of(y * rows, rows), rows)
    other = pl.ds(pl.multiple_of((1 - y) * rows, rows), rows)
    student_ref[own, :] = out_ref[...].astype(low)
    share = remote(student_ref.at[own], student_ref.at[own], sends, recvs, 0, peer)
    share.start()
    x_flip_ref[...] = flip(x_ref[own, :])

    def one_pair(pair, carry):
        cols = pl.ds(pl.multiple_of(pair * LOG_PAIR, LOG_PAIR), LOG_PAIR)
        grad_query, grad_keys, grad_values = pair_back(
            q_ref[:, cols], ga_ref[:, cols], af_ref[:, cols], log_ref[pair],
            k_ref[:, cols], v_ref[:, cols], bias_ref[...],
        )
        gq_ref[:, cols] = grad_query.astype(low)
        gk_ref[:, cols] = grad_keys.astype(low)
        gv_ref[:, cols] = grad_values.astype(low)
        return carry

    lax.fori_loop(0, width // LOG_PAIR, one_pair, 0)
    copies = [
        remote(source.at[other], come_ref.at[at], sends, recvs, 1 + at, peer)
        for at, source in enumerate((gk_ref, gv_ref))
    ]
    for copy in copies:
        copy.start()
    sums_ref[...] = jnp.zeros(sums_ref.shape, f32)
    sums_ref[0:1, :] = jnp.sum(gq_ref[...].astype(f32), 0, keepdims=True)

    def weight_grad(base, value_ref):
        for half in range(2):
            grad_ref[half, :, base : base + part] = dnn(
                x_flip_ref[...], value_ref[:, half * part : (half + 1) * part]
            ).astype(low)

    def input_part(base, value_ref):
        total = dnt(value_ref[:, 0:part], w_ref[0, :, base : base + part])
        return total + dnt(value_ref[:, part:width], w_ref[1, :, base : base + part])

    weight_grad(0, gq_ref)
    total = g1_ref[...] + input_part(0, gq_ref)
    for at, source in enumerate((gk_ref, gv_ref)):
        copies[at].wait()
        gq_ref[...] = (source[own, :].astype(f32) + come_ref[at].astype(f32)).astype(low)
        weight_grad((1 + at) * part, gq_ref)
        total += input_part((1 + at) * part, gq_ref)
    sums_ref[1:2, :] = jnp.sum(gq_ref[...].astype(f32), 0, keepdims=True)
    input_ref[own, :] = total
    send_ref[...] = total.astype(low)
    copy = remote(send_ref, come_in_ref, sends, recvs, 3, peer)
    copy.start()
    copy.wait()
    input_ref[other, :] = come_in_ref[...].astype(f32)
    share.wait_send()
    remote(student_ref.at[other], student_ref.at[other], sends, recvs, 0, peer).wait_recv()


def attend_back_call(x, q, k, v, bias, logs, af, ga, g1, out, w, number):
    length, width = x.shape
    rows = length // 2
    return pl.pallas_call(
        attend_back_kernel,
        name="attention_backward",
        out_shape=[
            shape_of(2, width, 3 * width // 2, kind=low),
            shape_of(length, width),
            shape_of(length, width, kind=low),
            shape_of(12, width),
        ],
        in_specs=[VMEM_SPEC] * 11,
        out_specs=[VMEM_SPEC] * 4,
        scratch_shapes=[
            pltpu.VMEM((rows, width), low),
            pltpu.VMEM((length, width), low),
            pltpu.VMEM((length, width), low),
            pltpu.VMEM((2, rows, width), low),
            pltpu.VMEM((width, rows), low),
            pltpu.VMEM((rows, width), low),
            pltpu.VMEM((rows, width), low),
            pltpu.SemaphoreType.DMA((4,)),
            pltpu.SemaphoreType.DMA((4,)),
        ],
        compiler_params=pltpu.CompilerParams(
            vmem_limit_bytes=LIMIT, collective_id=number, has_side_effects=True
        ),
    )(x, q, k, v, bias, logs, af, ga, g1, out, w)


def adam_step(grad, first, second):
    first_new = beta_one * first + (1.0 - beta_one) * grad
    second_new = beta_two * second + (1.0 - beta_two) * grad * grad
    step = (
        first_new
        / (1.0 - beta_one**STEP)
        / (jnp.sqrt(second_new / (1.0 - beta_two**STEP)) + adam_eps)
    )
    return (first_new, second_new, step)


def shared_sum(value, mine_ref, come_ref, sends, recvs, ways, z):
    for at, way in enumerate(("twin", "x", "y")):
        mine_ref[at] = value
        copy = remote(mine_ref.at[at], come_ref.at[at], sends, recvs, at, ways[way])
        copy.start()
        copy.wait()
        value = value + come_ref[at]
    mine_ref[3] = value
    copies = []
    for step in range(3):
        copy = remote(mine_ref.at[3], come_ref.at[3 + step], sends, recvs, 3 + step, ways["z"][step])
        copy.start()
        copies.append(copy)
    for copy in copies:
        copy.wait()
    terms = [value] + [come_ref[3 + step] for step in range(3)]
    total = None
    for z_from in range(4):
        term = terms[0]
        for step in range(1, 4):
            term = jnp.where((z + 4 - step) % 4 == z_from, terms[step], term)
        total = term if total is None else total + term
    return total


def finish_kernel(
    chunks,
    ga_ref, gf_ref, vg_ref, vec_ref, vm_ref, vs_ref,
    aw, ow, uw, dw, am, om, um, dm, a2, o2, u2, d2,
    aw_o, ow_o, uw_o, dw_o, am_o, om_o, um_o, dm_o, a2_o, o2_o, u2_o, d2_o,
    vm_o, vs_o, vec_o, norm_o,
    one_ref, ax_ref, ay_ref, bx_ref, by_ref, z_ref, tot_ref, vmine, vcome, nmine, ncome,
    sends, recvs, zsends, zrecvs, vsends, vrecvs, nsends, nrecvs,
):
    at, y, z, x, core = place()
    ways = near()
    greet([ways["twin"], ways["x"], ways["y"]] + ways["z"])
    part = aw.shape[2]
    units = uw.shape[1]
    low_half, high_half = pl.ds(0, 2), pl.ds(2, 2)
    started = []

    def go(src, dst, kind, chunk, peer):
        copy = remote(src, dst, sends, recvs, (chunk, kind), peer)
        copy.start()
        started.append(copy)

    def landed(dst, kind, chunk):
        remote(dst, dst, sends, recvs, (chunk, kind), ways["x"]).wait_recv()

    def source(chunk):
        a, b = chunks[chunk]
        if b <= 3 * part:
            return (ga_ref, pl.ds(a, b - a))
        return (gf_ref, pl.ds(a, b - a))

    def cols(chunk):
        a, b = chunks[chunk]
        return pl.ds(a, b - a)

    for k in range(len(chunks)):
        ref, span = source(k)
        go(ref.at[:, :, :, 1 - core, :, span], one_ref.at[:, :, :, :, cols(k)], 0, k, ways["twin"])
    vector_total = shared_sum(vg_ref[...], vmine, vcome, vsends, vrecvs, ways, z)
    for k in range(len(chunks)):
        ref, span = source(k)
        here = cols(k)
        landed(one_ref.at[:, :, :, :, here], 0, k)

        def add_block(step, carry, ref=ref, span=span, here=here):
            yy, zz, xx = step // 8, (step // 2) % 4, step % 2
            one_ref[yy, zz, xx, :, here] = (
                one_ref[yy, zz, xx, :, here].astype(f32) + ref[yy, zz, xx, core, :, span].astype(f32)
            ).astype(low)
            return carry

        lax.fori_loop(0, 16, add_block, 0)
        go(one_ref.at[:, low_half, 1 - x, :, here], ax_ref.at[:, :, :, here], 1, k, ways["x"])
        go(one_ref.at[1 - y, high_half, :, :, here], by_ref.at[:, :, :, here], 2, k, ways["y"])
    for k in range(len(chunks)):
        here = cols(k)
        landed(ax_ref.at[:, :, :, here], 1, k)

        def add_x(step, carry, here=here):
            yy, zz = step // 2, step % 2
            ax_ref[yy, zz, :, here] = (
                ax_ref[yy, zz, :, here].astype(f32) + one_ref[yy, zz, x, :, here].astype(f32)
            ).astype(low)
            return carry

        lax.fori_loop(0, 4, add_x, 0)
        go(ax_ref.at[1 - y, :, :, here], ay_ref.at[:, :, here], 3, k, ways["y"])
        landed(by_ref.at[:, :, :, here], 2, k)

        def add_y(step, carry, here=here):
            zz, xx = step // 2, step % 2
            by_ref[zz, xx, :, here] = (
                by_ref[zz, xx, :, here].astype(f32) + one_ref[y, 2 + zz, xx, :, here].astype(f32)
            ).astype(low)
            return carry

        lax.fori_loop(0, 4, add_y, 0)
        go(by_ref.at[:, 1 - x, :, here], bx_ref.at[:, :, here], 4, k, ways["x"])
    zcopies = []
    for k in range(len(chunks)):
        here = cols(k)
        landed(ay_ref.at[:, :, here], 3, k)
        landed(bx_ref.at[:, :, here], 4, k)
        for zz in range(2):
            tot_ref[zz, :, here] = (
                ax_ref[y, zz, :, here].astype(f32) + ay_ref[zz, :, here].astype(f32)
            ).astype(low)
            tot_ref[2 + zz, :, here] = (
                by_ref[zz, x, :, here].astype(f32) + bx_ref[zz, :, here].astype(f32)
            ).astype(low)
        for step in range(3):
            copy = remote(
                tot_ref.at[(z + 1 + step) % 4, :, here], z_ref.at[step, :, here],
                zsends, zrecvs, (k, step), ways["z"][step],
            )
            copy.start()
            zcopies.append(copy)
    for copy in zcopies:
        copy.wait()
    for copy in started:
        copy.wait_send()

    def grad_of(a, b):
        total = tot_ref[z, :, a:b].astype(f32)
        for step in range(3):
            total += z_ref[step, :, a:b].astype(f32)
        return total

    lane = lane_index((8, LOG_PAIR))
    row = lax.broadcasted_iota(jnp.int32, (8, LOG_PAIR), 0)
    squares = jnp.zeros((8, LOG_PAIR), f32)

    def one_matrix(index, grad, w, first, second, w_o, first_o, second_o, squares):
        first_new, second_new, step = adam_step(grad, first[...], second[...])
        first_o[...] = first_new
        second_o[...] = second_new
        weight = w[...]
        step = step + decay_rate * weight
        w_o[...] = step
        for line, value in ((0, weight), (1, step)):
            total = jnp.sum(jnp.sum(value * value, -1, keepdims=True), 0, keepdims=True)
            squares = jnp.where((row == line) & (lane == index), total, squares)
        return squares

    for index in range(3):
        squares = one_matrix(
            index, grad_of(index * part, (index + 1) * part), aw.at[index], am.at[index], a2.at[index],
            aw_o.at[index], am_o.at[index], a2_o.at[index], squares,
        )
    squares = one_matrix(
        3, grad_of(3 * part, 4 * part), ow, om, o2, ow_o, om_o, o2_o, squares
    )
    squares = one_matrix(
        4, grad_of(4 * part, 4 * part + units), uw, um, u2, uw_o, um_o, u2_o, squares
    )
    squares = one_matrix(
        5, grad_of(4 * part + units, 4 * part + 2 * units), dw, dm, d2, dw_o, dm_o, d2_o, squares
    )
    vm_new, vs_new, vector_step = adam_step(vector_total, vm_ref[...], vs_ref[...])
    vm_o[...] = vm_new
    vs_o[...] = vs_new
    vec_o[...] = vec_ref[...] - vector_rate * vector_step
    norms = jnp.sqrt(shared_sum(squares, nmine, ncome, nsends, nrecvs, ways, z))
    ratio = norms[0:1, :] / norms[1:2, :]
    norm_o[...] = jnp.where(row == 2, ratio, norms)

    def apply(index, w, w_o):
        w_o[...] = w[...] - matrix_rate * ratio[0:1, index : index + 1] * w_o[...]

    for index in range(3):
        apply(index, aw.at[index], aw_o.at[index])
    apply(3, ow, ow_o)
    apply(4, uw, uw_o)
    apply(5, dw, dw_o)


def finish_call(grad_attn, grad_feed, vector_grad, vec, vm, vs, weights, firsts, seconds, number):
    part = weights[0].shape[2]
    units = weights[2].shape[1]
    lines = weights[0].shape[1]
    wide = 4 * part + 2 * units
    chunks = (
        (4 * part, 4 * part + units), (4 * part + units, wide), (3 * part, 4 * part), (0, 3 * part),
    )
    count = len(chunks)
    outs = [shape_of(*v.shape) for group in (weights, firsts, seconds) for v in group]
    outs += [shape_of(*vec.shape)] * 3 + [shape_of(8, LOG_PAIR)]
    sem = pltpu.SemaphoreType.DMA
    return pl.pallas_call(
        partial(finish_kernel, chunks),
        name="sum_and_update",
        out_shape=outs,
        in_specs=[VMEM_SPEC] * 18,
        out_specs=[VMEM_SPEC] * len(outs),
        scratch_shapes=[
            pltpu.VMEM((2, 4, 2, lines, wide), low),
            pltpu.VMEM((2, 2, lines, wide), low),
            pltpu.VMEM((2, lines, wide), low),
            pltpu.VMEM((2, lines, wide), low),
            pltpu.VMEM((2, 2, lines, wide), low),
            pltpu.VMEM((3, lines, wide), low),
            pltpu.VMEM((4, lines, wide), low),
            pltpu.VMEM((4,) + vec.shape, f32),
            pltpu.VMEM((6,) + vec.shape, f32),
            pltpu.VMEM((4, 8, LOG_PAIR), f32),
            pltpu.VMEM((6, 8, LOG_PAIR), f32),
            sem((count, 5)), sem((count, 5)), sem((count, 3)), sem((count, 3)),
            sem((6,)), sem((6,)), sem((6,)), sem((6,)),
        ],
        compiler_params=pltpu.CompilerParams(
            vmem_limit_bytes=LIMIT, collective_id=number, has_side_effects=True
        ),
    )(grad_attn, grad_feed, vector_grad, vec, vm, vs, *weights, *firsts, *seconds)


def gather_kernel(
    own_cuts, aim_cuts, ps_ref, pt_ref, gs_ref, gt_ref, local_sem, zsends, zrecvs, sends, recvs
):
    at, y, z, x, core = place()
    ways = near()
    greet([ways["twin"], ways["x"], ways["y"]] + ways["z"])
    chunks = [(0, a, b) for a, b in own_cuts] + [(1, a, b) for a, b in aim_cuts]
    started = []

    def go(ref, chunk, kind, peer):
        copy = remote(ref, ref, sends, recvs, (chunk, kind), peer)
        copy.start()
        started.append(copy)

    def landed(ref, chunk, kind):
        remote(ref, ref, sends, recvs, (chunk, kind), ways["x"]).wait_recv()

    def shard(chunk, zz):
        which, a, b = chunks[chunk]
        if which == 0:
            return gs_ref.at[y, zz, x, core, :, pl.ds(a, b - a)]
        return gt_ref.at[zz, x, core, :, pl.ds(a, b - a)]

    def column(chunk, yy, xx, cc):
        which, a, b = chunks[chunk]
        if which == 0:
            return gs_ref.at[yy, :, xx, cc, :, pl.ds(a, b - a)]
        return gt_ref.at[:, xx, cc, :, pl.ds(a, b - a)]

    def half_column(chunk, yy, xx, cc, half):
        which, a, b = chunks[chunk]
        return gs_ref.at[yy, pl.ds(2 * half, 2), xx, cc, :, pl.ds(a, b - a)]

    own = []
    for k, (which, a, b) in enumerate(chunks):
        source = (ps_ref, pt_ref)[which].at[:, pl.ds(a, b - a)]
        copy = pltpu.make_async_copy(source, shard(k, z), local_sem.at[k])
        copy.start()
        own.append(copy)
        for step in range(3):
            copy = remote(source, shard(k, z), zsends, zrecvs, (k, step), ways["z"][step])
            copy.start()
            started.append(copy)
    for k, (which, a, b) in enumerate(chunks):
        for step in range(3):
            came = shard(k, (z + 3 - step) % 4)
            remote(came, came, zsends, zrecvs, (k, step), ways["x"]).wait_recv()
        own[k].wait()
        go(column(k, y, x, core), k, 0, ways["x"])
        if which == 0:
            go(column(k, y, x, core), k, 1, ways["y"])
        go(column(k, y, x, core), k, 2, ways["twin"])
    for k, (which, a, b) in enumerate(chunks):
        landed(column(k, y, 1 - x, core), k, 0)
        if which == 0:
            go(half_column(k, y, 1 - x, core, 0), k, 3, ways["y"])
        go(column(k, y, 1 - x, core), k, 4, ways["twin"])
        if which == 0:
            landed(column(k, 1 - y, x, core), k, 1)
            go(half_column(k, 1 - y, x, core, 1), k, 5, ways["x"])
            go(column(k, 1 - y, x, core), k, 6, ways["twin"])
    for k, (which, a, b) in enumerate(chunks):
        if which == 0:
            landed(half_column(k, 1 - y, 1 - x, core, 0), k, 3)
            go(half_column(k, 1 - y, 1 - x, core, 0), k, 7, ways["twin"])
            landed(half_column(k, 1 - y, 1 - x, core, 1), k, 5)
            go(half_column(k, 1 - y, 1 - x, core, 1), k, 8, ways["twin"])
    for k, (which, a, b) in enumerate(chunks):
        landed(column(k, y, x, 1 - core), k, 2)
        landed(column(k, y, 1 - x, 1 - core), k, 4)
        if which == 0:
            landed(column(k, 1 - y, x, 1 - core), k, 6)
            landed(half_column(k, 1 - y, 1 - x, 1 - core, 0), k, 7)
            landed(half_column(k, 1 - y, 1 - x, 1 - core, 1), k, 8)
    for copy in started:
        copy.wait_send()


def gather_call(ps, pt, number):
    lines, wide = ps.shape
    own_cuts = tuple((wide * i // 6, wide * (i + 1) // 6) for i in range(6))
    aim_cuts = tuple((wide * i // 6, wide * (i + 1) // 6) for i in range(6))
    count = len(own_cuts) + len(aim_cuts)
    sem = pltpu.SemaphoreType.DMA
    return pl.pallas_call(
        partial(gather_kernel, own_cuts, aim_cuts),
        name="gather_weights",
        out_shape=[
            shape_of(2, 4, 2, 2, lines, wide, kind=low), shape_of(4, 2, 2, lines, wide, kind=low)
        ],
        in_specs=[VMEM_SPEC] * 2,
        out_specs=[ANY_SPEC] * 2,
        scratch_shapes=[
            sem((count,)), sem((count, 3)), sem((count, 3)), sem((count, 9)), sem((count, 9))
        ],
        compiler_params=pltpu.CompilerParams(
            vmem_limit_bytes=LIMIT, collective_id=number, has_side_effects=True
        ),
    )(ps, pt)


def split_kernels(
    tokens,
    teacher_tokens,
    cotangent,
    lengths,
    masked,
    attn_weight,
    out_weight,
    up_weight,
    down_weight,
    attn_first,
    out_first,
    up_first,
    down_first,
    attn_second,
    out_second,
    up_second,
    down_second,
    vectors,
    vector_first,
    vector_second,
    teacher_attn,
    teacher_out,
    teacher_up,
    teacher_down,
    teacher_vectors,
):
    seq_count, length, width = tokens.shape
    rows = length // 2
    y = lax.axis_index("mp")
    weights = (attn_weight, out_weight, up_weight, down_weight)
    x, aim_x = tokens[0], teacher_tokens[0]
    gs, gt = gather_call(
        shard_pack(*weights).astype(low),
        shard_pack(teacher_attn, teacher_out, teacher_up, teacher_down),
        0,
    )
    wide = gs.shape[-1]
    w, aim_w = gs.reshape(2, width, wide), gt.reshape(width, wide)
    vec = vectors.reshape(-1, width)
    bias = jnp.broadcast_to(
        jnp.where(jnp.arange(length) < lengths[0], 0.0, masked_score)[:, None], (length, LOG_PAIR)
    )
    aimed = teacher_call(
        aim_x, aim_w, teacher_vectors.astype(f32).reshape(-1, width), bias, masked[0][:, None], 1
    )
    q, k, v, a, af, logs, r1, z, u, r2, out = forward_call(x, w, vec, bias)
    cot = lax.dynamic_slice_in_dim(cotangent[0], y * rows, rows, 0)
    grad_feed, ga, g1, sums_feed = feed_back_call(
        out, cot, aimed, masked, r1, r2, z, u, a, w, vec
    )
    grad_attn, input_grad, student, sums_attn = attend_back_call(
        x, q, k, v, bias, logs, af, ga, g1, out, w, 2
    )

    def upright(group):
        return (group[0], group[1].T, group[2], group[3].T)

    outs = finish_call(
        grad_attn.reshape(gs.shape[:-1] + (grad_attn.shape[-1],)),
        grad_feed.reshape(gs.shape),
        sums_feed + sums_attn,
        vec,
        vector_first.reshape(-1, width),
        vector_second.reshape(-1, width),
        upright(weights),
        upright((attn_first, out_first, up_first, down_first)),
        upright((attn_second, out_second, up_second, down_second)),
        3,
    )
    norms = outs[15]
    return (
        student[None],
        input_grad[None],
        *upright(outs[:4]),
        *upright(outs[4:8]),
        *upright(outs[8:12]),
        *(value.reshape(-1) for value in outs[12:15]),
        norms[:2, :6],
        norms[2, :6],
    )


def solution(mesh):
    local = split_kernels if dict(mesh.shape) == {"dp": 16, "mp": 2} else split_rows
    return jax.shard_map(
        local,
        mesh=mesh,
        in_specs=(
            P("dp", None, None),
            P("dp", None, None),
            P("dp", None, None),
            P("dp"),
            P("dp", None),
            P(None, "dp", "mp"),
            P("mp", "dp"),
            P("dp", "mp"),
            P("mp", "dp"),
            P(None, "dp", "mp"),
            P("mp", "dp"),
            P("dp", "mp"),
            P("mp", "dp"),
            P(None, "dp", "mp"),
            P("mp", "dp"),
            P("dp", "mp"),
            P("mp", "dp"),
            P(),
            P(),
            P(),
            P(None, "dp", "mp"),
            P("mp", "dp"),
            P("dp", "mp"),
            P("mp", "dp"),
            P(),
        ),
        out_specs=(
            P("dp", None, None),
            P("dp", None, None),
            P(None, "dp", "mp"),
            P("mp", "dp"),
            P("dp", "mp"),
            P("mp", "dp"),
            P(None, "dp", "mp"),
            P("mp", "dp"),
            P("dp", "mp"),
            P("mp", "dp"),
            P(None, "dp", "mp"),
            P("mp", "dp"),
            P("dp", "mp"),
            P("mp", "dp"),
            P(),
            P(),
            P(),
            P(),
            P(),
        ),
        check_vma=False,
    )
```

```python
from functools import partial

import jax
import jax.numpy as jnp
from jax import lax
from jax.experimental import pallas as pl
from jax.experimental.pallas import tpu as pltpu
from jax.sharding import PartitionSpec as P

HDIM = 64
STEP = 5


beta_one = 0.9
beta_two = 0.999
adam_eps = 1e-06
decay_rate = 0.01
matrix_rate = 0.3
vector_rate = 0.2
cosine_weight = 32.0
cosine_eps = 1e-06
layer_eps = 1e-12
masked_score = -1e30


def layer_norm(row_values, gain_vec, shift_vec):
    center = row_values - jnp.mean(row_values, -1, keepdims=True)
    spread = jnp.mean(center * center, -1, keepdims=True)
    return center * lax.rsqrt(spread + layer_eps) * gain_vec + shift_vec


def vector_parts(packed, model_width):
    pieces = [
        packed[position * model_width : (position + 1) * model_width] for position in range(8)
    ]
    return pieces + [packed[8 * model_width :]]


def head_scores(query, key_rows, visible):
    scale_factor = query.shape[-1] ** (-0.5)
    scores = (
        jnp.einsum("sqe,ske->sqk", query, key_rows, preferred_element_type=jnp.float32)
        * scale_factor
    )
    return jnp.where(visible[:, None, :], scores, masked_score)


def head_forward(query, key_rows, value_rows, visible):
    scores = head_scores(query, key_rows, visible)
    row_peak = jnp.max(scores, -1, keepdims=True)
    exponent = jnp.exp(scores - row_peak)
    row_total = jnp.sum(exponent, -1, keepdims=True)
    weights_low = (exponent / row_total).astype(jnp.bfloat16)
    mixed = jnp.einsum("sqk,ske->sqe", weights_low, value_rows, preferred_element_type=jnp.float32)
    return (mixed.astype(jnp.bfloat16), (row_peak + jnp.log(row_total))[..., 0])


def adam_moments(grad_now, first_old, second_old):
    first_new = beta_one * first_old + (1.0 - beta_one) * grad_now
    second_new = beta_two * second_old + (1.0 - beta_two) * grad_now * grad_now
    step_now = (
        first_new
        / (1.0 - beta_one**STEP)
        / (jnp.sqrt(second_new / (1.0 - beta_two**STEP)) + adam_eps)
    )
    return (first_new, second_new, step_now)


def matrix_squares(attn_w, out_w, up_w, down_w):
    return jnp.concatenate(
        [
            jnp.sum(attn_w * attn_w, axis=(1, 2)),
            jnp.stack([jnp.sum(out_w * out_w), jnp.sum(up_w * up_w), jnp.sum(down_w * down_w)]),
        ]
    )


def shard_pack(attn_w, out_w, up_w, down_w):
    return jnp.concatenate(
        [attn_w[0], attn_w[1], attn_w[2], out_w.T, up_w, down_w.T], axis=1
    )


def cosine_pull(rows, places, aimed, row_start):
    row_count = rows.shape[0]
    local_at = places - row_start
    here = (local_at >= 0) & (local_at < row_count)
    picked = rows[jnp.clip(local_at, 0, row_count - 1)]
    inner = jnp.sum(picked * aimed, -1, keepdims=True)
    square_own = jnp.sum(picked * picked, -1, keepdims=True) + cosine_eps
    square_aim = jnp.sum(aimed * aimed, -1, keepdims=True) + cosine_eps
    inverse = lax.rsqrt(square_own) * lax.rsqrt(square_aim)
    pull = -cosine_weight * (aimed * inverse - picked * (inner * inverse / square_own))
    pull = jnp.where(here[:, None], pull, 0.0)
    return jnp.zeros_like(rows).at[jnp.clip(local_at, 0, row_count - 1)].add(pull)


def heads_of(flat):
    return flat.reshape(flat.shape[0], flat.shape[1] // HDIM, HDIM).transpose(1, 0, 2)


def flat_of(split):
    return split.transpose(1, 0, 2).reshape(split.shape[1], -1)


def dot32(left, right):
    return jnp.dot(left, right, preferred_element_type=jnp.float32)


def dot_nt(left, right):
    return lax.dot_general(
        left, right, (((1,), (1,)), ((), ())), preferred_element_type=jnp.float32
    )


def dot_tn(left, right):
    return lax.dot_general(
        left, right, (((0,), (0,)), ((), ())), preferred_element_type=jnp.float32
    )


def split_rows(
    tokens,
    teacher_tokens,
    cotangent,
    lengths,
    masked,
    attn_weight,
    out_weight,
    up_weight,
    down_weight,
    attn_first,
    out_first,
    up_first,
    down_first,
    attn_second,
    out_second,
    up_second,
    down_second,
    vectors,
    vector_first,
    vector_second,
    teacher_attn,
    teacher_out,
    teacher_up,
    teacher_down,
    teacher_vectors,
):
    low = jnp.bfloat16
    everyone = ("dp", "mp")
    shard_at = lax.axis_index("mp")
    halves = lax.axis_size("mp")
    seq_count, length, width = tokens.shape
    rows = length // halves
    row_start = shard_at * rows
    part = attn_weight.shape[2]
    units = up_weight.shape[1]
    cuts = [0, part, 2 * part, 3 * part, 4 * part, 4 * part + units, 4 * part + 2 * units]
    visible = (jnp.arange(length) < lengths[0])[None, None, :]
    places = masked[0]

    student = lax.all_gather(
        shard_pack(attn_weight, out_weight, up_weight, down_weight).astype(low),
        ("mp", "dp"),
        axis=0,
        tiled=True,
    ).reshape(halves, width, cuts[6])
    teacher = lax.all_gather(
        shard_pack(teacher_attn, teacher_out, teacher_up, teacher_down),
        "dp",
        axis=0,
        tiled=True,
    )

    def whole(index):
        return jnp.concatenate(
            [student[half, :, cuts[index] : cuts[index + 1]] for half in range(halves)], axis=1
        )

    teacher_parts = vector_parts(teacher_vectors.astype(jnp.float32), width)
    bias_q = lax.dynamic_slice_in_dim(teacher_parts[0], shard_at * part, part)
    bias_v = lax.dynamic_slice_in_dim(teacher_parts[1], shard_at * part, part)
    bias_up = lax.dynamic_slice_in_dim(teacher_parts[8], shard_at * units, units)
    teacher_rows = teacher_tokens[0]
    listed = teacher_rows[places]
    t_query = (dot32(listed, teacher[:, : cuts[1]]) + bias_q).astype(low)
    t_keys = dot32(teacher_rows, teacher[:, cuts[1] : cuts[2]]).astype(low)
    t_values = (dot32(teacher_rows, teacher[:, cuts[2] : cuts[3]]) + bias_v).astype(low)
    t_mixed, unused_log = head_forward(
        heads_of(t_query), heads_of(t_keys), heads_of(t_values), visible[0]
    )
    t_branch = lax.psum(dot_nt(flat_of(t_mixed), teacher[:, cuts[3] : cuts[4]]), "mp")
    t_first = listed.astype(jnp.float32) + t_branch + teacher_parts[2]
    t_normed = layer_norm(t_first, teacher_parts[3], teacher_parts[4])
    t_gate = dot32(t_normed.astype(low), teacher[:, cuts[4] : cuts[5]]) + bias_up
    t_act = jax.nn.gelu(t_gate, approximate=False).astype(low)
    t_feed = lax.psum(dot_nt(t_act, teacher[:, cuts[5] : cuts[6]]), "mp")
    aimed = layer_norm(t_normed + t_feed + teacher_parts[5], teacher_parts[6], teacher_parts[7])

    pieces = vector_parts(vectors, width)
    all_rows = tokens[0]
    own_rows = lax.dynamic_slice_in_dim(all_rows, row_start, rows, 0)
    w_q, w_k, w_v, w_out, w_up, w_down = [whole(index) for index in range(6)]
    query = heads_of((dot32(own_rows, w_q) + pieces[0]).astype(low))
    keys = heads_of(dot32(all_rows, w_k).astype(low))
    values = heads_of((dot32(all_rows, w_v) + pieces[1]).astype(low))
    mixed, log_total = lax.map(
        lambda g: jax.tree.map(
            lambda v: v[0], head_forward(g[0][None], g[1][None], g[2][None], visible[0])
        ),
        (query, keys, values),
    )
    attended = flat_of(mixed)
    first_sum = own_rows.astype(jnp.float32) + dot_nt(attended, w_out) + pieces[2]
    normed = layer_norm(first_sum, pieces[3], pieces[4])
    normed_low = normed.astype(low)
    gate_in = dot32(normed_low, w_up) + pieces[8]
    activated = jax.nn.gelu(gate_in, approximate=False).astype(low)
    second_sum = normed + dot_nt(activated, w_down) + pieces[5]
    outcome = layer_norm(second_sum, pieces[6], pieces[7])
    student_out = lax.all_gather(outcome.astype(low), "mp", axis=0, tiled=True)[None]

    own_cotangent = lax.dynamic_slice_in_dim(cotangent[0], row_start, rows, 0)
    grad_top = own_cotangent.astype(jnp.float32) + cosine_pull(outcome, places, aimed, row_start)
    unused_top, pull_top = jax.vjp(layer_norm, second_sum, pieces[6], pieces[7])
    grad_second, grad_gain_two, grad_shift_two = pull_top(grad_top)
    feed_low = grad_second.astype(low)
    grad_down = dot_tn(feed_low, activated)
    grad_act = dot32(feed_low, w_down)
    unused_gelu, pull_gelu = jax.vjp(partial(jax.nn.gelu, approximate=False), gate_in)
    (grad_gate,) = pull_gelu(grad_act)
    gate_low = grad_gate.astype(low)
    grad_up = dot_tn(normed_low, gate_low)
    grad_normed = grad_second + dot_nt(gate_low, w_up)
    unused_mid, pull_mid = jax.vjp(layer_norm, first_sum, pieces[3], pieces[4])
    grad_first, grad_gain_one, grad_shift_one = pull_mid(grad_normed)
    branch_low = grad_first.astype(low)
    grad_out = dot_tn(branch_low, attended)
    grad_heads = heads_of(dot32(branch_low, w_out).astype(low))

    def one_head(g):
        query_h, keys_h, values_h, mixed_h, log_h = g
        scale_factor = HDIM**-0.5
        scores = jnp.where(visible[0], dot_nt(query_h, keys_h) * scale_factor, masked_score)
        probs = jnp.exp(scores - log_h[:, None])
        grad_probs = dot_nt(mixed_h, values_h)
        inner = jnp.sum(probs * grad_probs, -1, keepdims=True)
        grad_scores = (probs * (grad_probs - inner)).astype(low)
        return (
            (dot32(grad_scores, keys_h) * scale_factor).astype(low),
            (dot_tn(grad_scores, query_h) * scale_factor).astype(low),
            dot_tn(probs.astype(low), mixed_h).astype(low),
        )

    grad_query, grad_keys, grad_values = lax.map(
        one_head, (query, keys, values, grad_heads, log_total)
    )
    grad_query = flat_of(grad_query)

    def row_sum(term):
        other = lax.dynamic_slice_in_dim(term, (1 - shard_at) * rows, rows, 0)
        mine = lax.dynamic_slice_in_dim(term, row_start, rows, 0)
        came = lax.ppermute(other, "mp", [(0, 1), (1, 0)])
        return (mine.astype(jnp.float32) + came.astype(jnp.float32)).astype(low)

    grad_keys = row_sum(flat_of(grad_keys))
    grad_values = row_sum(flat_of(grad_values))
    grad_q = dot_tn(own_rows, grad_query)
    grad_k = dot_tn(own_rows, grad_keys)
    grad_v = dot_tn(own_rows, grad_values)
    input_own = (
        grad_first + dot_nt(grad_query, w_q) + dot_nt(grad_keys, w_k) + dot_nt(grad_values, w_v)
    )
    input_grad = lax.all_gather(input_own, "mp", axis=0, tiled=True)[None]

    def half_of(matrix, half):
        span = matrix.shape[1] // halves
        return matrix[:, half * span : (half + 1) * span]

    grads = [grad_q, grad_k, grad_v, grad_out, grad_up, grad_down]
    packed_grad = jnp.concatenate(
        [
            jnp.concatenate([half_of(g, half) for g in grads], axis=1).astype(low)
            for half in range(halves)
        ],
        axis=0,
    )
    summed = lax.psum_scatter(
        packed_grad, ("mp", "dp"), scatter_dimension=0, tiled=True
    ).astype(jnp.float32)
    summed_attn = jnp.stack([summed[:, cuts[i] : cuts[i + 1]] for i in range(3)])
    summed_out = summed[:, cuts[3] : cuts[4]].T
    summed_up = summed[:, cuts[4] : cuts[5]]
    summed_down = summed[:, cuts[5] : cuts[6]].T

    vector_grad = jnp.concatenate(
        [
            jnp.sum(grad_query.astype(jnp.float32), 0),
            jnp.sum(grad_values.astype(jnp.float32), 0),
            jnp.sum(branch_low.astype(jnp.float32), 0),
            grad_gain_one,
            grad_shift_one,
            jnp.sum(feed_low.astype(jnp.float32), 0),
            grad_gain_two,
            grad_shift_two,
            jnp.sum(gate_low.astype(jnp.float32), 0),
        ]
    )
    return (student_out, input_grad) + lamb_update(
        (summed_attn, summed_out, summed_up, summed_down),
        (attn_weight, out_weight, up_weight, down_weight),
        (attn_first, out_first, up_first, down_first),
        (attn_second, out_second, up_second, down_second),
        vector_grad,
        vectors,
        vector_first,
        vector_second,
    )


def lamb_update(grads, weights, firsts, seconds, vector_grad, vectors, vector_first, vector_second):
    moments, squares, steps = [], [], []
    for grad_now, weight, first_old, second_old in zip(grads, weights, firsts, seconds):
        first_new, second_new, step_now = adam_moments(grad_now, first_old, second_old)
        moments.append(first_new)
        squares.append(second_new)
        steps.append(step_now + decay_rate * weight)
    weight_total, update_total, vector_total = lax.psum(
        (matrix_squares(*weights), matrix_squares(*steps), vector_grad), ("dp", "mp")
    )
    weight_norms = jnp.sqrt(weight_total)
    update_norms = jnp.sqrt(update_total)
    trust_ratio = weight_norms / update_norms
    ratios = [trust_ratio[0:3][:, None, None], trust_ratio[3], trust_ratio[4], trust_ratio[5]]
    updated = [
        weight - matrix_rate * ratio * step for weight, ratio, step in zip(weights, ratios, steps)
    ]
    vector_moment, vector_square, step_vector = adam_moments(
        vector_total, vector_first, vector_second
    )
    vector_updated = vectors - vector_rate * step_vector
    return (
        *updated,
        *moments,
        *squares,
        vector_moment,
        vector_square,
        vector_updated,
        jnp.stack([weight_norms, update_norms]),
        trust_ratio,
    )


LOG_PAIR = 128
MESH = pl.DeviceIdType.MESH
low = jnp.bfloat16
f32 = jnp.float32
VMEM_SPEC = pl.BlockSpec(memory_space=pltpu.VMEM)
ANY_SPEC = pl.BlockSpec(memory_space=pl.ANY)
FIRST_LIMIT = 64 * 2**20
LIMIT = 60 * 2**20


def dnn(left, right):
    return jnp.dot(left, right, preferred_element_type=f32)


def dnt(left, right):
    return lax.dot_general(left, right, (((1,), (1,)), ((), ())), preferred_element_type=f32)


def lane_index(shape):
    return lax.broadcasted_iota(jnp.int32, shape, 1)


def split_three(value):
    top = value.astype(low).astype(f32)
    rest = value - top
    middle = rest.astype(low).astype(f32)
    return (top, middle, rest - middle)


def flip(value):
    return value.astype(f32).T.astype(low)


def place():
    at = lax.axis_index("dp")
    return (at, lax.axis_index("mp"), at // 4, (at // 2) % 2, at % 2)


def near():
    at, y, z, x, core = place()
    return dict(
        twin=(at + 1 - 2 * core, y),
        x=(at + 2 - 4 * x, y),
        y=(at, 1 - y),
        z=[(((z + step) % 4) * 4 + 2 * x + core, y) for step in (1, 2, 3)],
    )


def greet(peers):
    sem = pltpu.get_barrier_semaphore()
    for peer in peers:
        pl.semaphore_signal(sem, inc=1, device_id=peer, device_id_type=MESH)
    pl.semaphore_wait(sem, len(peers))


def remote(src, dst, sends, recvs, at, peer):
    return pltpu.make_async_remote_copy(
        src_ref=src,
        dst_ref=dst,
        send_sem=sends.at[at],
        recv_sem=recvs.at[at],
        device_id=peer,
        device_id_type=MESH,
    )


def row_norm(rows):
    center = rows - jnp.mean(rows, -1, keepdims=True)
    scale = lax.rsqrt(jnp.mean(center * center, -1, keepdims=True) + layer_eps)
    return (center * scale, scale)


def norm_pull(grad, unit, scale, gain):
    lifted = grad * gain
    return scale * (
        lifted
        - jnp.mean(lifted, -1, keepdims=True)
        - unit * jnp.mean(lifted * unit, -1, keepdims=True)
    )


def normal_share(value):
    return 0.5 * (1.0 + lax.erf(value * 0.7071067811865476))


def pair_forward(query, keys, values, bias):
    count, span = query.shape[0], keys.shape[0]
    lane_q, lane_k = lane_index((count, LOG_PAIR)), lane_index((span, LOG_PAIR))
    outs, logs = [], []
    for head in range(2):
        spare = HDIM * (1 - head)
        keys_now = jnp.where(
            lane_k // HDIM == head,
            keys.astype(f32),
            jnp.where(lane_k == spare, bias, 0.0),
        ).astype(low)
        query_now = jnp.where(
            lane_q // HDIM == head,
            query.astype(f32),
            jnp.where(lane_q == spare, 1.0, 0.0),
        ).astype(low)
        scores = dnt(query_now, keys_now)
        peak = jnp.max(scores, -1, keepdims=True)
        exponent = jnp.exp(scores - peak)
        total = jnp.sum(exponent, -1, keepdims=True)
        outs.append(dnn((exponent * (1.0 / total)).astype(low), values))
        logs.append(peak + jnp.log(total))
    return (
        jnp.where(lane_q < HDIM, outs[0], outs[1]),
        jnp.where(lane_q < HDIM, logs[0], logs[1]),
    )


def shape_of(*dims, kind=f32):
    return jax.ShapeDtypeStruct(dims, kind)


def pair_back(query, grad_mixed, mixed, logs, keys, values, bias):
    count, span = query.shape[0], keys.shape[0]
    lane_q, lane_k = lane_index((count, LOG_PAIR)), lane_index((span, LOG_PAIR))
    query_wide, grad_wide = query.astype(f32), grad_mixed.astype(f32)
    keys_wide, values_wide = keys.astype(f32), values.astype(f32)
    product = grad_wide * mixed
    grad_keys, grad_values, grad_query = [], [], []
    for head in range(2):
        spare = HDIM * (1 - head)
        own_q, own_k = lane_q // HDIM == head, lane_k // HDIM == head
        inner = jnp.sum(jnp.where(own_q, product, 0.0), -1, keepdims=True)
        query_now = jnp.where(own_q, query_wide, jnp.where(lane_q == spare, 1.0, 0.0))
        grad_now = jnp.where(own_q, grad_wide, 0.0)
        for place_at, (log_term, inner_term) in enumerate(
            zip(split_three(logs[:, HDIM * head : HDIM * head + 1]), split_three(inner))
        ):
            here = lane_q == spare + 1 + place_at
            query_now = jnp.where(here, log_term, query_now)
            grad_now = jnp.where(here, inner_term, grad_now)
        minus = jnp.where((lane_k > spare) & (lane_k < spare + 4), -1.0, 0.0)
        keys_now = jnp.where(own_k, keys_wide, jnp.where(lane_k == spare, bias, minus)).astype(low)
        values_now = jnp.where(own_k, values_wide, minus).astype(low)
        probs = jnp.exp(dnt(keys_now, query_now.astype(low)))
        grad_scores = (probs * dnt(values_now, grad_now.astype(low))).astype(low)
        grad_keys.append(dnn(grad_scores, query))
        grad_values.append(dnn(probs.astype(low), grad_mixed))
        flipped = keys_wide.T[HDIM * head : HDIM * (head + 1)].astype(low)
        grad_query.append(dnn(flipped, grad_scores))
    return (
        jnp.concatenate(grad_query, 0).T * HDIM**-0.5,
        jnp.where(lane_k < HDIM, grad_keys[0], grad_keys[1]),
        jnp.where(lane_k < HDIM, grad_values[0], grad_values[1]),
    )


def adam_step(grad, first, second):
    first_new = beta_one * first + (1.0 - beta_one) * grad
    second_new = beta_two * second + (1.0 - beta_two) * grad * grad
    step = (
        first_new
        / (1.0 - beta_one**STEP)
        / (jnp.sqrt(second_new / (1.0 - beta_two**STEP)) + adam_eps)
    )
    return (first_new, second_new, step)


def block_of(ref, cols):
    value = ref[:, :, :, :, cols]
    return value.reshape(-1, value.shape[-1])


def gather_steps(chunks, gs_ref, gt_ref, ps_ref, pt_ref, local_sem, zsends, zrecvs, sends, recvs, started):
    at, y, z, x, core = place()
    ways = near()

    def go(ref, chunk, kind, peer):
        copy = remote(ref, ref, sends, recvs, (chunk, kind), peer)
        copy.start()
        started.append(copy)

    def landed(ref, chunk, kind):
        remote(ref, ref, sends, recvs, (chunk, kind), ways["x"]).wait_recv()

    def shard(chunk, zz):
        which, a, b = chunks[chunk]
        if which == 0:
            return gs_ref.at[y, zz, x, core, :, pl.ds(a, b - a)]
        return gt_ref.at[zz, x, core, :, pl.ds(a, b - a)]

    def column(chunk, yy, xx, cc):
        which, a, b = chunks[chunk]
        if which == 0:
            return gs_ref.at[yy, :, xx, cc, :, pl.ds(a, b - a)]
        return gt_ref.at[:, xx, cc, :, pl.ds(a, b - a)]

    own = []
    for k, (which, a, b) in enumerate(chunks):
        source = (ps_ref, pt_ref)[which].at[:, pl.ds(a, b - a)]
        copy = pltpu.make_async_copy(source, shard(k, z), local_sem.at[k])
        copy.start()
        own.append(copy)
        for step in range(3):
            copy = remote(source, shard(k, z), zsends, zrecvs, (k, step), ways["z"][step])
            copy.start()
            started.append(copy)

    def along_z(k):
        for step in range(3):
            came = shard(k, (z + 3 - step) % 4)
            remote(came, came, zsends, zrecvs, (k, step), ways["x"]).wait_recv()
        own[k].wait()
        go(column(k, y, x, core), k, 0, ways["x"])
        if chunks[k][0] == 0:
            go(column(k, y, x, core), k, 1, ways["y"])
        go(column(k, y, x, core), k, 2, ways["twin"])

    def from_sides(k):
        landed(column(k, y, 1 - x, core), k, 0)
        if chunks[k][0] == 0:
            go(column(k, y, 1 - x, core), k, 3, ways["y"])
        go(column(k, y, 1 - x, core), k, 4, ways["twin"])
        if chunks[k][0] == 0:
            landed(column(k, 1 - y, x, core), k, 1)
            go(column(k, 1 - y, x, core), k, 5, ways["twin"])

    def last(k):
        if chunks[k][0] == 0:
            landed(column(k, 1 - y, 1 - x, core), k, 3)
            go(column(k, 1 - y, 1 - x, core), k, 6, ways["twin"])

    def whole(k):
        landed(column(k, y, x, 1 - core), k, 2)
        landed(column(k, y, 1 - x, 1 - core), k, 4)
        if chunks[k][0] == 0:
            landed(column(k, 1 - y, x, 1 - core), k, 5)
            landed(column(k, 1 - y, 1 - x, 1 - core), k, 6)

    count = len(chunks)
    for slot in range(count + 3):
        if slot < count:
            along_z(slot)
        if 0 <= slot - 1 < count:
            from_sides(slot - 1)
        if 0 <= slot - 2 < count:
            last(slot - 2)
        if 0 <= slot - 3 < count:
            whole(slot - 3)
        yield max(0, slot - 2)


def first_kernel(
    chunks,
    x_ref, tx_ref, cot_hbm, vec_ref, tvec_ref, length_ref, places_ref, places_col_ref,
    aw, ow, uw, dw, ta, to, tu, td,
    wa_hbm, q_hbm, k_hbm, v_hbm, af_hbm, log_hbm, ga_hbm, g1_hbm, one_hbm, out_low_hbm, sums_ref,
    gs_ref, gt_ref, ps_ref, pt_ref, bias_ref, q_ref, k_ref, v_ref, a_ref, af_ref, log_ref,
    tk_ref, tv_ref, part_ref, come_ref, aimed_ref, r1_ref, normed_ref, u_ref, slope_ref, r2_ref,
    out_ref, cot_ref, flip_ref, nflip_ref, ga_ref, one_ref, low_ref,
    local_sem, zsends, zrecvs, sends, recvs, tsends, trecvs, gsends, grecvs, copy_sem,
):
    at, y, z, x, core = place()
    ways = near()
    length, width = x_ref.shape
    rows = length // 2
    part = width // 2
    half_block = rows // 2
    own = pl.ds(pl.multiple_of(y * rows, rows), rows)
    kept = []

    def keep(src, dst):
        copy = pltpu.make_async_copy(src, dst, copy_sem.at[len(kept)])
        copy.start()
        kept.append(copy)
        return copy

    for index in range(3):
        ps_ref[:, index * part : (index + 1) * part] = aw[index].astype(low)
        pt_ref[:, index * part : (index + 1) * part] = ta[index]
    for base, source, aim in ((3 * part, ow, to), (4 * part, uw, tu), (8 * part, dw, td)):
        ps_ref[:, base : base + source.shape[1]] = source[...].astype(low)
        pt_ref[:, base : base + source.shape[1]] = aim[...]
    greet([ways["twin"], ways["x"], ways["y"]] + ways["z"])
    started = []
    steps = gather_steps(
        chunks, gs_ref, gt_ref, ps_ref, pt_ref, local_sem, zsends, zrecvs, sends, recvs, started
    )
    ready = [0]

    def tick():
        ready[0] = next(steps, len(chunks))

    def need(chunk):
        while ready[0] <= chunk:
            tick()

    cot_copy = keep(cot_hbm.at[own], cot_ref)
    bias_ref[...] = jnp.where(
        lax.broadcasted_iota(jnp.int32, bias_ref.shape, 0) < length_ref[0:1, 0:1], 0.0, masked_score
    )
    sums_ref[...] = jnp.zeros(sums_ref.shape, f32)

    def loop(count, body):
        def step(index, carry):
            body(index)
            return carry

        lax.fori_loop(0, count, step, 0)

    def span(index, block):
        return pl.ds(pl.multiple_of(index * block, block), block)

    need(2)
    keep(gs_ref.at[:, :, :, :, :, pl.ds(0, 3 * part)], wa_hbm)

    def keys_values(index):
        here = span(index, 256)
        for half in range(2):
            cols = slice(half * part, (half + 1) * part)
            k_ref[here, cols] = dnn(
                x_ref[here, :], block_of(gs_ref.at[half], slice(part, 2 * part))
            ).astype(low)
            v_ref[here, cols] = (
                dnn(x_ref[here, :], block_of(gs_ref.at[half], slice(2 * part, 3 * part)))
                + vec_ref[1:2, cols]
            ).astype(low)

    def queries(index):
        here = span(index, 256)
        from_x = pl.ds(pl.multiple_of(y * rows + index * 256, 256), 256)
        for half in range(2):
            cols = slice(half * part, (half + 1) * part)
            value = dnn(x_ref[from_x, :], block_of(gs_ref.at[half], slice(0, part)))
            value = (value + vec_ref[0:1, cols]).astype(low).astype(f32) * HDIM**-0.5
            q_ref[here, cols] = value.astype(low)

    def attend(first):
        def one_pair(index):
            pair = first + index
            cols = pl.ds(pl.multiple_of(pair * LOG_PAIR, LOG_PAIR), LOG_PAIR)
            keys, values, bias = k_ref[:, cols], v_ref[:, cols], bias_ref[...]
            for start in range(0, rows, 256):
                here = slice(start, start + 256)
                mixed, logs = pair_forward(q_ref[here, cols], keys, values, bias)
                a_ref[here, cols] = mixed.astype(low)
                af_ref[here, cols] = mixed
                log_ref[pair, here, :] = logs

        return one_pair

    loop(length // 256, keys_values)
    tick()
    loop(rows // 256, queries)
    for first in (0, 2, 4):
        loop(2, attend(first))
        tick()
    for src, dst in (
        (q_ref, q_hbm), (k_ref, k_hbm), (v_ref, v_hbm), (af_ref, af_hbm), (log_ref, log_hbm)
    ):
        keep(src, dst)

    need(4)
    mine = pl.ds(pl.multiple_of(y * part, LOG_PAIR), part)
    count = places_col_ref.shape[0]

    def teacher_keys(index):
        here = span(index, 256)
        tk_ref[here, :] = dnn(tx_ref[here, :], block_of(gt_ref, slice(part, 2 * part))).astype(low)
        tv_ref[here, :] = (
            dnn(tx_ref[here, :], block_of(gt_ref, slice(2 * part, 3 * part))) + tvec_ref[1:2, mine]
        ).astype(low)

    loop(length // 256, teacher_keys)
    pick = jnp.where(places_col_ref[:, 0:1] == lane_index((count, length)), 1.0, 0.0).astype(low)
    listed = dnn(pick, tx_ref[...])
    query = dnn(listed.astype(low), block_of(gt_ref, slice(0, part))) + tvec_ref[0:1, mine]
    query = (query.astype(low).astype(f32) * HDIM**-0.5).astype(low)
    part_ref[0] = jnp.zeros((count, width), f32)
    for pair in range(part // LOG_PAIR):
        cols = slice(pair * LOG_PAIR, (pair + 1) * LOG_PAIR)
        mixed, unused = pair_forward(query[:, cols], tk_ref[:, cols], tv_ref[:, cols], bias_ref[...])
        a_cols = slice(3 * part + pair * LOG_PAIR, 3 * part + (pair + 1) * LOG_PAIR)
        part_ref[0] += dnt(mixed.astype(low), block_of(gt_ref, a_cols))
    swaps = [remote(part_ref.at[i], come_ref.at[i], tsends, trecvs, i, ways["y"]) for i in range(2)]
    swaps[0].start()
    need(6)
    swaps[0].wait()
    unit, unused = row_norm(listed + (part_ref[0] + come_ref[0]) + tvec_ref[2:3, :])
    normed = unit * tvec_ref[3:4, :] + tvec_ref[4:5, :]
    normed_low = normed.astype(low)
    part_ref[1] = jnp.zeros((count, width), f32)
    for piece in range(2):
        base = 4 * part + piece * width
        gate = dnn(normed_low, block_of(gt_ref, slice(base, base + width)))
        gate += tvec_ref[pl.ds(8 + 2 * y + piece, 1), :]
        active = (gate * normal_share(gate)).astype(low)
        part_ref[1] += dnt(active, block_of(gt_ref, slice(base + 2 * width, base + 3 * width)))
    swaps[1].start()

    need(7)
    tick()

    def project(index):
        here = span(index, 256)
        from_x = pl.ds(pl.multiple_of(y * rows + index * 256, 256), 256)
        first = x_ref[from_x, :].astype(f32) + vec_ref[2:3, :]
        for half in range(2):
            first += dnt(
                a_ref[here, half * part : (half + 1) * part],
                block_of(gs_ref.at[half], slice(3 * part, 4 * part)),
            )
        r1_ref[here, :] = first
        unit, unused = row_norm(first)
        normed = unit * vec_ref[3:4, :] + vec_ref[4:5, :]
        normed_ref[here, :] = normed.astype(low)
        nflip_ref[:, here] = flip(normed.astype(low))
        r2_ref[here, :] = normed + vec_ref[5:6, :]

    loop(rows // 256, project)
    swaps[1].wait()
    unit, unused = row_norm(normed + (part_ref[1] + come_ref[1]) + tvec_ref[5:6, :])
    aimed_ref[...] = unit * tvec_ref[6:7, :] + tvec_ref[7:8, :]

    def rise(piece):
        half, base = piece // 2, 4 * part + (piece % 2) * width

        def body(index):
            here = span(index, 256)
            cols = slice(piece * width, (piece + 1) * width)
            gate = dnn(normed_ref[here, :], block_of(gs_ref.at[half], slice(base, base + width)))
            gate += vec_ref[8 + piece : 9 + piece, :]
            share = normal_share(gate)
            u_ref[here, cols] = (gate * share).astype(low)
            slope_ref[here, cols] = (
                share + gate * (jnp.exp(-0.5 * gate * gate) * 0.3989422804014327)
            ).astype(low)

        loop(rows // 256, body)

    def fall(piece):
        half, base = piece // 2, 4 * part + (2 + piece % 2) * width

        def body(index):
            here = span(index, 256)
            r2_ref[here, :] += dnt(
                u_ref[here, piece * width : (piece + 1) * width],
                block_of(gs_ref.at[half], slice(base, base + width)),
            )

        loop(rows // 256, body)

    for chunk, work, pieces in ((8, rise, (0, 2)), (9, rise, (1, 3)), (10, fall, (0, 2)), (11, fall, (1, 3))):
        need(chunk)
        for piece in pieces:
            work(piece)
    for unused in steps:
        pass
    for copy in started:
        copy.wait_send()
    cot_copy.wait()

    def top(index):
        here = span(index, 256)
        row_at = lax.broadcasted_iota(jnp.int32, (256, places_ref.shape[1]), 0)
        pick = jnp.where(row_at + (y * rows + index * 256) == places_ref[0:1, :], 1.0, 0.0)
        times = jnp.sum(pick, -1, keepdims=True)
        aimed = jnp.dot(
            pick, aimed_ref[...], precision=lax.Precision.HIGHEST, preferred_element_type=f32
        ) / jnp.maximum(times, 1.0)
        unit, spread = row_norm(r2_ref[here, :])
        outcome = unit * vec_ref[6:7, :] + vec_ref[7:8, :]
        low_ref[here, :] = outcome.astype(low)
        inner = jnp.sum(outcome * aimed, -1, keepdims=True)
        square_own = jnp.sum(outcome * outcome, -1, keepdims=True) + cosine_eps
        square_aim = jnp.sum(aimed * aimed, -1, keepdims=True) + cosine_eps
        scale = cosine_weight * times * lax.rsqrt(square_own) * lax.rsqrt(square_aim)
        grad = cot_ref[here, :].astype(f32) - scale * (aimed - outcome * (inner / square_own))
        sums_ref[6:7, :] += jnp.sum(grad * unit, 0, keepdims=True)
        sums_ref[7:8, :] += jnp.sum(grad, 0, keepdims=True)
        back = norm_pull(grad, unit, spread, vec_ref[6:7, :])
        r2_ref[here, :] = back
        back_low = back.astype(low)
        sums_ref[5:6, :] += jnp.sum(back_low.astype(f32), 0, keepdims=True)
        ga_ref[here, :] = back_low
        flip_ref[:, here] = flip(back_low)

    loop(rows // 256, top)
    keep(low_ref, out_low_hbm)

    blocks = []

    def share_block(value, half, base, size):
        number = len(blocks)
        slot = pl.ds((number % 6) * width, size)
        if number >= 4:
            settle(number - 4)
        gt_ref[:, :, :, :, slot] = value.astype(low).reshape(gt_ref.shape[:4] + (size,))
        mine_cols = pl.ds(base - 3 * part, size)
        copy = remote(
            gt_ref.at[:, :, 1 - core, :, slot], one_ref.at[half, :, :, :, mine_cols],
            gsends, grecvs, number, ways["twin"],
        )
        copy.start()
        blocks.append((copy, half, mine_cols, slot))

    def settle(number):
        copy, half, cols, slot = blocks[number]
        copy.wait()
        one_ref[half, :, :, :, cols] = (
            one_ref[half, :, :, :, cols].astype(f32) + gt_ref[:, :, core, :, slot].astype(f32)
        ).astype(low)
        keep(one_ref.at[half, :, :, :, cols], one_hbm.at[half, :, :, :, cols])

    for piece in range(4):
        half, base = piece // 2, 4 * part + (piece % 2) * width
        cols = slice(piece * width, (piece + 1) * width)
        share_block(dnn(flip_ref[...], u_ref[:, cols]), half, base + 2 * width, width)

        def gate_back(index, half=half, base=base, cols=cols, piece=piece):
            here = span(index, 256)
            down = block_of(gs_ref.at[half], slice(base + 2 * width, base + 3 * width))
            gate_low = (dnn(ga_ref[here, :], down) * slope_ref[here, cols].astype(f32)).astype(low)
            slope_ref[here, cols] = gate_low
            sums_ref[8 + piece : 9 + piece, :] += jnp.sum(gate_low.astype(f32), 0, keepdims=True)
            r2_ref[here, :] += dnt(gate_low, block_of(gs_ref.at[half], slice(base, base + width)))

        loop(rows // 256, gate_back)
        share_block(dnn(nflip_ref[...], slope_ref[:, cols]), half, base, width)

    def middle(index):
        here = span(index, 256)
        grad = r2_ref[here, :]
        unit, spread = row_norm(r1_ref[here, :])
        sums_ref[3:4, :] += jnp.sum(grad * unit, 0, keepdims=True)
        sums_ref[4:5, :] += jnp.sum(grad, 0, keepdims=True)
        back = norm_pull(grad, unit, spread, vec_ref[3:4, :])
        out_ref[here, :] = back
        back_low = back.astype(low)
        sums_ref[2:3, :] += jnp.sum(back_low.astype(f32), 0, keepdims=True)
        flip_ref[:, here] = flip(back_low)
        for half in range(2):
            cols = slice(half * part, (half + 1) * part)
            ga_ref[here, cols] = dnn(
                back_low, block_of(gs_ref.at[half], slice(3 * part, 4 * part))
            ).astype(low)

    loop(rows // 256, middle)
    keep(out_ref, g1_hbm)
    keep(ga_ref, ga_hbm)
    for half in range(2):
        share_block(
            dnn(flip_ref[...], a_ref[:, half * part : (half + 1) * part]), half, 3 * part, part
        )
    for number in range(len(blocks) - 4, len(blocks)):
        settle(number)
    for copy in kept:
        if copy is not cot_copy:
            copy.wait()


def first_call(x, tx, cot, vec, tvec, lengths, masked, weights, teacher, number):
    length, width = x.shape
    rows, part, hidden = length // 2, width // 2, 4 * width
    lines = weights[0].shape[1]
    wide = 4 * part + 2 * weights[2].shape[1]
    third = part
    chunks = tuple(
        [(0, i * part, (i + 1) * part) for i in range(3)]
        + [(1, 0, width), (1, width, 2 * width), (1, 2 * width, 4 * width), (1, 4 * width, 6 * width)]
        + [(0, 3 * part, 4 * part)]
        + [(0, (2 + i) * width, (3 + i) * width) for i in range(4)]
    )
    count = len(chunks)
    listed = masked.shape[1]
    pairs = width // LOG_PAIR
    sem = pltpu.SemaphoreType.DMA
    vm = pltpu.VMEM
    return pl.pallas_call(
        partial(first_kernel, chunks),
        name="gather_forward",
        out_shape=[
            shape_of(2, 4, 2, 2, lines, 3 * part, kind=low),
            shape_of(rows, width, kind=low),
            shape_of(length, width, kind=low),
            shape_of(length, width, kind=low),
            shape_of(rows, width),
            shape_of(pairs, rows, LOG_PAIR),
            shape_of(rows, width, kind=low),
            shape_of(rows, width),
            shape_of(2, 4, 2, lines, wide - 3 * part, kind=low),
            shape_of(rows, width, kind=low),
            shape_of(*vec.shape),
        ],
        in_specs=[VMEM_SPEC] * 2 + [ANY_SPEC] + [VMEM_SPEC] * 13,
        out_specs=[ANY_SPEC] * 10 + [VMEM_SPEC],
        scratch_shapes=[
            vm((2, 4, 2, 2, lines, wide), low),
            vm((4, 2, 2, lines, wide), low),
            vm((lines, wide), low),
            vm((lines, wide), low),
            vm((length, LOG_PAIR), f32),
            vm((rows, width), low),
            vm((length, width), low),
            vm((length, width), low),
            vm((rows, width), low),
            vm((rows, width), f32),
            vm((pairs, rows, LOG_PAIR), f32),
            vm((length, part), low),
            vm((length, part), low),
            vm((2, listed, width), f32),
            vm((2, listed, width), f32),
            vm((listed, width), f32),
            vm((rows, width), f32),
            vm((rows, width), low),
            vm((rows, hidden), low),
            vm((rows, hidden), low),
            vm((rows, width), f32),
            vm((rows, width), f32),
            vm((rows, width), low),
            vm((width, rows), low),
            vm((width, rows), low),
            vm((rows, width), low),
            vm((2, 4, 2, lines, wide - 3 * part), low),
            vm((rows, width), low),
            sem((count,)), sem((count, 3)), sem((count, 3)), sem((count, 7)), sem((count, 7)),
            sem((2,)), sem((2,)), sem((10,)), sem((10,)), sem((20,)),
        ],
        compiler_params=pltpu.CompilerParams(
            vmem_limit_bytes=FIRST_LIMIT, collective_id=number, has_side_effects=True
        ),
    )(x, tx, cot, vec, tvec, lengths, masked, masked.T, *weights, *teacher)


def sum_steps(chunks, one_hbm, one_ref, h_ref, ax_ref, zr_ref, tot_ref, own_ref, yr_ref, load_sem, sends, recvs, zsends, zrecvs, started):
    at, y, z, x, core = place()
    ways = near()
    count = len(chunks)
    split = one_ref.shape[-1]
    loads = {}

    def source(k, xx):
        a, b = chunks[k]
        if b <= split:
            return one_ref.at[:, :, xx, :, pl.ds(a, b - a)]
        return one_hbm.at[:, :, xx, :, pl.ds(a - split, b - a)]

    def span(k):
        a, b = chunks[k]
        return pl.ds(a, b - a)

    def begin(k):
        copy = remote(
            source(k, 1 - x), ax_ref.at[:, :, :, span(k)], sends, recvs, (k, 0), ways["x"]
        )
        copy.start()
        started.append(copy)
        loads[k] = pltpu.make_async_copy(source(k, x), h_ref.at[:, :, :, span(k)], load_sem.at[k])
        loads[k].start()

    def over_x(k):
        here = span(k)
        loads[k].wait()
        came = ax_ref.at[:, :, :, here]
        remote(came, came, sends, recvs, (k, 0), ways["x"]).wait_recv()

        def add(step, carry):
            yy, zz = step // 4, step % 4
            h_ref[yy, zz, :, here] = (
                h_ref[yy, zz, :, here].astype(f32) + ax_ref[yy, zz, :, here].astype(f32)
            ).astype(low)
            return carry

        lax.fori_loop(0, 8, add, 0)
        for step in range(3):
            copy = remote(
                h_ref.at[:, (z + 1 + step) % 4, :, here], zr_ref.at[step, :, :, here],
                zsends, zrecvs, (k, step), ways["z"][step],
            )
            copy.start()
            started.append(copy)

    def over_z(k):
        here = span(k)
        for step in range(3):
            came = zr_ref.at[step, :, :, here]
            remote(came, came, zsends, zrecvs, (k, step), ways["x"]).wait_recv()
        for yy in range(2):
            total = h_ref[yy, z, :, here].astype(f32)
            for step in range(3):
                total += zr_ref[step, yy, :, here].astype(f32)
            tot_ref[yy, :, here] = total.astype(low)
        copy = remote(
            tot_ref.at[1 - y, :, here], yr_ref.at[:, here], sends, recvs, (k, 1), ways["y"]
        )
        copy.start()
        started.append(copy)

    def over_y(k):
        here = span(k)
        came = yr_ref.at[:, here]
        remote(came, came, sends, recvs, (k, 1), ways["y"]).wait_recv()
        own_ref[:, here] = tot_ref[y, :, here].astype(f32) + yr_ref[:, here].astype(f32)

    def steps():
        for slot in range(count + 2):
            if slot < count:
                over_x(slot)
            if 0 <= slot - 1 < count:
                over_z(slot - 1)
            if 0 <= slot - 2 < count:
                over_y(slot - 2)
            yield max(0, slot - 1)

    return begin, steps()


def shared_steps(value, result, mine_ref, come_ref, sends, recvs):
    at, y, z, x, core = place()
    ways = near()
    for index, way in enumerate(("twin", "x", "y")):
        mine_ref[index] = value
        copy = remote(mine_ref.at[index], come_ref.at[index], sends, recvs, index, ways[way])
        copy.start()
        yield
        copy.wait()
        value = mine_ref[index] + come_ref[index]
    mine_ref[3] = value
    copies = []
    for step in range(3):
        copy = remote(
            mine_ref.at[3], come_ref.at[3 + step], sends, recvs, 3 + step, ways["z"][step]
        )
        copy.start()
        copies.append(copy)
    yield
    for copy in copies:
        copy.wait()
    terms = [mine_ref[3]] + [come_ref[3 + step] for step in range(3)]
    total = None
    for z_from in range(4):
        term = terms[0]
        for step in range(1, 4):
            term = jnp.where((z + 4 - step) % 4 == z_from, terms[step], term)
        total = term if total is None else total + term
    result.append(total)


def second_kernel(
    chunks,
    x_ref, q_ref, k_ref, v_ref, length_ref, log_ref, af_ref, ga_ref, vg_ref, vec_ref, vm_ref, vs_ref,
    g1_hbm, wa_hbm, one_hbm, student_hbm,
    aw, ow, uw, dw, am, om, um, dm, a2, o2, u2, d2,
    input_ref, student_ref,
    aw_o, ow_o, uw_o, dw_o, am_o, om_o, um_o, dm_o, a2_o, o2_o, u2_o, d2_o,
    vm_o, vs_o, vec_o, norm_o,
    bias_ref, gq_ref, gk_ref, gv_ref, come_ref, flip_ref, g1_ref, wa_ref, stage_ref, one_ref,
    h_ref, ax_ref, zr_ref, tot_ref, own_ref, yr_ref, send_ref, come_in_ref,
    vmine, vcome, nmine, ncome,
    load_sem, sends, recvs, zsends, zrecvs, ksends, krecvs, tsends, trecvs, jsends, jrecvs,
    vsends, vrecvs, nsends, nrecvs, copy_sem,
):
    at, y, z, x, core = place()
    ways = near()
    greet([ways["twin"], ways["x"], ways["y"]] + ways["z"])
    rows, width = q_ref.shape
    part = width // 2
    pairs = width // LOG_PAIR
    own = pl.ds(pl.multiple_of(y * rows, rows), rows)
    other = pl.ds(pl.multiple_of((1 - y) * rows, rows), rows)
    started = []
    begin, steps = sum_steps(
        chunks, one_hbm, one_ref, h_ref, ax_ref, zr_ref, tot_ref, own_ref, yr_ref,
        load_sem, sends, recvs, zsends, zrecvs, started,
    )
    feed_chunks = [k for k, (a, b) in enumerate(chunks) if a >= 3 * part]
    for k in feed_chunks:
        begin(k)
    done = [0]

    def tick():
        done[0] = next(steps, len(chunks))

    early = [
        pltpu.make_async_copy(g1_hbm, g1_ref, copy_sem.at[0]),
        pltpu.make_async_copy(wa_hbm, wa_ref, copy_sem.at[1]),
        pltpu.make_async_copy(student_hbm, student_ref.at[own], copy_sem.at[2]),
    ]
    for copy in early:
        copy.start()
    bias_ref[...] = jnp.where(
        lax.broadcasted_iota(jnp.int32, bias_ref.shape, 0) < length_ref[0:1, 0:1], 0.0, masked_score
    )
    flip_ref[...] = flip(x_ref[own, :])

    def swap(which, pair):
        cols = pl.ds(pl.multiple_of(pair * LOG_PAIR, LOG_PAIR), LOG_PAIR)
        source = (gk_ref, gv_ref)[which]
        return remote(
            source.at[other, cols], come_ref.at[which, :, cols], ksends, krecvs,
            (which, pair), ways["y"],
        )

    def one_pair(pair, carry):
        cols = pl.ds(pl.multiple_of(pair * LOG_PAIR, LOG_PAIR), LOG_PAIR)
        grad_query, grad_keys, grad_values = pair_back(
            q_ref[:, cols], ga_ref[:, cols], af_ref[:, cols], log_ref[pair],
            k_ref[:, cols], v_ref[:, cols], bias_ref[...],
        )
        gq_ref[:, cols] = grad_query.astype(low)
        gk_ref[:, cols] = grad_keys.astype(low)
        gv_ref[:, cols] = grad_values.astype(low)
        swap(0, pair).start()
        swap(1, pair).start()
        return carry

    for first in range(0, pairs, 2):
        lax.fori_loop(first, first + 2, one_pair, 0)
        if first < 4:
            tick()
    for copy in early:
        copy.wait()
    share = remote(student_ref.at[own], student_ref.at[own], jsends, jrecvs, 0, ways["y"])
    share.start()

    def weight_grad(index, value_ref):
        for half in range(2):
            cols = pl.ds(index * part, part)
            block = dnn(flip_ref[...], value_ref[:, half * part : (half + 1) * part])
            stage_ref[half, :, :, :, :, cols] = block.astype(low).reshape(
                stage_ref.shape[1:5] + (part,)
            )
        copy = remote(
            stage_ref.at[:, :, :, 1 - core, :, cols], one_ref.at[:, :, :, :, cols],
            tsends, trecvs, index, ways["twin"],
        )
        copy.start()
        return copy

    def settle(index, copy):
        copy.wait()
        cols = pl.ds(index * part, part)

        def add(step, carry):
            half, zz = step // 4, step % 4
            one_ref[half, zz, :, :, cols] = (
                one_ref[half, zz, :, :, cols].astype(f32)
                + stage_ref[half, zz, :, core, :, cols].astype(f32)
            ).astype(low)
            return carry

        lax.fori_loop(0, 8, add, 0)
        begin([k for k, (a, b) in enumerate(chunks) if a == index * part][0])

    def input_part(index, value_ref):
        total = None
        for half in range(2):
            term = dnt(
                value_ref[:, half * part : (half + 1) * part],
                block_of(wa_ref.at[half], slice(index * part, (index + 1) * part)),
            )
            total = term if total is None else total + term
        return total

    copy = weight_grad(0, gq_ref)
    g1_ref[...] += input_part(0, gq_ref)
    vg_top = jnp.sum(gq_ref[...].astype(f32), 0, keepdims=True)
    settle(0, copy)
    for index, source in ((1, gk_ref), (2, gv_ref)):

        def landed(pair, carry, index=index):
            swap(index - 1, pair).wait()
            return carry

        lax.fori_loop(0, pairs, landed, 0)
        gq_ref[...] = (
            source[own, :].astype(f32) + come_ref[index - 1].astype(f32)
        ).astype(low)
        copy = weight_grad(index, gq_ref)
        g1_ref[...] += input_part(index, gq_ref)
        settle(index, copy)
    vg_next = jnp.sum(gq_ref[...].astype(f32), 0, keepdims=True)
    line = lax.broadcasted_iota(jnp.int32, vg_ref.shape, 0)
    vector_grad = jnp.where(line == 0, vg_top, jnp.where(line == 1, vg_next, vg_ref[...]))
    input_ref[own, :] = g1_ref[...]
    send_ref[...] = g1_ref[...].astype(low)
    join = remote(send_ref, come_in_ref, jsends, jrecvs, 1, ways["y"])
    join.start()
    vector_total = []
    vector_steps = shared_steps(vector_grad, vector_total, vmine, vcome, vsends, vrecvs)
    next(vector_steps, None)

    lane = lane_index((8, LOG_PAIR))
    row = lax.broadcasted_iota(jnp.int32, (8, LOG_PAIR), 0)
    squares = [jnp.zeros((8, LOG_PAIR), f32)]

    def one_matrix(index, a, w, first, second, w_o, first_o, second_o):
        grad = own_ref[:, a : a + w.shape[-1]]
        first_new, second_new, step = adam_step(grad, first[...], second[...])
        first_o[...] = first_new
        second_o[...] = second_new
        weight = w[...]
        step = step + decay_rate * weight
        w_o[...] = step
        for at_line, value in ((0, weight), (1, step)):
            total = jnp.sum(jnp.sum(value * value, -1, keepdims=True), 0, keepdims=True)
            squares[0] = jnp.where((row == at_line) & (lane == index), total, squares[0])

    todo = [
        (5, 8 * part, (4, 4 + 0), (dw, dm, d2, dw_o, dm_o, d2_o)),
        (4, 4 * part, (4, 4 + 0), (uw, um, u2, uw_o, um_o, u2_o)),
        (3, 3 * part, (0, 0), (ow, om, o2, ow_o, om_o, o2_o)),
    ] + [
        (i, i * part, (0, 0), tuple(r.at[i] for r in (aw, am, a2, aw_o, am_o, a2_o)))
        for i in range(3)
    ]
    needs = [2, 4, 5, 6, 7, 8]
    for index, (number, a, unused, refs) in enumerate(todo):
        while done[0] < needs[index]:
            tick()
            next(vector_steps, None)
        one_matrix(number, a, *refs)
    for unused in vector_steps:
        pass
    for unused in steps:
        pass
    squares_total = []
    norm_steps = shared_steps(squares[0], squares_total, nmine, ncome, nsends, nrecvs)
    next(norm_steps)
    vm_new, vs_new, vector_step = adam_step(vector_total[0], vm_ref[...], vs_ref[...])
    vm_o[...] = vm_new
    vs_o[...] = vs_new
    vec_o[...] = vec_ref[...] - vector_rate * vector_step
    join.wait()
    input_ref[other, :] = come_in_ref[...].astype(f32)
    for unused in norm_steps:
        pass
    norms = jnp.sqrt(squares_total[0])
    ratio = norms[0:1, :] / norms[1:2, :]
    norm_o[...] = jnp.where(row == 2, ratio, norms)
    for number, a, unused, refs in todo:
        refs[3][...] = refs[0][...] - matrix_rate * ratio[0:1, number : number + 1] * refs[3][...]
    for copy in started:
        copy.wait_send()
    share.wait_send()
    remote(student_ref.at[other], student_ref.at[other], jsends, jrecvs, 0, ways["y"]).wait_recv()


def second_call(x, q, k, v, lengths, logs, af, ga, vg, vec, vm, vs, g1, wa, one, student, weights, firsts, seconds, number):
    length, width = x.shape
    rows, part = length // 2, width // 2
    lines = weights[0].shape[1]
    wide = 4 * part + 2 * weights[2].shape[1]
    chunks = tuple(
        [(8 * part, 10 * part), (10 * part, 12 * part), (4 * part, 6 * part), (6 * part, 8 * part)]
        + [(3 * part, 4 * part)]
        + [(i * part, (i + 1) * part) for i in range(3)]
    )
    count = len(chunks)
    outs = [shape_of(length, width), shape_of(length, width, kind=low)]
    outs += [shape_of(*value.shape) for group in (weights, firsts, seconds) for value in group]
    outs += [shape_of(*vec.shape)] * 3 + [shape_of(8, LOG_PAIR)]
    sem, buf = pltpu.SemaphoreType.DMA, pltpu.VMEM
    pairs = width // LOG_PAIR
    return pl.pallas_call(
        partial(second_kernel, chunks),
        name="attention_backward_update",
        out_shape=outs,
        in_specs=[VMEM_SPEC] * 12 + [ANY_SPEC] * 4 + [VMEM_SPEC] * 12,
        out_specs=[VMEM_SPEC] * len(outs),
        scratch_shapes=[
            buf((length, LOG_PAIR), f32),
            buf((rows, width), low),
            buf((length, width), low),
            buf((length, width), low),
            buf((2, rows, width), low),
            buf((width, rows), low),
            buf((rows, width), f32),
            buf((2, 4, 2, 2, lines, 3 * part), low),
            buf((2, 4, 2, 2, lines, 3 * part), low),
            buf((2, 4, 2, lines, 3 * part), low),
            buf((2, 4, lines, wide), low),
            buf((2, 4, lines, wide), low),
            buf((3, 2, lines, wide), low),
            buf((2, lines, wide), low),
            buf((lines, wide), f32),
            buf((lines, wide), low),
            buf((rows, width), low),
            buf((rows, width), low),
            buf((4,) + vec.shape, f32),
            buf((6,) + vec.shape, f32),
            buf((4, 8, LOG_PAIR), f32),
            buf((6, 8, LOG_PAIR), f32),
            sem((count,)), sem((count, 2)), sem((count, 2)), sem((count, 3)), sem((count, 3)),
            sem((2, pairs)), sem((2, pairs)), sem((3,)), sem((3,)), sem((2,)), sem((2,)),
            sem((6,)), sem((6,)), sem((6,)), sem((6,)), sem((3,)),
        ],
        compiler_params=pltpu.CompilerParams(
            vmem_limit_bytes=LIMIT, collective_id=number, has_side_effects=True
        ),
    )(x, q, k, v, lengths, logs, af, ga, vg, vec, vm, vs, g1, wa, one, student, *weights, *firsts, *seconds)


def split_kernels(
    tokens,
    teacher_tokens,
    cotangent,
    lengths,
    masked,
    attn_weight,
    out_weight,
    up_weight,
    down_weight,
    attn_first,
    out_first,
    up_first,
    down_first,
    attn_second,
    out_second,
    up_second,
    down_second,
    vectors,
    vector_first,
    vector_second,
    teacher_attn,
    teacher_out,
    teacher_up,
    teacher_down,
    teacher_vectors,
):
    width = tokens.shape[2]

    def upright(group):
        return (group[0], group[1].T, group[2], group[3].T)

    weights = upright((attn_weight, out_weight, up_weight, down_weight))
    vec = vectors.reshape(-1, width)
    spans = lengths.reshape(1, 1)
    wa, q, k, v, af, logs, ga, g1, one, student, sums = first_call(
        tokens[0],
        teacher_tokens[0],
        cotangent[0],
        vec,
        teacher_vectors.astype(f32).reshape(-1, width),
        spans,
        masked,
        weights,
        upright((teacher_attn, teacher_out, teacher_up, teacher_down)),
        0,
    )
    outs = second_call(
        tokens[0], q, k, v, spans, logs, af, ga, sums, vec,
        vector_first.reshape(-1, width),
        vector_second.reshape(-1, width),
        g1, wa, one, student,
        weights,
        upright((attn_first, out_first, up_first, down_first)),
        upright((attn_second, out_second, up_second, down_second)),
        1,
    )
    norms = outs[17]
    return (
        outs[1][None],
        outs[0][None],
        *upright(outs[2:6]),
        *upright(outs[6:10]),
        *upright(outs[10:14]),
        *(value.reshape(-1) for value in outs[14:17]),
        norms[:2, :6],
        norms[2, :6],
    )


def solution(mesh):
    local = split_kernels if dict(mesh.shape) == {"dp": 16, "mp": 2} else split_rows
    return jax.shard_map(
        local,
        mesh=mesh,
        in_specs=(
            P("dp", None, None),
            P("dp", None, None),
            P("dp", None, None),
            P("dp"),
            P("dp", None),
            P(None, "dp", "mp"),
            P("mp", "dp"),
            P("dp", "mp"),
            P("mp", "dp"),
            P(None, "dp", "mp"),
            P("mp", "dp"),
            P("dp", "mp"),
            P("mp", "dp"),
            P(None, "dp", "mp"),
            P("mp", "dp"),
            P("dp", "mp"),
            P("mp", "dp"),
            P(),
            P(),
            P(),
            P(None, "dp", "mp"),
            P("mp", "dp"),
            P("dp", "mp"),
            P("mp", "dp"),
            P(),
        ),
        out_specs=(
            P("dp", None, None),
            P("dp", None, None),
            P(None, "dp", "mp"),
            P("mp", "dp"),
            P("dp", "mp"),
            P("mp", "dp"),
            P(None, "dp", "mp"),
            P("mp", "dp"),
            P("dp", "mp"),
            P("mp", "dp"),
            P(None, "dp", "mp"),
            P("mp", "dp"),
            P("dp", "mp"),
            P("mp", "dp"),
            P(),
            P(),
            P(),
            P(),
            P(),
        ),
        check_vma=False,
    )
```

```python
from functools import partial

import jax
import jax.numpy as jnp
from jax import lax
from jax.experimental import pallas as pl
from jax.experimental.pallas import tpu as pltpu
from jax.sharding import PartitionSpec as P

HDIM = 64
STEP = 5


beta_one = 0.9
beta_two = 0.999
adam_eps = 1e-06
decay_rate = 0.01
matrix_rate = 0.3
vector_rate = 0.2
cosine_weight = 32.0
cosine_eps = 1e-06
layer_eps = 1e-12
masked_score = -1e30


def layer_norm(row_values, gain_vec, shift_vec):
    center = row_values - jnp.mean(row_values, -1, keepdims=True)
    spread = jnp.mean(center * center, -1, keepdims=True)
    return center * lax.rsqrt(spread + layer_eps) * gain_vec + shift_vec


def vector_parts(packed, model_width):
    pieces = [
        packed[position * model_width : (position + 1) * model_width] for position in range(8)
    ]
    return pieces + [packed[8 * model_width :]]


def head_scores(query, key_rows, visible):
    scale_factor = query.shape[-1] ** (-0.5)
    scores = (
        jnp.einsum("sqe,ske->sqk", query, key_rows, preferred_element_type=jnp.float32)
        * scale_factor
    )
    return jnp.where(visible[:, None, :], scores, masked_score)


def head_forward(query, key_rows, value_rows, visible):
    scores = head_scores(query, key_rows, visible)
    row_peak = jnp.max(scores, -1, keepdims=True)
    exponent = jnp.exp(scores - row_peak)
    row_total = jnp.sum(exponent, -1, keepdims=True)
    weights_low = (exponent / row_total).astype(jnp.bfloat16)
    mixed = jnp.einsum("sqk,ske->sqe", weights_low, value_rows, preferred_element_type=jnp.float32)
    return (mixed.astype(jnp.bfloat16), (row_peak + jnp.log(row_total))[..., 0])


def adam_moments(grad_now, first_old, second_old):
    first_new = beta_one * first_old + (1.0 - beta_one) * grad_now
    second_new = beta_two * second_old + (1.0 - beta_two) * grad_now * grad_now
    step_now = (
        first_new
        / (1.0 - beta_one**STEP)
        / (jnp.sqrt(second_new / (1.0 - beta_two**STEP)) + adam_eps)
    )
    return (first_new, second_new, step_now)


def matrix_squares(attn_w, out_w, up_w, down_w):
    return jnp.concatenate(
        [
            jnp.sum(attn_w * attn_w, axis=(1, 2)),
            jnp.stack([jnp.sum(out_w * out_w), jnp.sum(up_w * up_w), jnp.sum(down_w * down_w)]),
        ]
    )


def shard_pack(attn_w, out_w, up_w, down_w):
    return jnp.concatenate(
        [attn_w[0], attn_w[1], attn_w[2], out_w.T, up_w, down_w.T], axis=1
    )


def cosine_pull(rows, places, aimed, row_start):
    row_count = rows.shape[0]
    local_at = places - row_start
    here = (local_at >= 0) & (local_at < row_count)
    picked = rows[jnp.clip(local_at, 0, row_count - 1)]
    inner = jnp.sum(picked * aimed, -1, keepdims=True)
    square_own = jnp.sum(picked * picked, -1, keepdims=True) + cosine_eps
    square_aim = jnp.sum(aimed * aimed, -1, keepdims=True) + cosine_eps
    inverse = lax.rsqrt(square_own) * lax.rsqrt(square_aim)
    pull = -cosine_weight * (aimed * inverse - picked * (inner * inverse / square_own))
    pull = jnp.where(here[:, None], pull, 0.0)
    return jnp.zeros_like(rows).at[jnp.clip(local_at, 0, row_count - 1)].add(pull)


def heads_of(flat):
    return flat.reshape(flat.shape[0], flat.shape[1] // HDIM, HDIM).transpose(1, 0, 2)


def flat_of(split):
    return split.transpose(1, 0, 2).reshape(split.shape[1], -1)


def dot32(left, right):
    return jnp.dot(left, right, preferred_element_type=jnp.float32)


def dot_nt(left, right):
    return lax.dot_general(
        left, right, (((1,), (1,)), ((), ())), preferred_element_type=jnp.float32
    )


def dot_tn(left, right):
    return lax.dot_general(
        left, right, (((0,), (0,)), ((), ())), preferred_element_type=jnp.float32
    )


def split_rows(
    tokens,
    teacher_tokens,
    cotangent,
    lengths,
    masked,
    attn_weight,
    out_weight,
    up_weight,
    down_weight,
    attn_first,
    out_first,
    up_first,
    down_first,
    attn_second,
    out_second,
    up_second,
    down_second,
    vectors,
    vector_first,
    vector_second,
    teacher_attn,
    teacher_out,
    teacher_up,
    teacher_down,
    teacher_vectors,
):
    low = jnp.bfloat16
    everyone = ("dp", "mp")
    shard_at = lax.axis_index("mp")
    halves = lax.axis_size("mp")
    seq_count, length, width = tokens.shape
    rows = length // halves
    row_start = shard_at * rows
    part = attn_weight.shape[2]
    units = up_weight.shape[1]
    cuts = [0, part, 2 * part, 3 * part, 4 * part, 4 * part + units, 4 * part + 2 * units]
    visible = (jnp.arange(length) < lengths[0])[None, None, :]
    places = masked[0]

    student = lax.all_gather(
        shard_pack(attn_weight, out_weight, up_weight, down_weight).astype(low),
        ("mp", "dp"),
        axis=0,
        tiled=True,
    ).reshape(halves, width, cuts[6])
    teacher = lax.all_gather(
        shard_pack(teacher_attn, teacher_out, teacher_up, teacher_down),
        "dp",
        axis=0,
        tiled=True,
    )

    def whole(index):
        return jnp.concatenate(
            [student[half, :, cuts[index] : cuts[index + 1]] for half in range(halves)], axis=1
        )

    teacher_parts = vector_parts(teacher_vectors.astype(jnp.float32), width)
    bias_q = lax.dynamic_slice_in_dim(teacher_parts[0], shard_at * part, part)
    bias_v = lax.dynamic_slice_in_dim(teacher_parts[1], shard_at * part, part)
    bias_up = lax.dynamic_slice_in_dim(teacher_parts[8], shard_at * units, units)
    teacher_rows = teacher_tokens[0]
    listed = teacher_rows[places]
    t_query = (dot32(listed, teacher[:, : cuts[1]]) + bias_q).astype(low)
    t_keys = dot32(teacher_rows, teacher[:, cuts[1] : cuts[2]]).astype(low)
    t_values = (dot32(teacher_rows, teacher[:, cuts[2] : cuts[3]]) + bias_v).astype(low)
    t_mixed, unused_log = head_forward(
        heads_of(t_query), heads_of(t_keys), heads_of(t_values), visible[0]
    )
    t_branch = lax.psum(dot_nt(flat_of(t_mixed), teacher[:, cuts[3] : cuts[4]]), "mp")
    t_first = listed.astype(jnp.float32) + t_branch + teacher_parts[2]
    t_normed = layer_norm(t_first, teacher_parts[3], teacher_parts[4])
    t_gate = dot32(t_normed.astype(low), teacher[:, cuts[4] : cuts[5]]) + bias_up
    t_act = jax.nn.gelu(t_gate, approximate=False).astype(low)
    t_feed = lax.psum(dot_nt(t_act, teacher[:, cuts[5] : cuts[6]]), "mp")
    aimed = layer_norm(t_normed + t_feed + teacher_parts[5], teacher_parts[6], teacher_parts[7])

    pieces = vector_parts(vectors, width)
    all_rows = tokens[0]
    own_rows = lax.dynamic_slice_in_dim(all_rows, row_start, rows, 0)
    w_q, w_k, w_v, w_out, w_up, w_down = [whole(index) for index in range(6)]
    query = heads_of((dot32(own_rows, w_q) + pieces[0]).astype(low))
    keys = heads_of(dot32(all_rows, w_k).astype(low))
    values = heads_of((dot32(all_rows, w_v) + pieces[1]).astype(low))
    mixed, log_total = lax.map(
        lambda g: jax.tree.map(
            lambda v: v[0], head_forward(g[0][None], g[1][None], g[2][None], visible[0])
        ),
        (query, keys, values),
    )
    attended = flat_of(mixed)
    first_sum = own_rows.astype(jnp.float32) + dot_nt(attended, w_out) + pieces[2]
    normed = layer_norm(first_sum, pieces[3], pieces[4])
    normed_low = normed.astype(low)
    gate_in = dot32(normed_low, w_up) + pieces[8]
    activated = jax.nn.gelu(gate_in, approximate=False).astype(low)
    second_sum = normed + dot_nt(activated, w_down) + pieces[5]
    outcome = layer_norm(second_sum, pieces[6], pieces[7])
    student_out = lax.all_gather(outcome.astype(low), "mp", axis=0, tiled=True)[None]

    own_cotangent = lax.dynamic_slice_in_dim(cotangent[0], row_start, rows, 0)
    grad_top = own_cotangent.astype(jnp.float32) + cosine_pull(outcome, places, aimed, row_start)
    unused_top, pull_top = jax.vjp(layer_norm, second_sum, pieces[6], pieces[7])
    grad_second, grad_gain_two, grad_shift_two = pull_top(grad_top)
    feed_low = grad_second.astype(low)
    grad_down = dot_tn(feed_low, activated)
    grad_act = dot32(feed_low, w_down)
    unused_gelu, pull_gelu = jax.vjp(partial(jax.nn.gelu, approximate=False), gate_in)
    (grad_gate,) = pull_gelu(grad_act)
    gate_low = grad_gate.astype(low)
    grad_up = dot_tn(normed_low, gate_low)
    grad_normed = grad_second + dot_nt(gate_low, w_up)
    unused_mid, pull_mid = jax.vjp(layer_norm, first_sum, pieces[3], pieces[4])
    grad_first, grad_gain_one, grad_shift_one = pull_mid(grad_normed)
    branch_low = grad_first.astype(low)
    grad_out = dot_tn(branch_low, attended)
    grad_heads = heads_of(dot32(branch_low, w_out).astype(low))

    def one_head(g):
        query_h, keys_h, values_h, mixed_h, log_h = g
        scale_factor = HDIM**-0.5
        scores = jnp.where(visible[0], dot_nt(query_h, keys_h) * scale_factor, masked_score)
        probs = jnp.exp(scores - log_h[:, None])
        grad_probs = dot_nt(mixed_h, values_h)
        inner = jnp.sum(probs * grad_probs, -1, keepdims=True)
        grad_scores = (probs * (grad_probs - inner)).astype(low)
        return (
            (dot32(grad_scores, keys_h) * scale_factor).astype(low),
            (dot_tn(grad_scores, query_h) * scale_factor).astype(low),
            dot_tn(probs.astype(low), mixed_h).astype(low),
        )

    grad_query, grad_keys, grad_values = lax.map(
        one_head, (query, keys, values, grad_heads, log_total)
    )
    grad_query = flat_of(grad_query)

    def row_sum(term):
        other = lax.dynamic_slice_in_dim(term, (1 - shard_at) * rows, rows, 0)
        mine = lax.dynamic_slice_in_dim(term, row_start, rows, 0)
        came = lax.ppermute(other, "mp", [(0, 1), (1, 0)])
        return (mine.astype(jnp.float32) + came.astype(jnp.float32)).astype(low)

    grad_keys = row_sum(flat_of(grad_keys))
    grad_values = row_sum(flat_of(grad_values))
    grad_q = dot_tn(own_rows, grad_query)
    grad_k = dot_tn(own_rows, grad_keys)
    grad_v = dot_tn(own_rows, grad_values)
    input_own = (
        grad_first + dot_nt(grad_query, w_q) + dot_nt(grad_keys, w_k) + dot_nt(grad_values, w_v)
    )
    input_grad = lax.all_gather(input_own, "mp", axis=0, tiled=True)[None]

    def half_of(matrix, half):
        span = matrix.shape[1] // halves
        return matrix[:, half * span : (half + 1) * span]

    grads = [grad_q, grad_k, grad_v, grad_out, grad_up, grad_down]
    packed_grad = jnp.concatenate(
        [
            jnp.concatenate([half_of(g, half) for g in grads], axis=1).astype(low)
            for half in range(halves)
        ],
        axis=0,
    )
    summed = lax.psum_scatter(
        packed_grad, ("mp", "dp"), scatter_dimension=0, tiled=True
    ).astype(jnp.float32)
    summed_attn = jnp.stack([summed[:, cuts[i] : cuts[i + 1]] for i in range(3)])
    summed_out = summed[:, cuts[3] : cuts[4]].T
    summed_up = summed[:, cuts[4] : cuts[5]]
    summed_down = summed[:, cuts[5] : cuts[6]].T

    vector_grad = jnp.concatenate(
        [
            jnp.sum(grad_query.astype(jnp.float32), 0),
            jnp.sum(grad_values.astype(jnp.float32), 0),
            jnp.sum(branch_low.astype(jnp.float32), 0),
            grad_gain_one,
            grad_shift_one,
            jnp.sum(feed_low.astype(jnp.float32), 0),
            grad_gain_two,
            grad_shift_two,
            jnp.sum(gate_low.astype(jnp.float32), 0),
        ]
    )
    return (student_out, input_grad) + lamb_update(
        (summed_attn, summed_out, summed_up, summed_down),
        (attn_weight, out_weight, up_weight, down_weight),
        (attn_first, out_first, up_first, down_first),
        (attn_second, out_second, up_second, down_second),
        vector_grad,
        vectors,
        vector_first,
        vector_second,
    )


def lamb_update(grads, weights, firsts, seconds, vector_grad, vectors, vector_first, vector_second):
    moments, squares, steps = [], [], []
    for grad_now, weight, first_old, second_old in zip(grads, weights, firsts, seconds):
        first_new, second_new, step_now = adam_moments(grad_now, first_old, second_old)
        moments.append(first_new)
        squares.append(second_new)
        steps.append(step_now + decay_rate * weight)
    weight_total, update_total, vector_total = lax.psum(
        (matrix_squares(*weights), matrix_squares(*steps), vector_grad), ("dp", "mp")
    )
    weight_norms = jnp.sqrt(weight_total)
    update_norms = jnp.sqrt(update_total)
    trust_ratio = weight_norms / update_norms
    ratios = [trust_ratio[0:3][:, None, None], trust_ratio[3], trust_ratio[4], trust_ratio[5]]
    updated = [
        weight - matrix_rate * ratio * step for weight, ratio, step in zip(weights, ratios, steps)
    ]
    vector_moment, vector_square, step_vector = adam_moments(
        vector_total, vector_first, vector_second
    )
    vector_updated = vectors - vector_rate * step_vector
    return (
        *updated,
        *moments,
        *squares,
        vector_moment,
        vector_square,
        vector_updated,
        jnp.stack([weight_norms, update_norms]),
        trust_ratio,
    )


LOG_PAIR = 128
MESH = pl.DeviceIdType.MESH
low = jnp.bfloat16
f32 = jnp.float32
VMEM_SPEC = pl.BlockSpec(memory_space=pltpu.VMEM)
ANY_SPEC = pl.BlockSpec(memory_space=pl.ANY)
AHEAD = 2
FIRST_LIMIT = 64 * 2**20
LIMIT = 60 * 2**20


def dnn(left, right):
    return jnp.dot(left, right, preferred_element_type=f32)


def dnt(left, right):
    return lax.dot_general(left, right, (((1,), (1,)), ((), ())), preferred_element_type=f32)


def lane_index(shape):
    return lax.broadcasted_iota(jnp.int32, shape, 1)


def split_three(value):
    top = value.astype(low).astype(f32)
    rest = value - top
    middle = rest.astype(low).astype(f32)
    return (top, middle, rest - middle)


def flip(value):
    return value.astype(f32).T.astype(low)


def place():
    at = lax.axis_index("dp")
    return (at, lax.axis_index("mp"), at // 4, (at // 2) % 2, at % 2)


def near():
    at, y, z, x, core = place()
    return dict(
        twin=(at + 1 - 2 * core, y),
        x=(at + 2 - 4 * x, y),
        y=(at, 1 - y),
        z=[(((z + step) % 4) * 4 + 2 * x + core, y) for step in (1, 2, 3)],
    )


def greet(peers):
    sem = pltpu.get_barrier_semaphore()
    for peer in peers:
        pl.semaphore_signal(sem, inc=1, device_id=peer, device_id_type=MESH)
    pl.semaphore_wait(sem, len(peers))


def remote(src, dst, sends, recvs, at, peer):
    return pltpu.make_async_remote_copy(
        src_ref=src,
        dst_ref=dst,
        send_sem=sends.at[at],
        recv_sem=recvs.at[at],
        device_id=peer,
        device_id_type=MESH,
    )


def row_norm(rows):
    center = rows - jnp.mean(rows, -1, keepdims=True)
    scale = lax.rsqrt(jnp.mean(center * center, -1, keepdims=True) + layer_eps)
    return (center * scale, scale)


def norm_pull(grad, unit, scale, gain):
    lifted = grad * gain
    return scale * (
        lifted
        - jnp.mean(lifted, -1, keepdims=True)
        - unit * jnp.mean(lifted * unit, -1, keepdims=True)
    )


def normal_share(value):
    return 0.5 * (1.0 + lax.erf(value * 0.7071067811865476))


def pair_forward(query, keys, values, bias):
    count, span = query.shape[0], keys.shape[0]
    lane_q, lane_k = lane_index((count, LOG_PAIR)), lane_index((span, LOG_PAIR))
    outs, logs = [], []
    for head in range(2):
        spare = HDIM * (1 - head)
        keys_now = jnp.where(
            lane_k // HDIM == head,
            keys.astype(f32),
            jnp.where(lane_k == spare, bias, 0.0),
        ).astype(low)
        query_now = jnp.where(
            lane_q // HDIM == head,
            query.astype(f32),
            jnp.where(lane_q == spare, 1.0, 0.0),
        ).astype(low)
        scores = dnt(query_now, keys_now)
        peak = jnp.max(scores, -1, keepdims=True)
        exponent = jnp.exp(scores - peak)
        total = jnp.sum(exponent, -1, keepdims=True)
        outs.append(dnn((exponent * (1.0 / total)).astype(low), values))
        logs.append(peak + jnp.log(total))
    return (
        jnp.where(lane_q < HDIM, outs[0], outs[1]),
        jnp.where(lane_q < HDIM, logs[0], logs[1]),
    )


def shape_of(*dims, kind=f32):
    return jax.ShapeDtypeStruct(dims, kind)


def pair_back_rows(query, grad_mixed, mixed, logs):
    lane_q = lane_index(query.shape)
    query_wide, grad_wide = query.astype(f32), grad_mixed.astype(f32)
    product = grad_wide * mixed.astype(f32)
    sides = []
    for head in range(2):
        spare = HDIM * (1 - head)
        own_q = lane_q // HDIM == head
        inner = jnp.sum(jnp.where(own_q, product, 0.0), -1, keepdims=True)
        query_now = jnp.where(own_q, query_wide, jnp.where(lane_q == spare, 1.0, 0.0))
        grad_now = jnp.where(own_q, grad_wide, 0.0)
        for place_at, (log_term, inner_term) in enumerate(
            zip(split_three(logs[:, HDIM * head : HDIM * head + 1]), split_three(inner))
        ):
            here = lane_q == spare + 1 + place_at
            query_now = jnp.where(here, log_term, query_now)
            grad_now = jnp.where(here, inner_term, grad_now)
        sides.append((query_now.astype(low), grad_now.astype(low)))
    return sides


def pair_back_keys(query, grad_mixed, sides, keys, values, bias):
    lane_k = lane_index(keys.shape)
    keys_wide, values_wide = keys.astype(f32), values.astype(f32)
    grad_keys, grad_values, grad_query = [], [], []
    for head, (query_now, grad_now) in enumerate(sides):
        spare = HDIM * (1 - head)
        own_k = lane_k // HDIM == head
        minus = jnp.where((lane_k > spare) & (lane_k < spare + 4), -1.0, 0.0)
        keys_now = jnp.where(own_k, keys_wide, jnp.where(lane_k == spare, bias, minus)).astype(low)
        values_now = jnp.where(own_k, values_wide, minus).astype(low)
        probs = jnp.exp(dnt(keys_now, query_now))
        grad_scores = (probs * dnt(values_now, grad_now)).astype(low)
        grad_keys.append(dnn(grad_scores, query))
        grad_values.append(dnn(probs.astype(low), grad_mixed))
        flipped = keys_wide.T[HDIM * head : HDIM * (head + 1)].astype(low)
        grad_query.append(dnn(flipped, grad_scores))
    return (
        jnp.concatenate(grad_query, 0),
        jnp.where(lane_k < HDIM, grad_keys[0], grad_keys[1]),
        jnp.where(lane_k < HDIM, grad_values[0], grad_values[1]),
    )


def adam_step(grad, first, second):
    first_new = beta_one * first + (1.0 - beta_one) * grad
    second_new = beta_two * second + (1.0 - beta_two) * grad * grad
    step = (
        first_new
        / (1.0 - beta_one**STEP)
        / (jnp.sqrt(second_new / (1.0 - beta_two**STEP)) + adam_eps)
    )
    return (first_new, second_new, step)


def block_of(ref, cols):
    value = ref[:, :, :, :, cols]
    return value.reshape(-1, value.shape[-1])


def gather_steps(chunks, gs_ref, gt_ref, ps_ref, pt_ref, local_sem, zsends, zrecvs, sends, recvs, started):
    at, y, z, x, core = place()
    ways = near()

    def go(ref, chunk, kind, peer):
        copy = remote(ref, ref, sends, recvs, (chunk, kind), peer)
        copy.start()
        started.append(copy)

    def landed(ref, chunk, kind):
        remote(ref, ref, sends, recvs, (chunk, kind), ways["x"]).wait_recv()

    def shard(chunk, zz):
        which, a, b = chunks[chunk]
        if which == 0:
            return gs_ref.at[y, zz, x, core, :, pl.ds(a, b - a)]
        return gt_ref.at[zz, x, core, :, pl.ds(a, b - a)]

    def column(chunk, yy, xx, cc):
        which, a, b = chunks[chunk]
        if which == 0:
            return gs_ref.at[yy, :, xx, cc, :, pl.ds(a, b - a)]
        return gt_ref.at[:, xx, cc, :, pl.ds(a, b - a)]

    own = []

    def begin(k):
        which, a, b = chunks[k]
        source = (ps_ref, pt_ref)[which].at[:, pl.ds(a, b - a)]
        copy = pltpu.make_async_copy(source, shard(k, z), local_sem.at[k])
        copy.start()
        own.append(copy)
        for step in range(3):
            copy = remote(source, shard(k, z), zsends, zrecvs, (k, step), ways["z"][step])
            copy.start()
            started.append(copy)

    def along_z(k):
        for step in range(3):
            came = shard(k, (z + 3 - step) % 4)
            remote(came, came, zsends, zrecvs, (k, step), ways["x"]).wait_recv()
        own[k].wait()
        go(column(k, y, x, core), k, 0, ways["x"])
        if chunks[k][0] == 0:
            go(column(k, y, x, core), k, 1, ways["y"])
        go(column(k, y, x, core), k, 2, ways["twin"])

    def from_sides(k):
        landed(column(k, y, 1 - x, core), k, 0)
        if chunks[k][0] == 0:
            go(column(k, y, 1 - x, core), k, 3, ways["y"])
        go(column(k, y, 1 - x, core), k, 4, ways["twin"])
        if chunks[k][0] == 0:
            landed(column(k, 1 - y, x, core), k, 1)
            go(column(k, 1 - y, x, core), k, 5, ways["twin"])

    def last(k):
        if chunks[k][0] == 0:
            landed(column(k, 1 - y, 1 - x, core), k, 3)
            go(column(k, 1 - y, 1 - x, core), k, 6, ways["twin"])

    def whole(k):
        landed(column(k, y, x, 1 - core), k, 2)
        landed(column(k, y, 1 - x, 1 - core), k, 4)
        if chunks[k][0] == 0:
            landed(column(k, 1 - y, x, 1 - core), k, 5)
            landed(column(k, 1 - y, 1 - x, 1 - core), k, 6)

    count = len(chunks)
    for k in range(AHEAD):
        begin(k)
    for slot in range(count + 3):
        if slot + AHEAD < count:
            begin(slot + AHEAD)
        if slot < count:
            along_z(slot)
        if 0 <= slot - 1 < count:
            from_sides(slot - 1)
        if 0 <= slot - 2 < count:
            last(slot - 2)
        if 0 <= slot - 3 < count:
            whole(slot - 3)
        yield max(0, slot - 2)


def sum_steps(chunks, given, ax_at, h_at, zr_at, before_x, before_z, tot_ref, own_ref, yr_ref, sends, recvs, zsends, zrecvs, started):
    at, y, z, x, core = place()
    ways = near()
    count = len(chunks)

    def span(k):
        a, b = chunks[k]
        return pl.ds(a, b - a)

    def begin(k):
        if k in before_x:
            before_x[k]()
        copy = remote(given(k, 1 - x), ax_at(k), sends, recvs, (k, 0), ways["x"])
        copy.start()
        started.append(copy)

    def over_x(k):
        remote(ax_at(k), ax_at(k), sends, recvs, (k, 0), ways["x"]).wait_recv()
        came = ax_at(k)

        def add(step, carry):
            yy, zz = step // 4, step % 4
            block = h_at(k, yy, zz)
            block[...] = (block[...].astype(f32) + came[yy, zz].astype(f32)).astype(low)
            return carry

        lax.fori_loop(0, 8, add, 0)
        if k in before_z:
            before_z[k]()
        for step in range(3):
            copy = remote(
                h_at(k, slice(None), (z + 1 + step) % 4), zr_at(k, step),
                zsends, zrecvs, (k, step), ways["z"][step],
            )
            copy.start()
            started.append(copy)

    def over_z(k):
        here = span(k)
        for step in range(3):
            came = zr_at(k, step)
            remote(came, came, zsends, zrecvs, (k, step), ways["x"]).wait_recv()
        for yy in range(2):
            total = h_at(k, yy, z)[...].astype(f32)
            for step in range(3):
                total += zr_at(k, step)[yy].astype(f32)
            tot_ref[yy, :, here] = total.astype(low)
        copy = remote(
            tot_ref.at[1 - y, :, here], yr_ref.at[:, here], sends, recvs, (k, 1), ways["y"]
        )
        copy.start()
        started.append(copy)

    def over_y(k):
        here = span(k)
        came = yr_ref.at[:, here]
        remote(came, came, sends, recvs, (k, 1), ways["y"]).wait_recv()
        own_ref[:, here] = tot_ref[y, :, here].astype(f32) + yr_ref[:, here].astype(f32)

    def steps():
        for slot in range(count + 2):
            if slot < count:
                over_x(slot)
            if 0 <= slot - 1 < count:
                over_z(slot - 1)
            if 0 <= slot - 2 < count:
                over_y(slot - 2)
            yield max(0, slot - 1)

    return begin, steps()


def shared_steps(value, result, mine_at, come_at, sends, recvs):
    at, y, z, x, core = place()
    ways = near()
    for index, way in enumerate(("twin", "x", "y")):
        mine_at(index)[...] = value
        copy = remote(mine_at(index), come_at(index), sends, recvs, index, ways[way])
        copy.start()
        yield
        copy.wait()
        value = mine_at(index)[...] + come_at(index)[...]
    mine_at(3)[...] = value
    copies = []
    for step in range(3):
        copy = remote(
            mine_at(3), come_at(3 + step), sends, recvs, 3 + step, ways["z"][step]
        )
        copy.start()
        copies.append(copy)
    yield
    for copy in copies:
        copy.wait()
    terms = [mine_at(3)[...]] + [come_at(3 + step)[...] for step in range(3)]
    total = None
    for z_from in range(4):
        term = terms[0]
        for step in range(1, 4):
            term = jnp.where((z + 4 - step) % 4 == z_from, terms[step], term)
        total = term if total is None else total + term
    result.append(total)


def first_kernel(
    chunks,
    x_ref, tx_ref, cot_hbm, vec_ref, tvec_ref, length_ref, places_ref, places_col_ref,
    aw, ow, uw, dw, ta, to, tu, td,
    wa_hbm, input_hbm, student_hbm, total_ref, vector_ref,
    sums_ref,
    gs_ref, gt_ref, ps_ref, pt_ref, q_ref, k_ref, v_ref, a_ref, log_ref,
    tk_ref, tv_ref, part_ref, come_ref, r1_ref, normed_ref, u_ref, slope_ref, r2_ref,
    cot_ref, flip_ref, nflip_ref, ga_ref, one_ref, zr_ref, tot_ref, yr_ref,
    local_sem, zsends, zrecvs, sends, recvs, tsends, trecvs, gsends, grecvs, copy_sem,
    fsends, frecvs, fzsends, fzrecvs, ksends, krecvs, vsends, vrecvs,
    free_x, free_y, free_z, free_twin,
):
    at, y, z, x, core = place()
    ways = near()
    length, width = x_ref.shape
    rows = length // 2
    part = width // 2
    half_block = rows // 2
    own = pl.ds(pl.multiple_of(y * rows, rows), rows)
    kept = []

    def keep(src, dst):
        copy = pltpu.make_async_copy(src, dst, copy_sem.at[len(kept)])
        copy.start()
        kept.append(copy)
        return copy

    for index in range(3):
        ps_ref[:, index * part : (index + 1) * part] = aw[index].astype(low)
        pt_ref[:, index * part : (index + 1) * part] = ta[index]
    for base, source, aim in ((3 * part, ow, to), (4 * part, uw, tu), (8 * part, dw, td)):
        ps_ref[:, base : base + source.shape[1]] = source[...].astype(low)
        pt_ref[:, base : base + source.shape[1]] = aim[...]
    greet([ways["twin"], ways["x"], ways["y"]] + ways["z"])
    started = []
    steps = gather_steps(
        chunks, gs_ref, gt_ref, ps_ref, pt_ref, local_sem, zsends, zrecvs, sends, recvs, started
    )
    ready = [0]

    def tick():
        ready[0] = next(steps, len(chunks))

    def need(chunk):
        while ready[0] <= chunk:
            tick()

    cot_copy = keep(cot_hbm.at[own], cot_ref)

    def key_bias():
        row_at = lax.broadcasted_iota(jnp.int32, (length, LOG_PAIR), 0)
        return jnp.where(row_at < length_ref[0:1, 0:1], 0.0, masked_score)

    sums_ref[...] = jnp.zeros(sums_ref.shape, f32)

    def loop(count, body):
        def step(index, carry):
            body(index)
            return carry

        lax.fori_loop(0, count, step, 0)

    def span(index, block):
        return pl.ds(pl.multiple_of(index * block, block), block)

    need(3)
    wa_copy = keep(gs_ref.at[:, :, :, :, :, pl.ds(0, 3 * part)], wa_hbm)

    def keys_values(index):
        here = span(index, 256)
        for half in range(2):
            cols = slice(half * part, (half + 1) * part)
            k_ref[here, cols] = dnn(
                x_ref[here, :], block_of(gs_ref.at[half], slice(part, 2 * part))
            ).astype(low)
            v_ref[here, cols] = (
                dnn(x_ref[here, :], block_of(gs_ref.at[half], slice(2 * part, 3 * part)))
                + vec_ref[1:2, cols]
            ).astype(low)

    def queries(index):
        here = span(index, 256)
        from_x = pl.ds(pl.multiple_of(y * rows + index * 256, 256), 256)
        for half in range(2):
            cols = slice(half * part, (half + 1) * part)
            value = dnn(x_ref[from_x, :], block_of(gs_ref.at[half], slice(0, part)))
            value = (value + vec_ref[0:1, cols]).astype(low).astype(f32) * HDIM**-0.5
            q_ref[here, cols] = value.astype(low)

    def attend(first):
        def one_pair(index):
            pair = first + index
            cols = pl.ds(pl.multiple_of(pair * LOG_PAIR, LOG_PAIR), LOG_PAIR)
            keys, values, bias = k_ref[:, cols], v_ref[:, cols], key_bias()
            for start in range(0, rows, 256):
                here = slice(start, start + 256)
                mixed, logs = pair_forward(q_ref[here, cols], keys, values, bias)
                a_ref[here, cols] = mixed.astype(low)
                log_ref[pair, here, :] = logs

        return one_pair

    loop(length // 256, keys_values)
    tick()
    loop(rows // 256, queries)
    for first in (0, 2, 4):
        loop(2, attend(first))
        tick()

    need(4)
    mine = pl.ds(pl.multiple_of(y * part, LOG_PAIR), part)
    count = places_col_ref.shape[0]

    def teacher_keys(index):
        here = span(index, 256)
        tk_ref[here, :] = dnn(tx_ref[here, :], block_of(gt_ref, slice(part, 2 * part))).astype(low)
        tv_ref[here, :] = (
            dnn(tx_ref[here, :], block_of(gt_ref, slice(2 * part, 3 * part))) + tvec_ref[1:2, mine]
        ).astype(low)

    loop(length // 256, teacher_keys)
    pick = jnp.where(places_col_ref[:, 0:1] == lane_index((count, length)), 1.0, 0.0).astype(low)
    listed = dnn(pick, tx_ref[...])
    query = dnn(listed.astype(low), block_of(gt_ref, slice(0, part))) + tvec_ref[0:1, mine]
    query = (query.astype(low).astype(f32) * HDIM**-0.5).astype(low)
    part_ref[0] = jnp.zeros((count, width), f32)
    for pair in range(part // LOG_PAIR):
        cols = slice(pair * LOG_PAIR, (pair + 1) * LOG_PAIR)
        mixed, unused = pair_forward(query[:, cols], tk_ref[:, cols], tv_ref[:, cols], key_bias())
        a_cols = slice(3 * part + pair * LOG_PAIR, 3 * part + (pair + 1) * LOG_PAIR)
        part_ref[0] += dnt(mixed.astype(low), block_of(gt_ref, a_cols))
    swaps = [remote(part_ref.at[i], come_ref.at[i], tsends, trecvs, i, ways["y"]) for i in range(2)]
    swaps[0].start()

    need(5)

    def project(index):
        here = span(index, 256)
        from_x = pl.ds(pl.multiple_of(y * rows + index * 256, 256), 256)
        first = x_ref[from_x, :].astype(f32) + vec_ref[2:3, :]
        for half in range(2):
            first += dnt(
                a_ref[here, half * part : (half + 1) * part],
                block_of(gs_ref.at[half], slice(3 * part, 4 * part)),
            )
        r1_ref[here, :] = first
        unit, unused = row_norm(first)
        normed = unit * vec_ref[3:4, :] + vec_ref[4:5, :]
        normed_ref[here, :] = normed.astype(low)
        nflip_ref[:, here] = flip(normed.astype(low))
        r2_ref[here, :] = normed + vec_ref[5:6, :]

    loop(rows // 256, project)

    def rise(piece):
        half, base = piece // 2, 4 * part + (piece % 2) * width

        def body(index):
            here = span(index, 256)
            cols = slice(piece * width, (piece + 1) * width)
            gate = dnn(normed_ref[here, :], block_of(gs_ref.at[half], slice(base, base + width)))
            gate += vec_ref[8 + piece : 9 + piece, :]
            share = normal_share(gate)
            u_ref[here, cols] = (gate * share).astype(low)
            slope_ref[here, cols] = (
                share + gate * (jnp.exp(-0.5 * gate * gate) * 0.3989422804014327)
            ).astype(low)

        loop(rows // 256, body)

    def fall(piece):
        half, base = piece // 2, 4 * part + (2 + piece % 2) * width

        def body(index):
            here = span(index, 256)
            r2_ref[here, :] += dnt(
                u_ref[here, piece * width : (piece + 1) * width],
                block_of(gs_ref.at[half], slice(base, base + width)),
            )

        loop(rows // 256, body)

    active = []

    def aim_rise(piece):
        base = 4 * part + piece * width
        gate = dnn(aim_normed.astype(low), block_of(gt_ref, slice(base, base + width)))
        gate += tvec_ref[pl.ds(8 + 2 * y + piece, 1), :]
        active.append((gate * normal_share(gate)).astype(low))

    def aim_fall(piece):
        base = 8 * part + piece * width
        term = dnt(active[piece], block_of(gt_ref, slice(base, base + width)))
        part_ref[1] = term if piece == 0 else part_ref[1] + term

    need(6)
    swaps[0].wait()
    unit, unused = row_norm(listed + (part_ref[0] + come_ref[0]) + tvec_ref[2:3, :])
    aim_normed = unit * tvec_ref[3:4, :] + tvec_ref[4:5, :]
    aim_rise(0)
    for chunk, work in (
        (7, lambda: (rise(0), rise(2))),
        (8, lambda: aim_rise(1)),
        (9, lambda: (rise(1), rise(3))),
        (10, lambda: aim_fall(0)),
        (11, lambda: (fall(0), fall(2))),
        (12, lambda: (aim_fall(1), swaps[1].start())),
        (13, lambda: (fall(1), fall(3))),
    ):
        need(chunk)
        work()
    swaps[1].wait()
    unit, unused = row_norm(aim_normed + (part_ref[1] + come_ref[1]) + tvec_ref[5:6, :])
    part_ref[0] = unit * tvec_ref[6:7, :] + tvec_ref[7:8, :]
    for unused in steps:
        pass
    for copy in started:
        copy.wait_send()
    wa_copy.wait()
    pl.semaphore_signal(free_x, inc=1, device_id=ways["x"], device_id_type=MESH)
    cot_copy.wait()

    def top(index):
        here = span(index, 256)
        row_at = lax.broadcasted_iota(jnp.int32, (256, places_ref.shape[1]), 0)
        pick = jnp.where(row_at + (y * rows + index * 256) == places_ref[0:1, :], 1.0, 0.0)
        times = jnp.sum(pick, -1, keepdims=True)
        aimed = jnp.dot(
            pick, part_ref[0], precision=lax.Precision.HIGHEST, preferred_element_type=f32
        ) / jnp.maximum(times, 1.0)
        unit, spread = row_norm(r2_ref[here, :])
        outcome = unit * vec_ref[6:7, :] + vec_ref[7:8, :]
        inner = jnp.sum(outcome * aimed, -1, keepdims=True)
        square_own = jnp.sum(outcome * outcome, -1, keepdims=True) + cosine_eps
        square_aim = jnp.sum(aimed * aimed, -1, keepdims=True) + cosine_eps
        scale = cosine_weight * times * lax.rsqrt(square_own) * lax.rsqrt(square_aim)
        grad = cot_ref[here, :].astype(f32) - scale * (aimed - outcome * (inner / square_own))
        cot_ref[here, :] = outcome.astype(low)
        sums_ref[6:7, :] += jnp.sum(grad * unit, 0, keepdims=True)
        sums_ref[7:8, :] += jnp.sum(grad, 0, keepdims=True)
        back = norm_pull(grad, unit, spread, vec_ref[6:7, :])
        r2_ref[here, :] = back
        back_low = back.astype(low)
        sums_ref[5:6, :] += jnp.sum(back_low.astype(f32), 0, keepdims=True)
        ga_ref[here, :] = back_low
        flip_ref[:, here] = flip(back_low)

    loop(rows // 256, top)
    keep(cot_ref, student_hbm.at[own])
    share = remote(cot_ref, student_hbm.at[own], ksends, krecvs, (2, 0), ways["y"])
    share.start()

    sum_sent = []
    wide_at = [8 * part, 10 * part, 4 * part, 6 * part]
    cuts = [(a, a + width) for a in wide_at] + [(3 * part, 4 * part)]
    cuts += [(i * part, (i + 1) * part) for i in range(3)]
    spare_at = 6 * part

    def feed_cols(k):
        a, b = cuts[k]
        return pl.ds(a - 3 * part, b - a)

    def spare_cols(k):
        a, b = cuts[k]
        return pl.ds(spare_at + a, b - a)

    def given(k, xx):
        if k < 5:
            return one_ref.at[:, :, xx, :, feed_cols(k)]
        return gs_ref.at[:, :, xx, 0, :, spare_cols(k)]

    def ax_at(k):
        if k < 4:
            return gs_ref.at[:, :, k // 2, k % 2, :, pl.ds(0, width)]
        if k == 4:
            return gs_ref.at[:, :, 0, 0, :, pl.ds(width, part)]
        return gs_ref.at[:, :, 0, 1, :, spare_cols(k)]

    def h_at(k, yy, zz):
        return given(k, x).at[yy, zz]

    def zr_at(k, step):
        if k < 5:
            return zr_ref.at[step, :, :, feed_cols(k)]
        return gs_ref.at[:, step, 1, 1, :, spare_cols(k)]

    def wait_for(sem, amount):
        return lambda: pl.semaphore_wait(sem, amount)

    sum_begin, sums = sum_steps(
        cuts, given, ax_at, h_at, zr_at,
        {0: wait_for(free_x, 1), 5: wait_for(free_x, 1)}, {5: wait_for(free_z, 3)},
        tot_ref, total_ref, yr_ref, fsends, frecvs, fzsends, fzrecvs, sum_sent,
    )
    blocks = []

    def share_block(value, half):
        number = len(blocks)
        k, size = number // 2, value.shape[1]
        slot = pl.ds((number % 6) * width, size)
        if number >= 2:
            settle(number - 2)
        gt_ref[:, :, :, :, slot] = value.astype(low).reshape(gt_ref.shape[:4] + (size,))
        if k < 5:
            target = one_ref.at[half, :, :, :, feed_cols(k)]
        else:
            target = gs_ref.at[half, :, :, 0, :, spare_cols(k)]
        copy = remote(
            gt_ref.at[:, :, 1 - core, :, slot], target, gsends, grecvs, number, ways["twin"]
        )
        copy.start()
        blocks.append((copy, target, slot))

    settled = set()

    def settle(number):
        if number in settled:
            return
        settled.add(number)
        copy, target, slot = blocks[number]
        copy.wait()

        def add(zz, carry):
            target[zz] = (
                target[zz].astype(f32) + gt_ref[zz, :, core, :, slot].astype(f32)
            ).astype(low)
            return carry

        lax.fori_loop(0, 4, add, 0)
        if number % 2 == 1:
            sum_begin(number // 2)

    def down_grad(piece):
        half, cols = piece // 2, slice(piece * width, (piece + 1) * width)
        share_block(dnn(flip_ref[...], u_ref[:, cols]), half)

    def gate_pull(piece):
        half, base = piece // 2, 4 * part + (piece % 2) * width
        cols = slice(piece * width, (piece + 1) * width)

        def gate_back(index):
            here = span(index, 256)
            down = block_of(gs_ref.at[half], slice(base + 2 * width, base + 3 * width))
            gate_low = (dnn(ga_ref[here, :], down) * slope_ref[here, cols].astype(f32)).astype(low)
            slope_ref[here, cols] = gate_low
            sums_ref[8 + piece : 9 + piece, :] += jnp.sum(gate_low.astype(f32), 0, keepdims=True)
            r2_ref[here, :] += dnt(gate_low, block_of(gs_ref.at[half], slice(base, base + width)))

        loop(rows // 256, gate_back)
        share_block(dnn(nflip_ref[...], slope_ref[:, cols]), half)

    for piece in (0, 2, 1, 3):
        down_grad(piece)
    for piece in (0, 2, 1, 3):
        gate_pull(piece)

    def middle(index):
        here = span(index, 256)
        grad = r2_ref[here, :]
        unit, spread = row_norm(r1_ref[here, :])
        sums_ref[3:4, :] += jnp.sum(grad * unit, 0, keepdims=True)
        sums_ref[4:5, :] += jnp.sum(grad, 0, keepdims=True)
        back = norm_pull(grad, unit, spread, vec_ref[3:4, :])
        r1_ref[here, :] = back
        back_low = back.astype(low)
        sums_ref[2:3, :] += jnp.sum(back_low.astype(f32), 0, keepdims=True)
        flip_ref[:, here] = flip(back_low)
        for half in range(2):
            cols = slice(half * part, (half + 1) * part)
            ga_ref[here, cols] = dnn(
                back_low, block_of(gs_ref.at[half], slice(3 * part, 4 * part))
            ).astype(low)

    loop(rows // 256, middle)
    for half in range(2):
        share_block(dnn(flip_ref[...], a_ref[:, half * part : (half + 1) * part]), half)
    for sem, peer in (
        [(free_y, ways["y"]), (free_x, ways["x"]), (free_twin, ways["twin"])]
        + [(free_z, peer) for peer in ways["z"]]
    ):
        pl.semaphore_signal(sem, inc=1, device_id=peer, device_id_type=MESH)
    wa_ref = gs_ref.at[:, :, :, :, :, pl.ds(3 * part, 3 * part)]
    wa_back = keep(wa_hbm, wa_ref)
    next(sums)
    for number in (8, 9):
        settle(number)
    pl.semaphore_wait(free_y, 1)
    pairs = width // LOG_PAIR

    def lanes_at(base, pair):
        return pl.ds(pl.multiple_of(base + pair * LOG_PAIR, LOG_PAIR), LOG_PAIR)

    def swap(which, pair):
        return remote(
            u_ref.at[:, lanes_at((2 * which + 1 - y) * width, pair)],
            slope_ref.at[:, lanes_at(which * width, pair)],
            ksends, krecvs, (which, pair), ways["y"],
        )

    def one_pair(pair, carry):
        cols = lanes_at(0, pair)
        query, grad_mixed = q_ref[:, cols], ga_ref[:, cols]
        sides = pair_back_rows(query, grad_mixed, a_ref[:, cols], log_ref[pair])
        grad_query = None
        for half in range(2):
            here = slice(half * rows, (half + 1) * rows)
            term, *both = pair_back_keys(
                query, grad_mixed, sides, k_ref[here, cols], v_ref[here, cols], key_bias()[here]
            )
            grad_query = term if grad_query is None else grad_query + term
            for which, value in enumerate(both):
                u_ref[:, lanes_at((2 * which + half) * width, pair)] = value.astype(low)
        normed_ref[:, cols] = (grad_query.T * HDIM**-0.5).astype(low)
        swap(0, pair).start()
        swap(1, pair).start()
        return carry

    for first in range(0, pairs, 2):
        lax.fori_loop(first, first + 2, one_pair, 0)
        next(sums, None)
    flip_ref[...] = flip(x_ref[own, :])
    wa_back.wait()

    def finish(index, grad):
        for half in range(2):
            if index == 0 and half == 0:
                pl.semaphore_wait(free_twin, 1)
            share_block(dnn(flip_ref[...], grad[:, half * part : (half + 1) * part]), half)
        for half in range(2):
            r1_ref[...] += dnt(
                grad[:, half * part : (half + 1) * part],
                block_of(
                    gs_ref.at[half], slice((3 + index) * part, (4 + index) * part)
                ),
            )

    finish(0, normed_ref)
    next(sums, None)
    for which in range(2):

        def landed(pair, carry, which=which):
            swap(which, pair).wait()
            return carry

        lax.fori_loop(0, pairs, landed, 0)
        mine_now = u_ref[:, pl.ds(pl.multiple_of((2 * which + y) * width, LOG_PAIR), width)]
        total = mine_now.astype(f32) + slope_ref[:, which * width : (which + 1) * width].astype(f32)
        grad = slope_ref.at[:, pl.ds((2 + which) * width, width)]
        grad[...] = total.astype(low)
        finish(1 + which, grad)
    for number in (14, 15):
        settle(number)
    keep(r1_ref, input_hbm.at[own])
    ga_ref[...] = r1_ref[...].astype(low)
    joins = [
        remote(
            ga_ref.at[:, pl.ds(half * part, part)], tk_ref.at[pl.ds(half * rows, rows)],
            ksends, krecvs, (2, 1 + half), ways["y"],
        )
        for half in range(2)
    ]
    for join in joins:
        join.start()
    line = lax.broadcasted_iota(jnp.int32, sums_ref.shape, 0)
    vector_grad = jnp.where(
        line == 0,
        jnp.sum(normed_ref[...].astype(f32), 0, keepdims=True),
        jnp.where(
            line == 1,
            jnp.sum(slope_ref[:, 3 * width : 4 * width].astype(f32), 0, keepdims=True),
            sums_ref[...],
        ),
    )
    vector_grad = jnp.concatenate(
        [vector_grad, jnp.zeros((16 - vector_grad.shape[0], width), f32)], 0
    )
    vector_total = []
    vector_steps = shared_steps(
        vector_grad, vector_total,
        lambda i: part_ref.at[0, pl.ds(16 * i, 16)],
        lambda i: come_ref.at[0, pl.ds(16 * i, 16)],
        vsends, vrecvs,
    )
    for unused in sums:
        next(vector_steps, None)
    for unused in vector_steps:
        pass
    vector_ref[...] = vector_total[0][: vector_ref.shape[0]]
    for half in range(2):
        joins[half].wait()
        r2_ref[:, half * part : (half + 1) * part] = tk_ref[
            half * rows : (half + 1) * rows, :
        ].astype(f32)
    other = pl.ds(pl.multiple_of((1 - y) * rows, rows), rows)
    keep(r2_ref, input_hbm.at[other])
    for copy in kept:
        if copy is not cot_copy and copy is not wa_copy and copy is not wa_back:
            copy.wait()
    for copy in sum_sent:
        copy.wait_send()
    share.wait_send()
    rest = student_hbm.at[other]
    remote(rest, rest, ksends, krecvs, (2, 0), ways["y"]).wait_recv()


def first_call(x, tx, cot, vec, tvec, lengths, masked, weights, teacher, number):
    length, width = x.shape
    rows, part, hidden = length // 2, width // 2, 4 * width
    lines = weights[0].shape[1]
    wide = 4 * part + 2 * weights[2].shape[1]
    chunks = tuple(
        [(0, 0, part), (0, part, 2 * part), (1, 0, width), (0, 2 * part, 3 * part)]
        + [(1, width, 2 * width), (0, 3 * part, 4 * part), (1, 2 * width, 3 * width)]
        + [(0, 2 * width, 3 * width), (1, 3 * width, 4 * width), (0, 3 * width, 4 * width)]
        + [(1, 4 * width, 5 * width), (0, 4 * width, 5 * width), (1, 5 * width, 6 * width)]
        + [(0, 5 * width, 6 * width)]
    )
    count = len(chunks)
    listed = masked.shape[1]
    pairs = width // LOG_PAIR
    sem = pltpu.SemaphoreType.DMA
    vm = pltpu.VMEM
    return pl.pallas_call(
        partial(first_kernel, chunks),
        name="gather_forward",
        out_shape=[
            shape_of(2, 4, 2, 2, lines, 3 * part, kind=low),
            shape_of(length, width),
            shape_of(length, width, kind=low),
            shape_of(lines, wide),
            shape_of(*vec.shape),
        ],
        in_specs=[VMEM_SPEC] * 2 + [ANY_SPEC] + [VMEM_SPEC] * 13,
        out_specs=[ANY_SPEC] * 3 + [VMEM_SPEC] * 2,
        scratch_shapes=[
            vm(vec.shape, f32),
            vm((2, 4, 2, 2, lines, wide), low),
            vm((4, 2, 2, lines, wide), low),
            vm((lines, wide), low),
            vm((lines, wide), low),
            vm((rows, width), low),
            vm((length, width), low),
            vm((length, width), low),
            vm((rows, width), low),
            vm((pairs, rows, LOG_PAIR), f32),
            vm((length, part), low),
            vm((length, part), low),
            vm((2, listed, width), f32),
            vm((2, listed, width), f32),
            vm((rows, width), f32),
            vm((rows, width), low),
            vm((rows, hidden), low),
            vm((rows, hidden), low),
            vm((rows, width), f32),
            vm((rows, width), low),
            vm((width, rows), low),
            vm((width, rows), low),
            vm((rows, width), low),
            vm((2, 4, 2, lines, wide - 3 * part), low),
            vm((3, 2, lines, wide - 3 * part), low),
            vm((2, lines, wide), low),
            vm((lines, wide), low),
            sem((count,)), sem((count, 3)), sem((count, 3)), sem((count, 7)), sem((count, 7)),
            sem((2,)), sem((2,)), sem((16,)), sem((16,)), sem((8,)),
            sem((8, 2)), sem((8, 2)), sem((8, 3)), sem((8, 3)), sem((3, pairs)), sem((3, pairs)),
            sem((6,)), sem((6,)),
            pltpu.SemaphoreType.REGULAR, pltpu.SemaphoreType.REGULAR,
            pltpu.SemaphoreType.REGULAR, pltpu.SemaphoreType.REGULAR,
        ],
        compiler_params=pltpu.CompilerParams(
            vmem_limit_bytes=FIRST_LIMIT, collective_id=number, has_side_effects=True
        ),
    )(x, tx, cot, vec, tvec, lengths, masked, masked.T, *weights, *teacher)


def matrices(grad_ref, part, groups):
    attn, out, up, down = range(4)
    plan = [(0, attn, 0), (1, attn, 1), (2, attn, 2), (3, out, None), (4, up, None), (5, down, None)]
    at = 0
    for index, which, slot in plan:
        refs = [group[which] if slot is None else group[which].at[slot] for group in groups]
        size = refs[0].shape[-1]
        yield index, grad_ref[:, at : at + size], refs
        at += size


def norm_kernel(grad_ref, *rest):
    weights, firsts, seconds = rest[0:4], rest[4:8], rest[8:12]
    norm_o, mine_ref, come_ref, sends, recvs = rest[12:]
    at, y, z, x, core = place()
    ways = near()
    greet([ways["twin"], ways["x"], ways["y"]] + ways["z"])
    lane = lane_index((8, LOG_PAIR))
    row = lax.broadcasted_iota(jnp.int32, (8, LOG_PAIR), 0)
    squares = jnp.zeros((8, LOG_PAIR), f32)
    for index, grad, (w, first, second) in matrices(grad_ref, 0, (weights, firsts, seconds)):
        unused, unused_too, step = adam_step(grad, first[...], second[...])
        for line, value in ((0, w[...]), (1, step + decay_rate * w[...])):
            total = jnp.sum(jnp.sum(value * value, -1, keepdims=True), 0, keepdims=True)
            squares = jnp.where((row == line) & (lane == index), total, squares)
    result = []
    for unused in shared_steps(
        squares, result, lambda i: mine_ref.at[i], lambda i: come_ref.at[i], sends, recvs
    ):
        pass
    norms = jnp.sqrt(result[0])
    norm_o[...] = jnp.where(row == 2, norms[0:1, :] / norms[1:2, :], norms)


def update_kernel(grad_ref, norm_ref, total_ref, vec_ref, vm_ref, vs_ref, *rest):
    groups = [rest[i : i + 4] for i in range(0, 24, 4)]
    vm_o, vs_o, vec_o = rest[24:]
    for index, grad, refs in matrices(grad_ref, 0, groups):
        w, first, second, w_o, first_o, second_o = refs
        first_new, second_new, step = adam_step(grad, first[...], second[...])
        first_o[...] = first_new
        second_o[...] = second_new
        weight = w[...]
        ratio = norm_ref[2:3, index : index + 1]
        w_o[...] = weight - matrix_rate * ratio * (step + decay_rate * weight)
    vm_new, vs_new, step = adam_step(total_ref[...], vm_ref[...], vs_ref[...])
    vm_o[...] = vm_new
    vs_o[...] = vs_new
    vec_o[...] = vec_ref[...] - vector_rate * step


def norm_call(grad, weights, firsts, seconds, number):
    sem = pltpu.SemaphoreType.DMA
    return pl.pallas_call(
        norm_kernel,
        name="norms",
        out_shape=shape_of(8, LOG_PAIR),
        in_specs=[VMEM_SPEC] * 13,
        out_specs=VMEM_SPEC,
        scratch_shapes=[
            pltpu.VMEM((4, 8, LOG_PAIR), f32), pltpu.VMEM((6, 8, LOG_PAIR), f32), sem((6,)), sem((6,))
        ],
        compiler_params=pltpu.CompilerParams(
            vmem_limit_bytes=LIMIT, collective_id=number, has_side_effects=True
        ),
    )(grad, *weights, *firsts, *seconds)


def update_call(grad, norms, total, vec, vm, vs, weights, firsts, seconds):
    outs = [shape_of(*value.shape) for group in (weights, firsts, seconds) for value in group]
    outs += [shape_of(*vec.shape)] * 3
    return pl.pallas_call(
        update_kernel,
        name="update",
        out_shape=outs,
        in_specs=[VMEM_SPEC] * 18,
        out_specs=[VMEM_SPEC] * len(outs),
        compiler_params=pltpu.CompilerParams(vmem_limit_bytes=LIMIT),
    )(grad, norms, total, vec, vm, vs, *weights, *firsts, *seconds)


def split_kernels(
    tokens,
    teacher_tokens,
    cotangent,
    lengths,
    masked,
    attn_weight,
    out_weight,
    up_weight,
    down_weight,
    attn_first,
    out_first,
    up_first,
    down_first,
    attn_second,
    out_second,
    up_second,
    down_second,
    vectors,
    vector_first,
    vector_second,
    teacher_attn,
    teacher_out,
    teacher_up,
    teacher_down,
    teacher_vectors,
):
    width = tokens.shape[2]

    def upright(group):
        return (group[0], group[1].T, group[2], group[3].T)

    weights = upright((attn_weight, out_weight, up_weight, down_weight))
    vec = vectors.reshape(-1, width)
    spans = lengths.reshape(1, 1)
    unused_wa, input_grad, student, grad, total = first_call(
        tokens[0],
        teacher_tokens[0],
        cotangent[0],
        vec,
        teacher_vectors.astype(f32).reshape(-1, width),
        spans,
        masked,
        weights,
        upright((teacher_attn, teacher_out, teacher_up, teacher_down)),
        0,
    )
    states = (
        weights,
        upright((attn_first, out_first, up_first, down_first)),
        upright((attn_second, out_second, up_second, down_second)),
    )
    norms = norm_call(grad, *states, 1)
    outs = update_call(
        grad, norms, total, vec,
        vector_first.reshape(-1, width),
        vector_second.reshape(-1, width),
        *states,
    )
    return (
        student[None],
        input_grad[None],
        *upright(outs[0:4]),
        *upright(outs[4:8]),
        *upright(outs[8:12]),
        *(value.reshape(-1) for value in outs[12:15]),
        norms[:2, :6],
        norms[2, :6],
    )


def solution(mesh):
    local = split_kernels if dict(mesh.shape) == {"dp": 16, "mp": 2} else split_rows
    return jax.shard_map(
        local,
        mesh=mesh,
        in_specs=(
            P("dp", None, None),
            P("dp", None, None),
            P("dp", None, None),
            P("dp"),
            P("dp", None),
            P(None, "dp", "mp"),
            P("mp", "dp"),
            P("dp", "mp"),
            P("mp", "dp"),
            P(None, "dp", "mp"),
            P("mp", "dp"),
            P("dp", "mp"),
            P("mp", "dp"),
            P(None, "dp", "mp"),
            P("mp", "dp"),
            P("dp", "mp"),
            P("mp", "dp"),
            P(),
            P(),
            P(),
            P(None, "dp", "mp"),
            P("mp", "dp"),
            P("dp", "mp"),
            P("mp", "dp"),
            P(),
        ),
        out_specs=(
            P("dp", None, None),
            P("dp", None, None),
            P(None, "dp", "mp"),
            P("mp", "dp"),
            P("dp", "mp"),
            P("mp", "dp"),
            P(None, "dp", "mp"),
            P("mp", "dp"),
            P("dp", "mp"),
            P("mp", "dp"),
            P(None, "dp", "mp"),
            P("mp", "dp"),
            P("dp", "mp"),
            P("mp", "dp"),
            P(),
            P(),
            P(),
            P(),
            P(),
        ),
        check_vma=False,
    )
```

```python
from functools import partial

import jax
import jax.numpy as jnp
from jax import lax
from jax.experimental import pallas as pl
from jax.experimental.pallas import tpu as pltpu
from jax.sharding import PartitionSpec as P

HDIM = 64
STEP = 5


beta_one = 0.9
beta_two = 0.999
adam_eps = 1e-06
decay_rate = 0.01
matrix_rate = 0.3
vector_rate = 0.2
cosine_weight = 32.0
cosine_eps = 1e-06
layer_eps = 1e-12
masked_score = -1e30


def layer_norm(row_values, gain_vec, shift_vec):
    center = row_values - jnp.mean(row_values, -1, keepdims=True)
    spread = jnp.mean(center * center, -1, keepdims=True)
    return center * lax.rsqrt(spread + layer_eps) * gain_vec + shift_vec


def vector_parts(packed, model_width):
    pieces = [
        packed[position * model_width : (position + 1) * model_width] for position in range(8)
    ]
    return pieces + [packed[8 * model_width :]]


def head_scores(query, key_rows, visible):
    scale_factor = query.shape[-1] ** (-0.5)
    scores = (
        jnp.einsum("sqe,ske->sqk", query, key_rows, preferred_element_type=jnp.float32)
        * scale_factor
    )
    return jnp.where(visible[:, None, :], scores, masked_score)


def head_forward(query, key_rows, value_rows, visible):
    scores = head_scores(query, key_rows, visible)
    row_peak = jnp.max(scores, -1, keepdims=True)
    exponent = jnp.exp(scores - row_peak)
    row_total = jnp.sum(exponent, -1, keepdims=True)
    weights_low = (exponent / row_total).astype(jnp.bfloat16)
    mixed = jnp.einsum("sqk,ske->sqe", weights_low, value_rows, preferred_element_type=jnp.float32)
    return (mixed.astype(jnp.bfloat16), (row_peak + jnp.log(row_total))[..., 0])


def adam_moments(grad_now, first_old, second_old):
    first_new = beta_one * first_old + (1.0 - beta_one) * grad_now
    second_new = beta_two * second_old + (1.0 - beta_two) * grad_now * grad_now
    step_now = (
        first_new
        / (1.0 - beta_one**STEP)
        / (jnp.sqrt(second_new / (1.0 - beta_two**STEP)) + adam_eps)
    )
    return (first_new, second_new, step_now)


def matrix_squares(attn_w, out_w, up_w, down_w):
    return jnp.concatenate(
        [
            jnp.sum(attn_w * attn_w, axis=(1, 2)),
            jnp.stack([jnp.sum(out_w * out_w), jnp.sum(up_w * up_w), jnp.sum(down_w * down_w)]),
        ]
    )


def shard_pack(attn_w, out_w, up_w, down_w):
    return jnp.concatenate(
        [attn_w[0], attn_w[1], attn_w[2], out_w.T, up_w, down_w.T], axis=1
    )


def cosine_pull(rows, places, aimed, row_start):
    row_count = rows.shape[0]
    local_at = places - row_start
    here = (local_at >= 0) & (local_at < row_count)
    picked = rows[jnp.clip(local_at, 0, row_count - 1)]
    inner = jnp.sum(picked * aimed, -1, keepdims=True)
    square_own = jnp.sum(picked * picked, -1, keepdims=True) + cosine_eps
    square_aim = jnp.sum(aimed * aimed, -1, keepdims=True) + cosine_eps
    inverse = lax.rsqrt(square_own) * lax.rsqrt(square_aim)
    pull = -cosine_weight * (aimed * inverse - picked * (inner * inverse / square_own))
    pull = jnp.where(here[:, None], pull, 0.0)
    return jnp.zeros_like(rows).at[jnp.clip(local_at, 0, row_count - 1)].add(pull)


def heads_of(flat):
    return flat.reshape(flat.shape[0], flat.shape[1] // HDIM, HDIM).transpose(1, 0, 2)


def flat_of(split):
    return split.transpose(1, 0, 2).reshape(split.shape[1], -1)


def dot32(left, right):
    return jnp.dot(left, right, preferred_element_type=jnp.float32)


def dot_nt(left, right):
    return lax.dot_general(
        left, right, (((1,), (1,)), ((), ())), preferred_element_type=jnp.float32
    )


def dot_tn(left, right):
    return lax.dot_general(
        left, right, (((0,), (0,)), ((), ())), preferred_element_type=jnp.float32
    )


def split_rows(
    tokens,
    teacher_tokens,
    cotangent,
    lengths,
    masked,
    attn_weight,
    out_weight,
    up_weight,
    down_weight,
    attn_first,
    out_first,
    up_first,
    down_first,
    attn_second,
    out_second,
    up_second,
    down_second,
    vectors,
    vector_first,
    vector_second,
    teacher_attn,
    teacher_out,
    teacher_up,
    teacher_down,
    teacher_vectors,
):
    low = jnp.bfloat16
    everyone = ("dp", "mp")
    shard_at = lax.axis_index("mp")
    halves = lax.axis_size("mp")
    seq_count, length, width = tokens.shape
    rows = length // halves
    row_start = shard_at * rows
    part = attn_weight.shape[2]
    units = up_weight.shape[1]
    cuts = [0, part, 2 * part, 3 * part, 4 * part, 4 * part + units, 4 * part + 2 * units]
    visible = (jnp.arange(length) < lengths[0])[None, None, :]
    places = masked[0]

    student = lax.all_gather(
        shard_pack(attn_weight, out_weight, up_weight, down_weight).astype(low),
        ("mp", "dp"),
        axis=0,
        tiled=True,
    ).reshape(halves, width, cuts[6])
    teacher = lax.all_gather(
        shard_pack(teacher_attn, teacher_out, teacher_up, teacher_down),
        "dp",
        axis=0,
        tiled=True,
    )

    def whole(index):
        return jnp.concatenate(
            [student[half, :, cuts[index] : cuts[index + 1]] for half in range(halves)], axis=1
        )

    teacher_parts = vector_parts(teacher_vectors.astype(jnp.float32), width)
    bias_q = lax.dynamic_slice_in_dim(teacher_parts[0], shard_at * part, part)
    bias_v = lax.dynamic_slice_in_dim(teacher_parts[1], shard_at * part, part)
    bias_up = lax.dynamic_slice_in_dim(teacher_parts[8], shard_at * units, units)
    teacher_rows = teacher_tokens[0]
    listed = teacher_rows[places]
    t_query = (dot32(listed, teacher[:, : cuts[1]]) + bias_q).astype(low)
    t_keys = dot32(teacher_rows, teacher[:, cuts[1] : cuts[2]]).astype(low)
    t_values = (dot32(teacher_rows, teacher[:, cuts[2] : cuts[3]]) + bias_v).astype(low)
    t_mixed, unused_log = head_forward(
        heads_of(t_query), heads_of(t_keys), heads_of(t_values), visible[0]
    )
    t_branch = lax.psum(dot_nt(flat_of(t_mixed), teacher[:, cuts[3] : cuts[4]]), "mp")
    t_first = listed.astype(jnp.float32) + t_branch + teacher_parts[2]
    t_normed = layer_norm(t_first, teacher_parts[3], teacher_parts[4])
    t_gate = dot32(t_normed.astype(low), teacher[:, cuts[4] : cuts[5]]) + bias_up
    t_act = jax.nn.gelu(t_gate, approximate=False).astype(low)
    t_feed = lax.psum(dot_nt(t_act, teacher[:, cuts[5] : cuts[6]]), "mp")
    aimed = layer_norm(t_normed + t_feed + teacher_parts[5], teacher_parts[6], teacher_parts[7])

    pieces = vector_parts(vectors, width)
    all_rows = tokens[0]
    own_rows = lax.dynamic_slice_in_dim(all_rows, row_start, rows, 0)
    w_q, w_k, w_v, w_out, w_up, w_down = [whole(index) for index in range(6)]
    query = heads_of((dot32(own_rows, w_q) + pieces[0]).astype(low))
    keys = heads_of(dot32(all_rows, w_k).astype(low))
    values = heads_of((dot32(all_rows, w_v) + pieces[1]).astype(low))
    mixed, log_total = lax.map(
        lambda g: jax.tree.map(
            lambda v: v[0], head_forward(g[0][None], g[1][None], g[2][None], visible[0])
        ),
        (query, keys, values),
    )
    attended = flat_of(mixed)
    first_sum = own_rows.astype(jnp.float32) + dot_nt(attended, w_out) + pieces[2]
    normed = layer_norm(first_sum, pieces[3], pieces[4])
    normed_low = normed.astype(low)
    gate_in = dot32(normed_low, w_up) + pieces[8]
    activated = jax.nn.gelu(gate_in, approximate=False).astype(low)
    second_sum = normed + dot_nt(activated, w_down) + pieces[5]
    outcome = layer_norm(second_sum, pieces[6], pieces[7])
    student_out = lax.all_gather(outcome.astype(low), "mp", axis=0, tiled=True)[None]

    own_cotangent = lax.dynamic_slice_in_dim(cotangent[0], row_start, rows, 0)
    grad_top = own_cotangent.astype(jnp.float32) + cosine_pull(outcome, places, aimed, row_start)
    unused_top, pull_top = jax.vjp(layer_norm, second_sum, pieces[6], pieces[7])
    grad_second, grad_gain_two, grad_shift_two = pull_top(grad_top)
    feed_low = grad_second.astype(low)
    grad_down = dot_tn(feed_low, activated)
    grad_act = dot32(feed_low, w_down)
    unused_gelu, pull_gelu = jax.vjp(partial(jax.nn.gelu, approximate=False), gate_in)
    (grad_gate,) = pull_gelu(grad_act)
    gate_low = grad_gate.astype(low)
    grad_up = dot_tn(normed_low, gate_low)
    grad_normed = grad_second + dot_nt(gate_low, w_up)
    unused_mid, pull_mid = jax.vjp(layer_norm, first_sum, pieces[3], pieces[4])
    grad_first, grad_gain_one, grad_shift_one = pull_mid(grad_normed)
    branch_low = grad_first.astype(low)
    grad_out = dot_tn(branch_low, attended)
    grad_heads = heads_of(dot32(branch_low, w_out).astype(low))

    def one_head(g):
        query_h, keys_h, values_h, mixed_h, log_h = g
        scale_factor = HDIM**-0.5
        scores = jnp.where(visible[0], dot_nt(query_h, keys_h) * scale_factor, masked_score)
        probs = jnp.exp(scores - log_h[:, None])
        grad_probs = dot_nt(mixed_h, values_h)
        inner = jnp.sum(probs * grad_probs, -1, keepdims=True)
        grad_scores = (probs * (grad_probs - inner)).astype(low)
        return (
            (dot32(grad_scores, keys_h) * scale_factor).astype(low),
            (dot_tn(grad_scores, query_h) * scale_factor).astype(low),
            dot_tn(probs.astype(low), mixed_h).astype(low),
        )

    grad_query, grad_keys, grad_values = lax.map(
        one_head, (query, keys, values, grad_heads, log_total)
    )
    grad_query = flat_of(grad_query)

    def row_sum(term):
        other = lax.dynamic_slice_in_dim(term, (1 - shard_at) * rows, rows, 0)
        mine = lax.dynamic_slice_in_dim(term, row_start, rows, 0)
        came = lax.ppermute(other, "mp", [(0, 1), (1, 0)])
        return (mine.astype(jnp.float32) + came.astype(jnp.float32)).astype(low)

    grad_keys = row_sum(flat_of(grad_keys))
    grad_values = row_sum(flat_of(grad_values))
    grad_q = dot_tn(own_rows, grad_query)
    grad_k = dot_tn(own_rows, grad_keys)
    grad_v = dot_tn(own_rows, grad_values)
    input_own = (
        grad_first + dot_nt(grad_query, w_q) + dot_nt(grad_keys, w_k) + dot_nt(grad_values, w_v)
    )
    input_grad = lax.all_gather(input_own, "mp", axis=0, tiled=True)[None]

    def half_of(matrix, half):
        span = matrix.shape[1] // halves
        return matrix[:, half * span : (half + 1) * span]

    grads = [grad_q, grad_k, grad_v, grad_out, grad_up, grad_down]
    packed_grad = jnp.concatenate(
        [
            jnp.concatenate([half_of(g, half) for g in grads], axis=1).astype(low)
            for half in range(halves)
        ],
        axis=0,
    )
    summed = lax.psum_scatter(
        packed_grad, ("mp", "dp"), scatter_dimension=0, tiled=True
    ).astype(jnp.float32)
    summed_attn = jnp.stack([summed[:, cuts[i] : cuts[i + 1]] for i in range(3)])
    summed_out = summed[:, cuts[3] : cuts[4]].T
    summed_up = summed[:, cuts[4] : cuts[5]]
    summed_down = summed[:, cuts[5] : cuts[6]].T

    vector_grad = jnp.concatenate(
        [
            jnp.sum(grad_query.astype(jnp.float32), 0),
            jnp.sum(grad_values.astype(jnp.float32), 0),
            jnp.sum(branch_low.astype(jnp.float32), 0),
            grad_gain_one,
            grad_shift_one,
            jnp.sum(feed_low.astype(jnp.float32), 0),
            grad_gain_two,
            grad_shift_two,
            jnp.sum(gate_low.astype(jnp.float32), 0),
        ]
    )
    return (student_out, input_grad) + lamb_update(
        (summed_attn, summed_out, summed_up, summed_down),
        (attn_weight, out_weight, up_weight, down_weight),
        (attn_first, out_first, up_first, down_first),
        (attn_second, out_second, up_second, down_second),
        vector_grad,
        vectors,
        vector_first,
        vector_second,
    )


def lamb_update(grads, weights, firsts, seconds, vector_grad, vectors, vector_first, vector_second):
    moments, squares, steps = [], [], []
    for grad_now, weight, first_old, second_old in zip(grads, weights, firsts, seconds):
        first_new, second_new, step_now = adam_moments(grad_now, first_old, second_old)
        moments.append(first_new)
        squares.append(second_new)
        steps.append(step_now + decay_rate * weight)
    weight_total, update_total, vector_total = lax.psum(
        (matrix_squares(*weights), matrix_squares(*steps), vector_grad), ("dp", "mp")
    )
    weight_norms = jnp.sqrt(weight_total)
    update_norms = jnp.sqrt(update_total)
    trust_ratio = weight_norms / update_norms
    ratios = [trust_ratio[0:3][:, None, None], trust_ratio[3], trust_ratio[4], trust_ratio[5]]
    updated = [
        weight - matrix_rate * ratio * step for weight, ratio, step in zip(weights, ratios, steps)
    ]
    vector_moment, vector_square, step_vector = adam_moments(
        vector_total, vector_first, vector_second
    )
    vector_updated = vectors - vector_rate * step_vector
    return (
        *updated,
        *moments,
        *squares,
        vector_moment,
        vector_square,
        vector_updated,
        jnp.stack([weight_norms, update_norms]),
        trust_ratio,
    )


LOG_PAIR = 128
MESH = pl.DeviceIdType.MESH
low = jnp.bfloat16
f32 = jnp.float32
VMEM_SPEC = pl.BlockSpec(memory_space=pltpu.VMEM)
ANY_SPEC = pl.BlockSpec(memory_space=pl.ANY)
AHEAD = 2
LEAD = 1
GATHER_ORDER = ((0, 0), (0, 1), (0, 2), (1, 0), (1, 1), (0, 3), (1, 2))
GATHER_ORDER += ((0, 4), (1, 3), (0, 5), (1, 4), (1, 5), (0, 6), (0, 7))
GATHER_OVER_X = ((0, 7),)
FIRST_LIMIT = 64 * 2**20
LIMIT = 60 * 2**20


def dnn(left, right):
    return jnp.dot(left, right, preferred_element_type=f32)


def dnt(left, right):
    return lax.dot_general(left, right, (((1,), (1,)), ((), ())), preferred_element_type=f32)


def lane_index(shape):
    return lax.broadcasted_iota(jnp.int32, shape, 1)


def split_three(value):
    top = value.astype(low).astype(f32)
    rest = value - top
    middle = rest.astype(low).astype(f32)
    return (top, middle, rest - middle)


def flip(value):
    return value.astype(f32).T.astype(low)


def place():
    at = lax.axis_index("dp")
    return (at, lax.axis_index("mp"), at // 4, (at // 2) % 2, at % 2)


def near():
    at, y, z, x, core = place()
    return dict(
        twin=(at + 1 - 2 * core, y),
        x=(at + 2 - 4 * x, y),
        y=(at, 1 - y),
        z=[(((z + step) % 4) * 4 + 2 * x + core, y) for step in (1, 2, 3)],
    )


def greet(peers):
    sem = pltpu.get_barrier_semaphore()
    for peer in peers:
        pl.semaphore_signal(sem, inc=1, device_id=peer, device_id_type=MESH)
    return lambda: pl.semaphore_wait(sem, len(peers))


def vector_rows(flat_ref, rows_ref):
    width = rows_ref.shape[1]
    for index in range(rows_ref.shape[0]):
        row = flat_ref[pl.ds(index * width, width)].reshape(1, width)
        rows_ref[index : index + 1, :] = row.astype(f32)


def remote(src, dst, sends, recvs, at, peer):
    return pltpu.make_async_remote_copy(
        src_ref=src,
        dst_ref=dst,
        send_sem=sends.at[at],
        recv_sem=recvs.at[at],
        device_id=peer,
        device_id_type=MESH,
    )


def row_norm(rows):
    center = rows - jnp.mean(rows, -1, keepdims=True)
    scale = lax.rsqrt(jnp.mean(center * center, -1, keepdims=True) + layer_eps)
    return (center * scale, scale)


def norm_pull(grad, unit, scale, gain):
    lifted = grad * gain
    return scale * (
        lifted
        - jnp.mean(lifted, -1, keepdims=True)
        - unit * jnp.mean(lifted * unit, -1, keepdims=True)
    )


def normal_share(value):
    return 0.5 * (1.0 + lax.erf(value * 0.7071067811865476))


def pair_forward(query, keys, values, bias):
    count, span = query.shape[0], keys.shape[0]
    lane_q, lane_k = lane_index((count, LOG_PAIR)), lane_index((span, LOG_PAIR))
    outs, logs = [], []
    for head in range(2):
        spare = HDIM * (1 - head)
        keys_now = jnp.where(
            lane_k // HDIM == head,
            keys.astype(f32),
            jnp.where(lane_k == spare, bias, 0.0),
        ).astype(low)
        query_now = jnp.where(
            lane_q // HDIM == head,
            query.astype(f32),
            jnp.where(lane_q == spare, 1.0, 0.0),
        ).astype(low)
        scores = dnt(query_now, keys_now)
        peak = jnp.max(scores, -1, keepdims=True)
        exponent = jnp.exp(scores - peak)
        total = jnp.sum(exponent, -1, keepdims=True)
        outs.append(dnn((exponent * (1.0 / total)).astype(low), values))
        logs.append(peak + jnp.log(total))
    return (
        jnp.where(lane_q < HDIM, outs[0], outs[1]),
        jnp.where(lane_q < HDIM, logs[0], logs[1]),
    )


def shape_of(*dims, kind=f32):
    return jax.ShapeDtypeStruct(dims, kind)


def pair_back_rows(query, grad_mixed, mixed, logs):
    lane_q = lane_index(query.shape)
    query_wide, grad_wide = query.astype(f32), grad_mixed.astype(f32)
    product = grad_wide * mixed.astype(f32)
    sides = []
    for head in range(2):
        spare = HDIM * (1 - head)
        own_q = lane_q // HDIM == head
        inner = jnp.sum(jnp.where(own_q, product, 0.0), -1, keepdims=True)
        query_now = jnp.where(own_q, query_wide, jnp.where(lane_q == spare, 1.0, 0.0))
        grad_now = jnp.where(own_q, grad_wide, 0.0)
        for place_at, (log_term, inner_term) in enumerate(
            zip(split_three(logs[:, HDIM * head : HDIM * head + 1]), split_three(inner))
        ):
            here = lane_q == spare + 1 + place_at
            query_now = jnp.where(here, log_term, query_now)
            grad_now = jnp.where(here, inner_term, grad_now)
        sides.append((query_now.astype(low), grad_now.astype(low)))
    return sides


def pair_back_keys(query, grad_mixed, sides, keys, values, bias):
    lane_k = lane_index(keys.shape)
    keys_wide, values_wide = keys.astype(f32), values.astype(f32)
    grad_keys, grad_values, grad_query = [], [], []
    for head, (query_now, grad_now) in enumerate(sides):
        spare = HDIM * (1 - head)
        own_k = lane_k // HDIM == head
        minus = jnp.where((lane_k > spare) & (lane_k < spare + 4), -1.0, 0.0)
        keys_now = jnp.where(own_k, keys_wide, jnp.where(lane_k == spare, bias, minus)).astype(low)
        values_now = jnp.where(own_k, values_wide, minus).astype(low)
        probs = jnp.exp(dnt(keys_now, query_now))
        grad_scores = (probs * dnt(values_now, grad_now)).astype(low)
        grad_keys.append(dnn(grad_scores, query))
        grad_values.append(dnn(probs.astype(low), grad_mixed))
        flipped = keys_wide.T[HDIM * head : HDIM * (head + 1)].astype(low)
        grad_query.append(dnn(flipped, grad_scores))
    return (
        jnp.concatenate(grad_query, 0),
        jnp.where(lane_k < HDIM, grad_keys[0], grad_keys[1]),
        jnp.where(lane_k < HDIM, grad_values[0], grad_values[1]),
    )


def adam_step(grad, first, second):
    first_new = beta_one * first + (1.0 - beta_one) * grad
    second_new = beta_two * second + (1.0 - beta_two) * grad * grad
    step = (
        first_new
        / (1.0 - beta_one**STEP)
        / (jnp.sqrt(second_new / (1.0 - beta_two**STEP)) + adam_eps)
    )
    return (first_new, second_new, step)


def block_of(ref, cols):
    value = ref[:, :, :, :, cols]
    return value.reshape(-1, value.shape[-1])


def gather_steps(chunks, gs_ref, gt_ref, ps_ref, pt_ref, local_sem, zsends, zrecvs, sends, recvs, started):
    at, y, z, x, core = place()
    ways = near()

    def go(ref, chunk, kind, peer):
        copy = remote(ref, ref, sends, recvs, (chunk, kind), peer)
        copy.start()
        started.append(copy)

    def landed(ref, chunk, kind):
        remote(ref, ref, sends, recvs, (chunk, kind), ways["x"]).wait_recv()

    def shard(chunk, zz):
        which, a, b, unused = chunks[chunk]
        if which == 0:
            return gs_ref.at[y, zz, x, core, :, pl.ds(a, b - a)]
        return gt_ref.at[zz, x, core, :, pl.ds(a, b - a)]

    def column(chunk, yy, xx, cc):
        which, a, b, unused = chunks[chunk]
        if which == 0:
            return gs_ref.at[yy, :, xx, cc, :, pl.ds(a, b - a)]
        return gt_ref.at[:, xx, cc, :, pl.ds(a, b - a)]

    own = []

    def begin(k):
        which, a, b, unused = chunks[k]
        source = (ps_ref, pt_ref)[which].at[:, pl.ds(a, b - a)]
        copy = pltpu.make_async_copy(source, shard(k, z), local_sem.at[k])
        copy.start()
        own.append(copy)
        for step in range(3):
            copy = remote(source, shard(k, z), zsends, zrecvs, (k, step), ways["z"][step])
            copy.start()
            started.append(copy)

    def along_z(k):
        for step in range(3):
            came = shard(k, (z + 3 - step) % 4)
            remote(came, came, zsends, zrecvs, (k, step), ways["x"]).wait_recv()
        own[k].wait()
        go(column(k, y, x, core), k, 0, ways["x"])
        if chunks[k][0] == 0:
            go(column(k, y, x, core), k, 1, ways["y"])
        go(column(k, y, x, core), k, 2, ways["twin"])

    def from_sides(k):
        landed(column(k, y, 1 - x, core), k, 0)
        if chunks[k][0] == 0 and not chunks[k][3]:
            go(column(k, y, 1 - x, core), k, 3, ways["y"])
        go(column(k, y, 1 - x, core), k, 4, ways["twin"])
        if chunks[k][0] == 0:
            landed(column(k, 1 - y, x, core), k, 1)
            if chunks[k][3]:
                go(column(k, 1 - y, x, core), k, 3, ways["x"])
            go(column(k, 1 - y, x, core), k, 5, ways["twin"])

    def last(k):
        if chunks[k][0] == 0:
            landed(column(k, 1 - y, 1 - x, core), k, 3)
            go(column(k, 1 - y, 1 - x, core), k, 6, ways["twin"])

    def whole(k):
        landed(column(k, y, x, 1 - core), k, 2)
        landed(column(k, y, 1 - x, 1 - core), k, 4)
        if chunks[k][0] == 0:
            landed(column(k, 1 - y, x, 1 - core), k, 5)
            landed(column(k, 1 - y, 1 - x, 1 - core), k, 6)

    count = len(chunks)
    for k in range(AHEAD + LEAD):
        begin(k)
    for k in range(LEAD):
        along_z(k)
    for slot in range(count + 2):
        if slot + LEAD + AHEAD < count:
            begin(slot + LEAD + AHEAD)
        if slot + LEAD < count:
            along_z(slot + LEAD)
        if slot < count:
            from_sides(slot)
        if 0 <= slot - 1 < count:
            last(slot - 1)
        if 0 <= slot - 2 < count:
            whole(slot - 2)
        yield max(0, slot - 1)


def sum_steps(chunks, given, ax_at, h_at, zr_at, before_x, before_z, tot_ref, own_ref, yr_ref, sends, recvs, zsends, zrecvs, started):
    at, y, z, x, core = place()
    ways = near()
    count = len(chunks)

    def span(k):
        a, b = chunks[k]
        return pl.ds(a, b - a)

    def begin(k):
        if k in before_x:
            before_x[k]()
        copy = remote(given(k, 1 - x), ax_at(k), sends, recvs, (k, 0), ways["x"])
        copy.start()
        started.append(copy)

    def over_x(k):
        remote(ax_at(k), ax_at(k), sends, recvs, (k, 0), ways["x"]).wait_recv()
        came = ax_at(k)

        def add(step, carry):
            yy, zz = step // 4, step % 4
            block = h_at(k, yy, zz)
            block[...] = (block[...].astype(f32) + came[yy, zz].astype(f32)).astype(low)
            return carry

        lax.fori_loop(0, 8, add, 0)
        if k in before_z:
            before_z[k]()
        for step in range(3):
            copy = remote(
                h_at(k, slice(None), (z + 1 + step) % 4), zr_at(k, step),
                zsends, zrecvs, (k, step), ways["z"][step],
            )
            copy.start()
            started.append(copy)

    def over_z(k):
        here = span(k)
        for step in range(3):
            came = zr_at(k, step)
            remote(came, came, zsends, zrecvs, (k, step), ways["x"]).wait_recv()
        for yy in range(2):
            total = h_at(k, yy, z)[...].astype(f32)
            for step in range(3):
                total += zr_at(k, step)[yy].astype(f32)
            tot_ref[yy, :, here] = total.astype(low)
        copy = remote(
            tot_ref.at[1 - y, :, here], yr_ref.at[:, here], sends, recvs, (k, 1), ways["y"]
        )
        copy.start()
        started.append(copy)

    def over_y(k):
        here = span(k)
        came = yr_ref.at[:, here]
        remote(came, came, sends, recvs, (k, 1), ways["y"]).wait_recv()
        own_ref[:, here] = tot_ref[y, :, here].astype(f32) + yr_ref[:, here].astype(f32)

    def steps():
        for slot in range(count + 2):
            if slot < count:
                over_x(slot)
            if 0 <= slot - 1 < count:
                over_z(slot - 1)
            if 0 <= slot - 2 < count:
                over_y(slot - 2)
            yield max(0, slot - 1)

    return begin, steps()


def shared_steps(value, result, mine_at, come_at, sends, recvs):
    at, y, z, x, core = place()
    ways = near()
    for index, way in enumerate(("twin", "x", "y")):
        mine_at(index)[...] = value
        copy = remote(mine_at(index), come_at(index), sends, recvs, index, ways[way])
        copy.start()
        yield
        copy.wait()
        value = mine_at(index)[...] + come_at(index)[...]
    mine_at(3)[...] = value
    copies = []
    for step in range(3):
        copy = remote(
            mine_at(3), come_at(3 + step), sends, recvs, 3 + step, ways["z"][step]
        )
        copy.start()
        copies.append(copy)
    yield
    for copy in copies:
        copy.wait()
    terms = [mine_at(3)[...]] + [come_at(3 + step)[...] for step in range(3)]
    total = None
    for z_from in range(4):
        term = terms[0]
        for step in range(1, 4):
            term = jnp.where((z + 4 - step) % 4 == z_from, terms[step], term)
        total = term if total is None else total + term
    result.append(total)


def first_kernel(
    chunks,
    x_hbm, tx_hbm, cot_hbm, vec_flat, tvec_flat, length_ref, places_ref,
    aw, ow, uw, dw, ta, to, tu, td,
    wa_hbm, input_hbm, student_hbm, total_ref, vector_ref,
    sums_ref, vec_ref, tvec_ref, x_ref, tx_ref, gs_ref, gt_ref, ps_ref, pt_ref, q_ref, k_ref,
    v_ref, a_ref, log_ref, tk_ref, tv_ref, part_ref, come_ref, aimed_ref, vmine_ref, vcome_ref,
    r1_ref, normed_ref, u_ref, slope_ref, r2_ref,
    cot_ref, flip_ref, nflip_ref, bflip_ref, ga_ref, one_ref, zr_ref, tot_ref, yr_ref,
    local_sem, zsends, zrecvs, sends, recvs, tsends, trecvs, gsends, grecvs, copy_sem,
    fsends, frecvs, fzsends, fzrecvs, ksends, krecvs, vsends, vrecvs,
    free_x, free_z, free_twin,
):
    at, y, z, x, core = place()
    ways = near()
    length, width = x_ref.shape
    rows = length // 2
    part = width // 2
    own = pl.ds(pl.multiple_of(y * rows, rows), rows)
    kept = []

    def keep(src, dst):
        copy = pltpu.make_async_copy(src, dst, copy_sem.at[len(kept)])
        copy.start()
        kept.append(copy)
        return copy

    met = greet([ways["twin"], ways["x"], ways["y"]] + ways["z"])
    x_copy, tx_copy = keep(x_hbm, x_ref), keep(tx_hbm, tx_ref)
    for index in range(3):
        ps_ref[:, index * part : (index + 1) * part] = aw[index].astype(low)
        pt_ref[:, index * part : (index + 1) * part] = ta[index]
    for base, source, aim in ((3 * part, ow, to), (4 * part, uw, tu), (8 * part, dw, td)):
        ps_ref[:, base : base + source.shape[1]] = source[...].astype(low)
        pt_ref[:, base : base + source.shape[1]] = aim[...]
    met()
    started = []
    steps = gather_steps(
        chunks, gs_ref, gt_ref, ps_ref, pt_ref, local_sem, zsends, zrecvs, sends, recvs, started
    )
    ready = [0]

    def tick():
        ready[0] = next(steps, len(chunks))

    def need(chunk):
        while ready[0] <= chunk:
            tick()

    cot_copy = keep(cot_hbm.at[own], cot_ref)

    def key_bias():
        row_at = lax.broadcasted_iota(jnp.int32, (length, LOG_PAIR), 0)
        return jnp.where(row_at < length_ref[0:1, 0:1], 0.0, masked_score)

    sums_ref[...] = jnp.zeros(sums_ref.shape, f32)

    def loop(count, body):
        def step(index, carry):
            body(index)
            return carry

        lax.fori_loop(0, count, step, 0)

    def span(index, block):
        if isinstance(index, int):
            return slice(index * block, (index + 1) * block)
        return pl.ds(pl.multiple_of(index * block, block), block)

    def whole(which, end):
        need(max(k for k, chunk in enumerate(chunks) if chunk[0] == which and chunk[2] <= end))

    tick()
    vector_rows(vec_flat, vec_ref)
    vector_rows(tvec_flat, tvec_ref)
    x_copy.wait()
    tx_copy.wait()
    whole(0, 3 * part)
    wa_copy = keep(gs_ref.at[:, :, :, :, :, pl.ds(0, 3 * part)], wa_hbm)

    def keys_values(index):
        here = span(index, 256)
        for half in range(2):
            cols = slice(half * part, (half + 1) * part)
            k_ref[here, cols] = dnn(
                x_ref[here, :], block_of(gs_ref.at[half], slice(part, 2 * part))
            ).astype(low)
            v_ref[here, cols] = (
                dnn(x_ref[here, :], block_of(gs_ref.at[half], slice(2 * part, 3 * part)))
                + vec_ref[1:2, cols]
            ).astype(low)

    def queries(index):
        here = span(index, 256)
        from_x = pl.ds(pl.multiple_of(y * rows + index * 256, 256), 256)
        for half in range(2):
            cols = slice(half * part, (half + 1) * part)
            value = dnn(x_ref[from_x, :], block_of(gs_ref.at[half], slice(0, part)))
            value = (value + vec_ref[0:1, cols]).astype(low).astype(f32) * HDIM**-0.5
            q_ref[here, cols] = value.astype(low)

    def attend(first):
        def one_pair(index):
            pair = first + index
            cols = pl.ds(pl.multiple_of(pair * LOG_PAIR, LOG_PAIR), LOG_PAIR)
            keys, values, bias = k_ref[:, cols], v_ref[:, cols], key_bias()
            for start in range(0, rows, 256):
                here = slice(start, start + 256)
                mixed, logs = pair_forward(q_ref[here, cols], keys, values, bias)
                a_ref[here, cols] = mixed.astype(low)
                log_ref[pair, here, :] = logs

        return one_pair

    for first in range(0, length // 256, 2):
        loop(2, lambda index, first=first: keys_values(first + index))
        tick()
    loop(rows // 256, queries)
    for pair in range(width // LOG_PAIR):
        tick()
        loop(1, attend(pair))

    whole(1, 3 * part)
    mine = pl.ds(pl.multiple_of(y * part, LOG_PAIR), part)
    count = places_ref.shape[1]

    def teacher_keys(index):
        here = span(index, 256)
        tk_ref[here, :] = dnn(tx_ref[here, :], block_of(gt_ref, slice(part, 2 * part))).astype(low)
        tv_ref[here, :] = (
            dnn(tx_ref[here, :], block_of(gt_ref, slice(2 * part, 3 * part))) + tvec_ref[1:2, mine]
        ).astype(low)

    loop(length // 256, teacher_keys)
    whole(1, 4 * part)
    diagonal = lax.broadcasted_iota(jnp.int32, (count, count), 0) == lane_index((count, count))
    places = jnp.where(diagonal, places_ref[...].astype(f32), 0.0)
    places = jnp.sum(places, -1, keepdims=True).astype(jnp.int32)
    pick = jnp.where(places == lane_index((count, length)), 1.0, 0.0).astype(low)
    listed = dnn(pick, tx_ref[...])
    query = dnn(listed.astype(low), block_of(gt_ref, slice(0, part))) + tvec_ref[0:1, mine]
    query = (query.astype(low).astype(f32) * HDIM**-0.5).astype(low)
    branch = jnp.zeros((count, width), f32)
    for pair in range(part // LOG_PAIR):
        cols = slice(pair * LOG_PAIR, (pair + 1) * LOG_PAIR)
        mixed, unused = pair_forward(query[:, cols], tk_ref[:, cols], tv_ref[:, cols], key_bias())
        a_cols = slice(3 * part + pair * LOG_PAIR, 3 * part + (pair + 1) * LOG_PAIR)
        branch += dnt(mixed.astype(low), block_of(gt_ref, a_cols))
    aimed_ref[...] = listed + branch
    part_ref[0] = branch.astype(low)
    swaps = [remote(part_ref.at[i], come_ref.at[i], tsends, trecvs, i, ways["y"]) for i in range(2)]
    swaps[0].start()

    whole(0, 4 * part)

    def project(index):
        here = span(index, 256)
        from_x = pl.ds(pl.multiple_of(y * rows + index * 256, 256), 256)
        first = x_ref[from_x, :].astype(f32) + vec_ref[2:3, :]
        for half in range(2):
            first += dnt(
                a_ref[here, half * part : (half + 1) * part],
                block_of(gs_ref.at[half], slice(3 * part, 4 * part)),
            )
        r1_ref[here, :] = first
        unit, unused = row_norm(first)
        normed = unit * vec_ref[3:4, :] + vec_ref[4:5, :]
        normed_ref[here, :] = normed.astype(low)
        nflip_ref[:, here] = flip(normed.astype(low))
        r2_ref[here, :] = normed + vec_ref[5:6, :]

    loop(rows // 256, project)

    def rise(piece):
        half, base = piece // 2, 4 * part + (piece % 2) * width

        def body(index):
            here = span(index, 256)
            cols = slice(piece * width, (piece + 1) * width)
            gate = dnn(normed_ref[here, :], block_of(gs_ref.at[half], slice(base, base + width)))
            gate += vec_ref[8 + piece : 9 + piece, :]
            share = normal_share(gate)
            u_ref[here, cols] = (gate * share).astype(low)
            slope_ref[here, cols] = (
                share + gate * (jnp.exp(-0.5 * gate * gate) * 0.3989422804014327)
            ).astype(low)

        loop(rows // 256, body)

    def fall(piece):
        half, base = piece // 2, 4 * part + (2 + piece % 2) * width

        def body(index):
            here = span(index, 256)
            r2_ref[here, :] += dnt(
                u_ref[here, piece * width : (piece + 1) * width],
                block_of(gs_ref.at[half], slice(base, base + width)),
            )

        loop(rows // 256, body)

    active = []

    def aim_rise(piece):
        base = 4 * part + piece * width
        gate = dnn(aim_normed.astype(low), block_of(gt_ref, slice(base, base + width)))
        gate += tvec_ref[pl.ds(8 + 2 * y + piece, 1), :]
        active.append((gate * normal_share(gate)).astype(low))

    def aim_fall(piece):
        base = 8 * part + piece * width
        return dnt(active[piece], block_of(gt_ref, slice(base, base + width)))

    whole(0, 6 * part)
    rise(0)
    rise(2)
    whole(1, 8 * part)
    swaps[0].wait()
    unit, unused = row_norm(aimed_ref[...] + come_ref[0].astype(f32) + tvec_ref[2:3, :])
    aim_normed = unit * tvec_ref[3:4, :] + tvec_ref[4:5, :]
    aim_rise(0)
    tick()
    aim_rise(1)
    whole(0, 8 * part)
    rise(1)
    rise(3)
    whole(0, 10 * part)
    fall(0)
    fall(2)
    whole(1, 12 * part)
    feed = aim_fall(0) + aim_fall(1)
    part_ref[1] = feed.astype(low)
    swaps[1].start()
    aimed_ref[...] = aim_normed + feed + tvec_ref[5:6, :]
    whole(0, 12 * part)
    fall(1)
    fall(3)
    swaps[1].wait()
    unit, unused = row_norm(aimed_ref[...] + come_ref[1].astype(f32))
    aimed_ref[...] = unit * tvec_ref[6:7, :] + tvec_ref[7:8, :]
    for unused in steps:
        pass
    for copy in started:
        copy.wait_send()
    wa_copy.wait()
    pl.semaphore_signal(free_x, inc=1, device_id=ways["x"], device_id_type=MESH)
    cot_copy.wait()

    def top(index):
        here = span(index, 256)
        row_at = lax.broadcasted_iota(jnp.int32, (256, places_ref.shape[1]), 0)
        pick = jnp.where(row_at + (y * rows + index * 256) == places_ref[0:1, :], 1.0, 0.0)
        times = jnp.sum(pick, -1, keepdims=True)
        aimed = jnp.dot(
            pick, aimed_ref[...], precision=lax.Precision.HIGHEST, preferred_element_type=f32
        ) / jnp.maximum(times, 1.0)
        unit, spread = row_norm(r2_ref[here, :])
        outcome = unit * vec_ref[6:7, :] + vec_ref[7:8, :]
        inner = jnp.sum(outcome * aimed, -1, keepdims=True)
        square_own = jnp.sum(outcome * outcome, -1, keepdims=True) + cosine_eps
        square_aim = jnp.sum(aimed * aimed, -1, keepdims=True) + cosine_eps
        scale = cosine_weight * times * lax.rsqrt(square_own) * lax.rsqrt(square_aim)
        grad = cot_ref[here, :].astype(f32) - scale * (aimed - outcome * (inner / square_own))
        cot_ref[here, :] = outcome.astype(low)
        sums_ref[6:7, :] += jnp.sum(grad * unit, 0, keepdims=True)
        sums_ref[7:8, :] += jnp.sum(grad, 0, keepdims=True)
        back = norm_pull(grad, unit, spread, vec_ref[6:7, :])
        r2_ref[here, :] = back
        back_low = back.astype(low)
        sums_ref[5:6, :] += jnp.sum(back_low.astype(f32), 0, keepdims=True)
        ga_ref[here, :] = back_low
        flip_ref[:, here] = flip(back_low)

    loop(rows // 256, top)
    keep(cot_ref, student_hbm.at[own])
    share = remote(cot_ref, student_hbm.at[own], ksends, krecvs, (2, 0), ways["y"])
    share.start()

    sum_sent = []
    cuts = [(i * part, (i + 1) * part) for i in (8, 9, 10, 11, 4, 5, 6, 7, 3, 0, 1, 2)]
    spared = 9
    spare_at = 6 * part

    def feed_cols(k):
        a, b = cuts[k]
        return pl.ds(a - 3 * part, b - a)

    def spare_cols(k):
        a, b = cuts[k]
        return pl.ds(spare_at + a, b - a)

    def given(k, xx):
        if k < spared:
            return one_ref.at[:, :, xx, :, feed_cols(k)]
        return gs_ref.at[:, :, xx, 0, :, spare_cols(k)]

    def ax_at(k):
        if k < spared:
            return gs_ref.at[:, :, k // 6, k // 3 % 2, :, pl.ds(k % 3 * part, part)]
        return gs_ref.at[:, :, 0, 1, :, spare_cols(k)]

    def h_at(k, yy, zz):
        return given(k, x).at[yy, zz]

    def zr_at(k, step):
        if k < spared:
            return zr_ref.at[step, :, :, feed_cols(k)]
        return gs_ref.at[:, step, 1, 1, :, spare_cols(k)]

    def wait_for(sem, amount):
        return lambda: pl.semaphore_wait(sem, amount)

    sum_begin, sums = sum_steps(
        cuts, given, ax_at, h_at, zr_at,
        {0: wait_for(free_x, 1), spared: wait_for(free_x, 1)}, {spared: wait_for(free_z, 3)},
        tot_ref, total_ref, yr_ref, fsends, frecvs, fzsends, fzrecvs, sum_sent,
    )
    blocks = []

    def share_block(value, half, k):
        number = len(blocks)
        size = value.shape[1]
        slot = pl.ds((number % 6) * width, size)
        if number >= 2:
            settle(number - 2)
        gt_ref[:, :, :, :, slot] = value.astype(low).reshape(gt_ref.shape[:4] + (size,))
        if k < spared:
            target = one_ref.at[half, :, :, :, pl.ds(cuts[k][0] - 3 * part, size)]
        else:
            target = gs_ref.at[half, :, :, 0, :, spare_cols(k)]
        copy = remote(
            gt_ref.at[:, :, 1 - core, :, slot], target, gsends, grecvs, number, ways["twin"]
        )
        copy.start()
        blocks.append((copy, target, slot, range(k, k + size // part) if number % 2 else ()))

    settled = set()

    def settle(number):
        if number in settled:
            return
        settled.add(number)
        copy, target, slot, closed = blocks[number]
        copy.wait()

        def add(zz, carry):
            target[zz] = (
                target[zz].astype(f32) + gt_ref[zz, :, core, :, slot].astype(f32)
            ).astype(low)
            return carry

        lax.fori_loop(0, 4, add, 0)
        for k in closed:
            sum_begin(k)

    def settle_all():
        for number in range(len(blocks)):
            settle(number)

    def down_grad(piece):
        cols = slice(piece * width, (piece + 1) * width)
        share_block(dnn(flip_ref[...], u_ref[:, cols]), piece // 2, 2 * (piece % 2))

    def up_grad(piece):
        cols = slice(piece * width, (piece + 1) * width)
        share_block(dnn(nflip_ref[...], slope_ref[:, cols]), piece // 2, 4 + 2 * (piece % 2))

    def gate_pull(piece):
        half, base = piece // 2, 4 * part + (piece % 2) * width
        cols = slice(piece * width, (piece + 1) * width)

        def gate_back(index):
            here = span(index, 256)
            down = block_of(gs_ref.at[half], slice(base + 2 * width, base + 3 * width))
            gate_low = (dnn(ga_ref[here, :], down) * slope_ref[here, cols].astype(f32)).astype(low)
            slope_ref[here, cols] = gate_low
            sums_ref[8 + piece : 9 + piece, :] += jnp.sum(gate_low.astype(f32), 0, keepdims=True)
            r2_ref[here, :] += dnt(gate_low, block_of(gs_ref.at[half], slice(base, base + width)))

        loop(rows // 256, gate_back)

    def middle(index):
        here = span(index, 256)
        grad = r2_ref[here, :]
        unit, spread = row_norm(r1_ref[here, :])
        sums_ref[3:4, :] += jnp.sum(grad * unit, 0, keepdims=True)
        sums_ref[4:5, :] += jnp.sum(grad, 0, keepdims=True)
        back = norm_pull(grad, unit, spread, vec_ref[3:4, :])
        r1_ref[here, :] = back
        back_low = back.astype(low)
        sums_ref[2:3, :] += jnp.sum(back_low.astype(f32), 0, keepdims=True)
        bflip_ref[:, here] = flip(back_low)
        for half in range(2):
            cols = slice(half * part, (half + 1) * part)
            ga_ref[here, cols] = dnn(
                back_low, block_of(gs_ref.at[half], slice(3 * part, 4 * part))
            ).astype(low)

    def swap(which, pair):
        source, target = ((k_ref, tk_ref), (v_ref, tv_ref))[which]
        other_rows = pl.ds(pl.multiple_of((1 - y) * rows, rows), rows)
        return remote(
            source.at[other_rows, pl.ds(pair * LOG_PAIR, LOG_PAIR)],
            target.at[pl.ds(pair // 3 * rows, rows), pl.ds(pair % 3 * LOG_PAIR, LOG_PAIR)],
            ksends, krecvs, (which, pair), ways["y"],
        )

    def one_pair(pair):
        cols = slice(pair * LOG_PAIR, (pair + 1) * LOG_PAIR)

        def body(unused):
            query, grad_mixed = q_ref[:, cols], ga_ref[:, cols]
            sides = pair_back_rows(query, grad_mixed, a_ref[:, cols], log_ref[pair])
            grad_query = None
            for half in range(2):
                here = slice(half * rows, (half + 1) * rows)
                term, grad_keys, grad_values = pair_back_keys(
                    query, grad_mixed, sides, k_ref[here, cols], v_ref[here, cols],
                    key_bias()[here],
                )
                grad_query = term if grad_query is None else grad_query + term
                k_ref[here, cols] = grad_keys.astype(low)
                v_ref[here, cols] = grad_values.astype(low)
            q_ref[:, cols] = (grad_query.T * HDIM**-0.5).astype(low)

        loop(1, body)
        swap(0, pair).start()
        swap(1, pair).start()

    down_grad(0)
    down_grad(2)
    gate_pull(0)
    settle_all()
    gate_pull(2)
    down_grad(1)
    gate_pull(1)
    next(sums)
    down_grad(3)
    gate_pull(3)
    settle_all()
    loop(rows // 256, middle)
    for sem, peer in (
        [(free_x, ways["x"]), (free_twin, ways["twin"])] + [(free_z, peer) for peer in ways["z"]]
    ):
        pl.semaphore_signal(sem, inc=1, device_id=peer, device_id_type=MESH)
    wa_back = keep(wa_hbm, gs_ref.at[:, :, :, :, :, pl.ds(3 * part, 3 * part)])
    next(sums)
    between = (
        (lambda: up_grad(0), lambda: up_grad(2)),
        (settle_all, lambda: next(sums), lambda: up_grad(1)),
        (lambda: up_grad(3), lambda: next(sums)),
        (settle_all, lambda: next(sums)),
        (lambda: out_grad(0), lambda: out_grad(1), lambda: next(sums)),
        (settle_all, lambda: next(sums)),
    )

    def out_grad(half):
        share_block(dnn(bflip_ref[...], a_ref[:, half * part : (half + 1) * part]), half, 8)

    for pair, works in enumerate(between):
        one_pair(pair)
        for work in works:
            work()
    flip_ref[...] = flip(x_ref[own, :])
    wa_back.wait()

    def finish(index, grad):
        for half in range(2):
            if index == 0 and half == 0:
                pl.semaphore_wait(free_twin, 1)
            share_block(
                dnn(flip_ref[...], grad[:, half * part : (half + 1) * part]), half, spared + index
            )
        for half in range(2):
            r1_ref[...] += dnt(
                grad[:, half * part : (half + 1) * part],
                block_of(gs_ref.at[half], slice((3 + index) * part, (4 + index) * part)),
            )

    finish(0, q_ref)
    settle_all()
    next(sums)
    for which in range(2):
        grad, come = ((k_ref, tk_ref), (v_ref, tv_ref))[which]
        for pair in range(width // LOG_PAIR):
            swap(which, pair).wait()
        for half in range(2):
            cols = slice(half * part, (half + 1) * part)
            grad[own, cols] = (
                grad[own, cols].astype(f32) + come[half * rows : (half + 1) * rows, :].astype(f32)
            ).astype(low)
        finish(1 + which, grad.at[own])
    settle_all()
    keep(r1_ref, input_hbm.at[own])
    ga_ref[...] = r1_ref[...].astype(low)
    join = remote(ga_ref, normed_ref, ksends, krecvs, (2, 1), ways["y"])
    join.start()
    line = lax.broadcasted_iota(jnp.int32, sums_ref.shape, 0)
    vector_grad = jnp.where(
        line == 0,
        jnp.sum(q_ref[...].astype(f32), 0, keepdims=True),
        jnp.where(line == 1, jnp.sum(v_ref[own, :].astype(f32), 0, keepdims=True), sums_ref[...]),
    )
    vector_grad = jnp.concatenate(
        [vector_grad, jnp.zeros((16 - vector_grad.shape[0], width), f32)], 0
    )
    vector_total = []
    vector_steps = shared_steps(
        vector_grad, vector_total,
        lambda i: vmine_ref.at[i],
        lambda i: vcome_ref.at[i],
        vsends, vrecvs,
    )
    next(vector_steps)
    for unused in sums:
        next(vector_steps, None)
    for unused in vector_steps:
        pass
    vector_ref[...] = vector_total[0][: vector_ref.shape[0]]
    join.wait()
    r2_ref[...] = normed_ref[...].astype(f32)
    other = pl.ds(pl.multiple_of((1 - y) * rows, rows), rows)
    keep(r2_ref, input_hbm.at[other])
    for copy in kept:
        if all(copy is not seen for seen in (cot_copy, x_copy, tx_copy, wa_copy, wa_back)):
            copy.wait()
    for copy in sum_sent:
        copy.wait_send()
    share.wait_send()
    rest = student_hbm.at[other]
    remote(rest, rest, ksends, krecvs, (2, 0), ways["y"]).wait_recv()


def first_call(x, tx, cot, vec, tvec, lengths, masked, weights, teacher, number):
    length, width = x.shape
    rows, part, hidden = length // 2, width // 2, 4 * width
    lines = weights[0].shape[1]
    wide = 4 * part + 2 * weights[2].shape[1]
    own_cuts = [(i, i + 1) for i in range(4)] + [(i, i + 2) for i in range(4, 12, 2)]
    aim_cuts = [(i, i + 2) for i in range(0, 12, 2)]
    order = []
    for which, index in GATHER_ORDER:
        a, b = (own_cuts, aim_cuts)[which][index]
        order.append((which, a * part, b * part, (which, index) in GATHER_OVER_X))
    chunks = tuple(order)
    count = len(chunks)
    listed = masked.shape[1]
    pairs = width // LOG_PAIR
    sem = pltpu.SemaphoreType.DMA
    vm = pltpu.VMEM
    return pl.pallas_call(
        partial(first_kernel, chunks),
        name="gather_forward",
        out_shape=[
            shape_of(2, 4, 2, 2, lines, 3 * part, kind=low),
            shape_of(length, width),
            shape_of(length, width, kind=low),
            shape_of(lines, wide),
            shape_of(12, width),
        ],
        in_specs=[ANY_SPEC] * 3 + [VMEM_SPEC] * 12,
        out_specs=[ANY_SPEC] * 3 + [VMEM_SPEC] * 2,
        scratch_shapes=[
            vm((12, width), f32),
            vm((12, width), f32),
            vm((12, width), f32),
            vm((length, width), low),
            vm((length, width), low),
            vm((2, 4, 2, 2, lines, wide), low),
            vm((4, 2, 2, lines, wide), low),
            vm((lines, wide), low),
            vm((lines, wide), low),
            vm((rows, width), low),
            vm((length, width), low),
            vm((length, width), low),
            vm((rows, width), low),
            vm((pairs, rows, LOG_PAIR), f32),
            vm((length, part), low),
            vm((length, part), low),
            vm((2, listed, width), low),
            vm((2, listed, width), low),
            vm((listed, width), f32),
            vm((4, 16, width), f32),
            vm((6, 16, width), f32),
            vm((rows, width), f32),
            vm((rows, width), low),
            vm((rows, hidden), low),
            vm((rows, hidden), low),
            vm((rows, width), f32),
            vm((rows, width), low),
            vm((width, rows), low),
            vm((width, rows), low),
            vm((width, rows), low),
            vm((rows, width), low),
            vm((2, 4, 2, lines, wide - 3 * part), low),
            vm((3, 2, lines, wide - 3 * part), low),
            vm((2, lines, wide), low),
            vm((lines, wide), low),
            sem((count,)), sem((count, 3)), sem((count, 3)), sem((count, 7)), sem((count, 7)),
            sem((2,)), sem((2,)), sem((16,)), sem((16,)), sem((10,)),
            sem((12, 2)), sem((12, 2)), sem((12, 3)), sem((12, 3)), sem((3, pairs)), sem((3, pairs)),
            sem((6,)), sem((6,)),
            pltpu.SemaphoreType.REGULAR, pltpu.SemaphoreType.REGULAR, pltpu.SemaphoreType.REGULAR,
        ],
        compiler_params=pltpu.CompilerParams(
            vmem_limit_bytes=FIRST_LIMIT, collective_id=number, has_side_effects=True
        ),
    )(x, tx, cot, vec, tvec, lengths, masked, *weights, *teacher)


def matrices(grad_ref, groups):
    attn, out, up, down = range(4)
    plan = [(0, attn, 0), (1, attn, 1), (2, attn, 2), (3, out, None), (4, up, None), (5, down, None)]
    at = 0
    for index, which, slot in plan:
        refs = [group[which] if slot is None else group[which].at[slot] for group in groups]
        size = refs[0].shape[-1]
        yield index, grad_ref[:, at : at + size], refs
        at += size


def norm_kernel(grad_ref, *rest):
    weights, firsts, seconds = rest[0:4], rest[4:8], rest[8:12]
    norm_o, terms_ref, sends, recvs = rest[12:]
    at, y, z, x, core = place()
    others = terms_ref.shape[0] - 1
    me = 2 * at + y

    def peer(step):
        there = (me + step) % (others + 1)
        return there // 2, there % 2

    barrier = pltpu.get_barrier_semaphore()

    def call(step, carry):
        pl.semaphore_signal(barrier, inc=1, device_id=peer(step), device_id_type=MESH)
        return carry

    lax.fori_loop(1, others + 1, call, 0)
    lane = lane_index((8, LOG_PAIR))
    row = lax.broadcasted_iota(jnp.int32, (8, LOG_PAIR), 0)
    squares = jnp.zeros((8, LOG_PAIR), f32)
    for index, grad, (w, first, second) in matrices(grad_ref, (weights, firsts, seconds)):
        unused, unused_too, step = adam_step(grad, first[...], second[...])
        for line, value in ((0, w[...]), (1, step + decay_rate * w[...])):
            total = jnp.sum(jnp.sum(value * value, -1, keepdims=True), 0, keepdims=True)
            squares = jnp.where((row == line) & (lane == index), total, squares)
    terms_ref[me] = squares
    pl.semaphore_wait(barrier, others)

    def send(step):
        return remote(terms_ref.at[me], terms_ref.at[me], sends, recvs, step - 1, peer(step))

    def begin(step, carry):
        send(step).start()
        return carry

    def landed(step, carry):
        came = terms_ref.at[(me + others + 1 - step) % (others + 1)]
        remote(came, came, sends, recvs, step - 1, peer(step)).wait_recv()
        return carry

    def left(step, carry):
        send(step).wait_send()
        return carry

    lax.fori_loop(1, others + 1, begin, 0)
    lax.fori_loop(1, others + 1, landed, 0)
    norms = jnp.sqrt(jnp.sum(terms_ref[...], 0))
    norm_o[...] = jnp.where(row == 2, norms[0:1, :] / norms[1:2, :], norms)
    lax.fori_loop(1, others + 1, left, 0)


def update_kernel(
    grad_ref, norm_ref, total_ref, vec_ref, vm_ref, vs_ref, student_hbm, input_hbm, *rest
):
    groups = [rest[i : i + 4] for i in range(0, 24, 4)]
    vm_o, vs_o, vec_o, norm_o, ratio_o, student_o, input_o = rest[24:31]
    student_ref, input_ref, copy_sem = rest[31:]
    passed = [(student_hbm, student_ref, student_o), (input_hbm, input_ref, input_o)]
    come = [pltpu.make_async_copy(a, b, copy_sem.at[i]) for i, (a, b, c) in enumerate(passed)]
    leave = [pltpu.make_async_copy(b, c, copy_sem.at[i]) for i, (a, b, c) in enumerate(passed)]
    for copy in come:
        copy.start()
    for index, grad, refs in matrices(grad_ref, groups):
        w, first, second, w_o, first_o, second_o = refs
        first_new, second_new, step = adam_step(grad, first[...], second[...])
        first_o[...] = first_new
        second_o[...] = second_new
        weight = w[...]
        ratio = norm_ref[2:3, index : index + 1]
        w_o[...] = weight - matrix_rate * ratio * (step + decay_rate * weight)
        if index == 3:
            for one, copy in zip(come, leave):
                one.wait()
                copy.start()
    width = total_ref.shape[1]
    for index in range(total_ref.shape[0]):
        here = pl.ds(index * width, width)
        first_new, second_new, step = adam_step(
            total_ref[index : index + 1, :],
            vm_ref[here].reshape(1, width),
            vs_ref[here].reshape(1, width),
        )
        vm_o[here] = first_new.reshape(width)
        vs_o[here] = second_new.reshape(width)
        vec_o[here] = vec_ref[here] - vector_rate * step.reshape(width)
    norm_o[...] = norm_ref[0:2, 0:6]
    ratio_o[...] = norm_ref[2:3, 0:6].reshape(6)
    for copy in leave:
        copy.wait()


def norm_call(grad, weights, firsts, seconds, number):
    sem = pltpu.SemaphoreType.DMA
    devices = lax.axis_size("dp") * lax.axis_size("mp")
    return pl.pallas_call(
        norm_kernel,
        name="norms",
        out_shape=shape_of(8, LOG_PAIR),
        in_specs=[VMEM_SPEC] * 13,
        out_specs=VMEM_SPEC,
        scratch_shapes=[
            pltpu.VMEM((devices, 8, LOG_PAIR), f32), sem((devices - 1,)), sem((devices - 1,))
        ],
        compiler_params=pltpu.CompilerParams(
            vmem_limit_bytes=LIMIT, collective_id=number, has_side_effects=True
        ),
    )(grad, *weights, *firsts, *seconds)


def update_call(grad, norms, total, vec, vm, vs, student, input_grad, weights, firsts, seconds):
    outs = [shape_of(*value.shape) for group in (weights, firsts, seconds) for value in group]
    outs += [shape_of(*vec.shape)] * 3 + [shape_of(2, 6), shape_of(6)]
    count = len(outs)
    outs += [shape_of(*student.shape, kind=low), shape_of(*input_grad.shape)]
    return pl.pallas_call(
        update_kernel,
        name="update",
        out_shape=outs,
        in_specs=[VMEM_SPEC] * 6 + [ANY_SPEC] * 2 + [VMEM_SPEC] * 12,
        out_specs=[VMEM_SPEC] * count + [ANY_SPEC] * 2,
        scratch_shapes=[
            pltpu.VMEM(student.shape, low),
            pltpu.VMEM(input_grad.shape, f32),
            pltpu.SemaphoreType.DMA((2,)),
        ],
        compiler_params=pltpu.CompilerParams(vmem_limit_bytes=LIMIT),
    )(grad, norms, total, vec, vm, vs, student, input_grad, *weights, *firsts, *seconds)


def split_kernels(
    tokens,
    teacher_tokens,
    cotangent,
    lengths,
    masked,
    attn_weight,
    out_weight,
    up_weight,
    down_weight,
    attn_first,
    out_first,
    up_first,
    down_first,
    attn_second,
    out_second,
    up_second,
    down_second,
    vectors,
    vector_first,
    vector_second,
    teacher_attn,
    teacher_out,
    teacher_up,
    teacher_down,
    teacher_vectors,
):
    def upright(group):
        return (group[0], group[1].T, group[2], group[3].T)

    weights = upright((attn_weight, out_weight, up_weight, down_weight))
    unused_wa, input_grad, student, grad, total = first_call(
        tokens[0],
        teacher_tokens[0],
        cotangent[0],
        vectors,
        teacher_vectors,
        lengths.reshape(1, 1),
        masked,
        weights,
        upright((teacher_attn, teacher_out, teacher_up, teacher_down)),
        0,
    )
    states = (
        weights,
        upright((attn_first, out_first, up_first, down_first)),
        upright((attn_second, out_second, up_second, down_second)),
    )
    norms = norm_call(grad, *states, 1)
    outs = update_call(
        grad, norms, total, vectors, vector_first, vector_second, student, input_grad, *states
    )
    return (
        outs[17][None],
        outs[18][None],
        *upright(outs[0:4]),
        *upright(outs[4:8]),
        *upright(outs[8:12]),
        *outs[12:17],
    )


def solution(mesh):
    local = split_kernels if dict(mesh.shape) == {"dp": 16, "mp": 2} else split_rows
    return jax.shard_map(
        local,
        mesh=mesh,
        in_specs=(
            P("dp", None, None),
            P("dp", None, None),
            P("dp", None, None),
            P("dp"),
            P("dp", None),
            P(None, "dp", "mp"),
            P("mp", "dp"),
            P("dp", "mp"),
            P("mp", "dp"),
            P(None, "dp", "mp"),
            P("mp", "dp"),
            P("dp", "mp"),
            P("mp", "dp"),
            P(None, "dp", "mp"),
            P("mp", "dp"),
            P("dp", "mp"),
            P("mp", "dp"),
            P(),
            P(),
            P(),
            P(None, "dp", "mp"),
            P("mp", "dp"),
            P("dp", "mp"),
            P("mp", "dp"),
            P(),
        ),
        out_specs=(
            P("dp", None, None),
            P("dp", None, None),
            P(None, "dp", "mp"),
            P("mp", "dp"),
            P("dp", "mp"),
            P("mp", "dp"),
            P(None, "dp", "mp"),
            P("mp", "dp"),
            P("dp", "mp"),
            P("mp", "dp"),
            P(None, "dp", "mp"),
            P("mp", "dp"),
            P("dp", "mp"),
            P("mp", "dp"),
            P(),
            P(),
            P(),
            P(),
            P(),
        ),
        check_vma=False,
    )
```

```python
from functools import partial

import jax
import jax.numpy as jnp
from jax import lax
from jax.experimental import pallas as pl
from jax.experimental.pallas import tpu as pltpu
from jax.sharding import PartitionSpec as P

HDIM = 64
STEP = 5


beta_one = 0.9
beta_two = 0.999
adam_eps = 1e-06
decay_rate = 0.01
matrix_rate = 0.3
vector_rate = 0.2
cosine_weight = 32.0
cosine_eps = 1e-06
layer_eps = 1e-12
masked_score = -1e30


def layer_norm(row_values, gain_vec, shift_vec):
    center = row_values - jnp.mean(row_values, -1, keepdims=True)
    spread = jnp.mean(center * center, -1, keepdims=True)
    return center * lax.rsqrt(spread + layer_eps) * gain_vec + shift_vec


def vector_parts(packed, model_width):
    pieces = [
        packed[position * model_width : (position + 1) * model_width] for position in range(8)
    ]
    return pieces + [packed[8 * model_width :]]


def head_scores(query, key_rows, visible):
    scale_factor = query.shape[-1] ** (-0.5)
    scores = (
        jnp.einsum("sqe,ske->sqk", query, key_rows, preferred_element_type=jnp.float32)
        * scale_factor
    )
    return jnp.where(visible[:, None, :], scores, masked_score)


def head_forward(query, key_rows, value_rows, visible):
    scores = head_scores(query, key_rows, visible)
    row_peak = jnp.max(scores, -1, keepdims=True)
    exponent = jnp.exp(scores - row_peak)
    row_total = jnp.sum(exponent, -1, keepdims=True)
    weights_low = (exponent / row_total).astype(jnp.bfloat16)
    mixed = jnp.einsum("sqk,ske->sqe", weights_low, value_rows, preferred_element_type=jnp.float32)
    return (mixed.astype(jnp.bfloat16), (row_peak + jnp.log(row_total))[..., 0])


def adam_moments(grad_now, first_old, second_old):
    first_new = beta_one * first_old + (1.0 - beta_one) * grad_now
    second_new = beta_two * second_old + (1.0 - beta_two) * grad_now * grad_now
    step_now = (
        first_new
        / (1.0 - beta_one**STEP)
        / (jnp.sqrt(second_new / (1.0 - beta_two**STEP)) + adam_eps)
    )
    return (first_new, second_new, step_now)


def matrix_squares(attn_w, out_w, up_w, down_w):
    return jnp.concatenate(
        [
            jnp.sum(attn_w * attn_w, axis=(1, 2)),
            jnp.stack([jnp.sum(out_w * out_w), jnp.sum(up_w * up_w), jnp.sum(down_w * down_w)]),
        ]
    )


def shard_pack(attn_w, out_w, up_w, down_w):
    return jnp.concatenate(
        [attn_w[0], attn_w[1], attn_w[2], out_w.T, up_w, down_w.T], axis=1
    )


def cosine_pull(rows, places, aimed, row_start):
    row_count = rows.shape[0]
    local_at = places - row_start
    here = (local_at >= 0) & (local_at < row_count)
    picked = rows[jnp.clip(local_at, 0, row_count - 1)]
    inner = jnp.sum(picked * aimed, -1, keepdims=True)
    square_own = jnp.sum(picked * picked, -1, keepdims=True) + cosine_eps
    square_aim = jnp.sum(aimed * aimed, -1, keepdims=True) + cosine_eps
    inverse = lax.rsqrt(square_own) * lax.rsqrt(square_aim)
    pull = -cosine_weight * (aimed * inverse - picked * (inner * inverse / square_own))
    pull = jnp.where(here[:, None], pull, 0.0)
    return jnp.zeros_like(rows).at[jnp.clip(local_at, 0, row_count - 1)].add(pull)


def heads_of(flat):
    return flat.reshape(flat.shape[0], flat.shape[1] // HDIM, HDIM).transpose(1, 0, 2)


def flat_of(split):
    return split.transpose(1, 0, 2).reshape(split.shape[1], -1)


def dot32(left, right):
    return jnp.dot(left, right, preferred_element_type=jnp.float32)


def dot_nt(left, right):
    return lax.dot_general(
        left, right, (((1,), (1,)), ((), ())), preferred_element_type=jnp.float32
    )


def dot_tn(left, right):
    return lax.dot_general(
        left, right, (((0,), (0,)), ((), ())), preferred_element_type=jnp.float32
    )


def split_rows(
    tokens,
    teacher_tokens,
    cotangent,
    lengths,
    masked,
    attn_weight,
    out_weight,
    up_weight,
    down_weight,
    attn_first,
    out_first,
    up_first,
    down_first,
    attn_second,
    out_second,
    up_second,
    down_second,
    vectors,
    vector_first,
    vector_second,
    teacher_attn,
    teacher_out,
    teacher_up,
    teacher_down,
    teacher_vectors,
):
    low = jnp.bfloat16
    everyone = ("dp", "mp")
    shard_at = lax.axis_index("mp")
    halves = lax.axis_size("mp")
    seq_count, length, width = tokens.shape
    rows = length // halves
    row_start = shard_at * rows
    part = attn_weight.shape[2]
    units = up_weight.shape[1]
    cuts = [0, part, 2 * part, 3 * part, 4 * part, 4 * part + units, 4 * part + 2 * units]
    visible = (jnp.arange(length) < lengths[0])[None, None, :]
    places = masked[0]

    student = lax.all_gather(
        shard_pack(attn_weight, out_weight, up_weight, down_weight).astype(low),
        ("mp", "dp"),
        axis=0,
        tiled=True,
    ).reshape(halves, width, cuts[6])
    teacher = lax.all_gather(
        shard_pack(teacher_attn, teacher_out, teacher_up, teacher_down),
        "dp",
        axis=0,
        tiled=True,
    )

    def whole(index):
        return jnp.concatenate(
            [student[half, :, cuts[index] : cuts[index + 1]] for half in range(halves)], axis=1
        )

    teacher_parts = vector_parts(teacher_vectors.astype(jnp.float32), width)
    bias_q = lax.dynamic_slice_in_dim(teacher_parts[0], shard_at * part, part)
    bias_v = lax.dynamic_slice_in_dim(teacher_parts[1], shard_at * part, part)
    bias_up = lax.dynamic_slice_in_dim(teacher_parts[8], shard_at * units, units)
    teacher_rows = teacher_tokens[0]
    listed = teacher_rows[places]
    t_query = (dot32(listed, teacher[:, : cuts[1]]) + bias_q).astype(low)
    t_keys = dot32(teacher_rows, teacher[:, cuts[1] : cuts[2]]).astype(low)
    t_values = (dot32(teacher_rows, teacher[:, cuts[2] : cuts[3]]) + bias_v).astype(low)
    t_mixed, unused_log = head_forward(
        heads_of(t_query), heads_of(t_keys), heads_of(t_values), visible[0]
    )
    t_branch = lax.psum(dot_nt(flat_of(t_mixed), teacher[:, cuts[3] : cuts[4]]), "mp")
    t_first = listed.astype(jnp.float32) + t_branch + teacher_parts[2]
    t_normed = layer_norm(t_first, teacher_parts[3], teacher_parts[4])
    t_gate = dot32(t_normed.astype(low), teacher[:, cuts[4] : cuts[5]]) + bias_up
    t_act = jax.nn.gelu(t_gate, approximate=False).astype(low)
    t_feed = lax.psum(dot_nt(t_act, teacher[:, cuts[5] : cuts[6]]), "mp")
    aimed = layer_norm(t_normed + t_feed + teacher_parts[5], teacher_parts[6], teacher_parts[7])

    pieces = vector_parts(vectors, width)
    all_rows = tokens[0]
    own_rows = lax.dynamic_slice_in_dim(all_rows, row_start, rows, 0)
    w_q, w_k, w_v, w_out, w_up, w_down = [whole(index) for index in range(6)]
    query = heads_of((dot32(own_rows, w_q) + pieces[0]).astype(low))
    keys = heads_of(dot32(all_rows, w_k).astype(low))
    values = heads_of((dot32(all_rows, w_v) + pieces[1]).astype(low))
    mixed, log_total = lax.map(
        lambda g: jax.tree.map(
            lambda v: v[0], head_forward(g[0][None], g[1][None], g[2][None], visible[0])
        ),
        (query, keys, values),
    )
    attended = flat_of(mixed)
    first_sum = own_rows.astype(jnp.float32) + dot_nt(attended, w_out) + pieces[2]
    normed = layer_norm(first_sum, pieces[3], pieces[4])
    normed_low = normed.astype(low)
    gate_in = dot32(normed_low, w_up) + pieces[8]
    activated = jax.nn.gelu(gate_in, approximate=False).astype(low)
    second_sum = normed + dot_nt(activated, w_down) + pieces[5]
    outcome = layer_norm(second_sum, pieces[6], pieces[7])
    student_out = lax.all_gather(outcome.astype(low), "mp", axis=0, tiled=True)[None]

    own_cotangent = lax.dynamic_slice_in_dim(cotangent[0], row_start, rows, 0)
    grad_top = own_cotangent.astype(jnp.float32) + cosine_pull(outcome, places, aimed, row_start)
    unused_top, pull_top = jax.vjp(layer_norm, second_sum, pieces[6], pieces[7])
    grad_second, grad_gain_two, grad_shift_two = pull_top(grad_top)
    feed_low = grad_second.astype(low)
    grad_down = dot_tn(feed_low, activated)
    grad_act = dot32(feed_low, w_down)
    unused_gelu, pull_gelu = jax.vjp(partial(jax.nn.gelu, approximate=False), gate_in)
    (grad_gate,) = pull_gelu(grad_act)
    gate_low = grad_gate.astype(low)
    grad_up = dot_tn(normed_low, gate_low)
    grad_normed = grad_second + dot_nt(gate_low, w_up)
    unused_mid, pull_mid = jax.vjp(layer_norm, first_sum, pieces[3], pieces[4])
    grad_first, grad_gain_one, grad_shift_one = pull_mid(grad_normed)
    branch_low = grad_first.astype(low)
    grad_out = dot_tn(branch_low, attended)
    grad_heads = heads_of(dot32(branch_low, w_out).astype(low))

    def one_head(g):
        query_h, keys_h, values_h, mixed_h, log_h = g
        scale_factor = HDIM**-0.5
        scores = jnp.where(visible[0], dot_nt(query_h, keys_h) * scale_factor, masked_score)
        probs = jnp.exp(scores - log_h[:, None])
        grad_probs = dot_nt(mixed_h, values_h)
        inner = jnp.sum(probs * grad_probs, -1, keepdims=True)
        grad_scores = (probs * (grad_probs - inner)).astype(low)
        return (
            (dot32(grad_scores, keys_h) * scale_factor).astype(low),
            (dot_tn(grad_scores, query_h) * scale_factor).astype(low),
            dot_tn(probs.astype(low), mixed_h).astype(low),
        )

    grad_query, grad_keys, grad_values = lax.map(
        one_head, (query, keys, values, grad_heads, log_total)
    )
    grad_query = flat_of(grad_query)

    def row_sum(term):
        other = lax.dynamic_slice_in_dim(term, (1 - shard_at) * rows, rows, 0)
        mine = lax.dynamic_slice_in_dim(term, row_start, rows, 0)
        came = lax.ppermute(other, "mp", [(0, 1), (1, 0)])
        return (mine.astype(jnp.float32) + came.astype(jnp.float32)).astype(low)

    grad_keys = row_sum(flat_of(grad_keys))
    grad_values = row_sum(flat_of(grad_values))
    grad_q = dot_tn(own_rows, grad_query)
    grad_k = dot_tn(own_rows, grad_keys)
    grad_v = dot_tn(own_rows, grad_values)
    input_own = (
        grad_first + dot_nt(grad_query, w_q) + dot_nt(grad_keys, w_k) + dot_nt(grad_values, w_v)
    )
    input_grad = lax.all_gather(input_own, "mp", axis=0, tiled=True)[None]

    def half_of(matrix, half):
        span = matrix.shape[1] // halves
        return matrix[:, half * span : (half + 1) * span]

    grads = [grad_q, grad_k, grad_v, grad_out, grad_up, grad_down]
    packed_grad = jnp.concatenate(
        [
            jnp.concatenate([half_of(g, half) for g in grads], axis=1).astype(low)
            for half in range(halves)
        ],
        axis=0,
    )
    summed = lax.psum_scatter(
        packed_grad, ("mp", "dp"), scatter_dimension=0, tiled=True
    ).astype(jnp.float32)
    summed_attn = jnp.stack([summed[:, cuts[i] : cuts[i + 1]] for i in range(3)])
    summed_out = summed[:, cuts[3] : cuts[4]].T
    summed_up = summed[:, cuts[4] : cuts[5]]
    summed_down = summed[:, cuts[5] : cuts[6]].T

    vector_grad = jnp.concatenate(
        [
            jnp.sum(grad_query.astype(jnp.float32), 0),
            jnp.sum(grad_values.astype(jnp.float32), 0),
            jnp.sum(branch_low.astype(jnp.float32), 0),
            grad_gain_one,
            grad_shift_one,
            jnp.sum(feed_low.astype(jnp.float32), 0),
            grad_gain_two,
            grad_shift_two,
            jnp.sum(gate_low.astype(jnp.float32), 0),
        ]
    )
    return (student_out, input_grad) + lamb_update(
        (summed_attn, summed_out, summed_up, summed_down),
        (attn_weight, out_weight, up_weight, down_weight),
        (attn_first, out_first, up_first, down_first),
        (attn_second, out_second, up_second, down_second),
        vector_grad,
        vectors,
        vector_first,
        vector_second,
    )


def lamb_update(grads, weights, firsts, seconds, vector_grad, vectors, vector_first, vector_second):
    moments, squares, steps = [], [], []
    for grad_now, weight, first_old, second_old in zip(grads, weights, firsts, seconds):
        first_new, second_new, step_now = adam_moments(grad_now, first_old, second_old)
        moments.append(first_new)
        squares.append(second_new)
        steps.append(step_now + decay_rate * weight)
    weight_total, update_total, vector_total = lax.psum(
        (matrix_squares(*weights), matrix_squares(*steps), vector_grad), ("dp", "mp")
    )
    weight_norms = jnp.sqrt(weight_total)
    update_norms = jnp.sqrt(update_total)
    trust_ratio = weight_norms / update_norms
    ratios = [trust_ratio[0:3][:, None, None], trust_ratio[3], trust_ratio[4], trust_ratio[5]]
    updated = [
        weight - matrix_rate * ratio * step for weight, ratio, step in zip(weights, ratios, steps)
    ]
    vector_moment, vector_square, step_vector = adam_moments(
        vector_total, vector_first, vector_second
    )
    vector_updated = vectors - vector_rate * step_vector
    return (
        *updated,
        *moments,
        *squares,
        vector_moment,
        vector_square,
        vector_updated,
        jnp.stack([weight_norms, update_norms]),
        trust_ratio,
    )


LOG_PAIR = 128
MESH = pl.DeviceIdType.MESH
low = jnp.bfloat16
f32 = jnp.float32
VMEM_SPEC = pl.BlockSpec(memory_space=pltpu.VMEM)
ANY_SPEC = pl.BlockSpec(memory_space=pl.ANY)
AHEAD = 2
LEAD = 1
GATHER = (
    (0, 0, 1, 0), (0, 1, 2, 0), (0, 2, 3, 0), (1, 0, 2, 0), (1, 2, 4, 0), (0, 3, 4, 0), (1, 4, 6, 0),
    (0, 4, 6, 0), (1, 6, 8, 0), (0, 6, 8, 0), (1, 8, 10, 0), (1, 10, 12, 0), (0, 8, 10, 0), (0, 10, 12, 1),
)
FIRST_LIMIT = 64 * 2**20
LIMIT = 60 * 2**20


def dnn(left, right):
    return jnp.dot(left, right, preferred_element_type=f32)


def dnt(left, right):
    return lax.dot_general(left, right, (((1,), (1,)), ((), ())), preferred_element_type=f32)


def lane_index(shape):
    return lax.broadcasted_iota(jnp.int32, shape, 1)


def split_three(value):
    top = value.astype(low).astype(f32)
    rest = value - top
    middle = rest.astype(low).astype(f32)
    return (top, middle, rest - middle)


def flip(value):
    return value.astype(f32).T.astype(low)


def place():
    at = lax.axis_index("dp")
    return (at, lax.axis_index("mp"), at // 4, (at // 2) % 2, at % 2)


def near():
    at, y, z, x, core = place()
    return dict(
        twin=(at + 1 - 2 * core, y),
        x=(at + 2 - 4 * x, y),
        y=(at, 1 - y),
        z=[(((z + step) % 4) * 4 + 2 * x + core, y) for step in (1, 2, 3)],
        za=((z + 1 - 2 * (z % 2)) * 4 + 2 * x + core, y),
        zb=((z + 2 - 4 * (z // 2)) * 4 + 2 * x + core, y),
    )


def greet(peers):
    sem = pltpu.get_barrier_semaphore()
    for peer in peers:
        pl.semaphore_signal(sem, inc=1, device_id=peer, device_id_type=MESH)
    return lambda: pl.semaphore_wait(sem, len(peers))


def vector_rows(flat_ref, rows_ref):
    width = rows_ref.shape[1]
    for index in range(rows_ref.shape[0]):
        row = flat_ref[pl.ds(index * width, width)].reshape(1, width)
        rows_ref[index : index + 1, :] = row.astype(f32)


def remote(src, dst, sends, recvs, at, peer):
    return pltpu.make_async_remote_copy(
        src_ref=src,
        dst_ref=dst,
        send_sem=sends.at[at],
        recv_sem=recvs.at[at],
        device_id=peer,
        device_id_type=MESH,
    )


def row_norm(rows):
    center = rows - jnp.mean(rows, -1, keepdims=True)
    scale = lax.rsqrt(jnp.mean(center * center, -1, keepdims=True) + layer_eps)
    return (center * scale, scale)


def norm_pull(grad, unit, scale, gain):
    lifted = grad * gain
    return scale * (
        lifted
        - jnp.mean(lifted, -1, keepdims=True)
        - unit * jnp.mean(lifted * unit, -1, keepdims=True)
    )


def normal_share(value):
    return 0.5 * (1.0 + lax.erf(value * 0.7071067811865476))


def pair_forward(query, keys, values, bias):
    count, span = query.shape[0], keys.shape[0]
    lane_q, lane_k = lane_index((count, LOG_PAIR)), lane_index((span, LOG_PAIR))
    outs, logs = [], []
    for head in range(2):
        spare = HDIM * (1 - head)
        keys_now = jnp.where(
            lane_k // HDIM == head,
            keys.astype(f32),
            jnp.where(lane_k == spare, bias, 0.0),
        ).astype(low)
        query_now = jnp.where(
            lane_q // HDIM == head,
            query.astype(f32),
            jnp.where(lane_q == spare, 1.0, 0.0),
        ).astype(low)
        scores = dnt(query_now, keys_now)
        peak = jnp.max(scores, -1, keepdims=True)
        exponent = jnp.exp(scores - peak)
        total = jnp.sum(exponent, -1, keepdims=True)
        outs.append(dnn((exponent * (1.0 / total)).astype(low), values))
        logs.append(peak + jnp.log(total))
    return (
        jnp.where(lane_q < HDIM, outs[0], outs[1]),
        jnp.where(lane_q < HDIM, logs[0], logs[1]),
    )


def shape_of(*dims, kind=f32):
    return jax.ShapeDtypeStruct(dims, kind)


def pair_back_rows(query, grad_mixed, mixed, logs):
    lane_q = lane_index(query.shape)
    query_wide, grad_wide = query.astype(f32), grad_mixed.astype(f32)
    product = grad_wide * mixed.astype(f32)
    sides = []
    for head in range(2):
        spare = HDIM * (1 - head)
        own_q = lane_q // HDIM == head
        inner = jnp.sum(jnp.where(own_q, product, 0.0), -1, keepdims=True)
        query_now = jnp.where(own_q, query_wide, jnp.where(lane_q == spare, 1.0, 0.0))
        grad_now = jnp.where(own_q, grad_wide, 0.0)
        for place_at, (log_term, inner_term) in enumerate(
            zip(split_three(logs[:, HDIM * head : HDIM * head + 1]), split_three(inner))
        ):
            here = lane_q == spare + 1 + place_at
            query_now = jnp.where(here, log_term, query_now)
            grad_now = jnp.where(here, inner_term, grad_now)
        sides.append((query_now.astype(low), grad_now.astype(low)))
    return sides


def pair_back_keys(query, grad_mixed, sides, keys, values, bias):
    lane_k = lane_index(keys.shape)
    keys_wide, values_wide = keys.astype(f32), values.astype(f32)
    grad_keys, grad_values, grad_query = [], [], []
    for head, (query_now, grad_now) in enumerate(sides):
        spare = HDIM * (1 - head)
        own_k = lane_k // HDIM == head
        minus = jnp.where((lane_k > spare) & (lane_k < spare + 4), -1.0, 0.0)
        keys_now = jnp.where(own_k, keys_wide, jnp.where(lane_k == spare, bias, minus)).astype(low)
        values_now = jnp.where(own_k, values_wide, minus).astype(low)
        probs = jnp.exp(dnt(keys_now, query_now))
        grad_scores = (probs * dnt(values_now, grad_now)).astype(low)
        grad_keys.append(dnn(grad_scores, query))
        grad_values.append(dnn(probs.astype(low), grad_mixed))
        flipped = keys_wide.T[HDIM * head : HDIM * (head + 1)].astype(low)
        grad_query.append(dnn(flipped, grad_scores))
    return (
        jnp.concatenate(grad_query, 0),
        jnp.where(lane_k < HDIM, grad_keys[0], grad_keys[1]),
        jnp.where(lane_k < HDIM, grad_values[0], grad_values[1]),
    )


def adam_step(grad, first, second):
    first_new = beta_one * first + (1.0 - beta_one) * grad
    second_new = beta_two * second + (1.0 - beta_two) * grad * grad
    step = (
        first_new
        / (1.0 - beta_one**STEP)
        / (jnp.sqrt(second_new / (1.0 - beta_two**STEP)) + adam_eps)
    )
    return (first_new, second_new, step)


def block_of(ref, cols):
    value = ref[:, :, :, :, cols]
    return value.reshape(-1, value.shape[-1])


def gather_steps(chunks, gs_ref, gt_ref, ps_ref, pt_ref, local_sem, zsends, zrecvs, sends, recvs, started):
    at, y, z, x, core = place()
    ways = near()

    def go(ref, chunk, kind, peer):
        copy = remote(ref, ref, sends, recvs, (chunk, kind), peer)
        copy.start()
        started.append(copy)

    def landed(ref, chunk, kind):
        remote(ref, ref, sends, recvs, (chunk, kind), ways["x"]).wait_recv()

    def shard(chunk, zz):
        which, a, b, unused = chunks[chunk]
        if which == 0:
            return gs_ref.at[y, zz, x, core, :, pl.ds(a, b - a)]
        return gt_ref.at[zz, x, core, :, pl.ds(a, b - a)]

    def column(chunk, yy, xx, cc):
        which, a, b, unused = chunks[chunk]
        if which == 0:
            return gs_ref.at[yy, :, xx, cc, :, pl.ds(a, b - a)]
        return gt_ref.at[:, xx, cc, :, pl.ds(a, b - a)]

    own = []
    near_z, far_z = z + 1 - 2 * (z % 2), z + 2 - 4 * (z // 2)
    last_z = near_z + 2 - 4 * (near_z // 2)

    def send_z(source, target, k, kind, way):
        copy = remote(source, target, zsends, zrecvs, (k, kind), ways[way])
        copy.start()
        started.append(copy)

    def landed_z(k, zz, kind):
        came = shard(k, zz)
        remote(came, came, zsends, zrecvs, (k, kind), ways["x"]).wait_recv()

    def begin(k):
        which, a, b, unused = chunks[k]
        source = (ps_ref, pt_ref)[which].at[:, pl.ds(a, b - a)]
        copy = pltpu.make_async_copy(source, shard(k, z), local_sem.at[k])
        copy.start()
        own.append(copy)
        send_z(source, shard(k, z), k, 0, "zb")
        send_z(source, shard(k, z), k, 1, "za")

    def hand_on(k):
        landed_z(k, far_z, 0)
        send_z(shard(k, far_z), shard(k, far_z), k, 2, "za")

    def along_z(k):
        landed_z(k, near_z, 1)
        landed_z(k, last_z, 2)
        own[k].wait()
        go(column(k, y, x, core), k, 0, ways["x"])
        if chunks[k][0] == 0:
            go(column(k, y, x, core), k, 1, ways["y"])
        go(column(k, y, x, core), k, 2, ways["twin"])

    def from_sides(k):
        landed(column(k, y, 1 - x, core), k, 0)
        if chunks[k][0] == 0 and not chunks[k][3]:
            go(column(k, y, 1 - x, core), k, 3, ways["y"])
        go(column(k, y, 1 - x, core), k, 4, ways["twin"])
        if chunks[k][0] == 0:
            landed(column(k, 1 - y, x, core), k, 1)
            if chunks[k][3]:
                go(column(k, 1 - y, x, core), k, 3, ways["x"])
            go(column(k, 1 - y, x, core), k, 5, ways["twin"])

    def last(k):
        if chunks[k][0] == 0:
            landed(column(k, 1 - y, 1 - x, core), k, 3)
            go(column(k, 1 - y, 1 - x, core), k, 6, ways["twin"])

    def whole(k):
        landed(column(k, y, x, 1 - core), k, 2)
        landed(column(k, y, 1 - x, 1 - core), k, 4)
        if chunks[k][0] == 0:
            landed(column(k, 1 - y, x, 1 - core), k, 5)
            landed(column(k, 1 - y, 1 - x, 1 - core), k, 6)

    count = len(chunks)
    for k in range(AHEAD + LEAD):
        begin(k)
    for k in range(LEAD + 1):
        hand_on(k)
    for k in range(LEAD):
        along_z(k)
    for slot in range(count + 2):
        if slot + LEAD + AHEAD < count:
            begin(slot + LEAD + AHEAD)
        if slot + LEAD + 1 < count:
            hand_on(slot + LEAD + 1)
        if slot + LEAD < count:
            along_z(slot + LEAD)
        if slot < count:
            from_sides(slot)
        if 0 <= slot - 1 < count:
            last(slot - 1)
        if 0 <= slot - 2 < count:
            whole(slot - 2)
        yield max(0, slot - 1)


def sum_steps(chunks, given, ax_at, h_at, zr_at, before_x, before_z, tot_ref, own_ref, yr_ref, sends, recvs, zsends, zrecvs, started):
    at, y, z, x, core = place()
    ways = near()
    count = len(chunks)

    def span(k):
        a, b = chunks[k]
        return pl.ds(a, b - a)

    def begin(k):
        if k in before_x:
            before_x[k]()
        copy = remote(given(k, 1 - x), ax_at(k), sends, recvs, (k, 0), ways["x"])
        copy.start()
        started.append(copy)

    def over_x(k):
        remote(ax_at(k), ax_at(k), sends, recvs, (k, 0), ways["x"]).wait_recv()
        came = ax_at(k)

        def add(step, carry):
            yy, zz = step // 4, step % 4
            block = h_at(k, yy, zz)
            block[...] = (block[...].astype(f32) + came[yy, zz].astype(f32)).astype(low)
            return carry

        lax.fori_loop(0, 8, add, 0)
        if k in before_z:
            before_z[k]()
        for step in range(3):
            copy = remote(
                h_at(k, slice(None), (z + 1 + step) % 4), zr_at(k, step),
                zsends, zrecvs, (k, step), ways["z"][step],
            )
            copy.start()
            started.append(copy)

    def over_z(k):
        here = span(k)
        for step in range(3):
            came = zr_at(k, step)
            remote(came, came, zsends, zrecvs, (k, step), ways["x"]).wait_recv()
        for yy in range(2):
            total = h_at(k, yy, z)[...].astype(f32)
            for step in range(3):
                total += zr_at(k, step)[yy].astype(f32)
            tot_ref[yy, :, here] = total.astype(low)
        copy = remote(
            tot_ref.at[1 - y, :, here], yr_ref.at[:, here], sends, recvs, (k, 1), ways["y"]
        )
        copy.start()
        started.append(copy)

    def over_y(k):
        here = span(k)
        came = yr_ref.at[:, here]
        remote(came, came, sends, recvs, (k, 1), ways["y"]).wait_recv()
        own_ref[:, here] = tot_ref[y, :, here].astype(f32) + yr_ref[:, here].astype(f32)

    def steps():
        for slot in range(count + 2):
            if slot < count:
                over_x(slot)
            if 0 <= slot - 1 < count:
                over_z(slot - 1)
            if 0 <= slot - 2 < count:
                over_y(slot - 2)
            yield max(0, slot - 1)

    return begin, steps()


def shared_steps(value, result, mine_at, come_at, sends, recvs):
    at, y, z, x, core = place()
    ways = near()
    for index, way in enumerate(("twin", "x", "y")):
        mine_at(index)[...] = value
        copy = remote(mine_at(index), come_at(index), sends, recvs, index, ways[way])
        copy.start()
        yield
        copy.wait()
        value = mine_at(index)[...] + come_at(index)[...]
    mine_at(3)[...] = value
    copies = []
    for step in range(3):
        copy = remote(
            mine_at(3), come_at(3 + step), sends, recvs, 3 + step, ways["z"][step]
        )
        copy.start()
        copies.append(copy)
    yield
    for copy in copies:
        copy.wait()
    terms = [mine_at(3)[...]] + [come_at(3 + step)[...] for step in range(3)]
    total = None
    for z_from in range(4):
        term = terms[0]
        for step in range(1, 4):
            term = jnp.where((z + 4 - step) % 4 == z_from, terms[step], term)
        total = term if total is None else total + term
    result.append(total)


def first_kernel(
    chunks,
    x_hbm, tx_hbm, cot_hbm, vec_flat, tvec_flat, length_ref, places_ref,
    aw, ow, uw, dw, ta, to, tu, td,
    wa_hbm, input_hbm, student_hbm, total_ref, vector_ref,
    sums_ref, vec_ref, tvec_ref, x_ref, tx_ref, gs_ref, gt_ref, ps_ref, pt_ref, q_ref, k_ref,
    v_ref, a_ref, log_ref, tk_ref, tv_ref, part_ref, come_ref, aimed_ref, vmine_ref, vcome_ref,
    r1_ref, normed_ref, u_ref, slope_ref, r2_ref,
    cot_ref, flip_ref, nflip_ref, bflip_ref, ga_ref, one_ref, zr_ref, tot_ref, yr_ref,
    local_sem, zsends, zrecvs, sends, recvs, tsends, trecvs, gsends, grecvs, copy_sem,
    fsends, frecvs, fzsends, fzrecvs, ksends, krecvs, vsends, vrecvs,
    free_x, free_z, free_twin,
):
    at, y, z, x, core = place()
    ways = near()
    length, width = x_ref.shape
    rows = length // 2
    part = width // 2
    own = pl.ds(pl.multiple_of(y * rows, rows), rows)
    kept = []

    def keep(src, dst):
        copy = pltpu.make_async_copy(src, dst, copy_sem.at[len(kept)])
        copy.start()
        kept.append(copy)
        return copy

    met = greet([ways["twin"], ways["x"], ways["y"]] + ways["z"])
    x_copy, tx_copy = keep(x_hbm, x_ref), keep(tx_hbm, tx_ref)
    for index in range(3):
        ps_ref[:, index * part : (index + 1) * part] = aw[index].astype(low)
        pt_ref[:, index * part : (index + 1) * part] = ta[index]
    for base, source, aim in ((3 * part, ow, to), (4 * part, uw, tu), (8 * part, dw, td)):
        ps_ref[:, base : base + source.shape[1]] = source[...].astype(low)
        pt_ref[:, base : base + source.shape[1]] = aim[...]
    met()
    started = []
    steps = gather_steps(
        chunks, gs_ref, gt_ref, ps_ref, pt_ref, local_sem, zsends, zrecvs, sends, recvs, started
    )
    ready = [0]

    def tick():
        ready[0] = next(steps, len(chunks))

    def need(chunk):
        while ready[0] <= chunk:
            tick()

    cot_copy = keep(cot_hbm.at[own], cot_ref)

    def key_bias():
        row_at = lax.broadcasted_iota(jnp.int32, (length, LOG_PAIR), 0)
        return jnp.where(row_at < length_ref[0:1, 0:1], 0.0, masked_score)

    sums_ref[...] = jnp.zeros(sums_ref.shape, f32)

    def loop(count, body):
        def step(index, carry):
            body(index)
            return carry

        lax.fori_loop(0, count, step, 0)

    def span(index, block):
        if isinstance(index, int):
            return slice(index * block, (index + 1) * block)
        return pl.ds(pl.multiple_of(index * block, block), block)

    def whole(which, end):
        need(max(k for k, chunk in enumerate(chunks) if chunk[0] == which and chunk[2] <= end))

    tick()
    vector_rows(vec_flat, vec_ref)
    vector_rows(tvec_flat, tvec_ref)
    x_copy.wait()
    tx_copy.wait()
    whole(0, 3 * part)
    wa_copy = keep(gs_ref.at[:, :, :, :, :, pl.ds(0, 3 * part)], wa_hbm)

    def keys_values(index):
        here = span(index, 256)
        for half in range(2):
            cols = slice(half * part, (half + 1) * part)
            k_ref[here, cols] = dnn(
                x_ref[here, :], block_of(gs_ref.at[half], slice(part, 2 * part))
            ).astype(low)
            v_ref[here, cols] = (
                dnn(x_ref[here, :], block_of(gs_ref.at[half], slice(2 * part, 3 * part)))
                + vec_ref[1:2, cols]
            ).astype(low)

    def queries(index):
        here = span(index, 256)
        from_x = pl.ds(pl.multiple_of(y * rows + index * 256, 256), 256)
        for half in range(2):
            cols = slice(half * part, (half + 1) * part)
            value = dnn(x_ref[from_x, :], block_of(gs_ref.at[half], slice(0, part)))
            value = (value + vec_ref[0:1, cols]).astype(low).astype(f32) * HDIM**-0.5
            q_ref[here, cols] = value.astype(low)

    def attend(first):
        def one_pair(index):
            pair = first + index
            cols = pl.ds(pl.multiple_of(pair * LOG_PAIR, LOG_PAIR), LOG_PAIR)
            keys, values, bias = k_ref[:, cols], v_ref[:, cols], key_bias()
            for start in range(0, rows, 256):
                here = slice(start, start + 256)
                mixed, logs = pair_forward(q_ref[here, cols], keys, values, bias)
                a_ref[here, cols] = mixed.astype(low)
                log_ref[pair, here, :] = logs

        return one_pair

    for first in range(0, length // 256, 2):
        loop(2, lambda index, first=first: keys_values(first + index))
        tick()
    loop(rows // 256, queries)
    for pair in range(width // LOG_PAIR):
        tick()
        loop(1, attend(pair))

    whole(1, 3 * part)
    mine = pl.ds(pl.multiple_of(y * part, LOG_PAIR), part)
    count = places_ref.shape[1]

    def teacher_keys(index):
        here = span(index, 256)
        tk_ref[here, :] = dnn(tx_ref[here, :], block_of(gt_ref, slice(part, 2 * part))).astype(low)
        tv_ref[here, :] = (
            dnn(tx_ref[here, :], block_of(gt_ref, slice(2 * part, 3 * part))) + tvec_ref[1:2, mine]
        ).astype(low)

    loop(length // 256, teacher_keys)
    whole(1, 4 * part)
    diagonal = lax.broadcasted_iota(jnp.int32, (count, count), 0) == lane_index((count, count))
    places = jnp.where(diagonal, places_ref[...].astype(f32), 0.0)
    places = jnp.sum(places, -1, keepdims=True).astype(jnp.int32)
    pick = jnp.where(places == lane_index((count, length)), 1.0, 0.0).astype(low)
    listed = dnn(pick, tx_ref[...])
    query = dnn(listed.astype(low), block_of(gt_ref, slice(0, part))) + tvec_ref[0:1, mine]
    query = (query.astype(low).astype(f32) * HDIM**-0.5).astype(low)
    branch = jnp.zeros((count, width), f32)
    for pair in range(part // LOG_PAIR):
        cols = slice(pair * LOG_PAIR, (pair + 1) * LOG_PAIR)
        mixed, unused = pair_forward(query[:, cols], tk_ref[:, cols], tv_ref[:, cols], key_bias())
        a_cols = slice(3 * part + pair * LOG_PAIR, 3 * part + (pair + 1) * LOG_PAIR)
        branch += dnt(mixed.astype(low), block_of(gt_ref, a_cols))
    aimed_ref[...] = listed + branch
    part_ref[0] = branch.astype(low)
    swaps = [remote(part_ref.at[i], come_ref.at[i], tsends, trecvs, i, ways["y"]) for i in range(2)]
    swaps[0].start()

    whole(0, 4 * part)

    def project(index):
        here = span(index, 256)
        from_x = pl.ds(pl.multiple_of(y * rows + index * 256, 256), 256)
        first = x_ref[from_x, :].astype(f32) + vec_ref[2:3, :]
        for half in range(2):
            first += dnt(
                a_ref[here, half * part : (half + 1) * part],
                block_of(gs_ref.at[half], slice(3 * part, 4 * part)),
            )
        r1_ref[here, :] = first
        unit, unused = row_norm(first)
        normed = unit * vec_ref[3:4, :] + vec_ref[4:5, :]
        normed_ref[here, :] = normed.astype(low)
        nflip_ref[:, here] = flip(normed.astype(low))
        r2_ref[here, :] = normed + vec_ref[5:6, :]

    loop(rows // 256, project)

    def rise(piece):
        half, base = piece // 2, 4 * part + (piece % 2) * width

        def body(index):
            here = span(index, 256)
            cols = slice(piece * width, (piece + 1) * width)
            gate = dnn(normed_ref[here, :], block_of(gs_ref.at[half], slice(base, base + width)))
            gate += vec_ref[8 + piece : 9 + piece, :]
            share = normal_share(gate)
            u_ref[here, cols] = (gate * share).astype(low)
            slope_ref[here, cols] = (
                share + gate * (jnp.exp(-0.5 * gate * gate) * 0.3989422804014327)
            ).astype(low)

        loop(rows // 256, body)

    def fall(piece):
        half, base = piece // 2, 4 * part + (2 + piece % 2) * width

        def body(index):
            here = span(index, 256)
            r2_ref[here, :] += dnt(
                u_ref[here, piece * width : (piece + 1) * width],
                block_of(gs_ref.at[half], slice(base, base + width)),
            )

        loop(rows // 256, body)

    active = []

    def aim_rise(piece):
        base = 4 * part + piece * width
        gate = dnn(aim_normed.astype(low), block_of(gt_ref, slice(base, base + width)))
        gate += tvec_ref[pl.ds(8 + 2 * y + piece, 1), :]
        active.append((gate * normal_share(gate)).astype(low))

    def aim_fall(piece):
        base = 8 * part + piece * width
        return dnt(active[piece], block_of(gt_ref, slice(base, base + width)))

    whole(0, 6 * part)
    rise(0)
    rise(2)
    whole(1, 8 * part)
    swaps[0].wait()
    unit, unused = row_norm(aimed_ref[...] + come_ref[0].astype(f32) + tvec_ref[2:3, :])
    aim_normed = unit * tvec_ref[3:4, :] + tvec_ref[4:5, :]
    aim_rise(0)
    tick()
    aim_rise(1)
    whole(0, 8 * part)
    rise(1)
    rise(3)
    whole(1, 12 * part)
    feed = aim_fall(0) + aim_fall(1)
    part_ref[1] = feed.astype(low)
    swaps[1].start()
    aimed_ref[...] = aim_normed + feed + tvec_ref[5:6, :]
    whole(0, 10 * part)
    fall(0)
    fall(2)
    whole(0, 12 * part)
    fall(1)
    fall(3)
    swaps[1].wait()
    unit, unused = row_norm(aimed_ref[...] + come_ref[1].astype(f32))
    aimed_ref[...] = unit * tvec_ref[6:7, :] + tvec_ref[7:8, :]
    for unused in steps:
        pass
    for copy in started:
        copy.wait_send()
    wa_copy.wait()
    pl.semaphore_signal(free_x, inc=1, device_id=ways["x"], device_id_type=MESH)
    cot_copy.wait()

    def top(index):
        here = span(index, 256)
        row_at = lax.broadcasted_iota(jnp.int32, (256, places_ref.shape[1]), 0)
        pick = jnp.where(row_at + (y * rows + index * 256) == places_ref[0:1, :], 1.0, 0.0)
        times = jnp.sum(pick, -1, keepdims=True)
        aimed = jnp.dot(
            pick, aimed_ref[...], precision=lax.Precision.HIGHEST, preferred_element_type=f32
        ) / jnp.maximum(times, 1.0)
        unit, spread = row_norm(r2_ref[here, :])
        outcome = unit * vec_ref[6:7, :] + vec_ref[7:8, :]
        inner = jnp.sum(outcome * aimed, -1, keepdims=True)
        square_own = jnp.sum(outcome * outcome, -1, keepdims=True) + cosine_eps
        square_aim = jnp.sum(aimed * aimed, -1, keepdims=True) + cosine_eps
        scale = cosine_weight * times * lax.rsqrt(square_own) * lax.rsqrt(square_aim)
        grad = cot_ref[here, :].astype(f32) - scale * (aimed - outcome * (inner / square_own))
        cot_ref[here, :] = outcome.astype(low)
        sums_ref[6:7, :] += jnp.sum(grad * unit, 0, keepdims=True)
        sums_ref[7:8, :] += jnp.sum(grad, 0, keepdims=True)
        back = norm_pull(grad, unit, spread, vec_ref[6:7, :])
        r2_ref[here, :] = back
        back_low = back.astype(low)
        sums_ref[5:6, :] += jnp.sum(back_low.astype(f32), 0, keepdims=True)
        ga_ref[here, :] = back_low
        flip_ref[:, here] = flip(back_low)

    loop(rows // 256, top)
    keep(cot_ref, student_hbm.at[own])
    share = remote(cot_ref, student_hbm.at[own], ksends, krecvs, (2, 0), ways["y"])
    share.start()

    sum_sent = []
    cuts = [(i * part, (i + 1) * part) for i in (8, 9, 10, 11, 4, 5, 6, 7, 3, 0, 1, 2)]
    spared = 9
    spare_at = 6 * part

    def feed_cols(k):
        a, b = cuts[k]
        return pl.ds(a - 3 * part, b - a)

    def spare_cols(k):
        a, b = cuts[k]
        return pl.ds(spare_at + a, b - a)

    def given(k, xx):
        if k < spared:
            return one_ref.at[:, :, xx, :, feed_cols(k)]
        return gs_ref.at[:, :, xx, 0, :, spare_cols(k)]

    def ax_at(k):
        if k < spared:
            return gs_ref.at[:, :, k // 6, k // 3 % 2, :, pl.ds(k % 3 * part, part)]
        return gs_ref.at[:, :, 0, 1, :, spare_cols(k)]

    def h_at(k, yy, zz):
        return given(k, x).at[yy, zz]

    def zr_at(k, step):
        if k < spared:
            return zr_ref.at[step, :, :, feed_cols(k)]
        return gs_ref.at[:, step, 1, 1, :, spare_cols(k)]

    def wait_for(sem, amount):
        return lambda: pl.semaphore_wait(sem, amount)

    sum_begin, sums = sum_steps(
        cuts, given, ax_at, h_at, zr_at,
        {0: wait_for(free_x, 1), spared: wait_for(free_x, 1)}, {spared: wait_for(free_z, 3)},
        tot_ref, total_ref, yr_ref, fsends, frecvs, fzsends, fzrecvs, sum_sent,
    )
    blocks = []

    def share_block(value, half, k, closes):
        number = len(blocks)
        size = value.shape[1]
        slot = pl.ds((number % 6) * width, size)
        if number >= 2:
            settle(number - 2)
        gt_ref[:, :, :, :, slot] = value.astype(low).reshape(gt_ref.shape[:4] + (size,))
        if k < spared:
            target = one_ref.at[half, :, :, :, pl.ds(cuts[k][0] - 3 * part, size)]
        else:
            target = gs_ref.at[half, :, :, 0, :, spare_cols(k)]
        copy = remote(
            gt_ref.at[:, :, 1 - core, :, slot], target, gsends, grecvs, number, ways["twin"]
        )
        copy.start()
        blocks.append((copy, target, slot, range(k, k + size // part) if closes else ()))

    settled = set()

    def settle(number):
        if number in settled:
            return
        settled.add(number)
        copy, target, slot, closed = blocks[number]
        copy.wait()

        def add(zz, carry):
            target[zz] = (
                target[zz].astype(f32) + gt_ref[zz, :, core, :, slot].astype(f32)
            ).astype(low)
            return carry

        lax.fori_loop(0, 4, add, 0)
        for k in closed:
            sum_begin(k)

    def settle_all():
        for number in range(len(blocks)):
            settle(number)

    def down_grad(piece):
        cols = slice(piece * width, (piece + 1) * width)
        share_block(
            dnn(flip_ref[...], u_ref[:, cols]), piece // 2, 2 * (piece % 2), piece // 2 == 1
        )

    def up_grad(piece):
        cols = slice(piece * width, (piece + 1) * width)
        share_block(
            dnn(nflip_ref[...], slope_ref[:, cols]), piece // 2, 4 + 2 * (piece % 2),
            piece // 2 == 1,
        )

    def gate_pull(piece):
        half, base = piece // 2, 4 * part + (piece % 2) * width
        cols = slice(piece * width, (piece + 1) * width)

        def gate_back(index):
            here = span(index, 256)
            down = block_of(gs_ref.at[half], slice(base + 2 * width, base + 3 * width))
            gate_low = (dnn(ga_ref[here, :], down) * slope_ref[here, cols].astype(f32)).astype(low)
            slope_ref[here, cols] = gate_low
            sums_ref[8 + piece : 9 + piece, :] += jnp.sum(gate_low.astype(f32), 0, keepdims=True)
            r2_ref[here, :] += dnt(gate_low, block_of(gs_ref.at[half], slice(base, base + width)))

        loop(rows // 256, gate_back)

    def middle(index):
        here = span(index, 256)
        grad = r2_ref[here, :]
        unit, spread = row_norm(r1_ref[here, :])
        sums_ref[3:4, :] += jnp.sum(grad * unit, 0, keepdims=True)
        sums_ref[4:5, :] += jnp.sum(grad, 0, keepdims=True)
        back = norm_pull(grad, unit, spread, vec_ref[3:4, :])
        r1_ref[here, :] = back
        back_low = back.astype(low)
        sums_ref[2:3, :] += jnp.sum(back_low.astype(f32), 0, keepdims=True)
        bflip_ref[:, here] = flip(back_low)
        for half in range(2):
            cols = slice(half * part, (half + 1) * part)
            ga_ref[here, cols] = dnn(
                back_low, block_of(gs_ref.at[half], slice(3 * part, 4 * part))
            ).astype(low)

    def swap(which, pair):
        source, target = ((k_ref, tk_ref), (v_ref, tv_ref))[which]
        other_rows = pl.ds(pl.multiple_of((1 - y) * rows, rows), rows)
        return remote(
            source.at[other_rows, pl.ds(pair * LOG_PAIR, LOG_PAIR)],
            target.at[pl.ds(pair // 3 * rows, rows), pl.ds(pair % 3 * LOG_PAIR, LOG_PAIR)],
            ksends, krecvs, (which, pair), ways["y"],
        )

    def one_pair(pair):
        cols = slice(pair * LOG_PAIR, (pair + 1) * LOG_PAIR)

        def body(unused):
            query, grad_mixed = q_ref[:, cols], ga_ref[:, cols]
            sides = pair_back_rows(query, grad_mixed, a_ref[:, cols], log_ref[pair])
            grad_query = None
            for half in range(2):
                here = slice(half * rows, (half + 1) * rows)
                term, grad_keys, grad_values = pair_back_keys(
                    query, grad_mixed, sides, k_ref[here, cols], v_ref[here, cols],
                    key_bias()[here],
                )
                grad_query = term if grad_query is None else grad_query + term
                k_ref[here, cols] = grad_keys.astype(low)
                v_ref[here, cols] = grad_values.astype(low)
            q_ref[:, cols] = (grad_query.T * HDIM**-0.5).astype(low)

        loop(1, body)
        swap(0, pair).start()
        swap(1, pair).start()

    down_grad(0)
    down_grad(2)
    gate_pull(0)
    settle_all()
    gate_pull(2)
    down_grad(1)
    gate_pull(1)
    next(sums)
    down_grad(3)
    gate_pull(3)
    settle_all()
    loop(rows // 256, middle)
    for sem, peer in (
        [(free_x, ways["x"]), (free_twin, ways["twin"])] + [(free_z, peer) for peer in ways["z"]]
    ):
        pl.semaphore_signal(sem, inc=1, device_id=peer, device_id_type=MESH)
    wa_back = keep(wa_hbm, gs_ref.at[:, :, :, :, :, pl.ds(3 * part, 3 * part)])
    next(sums)
    flip_ref[...] = flip(x_ref[own, :])

    def out_grad(half):
        value = dnn(bflip_ref[...], a_ref[:, half * part : (half + 1) * part])
        share_block(value, half, 8, half == 1)

    def finish(half, index):
        cols = slice(half * part, (half + 1) * part)
        if index == 0:
            grad = q_ref[:, cols]
        else:
            grads, come = ((k_ref, tk_ref), (v_ref, tv_ref))[index - 1]
            for pair in range(3 * half, 3 * half + 3):
                swap(index - 1, pair).wait()
            grad = (
                grads[own, cols].astype(f32) + come[half * rows : (half + 1) * rows, :].astype(f32)
            ).astype(low)
            grads[own, cols] = grad
        if half == 0 and index == 0:
            wa_back.wait()
            pl.semaphore_wait(free_twin, 1)
        share_block(dnn(flip_ref[...], grad), half, spared + index, half == 1)
        r1_ref[...] += dnt(
            grad, block_of(gs_ref.at[half], slice((3 + index) * part, (4 + index) * part))
        )

    between = (
        (lambda: up_grad(0), lambda: up_grad(2)),
        (settle_all, lambda: next(sums), lambda: up_grad(1)),
        (lambda: up_grad(3), lambda: next(sums)),
        (settle_all, lambda: next(sums), lambda: out_grad(0), lambda: out_grad(1)),
        (settle_all, lambda: next(sums), lambda: finish(0, 0)),
        (lambda: next(sums), lambda: finish(0, 1), lambda: finish(0, 2)),
    )
    for pair, works in enumerate(between):
        one_pair(pair)
        for work in works:
            work()
    for index in range(3):
        finish(1, index)
        settle_all()
        if index == 0:
            next(sums)
    keep(r1_ref, input_hbm.at[own])
    ga_ref[...] = r1_ref[...].astype(low)
    join = remote(ga_ref, normed_ref, ksends, krecvs, (2, 1), ways["y"])
    join.start()
    line = lax.broadcasted_iota(jnp.int32, sums_ref.shape, 0)
    vector_grad = jnp.where(
        line == 0,
        jnp.sum(q_ref[...].astype(f32), 0, keepdims=True),
        jnp.where(line == 1, jnp.sum(v_ref[own, :].astype(f32), 0, keepdims=True), sums_ref[...]),
    )
    vector_grad = jnp.concatenate(
        [vector_grad, jnp.zeros((16 - vector_grad.shape[0], width), f32)], 0
    )
    vector_total = []
    vector_steps = shared_steps(
        vector_grad, vector_total,
        lambda i: vmine_ref.at[i],
        lambda i: vcome_ref.at[i],
        vsends, vrecvs,
    )
    next(vector_steps)
    for unused in sums:
        next(vector_steps, None)
    for unused in vector_steps:
        pass
    vector_ref[...] = vector_total[0][: vector_ref.shape[0]]
    join.wait()
    r2_ref[...] = normed_ref[...].astype(f32)
    other = pl.ds(pl.multiple_of((1 - y) * rows, rows), rows)
    keep(r2_ref, input_hbm.at[other])
    for copy in kept:
        if all(copy is not seen for seen in (cot_copy, x_copy, tx_copy, wa_copy, wa_back)):
            copy.wait()
    for copy in sum_sent:
        copy.wait_send()
    share.wait_send()
    rest = student_hbm.at[other]
    remote(rest, rest, ksends, krecvs, (2, 0), ways["y"]).wait_recv()


def first_call(x, tx, cot, vec, tvec, lengths, masked, weights, teacher, number):
    length, width = x.shape
    rows, part, hidden = length // 2, width // 2, 4 * width
    lines = weights[0].shape[1]
    wide = 4 * part + 2 * weights[2].shape[1]
    chunks = tuple((which, a * part, b * part, over_x) for which, a, b, over_x in GATHER)
    count = len(chunks)
    listed = masked.shape[1]
    pairs = width // LOG_PAIR
    sem = pltpu.SemaphoreType.DMA
    vm = pltpu.VMEM
    return pl.pallas_call(
        partial(first_kernel, chunks),
        name="gather_forward",
        out_shape=[
            shape_of(2, 4, 2, 2, lines, 3 * part, kind=low),
            shape_of(length, width),
            shape_of(length, width, kind=low),
            shape_of(lines, wide),
            shape_of(12, width),
        ],
        in_specs=[ANY_SPEC] * 3 + [VMEM_SPEC] * 12,
        out_specs=[ANY_SPEC] * 3 + [VMEM_SPEC] * 2,
        scratch_shapes=[
            vm((12, width), f32),
            vm((12, width), f32),
            vm((12, width), f32),
            vm((length, width), low),
            vm((length, width), low),
            vm((2, 4, 2, 2, lines, wide), low),
            vm((4, 2, 2, lines, wide), low),
            vm((lines, wide), low),
            vm((lines, wide), low),
            vm((rows, width), low),
            vm((length, width), low),
            vm((length, width), low),
            vm((rows, width), low),
            vm((pairs, rows, LOG_PAIR), f32),
            vm((length, part), low),
            vm((length, part), low),
            vm((2, listed, width), low),
            vm((2, listed, width), low),
            vm((listed, width), f32),
            vm((4, 16, width), f32),
            vm((6, 16, width), f32),
            vm((rows, width), f32),
            vm((rows, width), low),
            vm((rows, hidden), low),
            vm((rows, hidden), low),
            vm((rows, width), f32),
            vm((rows, width), low),
            vm((width, rows), low),
            vm((width, rows), low),
            vm((width, rows), low),
            vm((rows, width), low),
            vm((2, 4, 2, lines, wide - 3 * part), low),
            vm((3, 2, lines, wide - 3 * part), low),
            vm((2, lines, wide), low),
            vm((lines, wide), low),
            sem((count,)), sem((count, 3)), sem((count, 3)), sem((count, 7)), sem((count, 7)),
            sem((2,)), sem((2,)), sem((16,)), sem((16,)), sem((10,)),
            sem((12, 2)), sem((12, 2)), sem((12, 3)), sem((12, 3)), sem((3, pairs)), sem((3, pairs)),
            sem((6,)), sem((6,)),
            pltpu.SemaphoreType.REGULAR, pltpu.SemaphoreType.REGULAR, pltpu.SemaphoreType.REGULAR,
        ],
        compiler_params=pltpu.CompilerParams(
            vmem_limit_bytes=FIRST_LIMIT, collective_id=number, has_side_effects=True
        ),
    )(x, tx, cot, vec, tvec, lengths, masked, *weights, *teacher)


def matrices(grad_ref, groups):
    attn, out, up, down = range(4)
    plan = [(0, attn, 0), (1, attn, 1), (2, attn, 2), (3, out, None), (4, up, None), (5, down, None)]
    at = 0
    for index, which, slot in plan:
        refs = [group[which] if slot is None else group[which].at[slot] for group in groups]
        size = refs[0].shape[-1]
        yield index, grad_ref[:, at : at + size], refs
        at += size


def norm_kernel(grad_ref, *rest):
    weights, firsts, seconds = rest[0:4], rest[4:8], rest[8:12]
    norm_o, terms_ref, sends, recvs = rest[12:]
    at, y, z, x, core = place()
    others = terms_ref.shape[0] - 1
    me = 2 * at + y

    def peer(step):
        there = (me + step) % (others + 1)
        return there // 2, there % 2

    barrier = pltpu.get_barrier_semaphore()

    def call(step, carry):
        pl.semaphore_signal(barrier, inc=1, device_id=peer(step), device_id_type=MESH)
        return carry

    lax.fori_loop(1, others + 1, call, 0)
    lane = lane_index((8, LOG_PAIR))
    row = lax.broadcasted_iota(jnp.int32, (8, LOG_PAIR), 0)
    squares = jnp.zeros((8, LOG_PAIR), f32)
    for index, grad, (w, first, second) in matrices(grad_ref, (weights, firsts, seconds)):
        unused, unused_too, step = adam_step(grad, first[...], second[...])
        for line, value in ((0, w[...]), (1, step + decay_rate * w[...])):
            total = jnp.sum(jnp.sum(value * value, -1, keepdims=True), 0, keepdims=True)
            squares = jnp.where((row == line) & (lane == index), total, squares)
    terms_ref[me] = squares
    pl.semaphore_wait(barrier, others)

    def send(step):
        return remote(terms_ref.at[me], terms_ref.at[me], sends, recvs, step - 1, peer(step))

    def begin(step, carry):
        send(step).start()
        return carry

    def landed(step, carry):
        came = terms_ref.at[(me + others + 1 - step) % (others + 1)]
        remote(came, came, sends, recvs, step - 1, peer(step)).wait_recv()
        return carry

    def left(step, carry):
        send(step).wait_send()
        return carry

    lax.fori_loop(1, others + 1, begin, 0)
    lax.fori_loop(1, others + 1, landed, 0)
    norms = jnp.sqrt(jnp.sum(terms_ref[...], 0))
    norm_o[...] = jnp.where(row == 2, norms[0:1, :] / norms[1:2, :], norms)
    lax.fori_loop(1, others + 1, left, 0)


def update_kernel(
    grad_ref, norm_ref, total_ref, vec_ref, vm_ref, vs_ref, student_hbm, input_hbm, *rest
):
    groups = [rest[i : i + 4] for i in range(0, 24, 4)]
    vm_o, vs_o, vec_o, norm_o, ratio_o, student_o, input_o = rest[24:31]
    student_ref, input_ref, copy_sem = rest[31:]
    passed = [(student_hbm, student_ref, student_o), (input_hbm, input_ref, input_o)]
    come = [pltpu.make_async_copy(a, b, copy_sem.at[i]) for i, (a, b, c) in enumerate(passed)]
    leave = [pltpu.make_async_copy(b, c, copy_sem.at[i]) for i, (a, b, c) in enumerate(passed)]
    for copy in come:
        copy.start()
    for index, grad, refs in matrices(grad_ref, groups):
        w, first, second, w_o, first_o, second_o = refs
        first_new, second_new, step = adam_step(grad, first[...], second[...])
        first_o[...] = first_new
        second_o[...] = second_new
        weight = w[...]
        ratio = norm_ref[2:3, index : index + 1]
        w_o[...] = weight - matrix_rate * ratio * (step + decay_rate * weight)
        if index == 3:
            for one, copy in zip(come, leave):
                one.wait()
                copy.start()
    width = total_ref.shape[1]
    for index in range(total_ref.shape[0]):
        here = pl.ds(index * width, width)
        first_new, second_new, step = adam_step(
            total_ref[index : index + 1, :],
            vm_ref[here].reshape(1, width),
            vs_ref[here].reshape(1, width),
        )
        vm_o[here] = first_new.reshape(width)
        vs_o[here] = second_new.reshape(width)
        vec_o[here] = vec_ref[here] - vector_rate * step.reshape(width)
    norm_o[...] = norm_ref[0:2, 0:6]
    ratio_o[...] = norm_ref[2:3, 0:6].reshape(6)
    for copy in leave:
        copy.wait()


def norm_call(grad, weights, firsts, seconds, number):
    sem = pltpu.SemaphoreType.DMA
    devices = lax.axis_size("dp") * lax.axis_size("mp")
    return pl.pallas_call(
        norm_kernel,
        name="norms",
        out_shape=shape_of(8, LOG_PAIR),
        in_specs=[VMEM_SPEC] * 13,
        out_specs=VMEM_SPEC,
        scratch_shapes=[
            pltpu.VMEM((devices, 8, LOG_PAIR), f32), sem((devices - 1,)), sem((devices - 1,))
        ],
        compiler_params=pltpu.CompilerParams(
            vmem_limit_bytes=LIMIT, collective_id=number, has_side_effects=True
        ),
    )(grad, *weights, *firsts, *seconds)


def update_call(grad, norms, total, vec, vm, vs, student, input_grad, weights, firsts, seconds):
    outs = [shape_of(*value.shape) for group in (weights, firsts, seconds) for value in group]
    outs += [shape_of(*vec.shape)] * 3 + [shape_of(2, 6), shape_of(6)]
    count = len(outs)
    outs += [shape_of(*student.shape, kind=low), shape_of(*input_grad.shape)]
    return pl.pallas_call(
        update_kernel,
        name="update",
        out_shape=outs,
        in_specs=[VMEM_SPEC] * 6 + [ANY_SPEC] * 2 + [VMEM_SPEC] * 12,
        out_specs=[VMEM_SPEC] * count + [ANY_SPEC] * 2,
        scratch_shapes=[
            pltpu.VMEM(student.shape, low),
            pltpu.VMEM(input_grad.shape, f32),
            pltpu.SemaphoreType.DMA((2,)),
        ],
        compiler_params=pltpu.CompilerParams(vmem_limit_bytes=LIMIT),
    )(grad, norms, total, vec, vm, vs, student, input_grad, *weights, *firsts, *seconds)


def split_kernels(
    tokens,
    teacher_tokens,
    cotangent,
    lengths,
    masked,
    attn_weight,
    out_weight,
    up_weight,
    down_weight,
    attn_first,
    out_first,
    up_first,
    down_first,
    attn_second,
    out_second,
    up_second,
    down_second,
    vectors,
    vector_first,
    vector_second,
    teacher_attn,
    teacher_out,
    teacher_up,
    teacher_down,
    teacher_vectors,
):
    def upright(group):
        return (group[0], group[1].T, group[2], group[3].T)

    weights = upright((attn_weight, out_weight, up_weight, down_weight))
    unused_wa, input_grad, student, grad, total = first_call(
        tokens[0],
        teacher_tokens[0],
        cotangent[0],
        vectors,
        teacher_vectors,
        lengths.reshape(1, 1),
        masked,
        weights,
        upright((teacher_attn, teacher_out, teacher_up, teacher_down)),
        0,
    )
    states = (
        weights,
        upright((attn_first, out_first, up_first, down_first)),
        upright((attn_second, out_second, up_second, down_second)),
    )
    norms = norm_call(grad, *states, 1)
    outs = update_call(
        grad, norms, total, vectors, vector_first, vector_second, student, input_grad, *states
    )
    return (
        outs[17][None],
        outs[18][None],
        *upright(outs[0:4]),
        *upright(outs[4:8]),
        *upright(outs[8:12]),
        *outs[12:17],
    )


def solution(mesh):
    local = split_kernels if dict(mesh.shape) == {"dp": 16, "mp": 2} else split_rows
    return jax.shard_map(
        local,
        mesh=mesh,
        in_specs=(
            P("dp", None, None),
            P("dp", None, None),
            P("dp", None, None),
            P("dp"),
            P("dp", None),
            P(None, "dp", "mp"),
            P("mp", "dp"),
            P("dp", "mp"),
            P("mp", "dp"),
            P(None, "dp", "mp"),
            P("mp", "dp"),
            P("dp", "mp"),
            P("mp", "dp"),
            P(None, "dp", "mp"),
            P("mp", "dp"),
            P("dp", "mp"),
            P("mp", "dp"),
            P(),
            P(),
            P(),
            P(None, "dp", "mp"),
            P("mp", "dp"),
            P("dp", "mp"),
            P("mp", "dp"),
            P(),
        ),
        out_specs=(
            P("dp", None, None),
            P("dp", None, None),
            P(None, "dp", "mp"),
            P("mp", "dp"),
            P("dp", "mp"),
            P("mp", "dp"),
            P(None, "dp", "mp"),
            P("mp", "dp"),
            P("dp", "mp"),
            P("mp", "dp"),
            P(None, "dp", "mp"),
            P("mp", "dp"),
            P("dp", "mp"),
            P("mp", "dp"),
            P(),
            P(),
            P(),
            P(),
            P(),
        ),
        check_vma=False,
    )
```

```python
from functools import partial

import jax
import jax.numpy as jnp
from jax import lax
from jax.experimental import pallas as pl
from jax.experimental.pallas import tpu as pltpu
from jax.sharding import PartitionSpec as P

HDIM = 64
STEP = 5


beta_one = 0.9
beta_two = 0.999
adam_eps = 1e-06
decay_rate = 0.01
matrix_rate = 0.3
vector_rate = 0.2
cosine_weight = 32.0
cosine_eps = 1e-06
layer_eps = 1e-12
masked_score = -1e30


def layer_norm(row_values, gain_vec, shift_vec):
    center = row_values - jnp.mean(row_values, -1, keepdims=True)
    spread = jnp.mean(center * center, -1, keepdims=True)
    return center * lax.rsqrt(spread + layer_eps) * gain_vec + shift_vec


def vector_parts(packed, model_width):
    pieces = [
        packed[position * model_width : (position + 1) * model_width] for position in range(8)
    ]
    return pieces + [packed[8 * model_width :]]


def head_scores(query, key_rows, visible):
    scale_factor = query.shape[-1] ** (-0.5)
    scores = (
        jnp.einsum("sqe,ske->sqk", query, key_rows, preferred_element_type=jnp.float32)
        * scale_factor
    )
    return jnp.where(visible[:, None, :], scores, masked_score)


def head_forward(query, key_rows, value_rows, visible):
    scores = head_scores(query, key_rows, visible)
    row_peak = jnp.max(scores, -1, keepdims=True)
    exponent = jnp.exp(scores - row_peak)
    row_total = jnp.sum(exponent, -1, keepdims=True)
    weights_low = (exponent / row_total).astype(jnp.bfloat16)
    mixed = jnp.einsum("sqk,ske->sqe", weights_low, value_rows, preferred_element_type=jnp.float32)
    return (mixed.astype(jnp.bfloat16), (row_peak + jnp.log(row_total))[..., 0])


def adam_moments(grad_now, first_old, second_old):
    first_new = beta_one * first_old + (1.0 - beta_one) * grad_now
    second_new = beta_two * second_old + (1.0 - beta_two) * grad_now * grad_now
    step_now = (
        first_new
        / (1.0 - beta_one**STEP)
        / (jnp.sqrt(second_new / (1.0 - beta_two**STEP)) + adam_eps)
    )
    return (first_new, second_new, step_now)


def matrix_squares(attn_w, out_w, up_w, down_w):
    return jnp.concatenate(
        [
            jnp.sum(attn_w * attn_w, axis=(1, 2)),
            jnp.stack([jnp.sum(out_w * out_w), jnp.sum(up_w * up_w), jnp.sum(down_w * down_w)]),
        ]
    )


def shard_pack(attn_w, out_w, up_w, down_w):
    return jnp.concatenate(
        [attn_w[0], attn_w[1], attn_w[2], out_w.T, up_w, down_w.T], axis=1
    )


def cosine_pull(rows, places, aimed, row_start):
    row_count = rows.shape[0]
    local_at = places - row_start
    here = (local_at >= 0) & (local_at < row_count)
    picked = rows[jnp.clip(local_at, 0, row_count - 1)]
    inner = jnp.sum(picked * aimed, -1, keepdims=True)
    square_own = jnp.sum(picked * picked, -1, keepdims=True) + cosine_eps
    square_aim = jnp.sum(aimed * aimed, -1, keepdims=True) + cosine_eps
    inverse = lax.rsqrt(square_own) * lax.rsqrt(square_aim)
    pull = -cosine_weight * (aimed * inverse - picked * (inner * inverse / square_own))
    pull = jnp.where(here[:, None], pull, 0.0)
    return jnp.zeros_like(rows).at[jnp.clip(local_at, 0, row_count - 1)].add(pull)


def heads_of(flat):
    return flat.reshape(flat.shape[0], flat.shape[1] // HDIM, HDIM).transpose(1, 0, 2)


def flat_of(split):
    return split.transpose(1, 0, 2).reshape(split.shape[1], -1)


def dot32(left, right):
    return jnp.dot(left, right, preferred_element_type=jnp.float32)


def dot_nt(left, right):
    return lax.dot_general(
        left, right, (((1,), (1,)), ((), ())), preferred_element_type=jnp.float32
    )


def dot_tn(left, right):
    return lax.dot_general(
        left, right, (((0,), (0,)), ((), ())), preferred_element_type=jnp.float32
    )


def split_rows(
    tokens,
    teacher_tokens,
    cotangent,
    lengths,
    masked,
    attn_weight,
    out_weight,
    up_weight,
    down_weight,
    attn_first,
    out_first,
    up_first,
    down_first,
    attn_second,
    out_second,
    up_second,
    down_second,
    vectors,
    vector_first,
    vector_second,
    teacher_attn,
    teacher_out,
    teacher_up,
    teacher_down,
    teacher_vectors,
):
    low = jnp.bfloat16
    everyone = ("dp", "mp")
    shard_at = lax.axis_index("mp")
    halves = lax.axis_size("mp")
    seq_count, length, width = tokens.shape
    rows = length // halves
    row_start = shard_at * rows
    part = attn_weight.shape[2]
    units = up_weight.shape[1]
    cuts = [0, part, 2 * part, 3 * part, 4 * part, 4 * part + units, 4 * part + 2 * units]
    visible = (jnp.arange(length) < lengths[0])[None, None, :]
    places = masked[0]

    student = lax.all_gather(
        shard_pack(attn_weight, out_weight, up_weight, down_weight).astype(low),
        ("mp", "dp"),
        axis=0,
        tiled=True,
    ).reshape(halves, width, cuts[6])
    teacher = lax.all_gather(
        shard_pack(teacher_attn, teacher_out, teacher_up, teacher_down),
        "dp",
        axis=0,
        tiled=True,
    )

    def whole(index):
        return jnp.concatenate(
            [student[half, :, cuts[index] : cuts[index + 1]] for half in range(halves)], axis=1
        )

    teacher_parts = vector_parts(teacher_vectors.astype(jnp.float32), width)
    bias_q = lax.dynamic_slice_in_dim(teacher_parts[0], shard_at * part, part)
    bias_v = lax.dynamic_slice_in_dim(teacher_parts[1], shard_at * part, part)
    bias_up = lax.dynamic_slice_in_dim(teacher_parts[8], shard_at * units, units)
    teacher_rows = teacher_tokens[0]
    listed = teacher_rows[places]
    t_query = (dot32(listed, teacher[:, : cuts[1]]) + bias_q).astype(low)
    t_keys = dot32(teacher_rows, teacher[:, cuts[1] : cuts[2]]).astype(low)
    t_values = (dot32(teacher_rows, teacher[:, cuts[2] : cuts[3]]) + bias_v).astype(low)
    t_mixed, unused_log = head_forward(
        heads_of(t_query), heads_of(t_keys), heads_of(t_values), visible[0]
    )
    t_branch = lax.psum(dot_nt(flat_of(t_mixed), teacher[:, cuts[3] : cuts[4]]), "mp")
    t_first = listed.astype(jnp.float32) + t_branch + teacher_parts[2]
    t_normed = layer_norm(t_first, teacher_parts[3], teacher_parts[4])
    t_gate = dot32(t_normed.astype(low), teacher[:, cuts[4] : cuts[5]]) + bias_up
    t_act = jax.nn.gelu(t_gate, approximate=False).astype(low)
    t_feed = lax.psum(dot_nt(t_act, teacher[:, cuts[5] : cuts[6]]), "mp")
    aimed = layer_norm(t_normed + t_feed + teacher_parts[5], teacher_parts[6], teacher_parts[7])

    pieces = vector_parts(vectors, width)
    all_rows = tokens[0]
    own_rows = lax.dynamic_slice_in_dim(all_rows, row_start, rows, 0)
    w_q, w_k, w_v, w_out, w_up, w_down = [whole(index) for index in range(6)]
    query = heads_of((dot32(own_rows, w_q) + pieces[0]).astype(low))
    keys = heads_of(dot32(all_rows, w_k).astype(low))
    values = heads_of((dot32(all_rows, w_v) + pieces[1]).astype(low))
    mixed, log_total = lax.map(
        lambda g: jax.tree.map(
            lambda v: v[0], head_forward(g[0][None], g[1][None], g[2][None], visible[0])
        ),
        (query, keys, values),
    )
    attended = flat_of(mixed)
    first_sum = own_rows.astype(jnp.float32) + dot_nt(attended, w_out) + pieces[2]
    normed = layer_norm(first_sum, pieces[3], pieces[4])
    normed_low = normed.astype(low)
    gate_in = dot32(normed_low, w_up) + pieces[8]
    activated = jax.nn.gelu(gate_in, approximate=False).astype(low)
    second_sum = normed + dot_nt(activated, w_down) + pieces[5]
    outcome = layer_norm(second_sum, pieces[6], pieces[7])
    student_out = lax.all_gather(outcome.astype(low), "mp", axis=0, tiled=True)[None]

    own_cotangent = lax.dynamic_slice_in_dim(cotangent[0], row_start, rows, 0)
    grad_top = own_cotangent.astype(jnp.float32) + cosine_pull(outcome, places, aimed, row_start)
    unused_top, pull_top = jax.vjp(layer_norm, second_sum, pieces[6], pieces[7])
    grad_second, grad_gain_two, grad_shift_two = pull_top(grad_top)
    feed_low = grad_second.astype(low)
    grad_down = dot_tn(feed_low, activated)
    grad_act = dot32(feed_low, w_down)
    unused_gelu, pull_gelu = jax.vjp(partial(jax.nn.gelu, approximate=False), gate_in)
    (grad_gate,) = pull_gelu(grad_act)
    gate_low = grad_gate.astype(low)
    grad_up = dot_tn(normed_low, gate_low)
    grad_normed = grad_second + dot_nt(gate_low, w_up)
    unused_mid, pull_mid = jax.vjp(layer_norm, first_sum, pieces[3], pieces[4])
    grad_first, grad_gain_one, grad_shift_one = pull_mid(grad_normed)
    branch_low = grad_first.astype(low)
    grad_out = dot_tn(branch_low, attended)
    grad_heads = heads_of(dot32(branch_low, w_out).astype(low))

    def one_head(g):
        query_h, keys_h, values_h, mixed_h, log_h = g
        scale_factor = HDIM**-0.5
        scores = jnp.where(visible[0], dot_nt(query_h, keys_h) * scale_factor, masked_score)
        probs = jnp.exp(scores - log_h[:, None])
        grad_probs = dot_nt(mixed_h, values_h)
        inner = jnp.sum(probs * grad_probs, -1, keepdims=True)
        grad_scores = (probs * (grad_probs - inner)).astype(low)
        return (
            (dot32(grad_scores, keys_h) * scale_factor).astype(low),
            (dot_tn(grad_scores, query_h) * scale_factor).astype(low),
            dot_tn(probs.astype(low), mixed_h).astype(low),
        )

    grad_query, grad_keys, grad_values = lax.map(
        one_head, (query, keys, values, grad_heads, log_total)
    )
    grad_query = flat_of(grad_query)

    def row_sum(term):
        other = lax.dynamic_slice_in_dim(term, (1 - shard_at) * rows, rows, 0)
        mine = lax.dynamic_slice_in_dim(term, row_start, rows, 0)
        came = lax.ppermute(other, "mp", [(0, 1), (1, 0)])
        return (mine.astype(jnp.float32) + came.astype(jnp.float32)).astype(low)

    grad_keys = row_sum(flat_of(grad_keys))
    grad_values = row_sum(flat_of(grad_values))
    grad_q = dot_tn(own_rows, grad_query)
    grad_k = dot_tn(own_rows, grad_keys)
    grad_v = dot_tn(own_rows, grad_values)
    input_own = (
        grad_first + dot_nt(grad_query, w_q) + dot_nt(grad_keys, w_k) + dot_nt(grad_values, w_v)
    )
    input_grad = lax.all_gather(input_own, "mp", axis=0, tiled=True)[None]

    def half_of(matrix, half):
        span = matrix.shape[1] // halves
        return matrix[:, half * span : (half + 1) * span]

    grads = [grad_q, grad_k, grad_v, grad_out, grad_up, grad_down]
    packed_grad = jnp.concatenate(
        [
            jnp.concatenate([half_of(g, half) for g in grads], axis=1).astype(low)
            for half in range(halves)
        ],
        axis=0,
    )
    summed = lax.psum_scatter(
        packed_grad, ("mp", "dp"), scatter_dimension=0, tiled=True
    ).astype(jnp.float32)
    summed_attn = jnp.stack([summed[:, cuts[i] : cuts[i + 1]] for i in range(3)])
    summed_out = summed[:, cuts[3] : cuts[4]].T
    summed_up = summed[:, cuts[4] : cuts[5]]
    summed_down = summed[:, cuts[5] : cuts[6]].T

    vector_grad = jnp.concatenate(
        [
            jnp.sum(grad_query.astype(jnp.float32), 0),
            jnp.sum(grad_values.astype(jnp.float32), 0),
            jnp.sum(branch_low.astype(jnp.float32), 0),
            grad_gain_one,
            grad_shift_one,
            jnp.sum(feed_low.astype(jnp.float32), 0),
            grad_gain_two,
            grad_shift_two,
            jnp.sum(gate_low.astype(jnp.float32), 0),
        ]
    )
    return (student_out, input_grad) + lamb_update(
        (summed_attn, summed_out, summed_up, summed_down),
        (attn_weight, out_weight, up_weight, down_weight),
        (attn_first, out_first, up_first, down_first),
        (attn_second, out_second, up_second, down_second),
        vector_grad,
        vectors,
        vector_first,
        vector_second,
    )


def lamb_update(grads, weights, firsts, seconds, vector_grad, vectors, vector_first, vector_second):
    moments, squares, steps = [], [], []
    for grad_now, weight, first_old, second_old in zip(grads, weights, firsts, seconds):
        first_new, second_new, step_now = adam_moments(grad_now, first_old, second_old)
        moments.append(first_new)
        squares.append(second_new)
        steps.append(step_now + decay_rate * weight)
    weight_total, update_total, vector_total = lax.psum(
        (matrix_squares(*weights), matrix_squares(*steps), vector_grad), ("dp", "mp")
    )
    weight_norms = jnp.sqrt(weight_total)
    update_norms = jnp.sqrt(update_total)
    trust_ratio = weight_norms / update_norms
    ratios = [trust_ratio[0:3][:, None, None], trust_ratio[3], trust_ratio[4], trust_ratio[5]]
    updated = [
        weight - matrix_rate * ratio * step for weight, ratio, step in zip(weights, ratios, steps)
    ]
    vector_moment, vector_square, step_vector = adam_moments(
        vector_total, vector_first, vector_second
    )
    vector_updated = vectors - vector_rate * step_vector
    return (
        *updated,
        *moments,
        *squares,
        vector_moment,
        vector_square,
        vector_updated,
        jnp.stack([weight_norms, update_norms]),
        trust_ratio,
    )


LOG_PAIR = 128
MESH = pl.DeviceIdType.MESH
low = jnp.bfloat16
f32 = jnp.float32
VMEM_SPEC = pl.BlockSpec(memory_space=pltpu.VMEM)
ANY_SPEC = pl.BlockSpec(memory_space=pl.ANY)
AHEAD = 2
LEAD = 1
GATHER = (
    (0, 0, 1, 0), (0, 1, 2, 0), (0, 2, 3, 0), (1, 0, 2, 0), (1, 2, 4, 0), (0, 3, 4, 0), (1, 4, 6, 0),
    (0, 4, 6, 0), (1, 6, 8, 0), (0, 6, 8, 0), (1, 8, 10, 0), (1, 10, 12, 0), (0, 8, 10, 0), (0, 10, 12, 1),
)
FIRST_LIMIT = 64 * 2**20
LIMIT = 60 * 2**20


def dnn(left, right):
    return jnp.dot(left, right, preferred_element_type=f32)


def dnt(left, right):
    return lax.dot_general(left, right, (((1,), (1,)), ((), ())), preferred_element_type=f32)


def lane_index(shape):
    return lax.broadcasted_iota(jnp.int32, shape, 1)


def split_three(value):
    top = value.astype(low).astype(f32)
    rest = value - top
    middle = rest.astype(low).astype(f32)
    return (top, middle, rest - middle)


def flip(value):
    return value.astype(f32).T.astype(low)


def place():
    at = lax.axis_index("dp")
    return (at, lax.axis_index("mp"), at // 4, (at // 2) % 2, at % 2)


def near():
    at, y, z, x, core = place()
    return dict(
        twin=(at + 1 - 2 * core, y),
        x=(at + 2 - 4 * x, y),
        y=(at, 1 - y),
        z=[(((z + step) % 4) * 4 + 2 * x + core, y) for step in (1, 2, 3)],
        za=((z + 1 - 2 * (z % 2)) * 4 + 2 * x + core, y),
        zb=((z + 2 - 4 * (z // 2)) * 4 + 2 * x + core, y),
    )


def greet(peers):
    sem = pltpu.get_barrier_semaphore()
    for peer in peers:
        pl.semaphore_signal(sem, inc=1, device_id=peer, device_id_type=MESH)
    return lambda: pl.semaphore_wait(sem, len(peers))


def vector_rows(flat_ref, rows_ref):
    width = rows_ref.shape[1]
    for index in range(rows_ref.shape[0]):
        row = flat_ref[pl.ds(index * width, width)].reshape(1, width)
        rows_ref[index : index + 1, :] = row.astype(f32)


def remote(src, dst, sends, recvs, at, peer):
    return pltpu.make_async_remote_copy(
        src_ref=src,
        dst_ref=dst,
        send_sem=sends.at[at],
        recv_sem=recvs.at[at],
        device_id=peer,
        device_id_type=MESH,
    )


def row_norm(rows):
    center = rows - jnp.mean(rows, -1, keepdims=True)
    scale = lax.rsqrt(jnp.mean(center * center, -1, keepdims=True) + layer_eps)
    return (center * scale, scale)


def norm_pull(grad, unit, scale, gain):
    lifted = grad * gain
    return scale * (
        lifted
        - jnp.mean(lifted, -1, keepdims=True)
        - unit * jnp.mean(lifted * unit, -1, keepdims=True)
    )


def normal_share(value):
    return 0.5 * (1.0 + lax.erf(value * 0.7071067811865476))


def pair_forward(query, keys, values, bias):
    count, span = query.shape[0], keys.shape[0]
    lane_q, lane_k = lane_index((count, LOG_PAIR)), lane_index((span, LOG_PAIR))
    outs, logs = [], []
    for head in range(2):
        spare = HDIM * (1 - head)
        keys_now = jnp.where(
            lane_k // HDIM == head,
            keys.astype(f32),
            jnp.where(lane_k == spare, bias, 0.0),
        ).astype(low)
        query_now = jnp.where(
            lane_q // HDIM == head,
            query.astype(f32),
            jnp.where(lane_q == spare, 1.0, 0.0),
        ).astype(low)
        scores = dnt(query_now, keys_now)
        peak = jnp.max(scores, -1, keepdims=True)
        exponent = jnp.exp(scores - peak)
        total = jnp.sum(exponent, -1, keepdims=True)
        outs.append(dnn((exponent * (1.0 / total)).astype(low), values))
        logs.append(peak + jnp.log(total))
    return (
        jnp.where(lane_q < HDIM, outs[0], outs[1]),
        jnp.where(lane_q < HDIM, logs[0], logs[1]),
    )


def shape_of(*dims, kind=f32):
    return jax.ShapeDtypeStruct(dims, kind)


def pair_back_rows(query, grad_mixed, mixed, logs):
    lane_q = lane_index(query.shape)
    query_wide, grad_wide = query.astype(f32), grad_mixed.astype(f32)
    product = grad_wide * mixed.astype(f32)
    sides = []
    for head in range(2):
        spare = HDIM * (1 - head)
        own_q = lane_q // HDIM == head
        inner = jnp.sum(jnp.where(own_q, product, 0.0), -1, keepdims=True)
        query_now = jnp.where(own_q, query_wide, jnp.where(lane_q == spare, 1.0, 0.0))
        grad_now = jnp.where(own_q, grad_wide, 0.0)
        for place_at, (log_term, inner_term) in enumerate(
            zip(split_three(logs[:, HDIM * head : HDIM * head + 1]), split_three(inner))
        ):
            here = lane_q == spare + 1 + place_at
            query_now = jnp.where(here, log_term, query_now)
            grad_now = jnp.where(here, inner_term, grad_now)
        sides.append((query_now.astype(low), grad_now.astype(low)))
    return sides


def pair_back_keys(query, grad_mixed, sides, keys, values, bias):
    lane_k = lane_index(keys.shape)
    keys_wide, values_wide = keys.astype(f32), values.astype(f32)
    grad_keys, grad_values, grad_query = [], [], []
    for head, (query_now, grad_now) in enumerate(sides):
        spare = HDIM * (1 - head)
        own_k = lane_k // HDIM == head
        minus = jnp.where((lane_k > spare) & (lane_k < spare + 4), -1.0, 0.0)
        keys_now = jnp.where(own_k, keys_wide, jnp.where(lane_k == spare, bias, minus)).astype(low)
        values_now = jnp.where(own_k, values_wide, minus).astype(low)
        probs = jnp.exp(dnt(keys_now, query_now))
        grad_scores = (probs * dnt(values_now, grad_now)).astype(low)
        grad_keys.append(dnn(grad_scores, query))
        grad_values.append(dnn(probs.astype(low), grad_mixed))
        flipped = keys_wide.T[HDIM * head : HDIM * (head + 1)].astype(low)
        grad_query.append(dnn(flipped, grad_scores))
    return (
        jnp.concatenate(grad_query, 0),
        jnp.where(lane_k < HDIM, grad_keys[0], grad_keys[1]),
        jnp.where(lane_k < HDIM, grad_values[0], grad_values[1]),
    )


def adam_step(grad, first, second):
    first_new = beta_one * first + (1.0 - beta_one) * grad
    second_new = beta_two * second + (1.0 - beta_two) * grad * grad
    step = (
        first_new
        / (1.0 - beta_one**STEP)
        / (jnp.sqrt(second_new / (1.0 - beta_two**STEP)) + adam_eps)
    )
    return (first_new, second_new, step)


def block_of(ref, cols):
    value = ref[:, :, :, :, cols]
    return value.reshape(-1, value.shape[-1])


def gather_steps(chunks, gs_ref, gt_ref, ps_ref, pt_ref, local_sem, zsends, zrecvs, sends, recvs, started):
    at, y, z, x, core = place()
    ways = near()

    def go(ref, chunk, kind, peer):
        copy = remote(ref, ref, sends, recvs, (chunk, kind), peer)
        copy.start()
        started.append(copy)

    def landed(ref, chunk, kind):
        remote(ref, ref, sends, recvs, (chunk, kind), ways["x"]).wait_recv()

    def shard(chunk, zz):
        which, a, b, unused = chunks[chunk]
        if which == 0:
            return gs_ref.at[y, zz, x, core, :, pl.ds(a, b - a)]
        return gt_ref.at[zz, x, core, :, pl.ds(a, b - a)]

    def column(chunk, yy, xx, cc):
        which, a, b, unused = chunks[chunk]
        if which == 0:
            return gs_ref.at[yy, :, xx, cc, :, pl.ds(a, b - a)]
        return gt_ref.at[:, xx, cc, :, pl.ds(a, b - a)]

    own = []
    near_z, far_z = z + 1 - 2 * (z % 2), z + 2 - 4 * (z // 2)
    last_z = near_z + 2 - 4 * (near_z // 2)

    def send_z(source, target, k, kind, way):
        copy = remote(source, target, zsends, zrecvs, (k, kind), ways[way])
        copy.start()
        started.append(copy)

    def landed_z(k, zz, kind):
        came = shard(k, zz)
        remote(came, came, zsends, zrecvs, (k, kind), ways["x"]).wait_recv()

    def begin(k):
        which, a, b, unused = chunks[k]
        source = (ps_ref, pt_ref)[which].at[:, pl.ds(a, b - a)]
        copy = pltpu.make_async_copy(source, shard(k, z), local_sem.at[k])
        copy.start()
        own.append(copy)
        send_z(source, shard(k, z), k, 0, "zb")
        send_z(source, shard(k, z), k, 1, "za")

    def hand_on(k):
        landed_z(k, far_z, 0)
        send_z(shard(k, far_z), shard(k, far_z), k, 2, "za")

    def along_z(k):
        landed_z(k, near_z, 1)
        landed_z(k, last_z, 2)
        own[k].wait()
        go(column(k, y, x, core), k, 0, ways["x"])
        if chunks[k][0] == 0:
            go(column(k, y, x, core), k, 1, ways["y"])
        go(column(k, y, x, core), k, 2, ways["twin"])

    def from_sides(k):
        landed(column(k, y, 1 - x, core), k, 0)
        if chunks[k][0] == 0 and not chunks[k][3]:
            go(column(k, y, 1 - x, core), k, 3, ways["y"])
        go(column(k, y, 1 - x, core), k, 4, ways["twin"])
        if chunks[k][0] == 0:
            landed(column(k, 1 - y, x, core), k, 1)
            if chunks[k][3]:
                go(column(k, 1 - y, x, core), k, 3, ways["x"])
            go(column(k, 1 - y, x, core), k, 5, ways["twin"])

    def last(k):
        if chunks[k][0] == 0:
            landed(column(k, 1 - y, 1 - x, core), k, 3)
            go(column(k, 1 - y, 1 - x, core), k, 6, ways["twin"])

    def whole(k):
        landed(column(k, y, x, 1 - core), k, 2)
        landed(column(k, y, 1 - x, 1 - core), k, 4)
        if chunks[k][0] == 0:
            landed(column(k, 1 - y, x, 1 - core), k, 5)
            landed(column(k, 1 - y, 1 - x, 1 - core), k, 6)

    count = len(chunks)
    for k in range(AHEAD + LEAD):
        begin(k)
    for k in range(LEAD + 1):
        hand_on(k)
    for k in range(LEAD):
        along_z(k)
    for slot in range(count + 2):
        if slot + LEAD + AHEAD < count:
            begin(slot + LEAD + AHEAD)
        if slot + LEAD + 1 < count:
            hand_on(slot + LEAD + 1)
        if slot + LEAD < count:
            along_z(slot + LEAD)
        if slot < count:
            from_sides(slot)
        if 0 <= slot - 1 < count:
            last(slot - 1)
        if 0 <= slot - 2 < count:
            whole(slot - 2)
        yield max(0, slot - 1)


def sum_steps(chunks, given, ax_at, h_at, zr_at, before_x, before_z, tot_ref, own_ref, yr_ref, sends, recvs, zsends, zrecvs, started):
    at, y, z, x, core = place()
    ways = near()
    count = len(chunks)

    def span(k):
        a, b = chunks[k]
        return pl.ds(a, b - a)

    def begin(k):
        if k in before_x:
            before_x[k]()
        copy = remote(given(k, 1 - x), ax_at(k), sends, recvs, (k, 0), ways["x"])
        copy.start()
        started.append(copy)

    def over_x(k):
        remote(ax_at(k), ax_at(k), sends, recvs, (k, 0), ways["x"]).wait_recv()
        came = ax_at(k)

        def add(step, carry):
            yy, zz = step // 4, step % 4
            block = h_at(k, yy, zz)
            block[...] = (block[...].astype(f32) + came[yy, zz].astype(f32)).astype(low)
            return carry

        lax.fori_loop(0, 8, add, 0)
        if k in before_z:
            before_z[k]()
        for step in range(3):
            copy = remote(
                h_at(k, slice(None), (z + 1 + step) % 4), zr_at(k, step),
                zsends, zrecvs, (k, step), ways["z"][step],
            )
            copy.start()
            started.append(copy)

    def over_z(k):
        here = span(k)
        for step in range(3):
            came = zr_at(k, step)
            remote(came, came, zsends, zrecvs, (k, step), ways["x"]).wait_recv()
        for yy in range(2):
            total = h_at(k, yy, z)[...].astype(f32)
            for step in range(3):
                total += zr_at(k, step)[yy].astype(f32)
            tot_ref[yy, :, here] = total.astype(low)
        copy = remote(
            tot_ref.at[1 - y, :, here], yr_ref.at[:, here], sends, recvs, (k, 1), ways["y"]
        )
        copy.start()
        started.append(copy)

    def over_y(k):
        here = span(k)
        came = yr_ref.at[:, here]
        remote(came, came, sends, recvs, (k, 1), ways["y"]).wait_recv()
        own_ref[:, here] = tot_ref[y, :, here].astype(f32) + yr_ref[:, here].astype(f32)

    def steps():
        for slot in range(count + 2):
            if slot < count:
                over_x(slot)
            if 0 <= slot - 1 < count:
                over_z(slot - 1)
            if 0 <= slot - 2 < count:
                over_y(slot - 2)
            yield max(0, slot - 1)

    return begin, steps()


def shared_steps(value, result, mine_at, come_at, sends, recvs):
    at, y, z, x, core = place()
    ways = near()
    for index, way in enumerate(("twin", "x", "y")):
        mine_at(index)[...] = value
        copy = remote(mine_at(index), come_at(index), sends, recvs, index, ways[way])
        copy.start()
        yield
        copy.wait()
        value = mine_at(index)[...] + come_at(index)[...]
    mine_at(3)[...] = value
    copies = []
    for step in range(3):
        copy = remote(
            mine_at(3), come_at(3 + step), sends, recvs, 3 + step, ways["z"][step]
        )
        copy.start()
        copies.append(copy)
    yield
    for copy in copies:
        copy.wait()
    terms = [mine_at(3)[...]] + [come_at(3 + step)[...] for step in range(3)]
    total = None
    for z_from in range(4):
        term = terms[0]
        for step in range(1, 4):
            term = jnp.where((z + 4 - step) % 4 == z_from, terms[step], term)
        total = term if total is None else total + term
    result.append(total)


def first_kernel(
    chunks,
    x_hbm, tx_hbm, cot_hbm, vec_flat, tvec_flat, length_ref, places_ref,
    aw, ow, uw, dw, ta, to, tu, td,
    wa_hbm, input_hbm, student_hbm, total_ref, vector_ref,
    sums_ref, vec_ref, tvec_ref, x_ref, tx_ref, gs_ref, gt_ref, ps_ref, pt_ref, q_ref, k_ref,
    v_ref, a_ref, log_ref, tk_ref, tv_ref, part_ref, come_ref, aimed_ref, vmine_ref, vcome_ref,
    r1_ref, normed_ref, u_ref, slope_ref, r2_ref,
    cot_ref, flip_ref, nflip_ref, bflip_ref, ga_ref, one_ref, zr_ref, tot_ref, yr_ref,
    local_sem, zsends, zrecvs, sends, recvs, tsends, trecvs, gsends, grecvs, copy_sem,
    fsends, frecvs, fzsends, fzrecvs, ksends, krecvs, vsends, vrecvs,
    free_x, free_z, free_twin,
):
    at, y, z, x, core = place()
    ways = near()
    length, width = x_ref.shape
    rows = length // 2
    part = width // 2
    own = pl.ds(pl.multiple_of(y * rows, rows), rows)
    kept = []

    def keep(src, dst):
        copy = pltpu.make_async_copy(src, dst, copy_sem.at[len(kept)])
        copy.start()
        kept.append(copy)
        return copy

    met = greet([ways["twin"], ways["x"], ways["y"]] + ways["z"])
    x_copy, tx_copy = keep(x_hbm, x_ref), keep(tx_hbm, tx_ref)
    for index in range(3):
        ps_ref[:, index * part : (index + 1) * part] = aw[index].astype(low)
        pt_ref[:, index * part : (index + 1) * part] = ta[index]
    for base, source, aim in ((3 * part, ow, to), (4 * part, uw, tu), (8 * part, dw, td)):
        ps_ref[:, base : base + source.shape[1]] = source[...].astype(low)
        pt_ref[:, base : base + source.shape[1]] = aim[...]
    met()
    started = []
    steps = gather_steps(
        chunks, gs_ref, gt_ref, ps_ref, pt_ref, local_sem, zsends, zrecvs, sends, recvs, started
    )
    ready = [0]

    def tick():
        ready[0] = next(steps, len(chunks))

    def need(chunk):
        while ready[0] <= chunk:
            tick()

    cot_copy = keep(cot_hbm.at[own], cot_ref)

    def key_bias():
        row_at = lax.broadcasted_iota(jnp.int32, (length, LOG_PAIR), 0)
        return jnp.where(row_at < length_ref[0:1, 0:1], 0.0, masked_score)

    sums_ref[...] = jnp.zeros(sums_ref.shape, f32)

    def loop(count, body):
        def step(index, carry):
            body(index)
            return carry

        lax.fori_loop(0, count, step, 0)

    def span(index, block):
        if isinstance(index, int):
            return slice(index * block, (index + 1) * block)
        return pl.ds(pl.multiple_of(index * block, block), block)

    def whole(which, end):
        need(max(k for k, chunk in enumerate(chunks) if chunk[0] == which and chunk[2] <= end))

    tick()
    vector_rows(vec_flat, vec_ref)
    vector_rows(tvec_flat, tvec_ref)
    x_copy.wait()
    tx_copy.wait()
    whole(0, 3 * part)
    wa_copy = keep(gs_ref.at[:, :, :, :, :, pl.ds(0, 3 * part)], wa_hbm)

    def keys_values(index):
        here = span(index, 256)
        for half in range(2):
            cols = slice(half * part, (half + 1) * part)
            k_ref[here, cols] = dnn(
                x_ref[here, :], block_of(gs_ref.at[half], slice(part, 2 * part))
            ).astype(low)
            v_ref[here, cols] = (
                dnn(x_ref[here, :], block_of(gs_ref.at[half], slice(2 * part, 3 * part)))
                + vec_ref[1:2, cols]
            ).astype(low)

    def queries(index):
        here = span(index, 256)
        from_x = pl.ds(pl.multiple_of(y * rows + index * 256, 256), 256)
        for half in range(2):
            cols = slice(half * part, (half + 1) * part)
            value = dnn(x_ref[from_x, :], block_of(gs_ref.at[half], slice(0, part)))
            value = (value + vec_ref[0:1, cols]).astype(low).astype(f32) * HDIM**-0.5
            q_ref[here, cols] = value.astype(low)

    def attend(first):
        def one_pair(index):
            pair = first + index
            cols = pl.ds(pl.multiple_of(pair * LOG_PAIR, LOG_PAIR), LOG_PAIR)
            keys, values, bias = k_ref[:, cols], v_ref[:, cols], key_bias()
            for start in range(0, rows, 256):
                here = slice(start, start + 256)
                mixed, logs = pair_forward(q_ref[here, cols], keys, values, bias)
                a_ref[here, cols] = mixed.astype(low)
                log_ref[pair, here, :] = logs

        return one_pair

    for first in range(0, length // 256, 2):
        loop(2, lambda index, first=first: keys_values(first + index))
        tick()
    loop(rows // 256, queries)
    for pair in range(width // LOG_PAIR):
        tick()
        loop(1, attend(pair))

    whole(1, 3 * part)
    mine = pl.ds(pl.multiple_of(y * part, LOG_PAIR), part)
    count = places_ref.shape[1]

    def teacher_keys(index):
        here = span(index, 256)
        tk_ref[here, :] = dnn(tx_ref[here, :], block_of(gt_ref, slice(part, 2 * part))).astype(low)
        tv_ref[here, :] = (
            dnn(tx_ref[here, :], block_of(gt_ref, slice(2 * part, 3 * part))) + tvec_ref[1:2, mine]
        ).astype(low)

    loop(length // 256, teacher_keys)
    whole(1, 4 * part)
    diagonal = lax.broadcasted_iota(jnp.int32, (count, count), 0) == lane_index((count, count))
    places = jnp.where(diagonal, places_ref[...].astype(f32), 0.0)
    places = jnp.sum(places, -1, keepdims=True).astype(jnp.int32)
    pick = jnp.where(places == lane_index((count, length)), 1.0, 0.0).astype(low)
    listed = dnn(pick, tx_ref[...])
    query = dnn(listed.astype(low), block_of(gt_ref, slice(0, part))) + tvec_ref[0:1, mine]
    query = (query.astype(low).astype(f32) * HDIM**-0.5).astype(low)
    branch = jnp.zeros((count, width), f32)
    for pair in range(part // LOG_PAIR):
        cols = slice(pair * LOG_PAIR, (pair + 1) * LOG_PAIR)
        mixed, unused = pair_forward(query[:, cols], tk_ref[:, cols], tv_ref[:, cols], key_bias())
        a_cols = slice(3 * part + pair * LOG_PAIR, 3 * part + (pair + 1) * LOG_PAIR)
        branch += dnt(mixed.astype(low), block_of(gt_ref, a_cols))
    aimed_ref[...] = listed + branch
    part_ref[0] = branch.astype(low)
    swaps = [remote(part_ref.at[i], come_ref.at[i], tsends, trecvs, i, ways["y"]) for i in range(2)]
    swaps[0].start()

    whole(0, 4 * part)

    def project(index):
        here = span(index, 256)
        from_x = pl.ds(pl.multiple_of(y * rows + index * 256, 256), 256)
        first = x_ref[from_x, :].astype(f32) + vec_ref[2:3, :]
        for half in range(2):
            first += dnt(
                a_ref[here, half * part : (half + 1) * part],
                block_of(gs_ref.at[half], slice(3 * part, 4 * part)),
            )
        r1_ref[here, :] = first
        unit, unused = row_norm(first)
        normed = unit * vec_ref[3:4, :] + vec_ref[4:5, :]
        normed_ref[here, :] = normed.astype(low)
        nflip_ref[:, here] = flip(normed.astype(low))
        r2_ref[here, :] = normed + vec_ref[5:6, :]

    loop(rows // 256, project)

    def rise(piece):
        half, base = piece // 2, 4 * part + (piece % 2) * width

        def body(index):
            here = span(index, 256)
            cols = slice(piece * width, (piece + 1) * width)
            gate = dnn(normed_ref[here, :], block_of(gs_ref.at[half], slice(base, base + width)))
            gate += vec_ref[8 + piece : 9 + piece, :]
            share = normal_share(gate)
            u_ref[here, cols] = (gate * share).astype(low)
            slope_ref[here, cols] = (
                share + gate * (jnp.exp(-0.5 * gate * gate) * 0.3989422804014327)
            ).astype(low)

        loop(rows // 256, body)

    def fall(piece):
        half, base = piece // 2, 4 * part + (2 + piece % 2) * width

        def body(index):
            here = span(index, 256)
            r2_ref[here, :] += dnt(
                u_ref[here, piece * width : (piece + 1) * width],
                block_of(gs_ref.at[half], slice(base, base + width)),
            )

        loop(rows // 256, body)

    active = []

    def aim_rise(piece):
        base = 4 * part + piece * width
        gate = dnn(aim_normed.astype(low), block_of(gt_ref, slice(base, base + width)))
        gate += tvec_ref[pl.ds(8 + 2 * y + piece, 1), :]
        active.append((gate * normal_share(gate)).astype(low))

    def aim_fall(piece):
        base = 8 * part + piece * width
        return dnt(active[piece], block_of(gt_ref, slice(base, base + width)))

    whole(0, 6 * part)
    rise(0)
    rise(2)
    whole(1, 8 * part)
    swaps[0].wait()
    unit, unused = row_norm(aimed_ref[...] + come_ref[0].astype(f32) + tvec_ref[2:3, :])
    aim_normed = unit * tvec_ref[3:4, :] + tvec_ref[4:5, :]
    aim_rise(0)
    tick()
    aim_rise(1)
    whole(0, 8 * part)
    rise(1)
    rise(3)
    whole(1, 12 * part)
    feed = aim_fall(0) + aim_fall(1)
    part_ref[1] = feed.astype(low)
    swaps[1].start()
    aimed_ref[...] = aim_normed + feed + tvec_ref[5:6, :]
    whole(0, 10 * part)
    fall(0)
    fall(2)
    whole(0, 12 * part)
    fall(1)
    fall(3)
    swaps[1].wait()
    unit, unused = row_norm(aimed_ref[...] + come_ref[1].astype(f32))
    aimed_ref[...] = unit * tvec_ref[6:7, :] + tvec_ref[7:8, :]
    for unused in steps:
        pass
    for copy in started:
        copy.wait_send()
    wa_copy.wait()
    pl.semaphore_signal(free_x, inc=1, device_id=ways["x"], device_id_type=MESH)
    cot_copy.wait()

    def top(index):
        here = span(index, 256)
        row_at = lax.broadcasted_iota(jnp.int32, (256, places_ref.shape[1]), 0)
        pick = jnp.where(row_at + (y * rows + index * 256) == places_ref[0:1, :], 1.0, 0.0)
        times = jnp.sum(pick, -1, keepdims=True)
        aimed = jnp.dot(
            pick, aimed_ref[...], precision=lax.Precision.HIGHEST, preferred_element_type=f32
        ) / jnp.maximum(times, 1.0)
        unit, spread = row_norm(r2_ref[here, :])
        outcome = unit * vec_ref[6:7, :] + vec_ref[7:8, :]
        inner = jnp.sum(outcome * aimed, -1, keepdims=True)
        square_own = jnp.sum(outcome * outcome, -1, keepdims=True) + cosine_eps
        square_aim = jnp.sum(aimed * aimed, -1, keepdims=True) + cosine_eps
        scale = cosine_weight * times * lax.rsqrt(square_own) * lax.rsqrt(square_aim)
        grad = cot_ref[here, :].astype(f32) - scale * (aimed - outcome * (inner / square_own))
        cot_ref[here, :] = outcome.astype(low)
        sums_ref[6:7, :] += jnp.sum(grad * unit, 0, keepdims=True)
        sums_ref[7:8, :] += jnp.sum(grad, 0, keepdims=True)
        back = norm_pull(grad, unit, spread, vec_ref[6:7, :])
        r2_ref[here, :] = back
        back_low = back.astype(low)
        sums_ref[5:6, :] += jnp.sum(back_low.astype(f32), 0, keepdims=True)
        ga_ref[here, :] = back_low
        flip_ref[:, here] = flip(back_low)

    loop(rows // 256, top)
    keep(cot_ref, student_hbm.at[own])
    share = remote(cot_ref, student_hbm.at[own], ksends, krecvs, (2, 0), ways["y"])
    share.start()

    sum_sent = []
    cuts = [(i * part, (i + 1) * part) for i in (8, 9, 10, 11, 4, 5, 6, 7, 3, 0, 1, 2)]
    spared = 9
    spare_at = 6 * part

    def feed_cols(k):
        a, b = cuts[k]
        return pl.ds(a - 3 * part, b - a)

    def spare_cols(k):
        a, b = cuts[k]
        return pl.ds(spare_at + a, b - a)

    def given(k, xx):
        if k < spared:
            return one_ref.at[:, :, xx, :, feed_cols(k)]
        return gs_ref.at[:, :, xx, 0, :, spare_cols(k)]

    def ax_at(k):
        if k < spared:
            return gs_ref.at[:, :, k // 6, k // 3 % 2, :, pl.ds(k % 3 * part, part)]
        return gs_ref.at[:, :, 0, 1, :, spare_cols(k)]

    def h_at(k, yy, zz):
        return given(k, x).at[yy, zz]

    def zr_at(k, step):
        if k < spared:
            return zr_ref.at[step, :, :, feed_cols(k)]
        return gs_ref.at[:, step, 1, 1, :, spare_cols(k)]

    def wait_for(sem, amount):
        return lambda: pl.semaphore_wait(sem, amount)

    sum_begin, sums = sum_steps(
        cuts, given, ax_at, h_at, zr_at,
        {0: wait_for(free_x, 1), spared: wait_for(free_x, 1)}, {spared: wait_for(free_z, 3)},
        tot_ref, total_ref, yr_ref, fsends, frecvs, fzsends, fzrecvs, sum_sent,
    )
    blocks = []

    def share_block(value, half, k, closes):
        number = len(blocks)
        size = value.shape[1]
        slot = pl.ds((number % 6) * width, size)
        if number >= 2:
            settle(number - 2)
        gt_ref[:, :, :, :, slot] = value.astype(low).reshape(gt_ref.shape[:4] + (size,))
        if k < spared:
            target = one_ref.at[half, :, :, :, pl.ds(cuts[k][0] - 3 * part, size)]
        else:
            target = gs_ref.at[half, :, :, 0, :, spare_cols(k)]
        copy = remote(
            gt_ref.at[:, :, 1 - core, :, slot], target, gsends, grecvs, number, ways["twin"]
        )
        copy.start()
        blocks.append((copy, target, slot, range(k, k + size // part) if closes else ()))

    settled = set()

    def settle(number):
        if number in settled:
            return
        settled.add(number)
        copy, target, slot, closed = blocks[number]
        copy.wait()

        def add(zz, carry):
            target[zz] = (
                target[zz].astype(f32) + gt_ref[zz, :, core, :, slot].astype(f32)
            ).astype(low)
            return carry

        lax.fori_loop(0, 4, add, 0)
        for k in closed:
            sum_begin(k)

    def settle_all():
        for number in range(len(blocks)):
            settle(number)

    def down_grad(piece):
        cols = slice(piece * width, (piece + 1) * width)
        share_block(
            dnn(flip_ref[...], u_ref[:, cols]), piece // 2, 2 * (piece % 2), piece // 2 == 1
        )

    def up_grad(piece):
        cols = slice(piece * width, (piece + 1) * width)
        share_block(
            dnn(nflip_ref[...], slope_ref[:, cols]), piece // 2, 4 + 2 * (piece % 2),
            piece // 2 == 1,
        )

    def gate_pull(piece):
        half, base = piece // 2, 4 * part + (piece % 2) * width
        cols = slice(piece * width, (piece + 1) * width)

        def gate_back(index):
            here = span(index, 256)
            down = block_of(gs_ref.at[half], slice(base + 2 * width, base + 3 * width))
            gate_low = (dnn(ga_ref[here, :], down) * slope_ref[here, cols].astype(f32)).astype(low)
            slope_ref[here, cols] = gate_low
            sums_ref[8 + piece : 9 + piece, :] += jnp.sum(gate_low.astype(f32), 0, keepdims=True)
            r2_ref[here, :] += dnt(gate_low, block_of(gs_ref.at[half], slice(base, base + width)))

        loop(rows // 256, gate_back)

    def middle(index):
        here = span(index, 256)
        grad = r2_ref[here, :]
        unit, spread = row_norm(r1_ref[here, :])
        sums_ref[3:4, :] += jnp.sum(grad * unit, 0, keepdims=True)
        sums_ref[4:5, :] += jnp.sum(grad, 0, keepdims=True)
        back = norm_pull(grad, unit, spread, vec_ref[3:4, :])
        r1_ref[here, :] = back
        back_low = back.astype(low)
        sums_ref[2:3, :] += jnp.sum(back_low.astype(f32), 0, keepdims=True)
        bflip_ref[:, here] = flip(back_low)
        for half in range(2):
            cols = slice(half * part, (half + 1) * part)
            ga_ref[here, cols] = dnn(
                back_low, block_of(gs_ref.at[half], slice(3 * part, 4 * part))
            ).astype(low)

    def swap(which, pair):
        source, target = ((k_ref, tk_ref), (v_ref, tv_ref))[which]
        other_rows = pl.ds(pl.multiple_of((1 - y) * rows, rows), rows)
        return remote(
            source.at[other_rows, pl.ds(pair * LOG_PAIR, LOG_PAIR)],
            target.at[pl.ds(pair // 3 * rows, rows), pl.ds(pair % 3 * LOG_PAIR, LOG_PAIR)],
            ksends, krecvs, (which, pair), ways["y"],
        )

    def one_pair(pair):
        cols = slice(pair * LOG_PAIR, (pair + 1) * LOG_PAIR)

        def body(unused):
            query, grad_mixed = q_ref[:, cols], ga_ref[:, cols]
            sides = pair_back_rows(query, grad_mixed, a_ref[:, cols], log_ref[pair])
            grad_query = None
            for half in range(2):
                here = slice(half * rows, (half + 1) * rows)
                term, grad_keys, grad_values = pair_back_keys(
                    query, grad_mixed, sides, k_ref[here, cols], v_ref[here, cols],
                    key_bias()[here],
                )
                grad_query = term if grad_query is None else grad_query + term
                k_ref[here, cols] = grad_keys.astype(low)
                v_ref[here, cols] = grad_values.astype(low)
            q_ref[:, cols] = (grad_query.T * HDIM**-0.5).astype(low)

        loop(1, body)
        swap(0, pair).start()
        swap(1, pair).start()

    down_grad(0)
    down_grad(2)
    gate_pull(0)
    settle_all()
    gate_pull(2)
    down_grad(1)
    gate_pull(1)
    next(sums)
    down_grad(3)
    gate_pull(3)
    settle_all()
    loop(rows // 256, middle)
    for sem, peer in (
        [(free_x, ways["x"]), (free_twin, ways["twin"])] + [(free_z, peer) for peer in ways["z"]]
    ):
        pl.semaphore_signal(sem, inc=1, device_id=peer, device_id_type=MESH)
    wa_back = keep(wa_hbm, gs_ref.at[:, :, :, :, :, pl.ds(3 * part, 3 * part)])
    next(sums)
    flip_ref[...] = flip(x_ref[own, :])

    def out_grad(half):
        value = dnn(bflip_ref[...], a_ref[:, half * part : (half + 1) * part])
        share_block(value, half, 8, half == 1)

    def finish(half, index):
        cols = slice(half * part, (half + 1) * part)
        if index == 0:
            grad = q_ref[:, cols]
        else:
            grads, come = ((k_ref, tk_ref), (v_ref, tv_ref))[index - 1]
            for pair in range(3 * half, 3 * half + 3):
                swap(index - 1, pair).wait()
            grad = (
                grads[own, cols].astype(f32) + come[half * rows : (half + 1) * rows, :].astype(f32)
            ).astype(low)
            grads[own, cols] = grad
        if half == 0 and index == 0:
            wa_back.wait()
            pl.semaphore_wait(free_twin, 1)
        share_block(dnn(flip_ref[...], grad), half, spared + index, half == 1)
        r1_ref[...] += dnt(
            grad, block_of(gs_ref.at[half], slice((3 + index) * part, (4 + index) * part))
        )

    between = (
        (lambda: up_grad(0), lambda: up_grad(2)),
        (settle_all, lambda: next(sums), lambda: up_grad(1)),
        (lambda: up_grad(3), lambda: next(sums)),
        (settle_all, lambda: next(sums), lambda: out_grad(0), lambda: out_grad(1)),
        (settle_all, lambda: next(sums), lambda: finish(0, 0)),
        (lambda: next(sums), lambda: finish(0, 1), lambda: finish(0, 2)),
    )
    for pair, works in enumerate(between):
        one_pair(pair)
        for work in works:
            work()
    for index in range(3):
        finish(1, index)
        settle_all()
        if index == 0:
            next(sums)
    keep(r1_ref, input_hbm.at[own])
    ga_ref[...] = r1_ref[...].astype(low)
    join = remote(ga_ref, normed_ref, ksends, krecvs, (2, 1), ways["y"])
    join.start()
    line = lax.broadcasted_iota(jnp.int32, sums_ref.shape, 0)
    vector_grad = jnp.where(
        line == 0,
        jnp.sum(q_ref[...].astype(f32), 0, keepdims=True),
        jnp.where(line == 1, jnp.sum(v_ref[own, :].astype(f32), 0, keepdims=True), sums_ref[...]),
    )
    vector_grad = jnp.concatenate(
        [vector_grad, jnp.zeros((16 - vector_grad.shape[0], width), f32)], 0
    )
    vector_total = []
    vector_steps = shared_steps(
        vector_grad, vector_total,
        lambda i: vmine_ref.at[i],
        lambda i: vcome_ref.at[i],
        vsends, vrecvs,
    )
    next(vector_steps)
    other = pl.ds(pl.multiple_of((1 - y) * rows, rows), rows)
    for number, unused in enumerate(sums):
        next(vector_steps, None)
        if number == 3:
            join.wait()
            r2_ref[...] = normed_ref[...].astype(f32)
            keep(r2_ref, input_hbm.at[other])
    for unused in vector_steps:
        pass
    vector_ref[...] = vector_total[0][: vector_ref.shape[0]]
    for copy in kept:
        if all(copy is not seen for seen in (cot_copy, x_copy, tx_copy, wa_copy, wa_back)):
            copy.wait()
    for copy in sum_sent:
        copy.wait_send()
    share.wait_send()
    rest = student_hbm.at[other]
    remote(rest, rest, ksends, krecvs, (2, 0), ways["y"]).wait_recv()


def first_call(x, tx, cot, vec, tvec, lengths, masked, weights, teacher, number):
    length, width = x.shape
    rows, part, hidden = length // 2, width // 2, 4 * width
    lines = weights[0].shape[1]
    wide = 4 * part + 2 * weights[2].shape[1]
    chunks = tuple((which, a * part, b * part, over_x) for which, a, b, over_x in GATHER)
    count = len(chunks)
    listed = masked.shape[1]
    pairs = width // LOG_PAIR
    sem = pltpu.SemaphoreType.DMA
    vm = pltpu.VMEM
    return pl.pallas_call(
        partial(first_kernel, chunks),
        name="gather_forward",
        out_shape=[
            shape_of(2, 4, 2, 2, lines, 3 * part, kind=low),
            shape_of(length, width),
            shape_of(length, width, kind=low),
            shape_of(lines, wide),
            shape_of(12, width),
        ],
        in_specs=[ANY_SPEC] * 3 + [VMEM_SPEC] * 12,
        out_specs=[ANY_SPEC] * 3 + [VMEM_SPEC] * 2,
        scratch_shapes=[
            vm((12, width), f32),
            vm((12, width), f32),
            vm((12, width), f32),
            vm((length, width), low),
            vm((length, width), low),
            vm((2, 4, 2, 2, lines, wide), low),
            vm((4, 2, 2, lines, wide), low),
            vm((lines, wide), low),
            vm((lines, wide), low),
            vm((rows, width), low),
            vm((length, width), low),
            vm((length, width), low),
            vm((rows, width), low),
            vm((pairs, rows, LOG_PAIR), f32),
            vm((length, part), low),
            vm((length, part), low),
            vm((2, listed, width), low),
            vm((2, listed, width), low),
            vm((listed, width), f32),
            vm((4, 16, width), f32),
            vm((6, 16, width), f32),
            vm((rows, width), f32),
            vm((rows, width), low),
            vm((rows, hidden), low),
            vm((rows, hidden), low),
            vm((rows, width), f32),
            vm((rows, width), low),
            vm((width, rows), low),
            vm((width, rows), low),
            vm((width, rows), low),
            vm((rows, width), low),
            vm((2, 4, 2, lines, wide - 3 * part), low),
            vm((3, 2, lines, wide - 3 * part), low),
            vm((2, lines, wide), low),
            vm((lines, wide), low),
            sem((count,)), sem((count, 3)), sem((count, 3)), sem((count, 7)), sem((count, 7)),
            sem((2,)), sem((2,)), sem((16,)), sem((16,)), sem((10,)),
            sem((12, 2)), sem((12, 2)), sem((12, 3)), sem((12, 3)), sem((3, pairs)), sem((3, pairs)),
            sem((6,)), sem((6,)),
            pltpu.SemaphoreType.REGULAR, pltpu.SemaphoreType.REGULAR, pltpu.SemaphoreType.REGULAR,
        ],
        compiler_params=pltpu.CompilerParams(
            vmem_limit_bytes=FIRST_LIMIT, collective_id=number, has_side_effects=True
        ),
    )(x, tx, cot, vec, tvec, lengths, masked, *weights, *teacher)


def matrices(grad_ref, groups):
    attn, out, up, down = range(4)
    plan = [(0, attn, 0), (1, attn, 1), (2, attn, 2), (3, out, None), (4, up, None), (5, down, None)]
    at = 0
    for index, which, slot in plan:
        refs = [group[which] if slot is None else group[which].at[slot] for group in groups]
        size = refs[0].shape[-1]
        yield index, grad_ref[:, at : at + size], refs
        at += size


def norm_kernel(grad_ref, *rest):
    weights, firsts, seconds = rest[0:4], rest[4:8], rest[8:12]
    norm_o, terms_ref, sends, recvs = rest[12:]
    at, y, z, x, core = place()
    others = terms_ref.shape[0] - 1
    me = 2 * at + y

    def peer(step):
        there = (me + step) % (others + 1)
        return there // 2, there % 2

    barrier = pltpu.get_barrier_semaphore()

    def call(step, carry):
        pl.semaphore_signal(barrier, inc=1, device_id=peer(step), device_id_type=MESH)
        return carry

    lax.fori_loop(1, others + 1, call, 0)
    lane = lane_index((8, LOG_PAIR))
    row = lax.broadcasted_iota(jnp.int32, (8, LOG_PAIR), 0)
    squares = jnp.zeros((8, LOG_PAIR), f32)
    for index, grad, (w, first, second) in matrices(grad_ref, (weights, firsts, seconds)):
        unused, unused_too, step = adam_step(grad, first[...], second[...])
        for line, value in ((0, w[...]), (1, step + decay_rate * w[...])):
            total = jnp.sum(jnp.sum(value * value, -1, keepdims=True), 0, keepdims=True)
            squares = jnp.where((row == line) & (lane == index), total, squares)
    terms_ref[me] = squares
    pl.semaphore_wait(barrier, others)

    def send(step):
        return remote(terms_ref.at[me], terms_ref.at[me], sends, recvs, step - 1, peer(step))

    def begin(step, carry):
        send(step).start()
        return carry

    def landed(step, carry):
        came = terms_ref.at[(me + others + 1 - step) % (others + 1)]
        remote(came, came, sends, recvs, step - 1, peer(step)).wait_recv()
        return carry

    def left(step, carry):
        send(step).wait_send()
        return carry

    lax.fori_loop(1, others + 1, begin, 0)
    lax.fori_loop(1, others + 1, landed, 0)
    norms = jnp.sqrt(jnp.sum(terms_ref[...], 0))
    norm_o[...] = jnp.where(row == 2, norms[0:1, :] / norms[1:2, :], norms)
    lax.fori_loop(1, others + 1, left, 0)


def update_kernel(
    grad_ref, norm_ref, total_ref, vec_ref, vm_ref, vs_ref, student_hbm, input_hbm, *rest
):
    groups = [rest[i : i + 4] for i in range(0, 24, 4)]
    vm_o, vs_o, vec_o, norm_o, ratio_o, student_o, input_o = rest[24:31]
    student_ref, input_ref, copy_sem = rest[31:]
    passed = [(student_hbm, student_ref, student_o), (input_hbm, input_ref, input_o)]
    come = [pltpu.make_async_copy(a, b, copy_sem.at[i]) for i, (a, b, c) in enumerate(passed)]
    leave = [pltpu.make_async_copy(b, c, copy_sem.at[i]) for i, (a, b, c) in enumerate(passed)]
    for copy in come:
        copy.start()
    for index, grad, refs in matrices(grad_ref, groups):
        w, first, second, w_o, first_o, second_o = refs
        first_new, second_new, step = adam_step(grad, first[...], second[...])
        first_o[...] = first_new
        second_o[...] = second_new
        weight = w[...]
        ratio = norm_ref[2:3, index : index + 1]
        w_o[...] = weight - matrix_rate * ratio * (step + decay_rate * weight)
        if index == 3:
            for one, copy in zip(come, leave):
                one.wait()
                copy.start()
    width = total_ref.shape[1]
    for index in range(total_ref.shape[0]):
        here = pl.ds(index * width, width)
        first_new, second_new, step = adam_step(
            total_ref[index : index + 1, :],
            vm_ref[here].reshape(1, width),
            vs_ref[here].reshape(1, width),
        )
        vm_o[here] = first_new.reshape(width)
        vs_o[here] = second_new.reshape(width)
        vec_o[here] = vec_ref[here] - vector_rate * step.reshape(width)
    norm_o[...] = norm_ref[0:2, 0:6]
    ratio_o[...] = norm_ref[2:3, 0:6].reshape(6)
    for copy in leave:
        copy.wait()


def norm_call(grad, weights, firsts, seconds, number):
    sem = pltpu.SemaphoreType.DMA
    devices = lax.axis_size("dp") * lax.axis_size("mp")
    return pl.pallas_call(
        norm_kernel,
        name="norms",
        out_shape=shape_of(8, LOG_PAIR),
        in_specs=[VMEM_SPEC] * 13,
        out_specs=VMEM_SPEC,
        scratch_shapes=[
            pltpu.VMEM((devices, 8, LOG_PAIR), f32), sem((devices - 1,)), sem((devices - 1,))
        ],
        compiler_params=pltpu.CompilerParams(
            vmem_limit_bytes=LIMIT, collective_id=number, has_side_effects=True
        ),
    )(grad, *weights, *firsts, *seconds)


def update_call(grad, norms, total, vec, vm, vs, student, input_grad, weights, firsts, seconds):
    outs = [shape_of(*value.shape) for group in (weights, firsts, seconds) for value in group]
    outs += [shape_of(*vec.shape)] * 3 + [shape_of(2, 6), shape_of(6)]
    count = len(outs)
    outs += [shape_of(*student.shape, kind=low), shape_of(*input_grad.shape)]
    return pl.pallas_call(
        update_kernel,
        name="update",
        out_shape=outs,
        in_specs=[VMEM_SPEC] * 6 + [ANY_SPEC] * 2 + [VMEM_SPEC] * 12,
        out_specs=[VMEM_SPEC] * count + [ANY_SPEC] * 2,
        scratch_shapes=[
            pltpu.VMEM(student.shape, low),
            pltpu.VMEM(input_grad.shape, f32),
            pltpu.SemaphoreType.DMA((2,)),
        ],
        compiler_params=pltpu.CompilerParams(vmem_limit_bytes=LIMIT),
    )(grad, norms, total, vec, vm, vs, student, input_grad, *weights, *firsts, *seconds)


def split_kernels(
    tokens,
    teacher_tokens,
    cotangent,
    lengths,
    masked,
    attn_weight,
    out_weight,
    up_weight,
    down_weight,
    attn_first,
    out_first,
    up_first,
    down_first,
    attn_second,
    out_second,
    up_second,
    down_second,
    vectors,
    vector_first,
    vector_second,
    teacher_attn,
    teacher_out,
    teacher_up,
    teacher_down,
    teacher_vectors,
):
    def upright(group):
        return (group[0], group[1].T, group[2], group[3].T)

    weights = upright((attn_weight, out_weight, up_weight, down_weight))
    unused_wa, input_grad, student, grad, total = first_call(
        tokens[0],
        teacher_tokens[0],
        cotangent[0],
        vectors,
        teacher_vectors,
        lengths.reshape(1, 1),
        masked,
        weights,
        upright((teacher_attn, teacher_out, teacher_up, teacher_down)),
        0,
    )
    states = (
        weights,
        upright((attn_first, out_first, up_first, down_first)),
        upright((attn_second, out_second, up_second, down_second)),
    )
    norms = norm_call(grad, *states, 1)
    outs = update_call(
        grad, norms, total, vectors, vector_first, vector_second, student, input_grad, *states
    )
    return (
        outs[17][None],
        outs[18][None],
        *upright(outs[0:4]),
        *upright(outs[4:8]),
        *upright(outs[8:12]),
        *outs[12:17],
    )


def solution(mesh):
    local = split_kernels if dict(mesh.shape) == {"dp": 16, "mp": 2} else split_rows
    return jax.shard_map(
        local,
        mesh=mesh,
        in_specs=(
            P("dp", None, None),
            P("dp", None, None),
            P("dp", None, None),
            P("dp"),
            P("dp", None),
            P(None, "dp", "mp"),
            P("mp", "dp"),
            P("dp", "mp"),
            P("mp", "dp"),
            P(None, "dp", "mp"),
            P("mp", "dp"),
            P("dp", "mp"),
            P("mp", "dp"),
            P(None, "dp", "mp"),
            P("mp", "dp"),
            P("dp", "mp"),
            P("mp", "dp"),
            P(),
            P(),
            P(),
            P(None, "dp", "mp"),
            P("mp", "dp"),
            P("dp", "mp"),
            P("mp", "dp"),
            P(),
        ),
        out_specs=(
            P("dp", None, None),
            P("dp", None, None),
            P(None, "dp", "mp"),
            P("mp", "dp"),
            P("dp", "mp"),
            P("mp", "dp"),
            P(None, "dp", "mp"),
            P("mp", "dp"),
            P("dp", "mp"),
            P("mp", "dp"),
            P(None, "dp", "mp"),
            P("mp", "dp"),
            P("dp", "mp"),
            P("mp", "dp"),
            P(),
            P(),
            P(),
            P(),
            P(),
        ),
        check_vma=False,
    )
```
